32 devices in a mesh: view: 4 (over z), tile: 8 (over y, x, core).
Axes of the slice: x: 2, y: 2, z: 4, core: 2. Of those that a mesh axis runs over, the one named last changes fastest.
Arguments:
- params: float32 [59, 262144], P(None, ('view', 'tile')), may hold values from -16 to 16, as said below
- send_list: int32 [32, 8192], P(('view', 'tile')), may hold values from 0 to 8191, as said below
- send_counts: int32 [32, 32], P(('view', 'tile')), may hold values from 0 to 256, as said below
- camera: float32 [8, 6], replicated, may hold values from -0.2 to 0.2
- ground_truth: float32 [8, 3, 128, 512], P('view', None, 'tile'), may hold values from 0 to 1
- tile_lists: int32 [8, 8, 32, 128], P('view', 'tile'), may hold values from 0 to 8191, as said below
- list_lengths: int32 [8, 8, 32], P('view', 'tile'), may hold values from 0 to 128, as said below
Outputs:
- gradients: float32 [59, 262144], P(None, ('view', 'tile'))
The draws below stay inside these ranges and needn't reach their ends.
Inputs may be any that keep to these rules, and one draw needn't show every extreme that they name: `params`: every Gaussian lies at camera depth 1 or more in every view. `send_list`: each row is an ordering of 0 to 8191. `send_counts`: each row sums to at most 8192; some destination gets 256 from every source. `tile_lists`: live entries name slots s * 256 + k with k < send_counts[s, d] of the tile's destination d; entries past the length name any slot. `list_lengths`: some tile's list is full in every draw.
All inputs are finite; a program needn't handle non-finite values.
Results may differ from the reference program's by a relative error of at most 0.0003.
Values sent between devices are 32-bit elements; how exact they have to be, the bound alone decides.
No kernel may reach another device: no remote copies, remote signals or barrier semaphores. Data moves between devices by JAX's collectives and lax.ppermute only.
A program may use at most 128 MiB of HBM per device.

```python
import jax
import jax.numpy as jnp
import numpy as np
from jax import lax

TILE = 16
VIEWS_DEV = 2
PARAMS = 59
TILE_COLS = 32
LIST = 128
G_DEV = 8192
VIEWS = 8
CAP = 256
HEIGHT = 128
WIDTH = 512
N_VIEW = 4
N_TILE = 8
DEVICES = 32


FOCAL = 1000.0


def matrix_product_drawn(left_side, right_side):
    return [[left_side[row_idx][0] * right_side[0][col_idx] + left_side[row_idx][1] * right_side[1][col_idx] + left_side[row_idx][2] * right_side[2][col_idx] for col_idx in range(3)] for row_idx in range(3)]


def rotation_drawn(angles):
    cos_a, sin_a = (jnp.cos(angles[0]), jnp.sin(angles[0]))
    cos_b, sin_b = (jnp.cos(angles[1]), jnp.sin(angles[1]))
    cos_c, sin_c = (jnp.cos(angles[2]), jnp.sin(angles[2]))
    about_x = [[1.0, 0.0, 0.0], [0.0, cos_a, -sin_a], [0.0, sin_a, cos_a]]
    about_y = [[cos_b, 0.0, sin_b], [0.0, 1.0, 0.0], [-sin_b, 0.0, cos_b]]
    about_z = [[cos_c, -sin_c, 0.0], [sin_c, cos_c, 0.0], [0.0, 0.0, 1.0]]
    return matrix_product_drawn(about_z, matrix_product_drawn(about_y, about_x))


def camera_values(key):
    cam_key = jax.random.fold_in(key, 11)
    angle_key, move_key = jax.random.split(cam_key)
    angles = jax.random.uniform(angle_key, (VIEWS, 3), jnp.float32, -0.03, 0.03)
    moves = jax.random.uniform(move_key, (VIEWS, 3), jnp.float32, -0.2, 0.2)
    return jnp.concatenate([angles, moves], axis=1)


def slot_plan(key):
    plan_key = jax.random.fold_in(key, 23)
    subkeys = jax.random.split(plan_key, 8)
    heavy_dest = jax.random.randint(subkeys[0], (DEVICES,), 0, 4) == 3
    load_level = jnp.where(heavy_dest, 4, 1).astype(jnp.int32)
    jitter = jax.random.randint(subkeys[1], (DEVICES, DEVICES), 0, CAP // 16 + 1)
    counts = load_level[None, :] * CAP // 4 - jitter
    full_dest = jax.random.randint(subkeys[2], (), 0, DEVICES)
    counts = jnp.where(jnp.arange(DEVICES)[None, :] == full_dest, CAP, counts).astype(jnp.int32)
    orders = jax.vmap(lambda sub_key: jax.random.permutation(sub_key, G_DEV))(jax.random.split(subkeys[3], DEVICES))
    home_cols = jax.random.randint(subkeys[4], (DEVICES, G_DEV), 0, TILE_COLS)
    depth_rank = jax.vmap(lambda sub_key: jax.random.permutation(sub_key, G_DEV))(jax.random.split(subkeys[5], DEVICES))
    moved_by = jax.random.randint(subkeys[6], (DEVICES, G_DEV), -1, 2) * (jax.random.randint(subkeys[7], (DEVICES, G_DEV), 0, 4) == 0).astype(jnp.int32)
    home_cols_two = jnp.clip(home_cols + moved_by, 0, TILE_COLS - 1)
    return (counts, orders.astype(jnp.int32), home_cols.astype(jnp.int32), home_cols_two.astype(jnp.int32), depth_rank.astype(jnp.int32))


def list_plan(key):
    counts, orders, home_cols, home_cols_two, depth_rank = slot_plan(key)
    limit_key = jax.random.fold_in(key, 29)
    limits = jax.random.randint(limit_key, (DEVICES, 2, TILE_COLS), LIST // 2, LIST + 1).astype(jnp.int32)
    is_full = jnp.all(counts == CAP, axis=0)
    limits = jnp.where(is_full[:, None, None], LIST, limits).astype(jnp.int32)
    slot_ids = jnp.arange(G_DEV, dtype=jnp.int32)
    col_ids = jnp.arange(TILE_COLS, dtype=jnp.int32)
    list_ids = jnp.arange(LIST, dtype=jnp.int32)

    def per_dest(target_counts, home_first, home_second, rank_row, limit_rows):
        is_live = slot_ids % CAP < target_counts[slot_ids // CAP]

        def per_view(home_row, limit_row):
            placed = jnp.where(is_live, home_row, TILE_COLS)
            order_key = placed * G_DEV + rank_row
            sequence = jnp.argsort(order_key)
            per_col = jnp.sum((placed[None, :] == col_ids[:, None]).astype(jnp.int32), axis=1)
            col_start = jnp.cumsum(per_col) - per_col
            spot_ids = jnp.minimum(col_start[:, None] + list_ids[None, :], G_DEV - 1)
            return (sequence[spot_ids].astype(jnp.int32), jnp.minimum(jnp.minimum(per_col, LIST), limit_row).astype(jnp.int32))
        first_lists, first_lengths = per_view(home_first, limit_rows[0])
        second_lists, second_lengths = per_view(home_second, limit_rows[1])
        return (jnp.stack([first_lists, second_lists]), jnp.stack([first_lengths, second_lengths]))
    all_lists, all_lengths = jax.vmap(per_dest)(counts.T, home_cols, home_cols_two, depth_rank, limits)
    all_lists = all_lists.reshape(N_VIEW, N_TILE, VIEWS_DEV, TILE_COLS, LIST).transpose(0, 2, 1, 3, 4).reshape(VIEWS, N_TILE, TILE_COLS, LIST)
    all_lengths = all_lengths.reshape(N_VIEW, N_TILE, VIEWS_DEV, TILE_COLS).transpose(0, 2, 1, 3).reshape(VIEWS, N_TILE, TILE_COLS)
    return (all_lists, all_lengths)


def draw_camera(key, part):
    shared = camera_values(key)
    key = jax.random.fold_in(key, 1)
    return shared


def draw_send_counts(key, part):
    shared = slot_plan(key)[0]
    key = jax.random.fold_in(key, 2)
    return shared


def draw_send_list(key, part):
    shared = slot_plan(key)[1]
    key = jax.random.fold_in(key, 4)
    return shared


def draw_tile_lists(key, part):
    planned = list_plan(key)
    key = jax.random.fold_in(key, 5)
    return planned[0]


def draw_list_lengths(key, part):
    planned = list_plan(key)
    key = jax.random.fold_in(key, 6)
    return planned[1]


def draw_params(key, part):
    counts, orders, home_cols, home_cols_two, depth_rank = slot_plan(key)
    cams = camera_values(key)
    key = jax.random.fold_in(key, 3)
    subkeys = jax.random.split(key, 12)
    position = jnp.argsort(orders, axis=1).astype(jnp.int32)
    run_ends = jnp.cumsum(counts, axis=1)
    run_starts = run_ends - counts
    target = jax.vmap(lambda end_row, pos_row: jnp.searchsorted(end_row, pos_row, side='right'))(run_ends, position).astype(jnp.int32)
    is_sent = target < DEVICES
    clipped = jnp.minimum(target, DEVICES - 1)
    inside_slot = position - jnp.take_along_axis(run_starts, clipped, axis=1)
    source_ids = jnp.arange(DEVICES, dtype=jnp.int32)[:, None]
    slot_index = jnp.clip(source_ids * CAP + inside_slot, 0, G_DEV - 1)
    home_sent = home_cols[clipped, slot_index]
    rank_sent = depth_rank[clipped, slot_index]
    random_dest = jax.random.randint(subkeys[0], (DEVICES, G_DEV), 0, DEVICES)
    random_col = jax.random.randint(subkeys[1], (DEVICES, G_DEV), 0, TILE_COLS)
    random_rank = jax.random.randint(subkeys[2], (DEVICES, G_DEV), 0, G_DEV)
    dest_eff = jnp.where(is_sent, clipped, random_dest)
    col_eff = jnp.where(is_sent, home_sent, random_col)
    rank_eff = jnp.where(is_sent, rank_sent, random_rank)
    offset_u = jax.random.uniform(subkeys[3], (DEVICES, G_DEV), jnp.float32, -2.0, TILE + 2.0)
    offset_v = jax.random.uniform(subkeys[4], (DEVICES, G_DEV), jnp.float32, -2.0, TILE + 2.0)
    pix_u = (col_eff * TILE).astype(jnp.float32) + offset_u
    pix_v = (dest_eff % N_TILE * TILE).astype(jnp.float32) + offset_v
    depth_val = 3.0 + 9.0 * (rank_eff.astype(jnp.float32) + jax.random.uniform(subkeys[5], (DEVICES, G_DEV), jnp.float32)) / G_DEV
    cam_rows = cams[VIEWS_DEV * (dest_eff // N_TILE)]
    cam_rot = rotation_drawn([cam_rows[..., 0], cam_rows[..., 1], cam_rows[..., 2]])
    relative = [(pix_u - WIDTH / 2.0) * depth_val / FOCAL - cam_rows[..., 3], (pix_v - HEIGHT / 2.0) * depth_val / FOCAL - cam_rows[..., 4], depth_val - cam_rows[..., 5]]
    world = [cam_rot[0][col_idx] * relative[0] + cam_rot[1][col_idx] * relative[1] + cam_rot[2][col_idx] * relative[2] for col_idx in range(3)]
    log_scales = jax.random.uniform(subkeys[6], (3, DEVICES, G_DEV), jnp.float32, -5.5, -3.9)
    quat_w = jax.random.uniform(subkeys[7], (1, DEVICES, G_DEV), jnp.float32, 0.5, 1.5)
    quat_rest = jax.random.uniform(subkeys[8], (3, DEVICES, G_DEV), jnp.float32, -1.0, 1.0)
    opacity_logit = jax.random.uniform(subkeys[9], (1, DEVICES, G_DEV), jnp.float32, -4.5, -1.5)
    colour_dc = jax.random.truncated_normal(subkeys[10], -2.5, 2.5, (3, 1, DEVICES, G_DEV), jnp.float32)
    colour_rest = 0.3 * jax.random.truncated_normal(subkeys[11], -2.5, 2.5, (3, 15, DEVICES, G_DEV), jnp.float32)
    sh_coeffs = jnp.concatenate([colour_dc, colour_rest], axis=1).reshape(48, DEVICES, G_DEV)
    stacked = jnp.concatenate([jnp.stack(world), log_scales, quat_w, quat_rest, opacity_logit, sh_coeffs], axis=0)
    return stacked.reshape(PARAMS, DEVICES * G_DEV).astype(jnp.float32)


def block_levels(rng, shape, cuts, least, top_value):
    def one(dim, parts):
        steps = jax.random.uniform(jax.random.fold_in(jax.random.fold_in(rng, 6), dim), (parts,), jnp.float32, least / len(cuts), top_value / len(cuts))
        return jnp.repeat(jnp.exp(steps), shape[dim] // parts).reshape((-1,) + (1,) * (len(shape) - dim - 1))

    gain = one(*cuts[0])
    for cut in cuts[1:]:
        gain = gain * one(*cut)
    return gain


def setup_inputs(seed: int = 0) -> dict:
    key_of = jax.random.split(jax.random.key(seed), 8)
    return {
        "params": draw_params(jax.random.fold_in(key_of[7], 71), 0),
        "send_list": draw_send_list(jax.random.fold_in(key_of[7], 71), 0),
        "send_counts": draw_send_counts(jax.random.fold_in(key_of[7], 71), 0),
        "camera": draw_camera(jax.random.fold_in(key_of[7], 71), 0),
        "ground_truth": jnp.clip(1.0 * jax.random.uniform(key_of[4], (VIEWS, 3, HEIGHT, WIDTH), jnp.float32) ** block_levels(key_of[4], (VIEWS, 3, HEIGHT, WIDTH), ((0, 4), (2, 8)), -0.2, 0.2), 0.0, 1.0),
        "tile_lists": draw_tile_lists(jax.random.fold_in(key_of[7], 71), 0),
        "list_lengths": draw_list_lengths(jax.random.fold_in(key_of[7], 71), 0),
    }


FOCAL = 1000.0
LOW_PASS = 0.3
SSIM_SHARE = 0.2
SMOOTH_EPS = 1e-06
SSIM_ONE = 0.0001
SSIM_TWO = 0.0009
HARMONIC_ZERO = 0.28209479177387814
HARMONIC_ONE = 0.4886025119029199
HARMONIC_TWO = (1.0925484305920792, -1.0925484305920792, 0.31539156525252005, -1.0925484305920792, 0.5462742152960396)
HARMONIC_THREE = (-0.5900435899266435, 2.890611442640554, -0.4570457994644658, 0.3731763325901154, -0.4570457994644658, 1.445305721320277, -0.5900435899266435)

def window_taps():
    offsets_np = np.arange(11) - 5.0
    weights = np.exp(-offsets_np * offsets_np / 4.5)
    weights = weights / weights.sum()
    return [float(weight) for weight in weights]

def matrix_product(left_side, right_side):
    return [[left_side[row_idx][0] * right_side[0][col_idx] + left_side[row_idx][1] * right_side[1][col_idx] + left_side[row_idx][2] * right_side[2][col_idx] for col_idx in range(3)] for row_idx in range(3)]

def rotation(angles):
    cos_a, sin_a = (jnp.cos(angles[0]), jnp.sin(angles[0]))
    cos_b, sin_b = (jnp.cos(angles[1]), jnp.sin(angles[1]))
    cos_c, sin_c = (jnp.cos(angles[2]), jnp.sin(angles[2]))
    about_x = [[1.0, 0.0, 0.0], [0.0, cos_a, -sin_a], [0.0, sin_a, cos_a]]
    about_y = [[cos_b, 0.0, sin_b], [0.0, 1.0, 0.0], [-sin_b, 0.0, cos_b]]
    about_z = [[cos_c, -sin_c, 0.0], [sin_c, cos_c, 0.0], [0.0, 0.0, 1.0]]
    return matrix_product(about_z, matrix_product(about_y, about_x))

def harmonics(dir_x, dir_y, dir_z):
    sq_x, sq_y, sq_z = (dir_x * dir_x, dir_y * dir_y, dir_z * dir_z)
    prod_xy, prod_yz, prod_xz = (dir_x * dir_y, dir_y * dir_z, dir_x * dir_z)
    return [HARMONIC_ZERO + 0.0 * dir_x, -HARMONIC_ONE * dir_y, HARMONIC_ONE * dir_z, -HARMONIC_ONE * dir_x, HARMONIC_TWO[0] * prod_xy, HARMONIC_TWO[1] * prod_yz, HARMONIC_TWO[2] * (2.0 * sq_z - sq_x - sq_y), HARMONIC_TWO[3] * prod_xz, HARMONIC_TWO[4] * (sq_x - sq_y), HARMONIC_THREE[0] * dir_y * (3.0 * sq_x - sq_y), HARMONIC_THREE[1] * prod_xy * dir_z, HARMONIC_THREE[2] * dir_y * (4.0 * sq_z - sq_x - sq_y), HARMONIC_THREE[3] * dir_z * (2.0 * sq_z - 3.0 * sq_x - 3.0 * sq_y), HARMONIC_THREE[4] * dir_x * (4.0 * sq_z - sq_x - sq_y), HARMONIC_THREE[5] * dir_z * (sq_x - sq_y), HARMONIC_THREE[6] * dir_x * (sq_x - 3.0 * sq_y)]

def project(gaussians, camera_row, image_width, image_height):
    mean_x, mean_y, mean_z = (gaussians[0], gaussians[1], gaussians[2])
    scales = [jnp.exp(gaussians[3 + axis_num]) for axis_num in range(3)]
    quat_norm = jnp.sqrt(gaussians[6] * gaussians[6] + gaussians[7] * gaussians[7] + gaussians[8] * gaussians[8] + gaussians[9] * gaussians[9])
    quat_w, quat_x, quat_y, quat_z = (gaussians[6] / quat_norm, gaussians[7] / quat_norm, gaussians[8] / quat_norm, gaussians[9] / quat_norm)
    quat_rot = [[1.0 - 2.0 * (quat_y * quat_y + quat_z * quat_z), 2.0 * (quat_x * quat_y - quat_w * quat_z), 2.0 * (quat_x * quat_z + quat_w * quat_y)], [2.0 * (quat_x * quat_y + quat_w * quat_z), 1.0 - 2.0 * (quat_x * quat_x + quat_z * quat_z), 2.0 * (quat_y * quat_z - quat_w * quat_x)], [2.0 * (quat_x * quat_z - quat_w * quat_y), 2.0 * (quat_y * quat_z + quat_w * quat_x), 1.0 - 2.0 * (quat_x * quat_x + quat_y * quat_y)]]
    cam_rot = rotation(camera_row[0:3])
    translation = camera_row[3:6]
    point = [cam_rot[row_idx][0] * mean_x + cam_rot[row_idx][1] * mean_y + cam_rot[row_idx][2] * mean_z + translation[row_idx] for row_idx in range(3)]
    rotated = matrix_product(cam_rot, quat_rot)
    spread = [[rotated[row_idx][col_idx] * scales[col_idx] for col_idx in range(3)] for row_idx in range(3)]
    inv_depth = 1.0 / point[2]
    jac_xx = FOCAL * inv_depth
    jac_xz = -FOCAL * point[0] * inv_depth * inv_depth
    jac_yz = -FOCAL * point[1] * inv_depth * inv_depth
    proj_x = [jac_xx * spread[0][col_idx] + jac_xz * spread[2][col_idx] for col_idx in range(3)]
    proj_y = [jac_xx * spread[1][col_idx] + jac_yz * spread[2][col_idx] for col_idx in range(3)]
    cov_xx = proj_x[0] * proj_x[0] + proj_x[1] * proj_x[1] + proj_x[2] * proj_x[2] + LOW_PASS
    cov_xy = proj_x[0] * proj_y[0] + proj_x[1] * proj_y[1] + proj_x[2] * proj_y[2]
    cov_yy = proj_y[0] * proj_y[0] + proj_y[1] * proj_y[1] + proj_y[2] * proj_y[2] + LOW_PASS
    determinant = cov_xx * cov_yy - cov_xy * cov_xy
    centre_u = FOCAL * point[0] * inv_depth + image_width / 2.0
    centre_v = FOCAL * point[1] * inv_depth + image_height / 2.0
    opacity = 0.99 * jax.nn.sigmoid(gaussians[10])
    anchor = [-(cam_rot[0][col_idx] * translation[0] + cam_rot[1][col_idx] * translation[1] + cam_rot[2][col_idx] * translation[2]) for col_idx in range(3)]
    ray_x, ray_y, ray_z = (mean_x - anchor[0], mean_y - anchor[1], mean_z - anchor[2])
    ray_len = jnp.sqrt(ray_x * ray_x + ray_y * ray_y + ray_z * ray_z)
    basis_list = harmonics(ray_x / ray_len, ray_y / ray_len, ray_z / ray_len)
    colours = []
    for channel in range(3):
        summed = 0.5 + 0.0 * mean_x
        for harmonic in range(16):
            summed = summed + basis_list[harmonic] * gaussians[11 + 16 * channel + harmonic]
        colours.append(summed)
    return jnp.stack([centre_u, centre_v, cov_yy / determinant, -cov_xy / determinant, cov_xx / determinant, opacity] + colours)

def composite(pieces, lengths, columns, tile_row, start_at, span_len):
    pieces = lax.slice_in_dim(pieces, start_at, start_at + span_len, axis=2)
    pixel_ids = jnp.arange(TILE * TILE, dtype=jnp.int32)
    pix_x = (columns[:, None] * TILE + pixel_ids[None, :] % TILE).astype(jnp.float32)
    pix_y = (tile_row * TILE + pixel_ids // TILE).astype(jnp.float32)
    delta_x = pieces[0][:, None, :] - pix_x[:, :, None]
    delta_y = pieces[1][:, None, :] - pix_y[None, :, None]
    exponent = -0.5 * (pieces[2][:, None, :] * delta_x * delta_x + pieces[4][:, None, :] * delta_y * delta_y) - pieces[3][:, None, :] * delta_x * delta_y
    list_ranks = start_at + jnp.arange(span_len, dtype=jnp.int32)
    live_mask = list_ranks[None, :] < lengths[:, None]
    opacity_at = jnp.where(live_mask[:, None, :], pieces[5][:, None, :] * jnp.exp(exponent), 0.0)
    log_keep = jnp.log1p(-opacity_at)
    before = jnp.cumsum(log_keep, axis=2) - log_keep
    weights = jnp.exp(before) * opacity_at
    colour = jnp.einsum('npc,knc->nkp', weights, pieces[6:9], precision=lax.Precision.HIGHEST)
    return (colour, lax.optimization_barrier(jnp.sum(log_keep, axis=2)))

def render(features, tile_lists_in, lengths, tile_row):
    slot_count = features.shape[2]
    tile_cols = tile_lists_in.shape[1]
    list_len = tile_lists_in.shape[2]
    feature_table = jnp.transpose(features, (1, 0, 2)).reshape(9, 2 * slot_count)
    view_base = (jnp.arange(2, dtype=jnp.int32) * slot_count)[:, None, None]
    flat_lists = (tile_lists_in + view_base).reshape(-1, 8, list_len)
    flat_lengths = lengths.reshape(-1, 8)
    columns = jnp.tile(jnp.arange(tile_cols, dtype=jnp.int32), 2).reshape(-1, 8)

    def one_block(block_items):
        block_lists, block_lengths, block_columns = block_items
        pieces = feature_table[:, block_lists]
        return composite(pieces, block_lengths, block_columns, tile_row, 0, list_len)[0]
    colours = lax.map(one_block, (flat_lists, flat_lengths, columns))
    colours = colours.reshape(2, tile_cols, 3, TILE, TILE)
    return jnp.transpose(colours, (0, 2, 3, 1, 4)).reshape(2, 3, TILE, tile_cols * TILE)

def blur_columns(images):
    col_total = images.shape[-1]
    padded_cols = jnp.pad(images, [(0, 0)] * (images.ndim - 1) + [(5, 5)])
    result = 0.0
    for shift_num, weight in enumerate(window_taps()):
        result = result + weight * padded_cols[..., shift_num:shift_num + col_total]
    return result

def blur_rows(images):
    row_total = images.shape[-2] - 10
    result = 0.0
    for shift_num, weight in enumerate(window_taps()):
        result = result + weight * images[..., shift_num:shift_num + row_total, :]
    return result

def structure_map(images, targets):

    def blurred(values):
        return blur_rows(blur_columns(values))
    mean_one = blurred(images)
    mean_two = blurred(targets)
    var_one = blurred(images * images) - mean_one * mean_one
    var_two = blurred(targets * targets) - mean_two * mean_two
    cross_var = blurred(images * targets) - mean_one * mean_two
    numerator = (2.0 * mean_one * mean_two + SSIM_ONE) * (2.0 * cross_var + SSIM_TWO)
    denominator = (mean_one * mean_one + mean_two * mean_two + SSIM_ONE) * (var_one + var_two + SSIM_TWO)
    return numerator / denominator

def image_loss(images, targets):
    pad_rows = ((0, 0), (0, 0), (5, 5), (0, 0))
    similarity = structure_map(jnp.pad(images, pad_rows), jnp.pad(targets, pad_rows))
    difference = images - targets
    return SSIM_SHARE * jnp.sum(1.0 - similarity) + (1.0 - SSIM_SHARE) * jnp.sum(jnp.sqrt(difference * difference + SMOOTH_EPS))

def reference(params, send_list, send_counts, camera, ground_truth, tile_lists, list_lengths):
    starts = jnp.cumsum(send_counts, axis=1) - send_counts
    sources = jnp.arange(DEVICES, dtype=jnp.int32)
    slot_range = jnp.arange(CAP, dtype=jnp.int32)
    grouped_lists = tile_lists.reshape(N_VIEW, VIEWS_DEV, N_TILE, TILE_COLS, LIST)
    grouped_lengths = list_lengths.reshape(N_VIEW, VIEWS_DEV, N_TILE, TILE_COLS)
    grouped_cams = camera.reshape(N_VIEW, VIEWS_DEV, 6)

    def total_loss(weights_in):

        def one_band(target):
            view_group = target // N_TILE
            tile_row = target % N_TILE
            slot_pos = jnp.minimum(starts[:, target][:, None] + slot_range[None, :], G_DEV - 1).astype(jnp.int32)
            local_ids = jnp.take_along_axis(send_list, slot_pos, axis=1)
            global_ids = (sources[:, None] * G_DEV + local_ids).reshape(-1)
            arrived = weights_in[:, global_ids]
            cams_here = grouped_cams[view_group]
            features = jnp.stack([project(arrived, [cams_here[view_slot, entry_num] for entry_num in range(6)], float(WIDTH), float(HEIGHT)) for view_slot in range(VIEWS_DEV)])
            return render(features, grouped_lists[view_group][:, tile_row], grouped_lengths[view_group][:, tile_row], tile_row)
        all_bands = lax.map(jax.checkpoint(one_band), sources)
        images = all_bands.reshape(N_VIEW, N_TILE, VIEWS_DEV, 3, TILE, WIDTH).transpose(0, 2, 3, 1, 4, 5).reshape(VIEWS, 3, HEIGHT, WIDTH)
        return image_loss(images, ground_truth)
    return jax.grad(total_loss)(params)
```

```python
import jax
import jax.numpy as jnp
import numpy as np
from jax import lax
from jax.experimental import pallas as pl
from jax.experimental.pallas import tpu as pltpu
from jax.sharding import PartitionSpec as P

TILE = 16


FOCAL = 1000.0
LOW_PASS = 0.3
SSIM_SHARE = 0.2
SMOOTH_EPS = 1e-06
SSIM_ONE = 0.0001
SSIM_TWO = 0.0009
HARMONIC_ZERO = 0.28209479177387814
HARMONIC_ONE = 0.4886025119029199
HARMONIC_TWO = (
    1.0925484305920792,
    -1.0925484305920792,
    0.31539156525252005,
    -1.0925484305920792,
    0.5462742152960396,
)
HARMONIC_THREE = (
    -0.5900435899266435,
    2.890611442640554,
    -0.4570457994644658,
    0.3731763325901154,
    -0.4570457994644658,
    1.445305721320277,
    -0.5900435899266435,
)


def padded_2(cells, sides, width):
    for axis, dim in sides:
        count = lax.axis_size(axis)
        ends = count - 1
        head = lax.slice_in_dim(cells, 0, width, axis=dim)
        tail = lax.slice_in_dim(cells, cells.shape[dim] - width, cells.shape[dim], axis=dim)
        cells = jnp.concatenate(
            [
                lax.ppermute(tail, axis, [(i, (i + 1) % count) for i in range(ends)]),
                cells,
                lax.ppermute(head, axis, [((i + 1) % count, i) for i in range(ends)]),
            ],
            axis=dim,
        )
    return cells


def from_behind(block, axis, distance):
    devices = range(lax.axis_size(axis))
    route = [(i - distance, i) for i in devices if i - distance in devices]
    return lax.ppermute(block, axis, route)


def window_taps():
    offsets_np = np.arange(11) - 5.0
    weights = np.exp(-offsets_np * offsets_np / 4.5)
    weights = weights / weights.sum()
    return [float(weight) for weight in weights]


def matrix_product(left_side, right_side):
    return [
        [
            left_side[row_idx][0] * right_side[0][col_idx]
            + left_side[row_idx][1] * right_side[1][col_idx]
            + left_side[row_idx][2] * right_side[2][col_idx]
            for col_idx in range(3)
        ]
        for row_idx in range(3)
    ]


def rotation(angles):
    cos_a, sin_a = (jnp.cos(angles[0]), jnp.sin(angles[0]))
    cos_b, sin_b = (jnp.cos(angles[1]), jnp.sin(angles[1]))
    cos_c, sin_c = (jnp.cos(angles[2]), jnp.sin(angles[2]))
    about_x = [[1.0, 0.0, 0.0], [0.0, cos_a, -sin_a], [0.0, sin_a, cos_a]]
    about_y = [[cos_b, 0.0, sin_b], [0.0, 1.0, 0.0], [-sin_b, 0.0, cos_b]]
    about_z = [[cos_c, -sin_c, 0.0], [sin_c, cos_c, 0.0], [0.0, 0.0, 1.0]]
    return matrix_product(about_z, matrix_product(about_y, about_x))


def harmonics(dir_x, dir_y, dir_z):
    sq_x, sq_y, sq_z = (dir_x * dir_x, dir_y * dir_y, dir_z * dir_z)
    prod_xy, prod_yz, prod_xz = (dir_x * dir_y, dir_y * dir_z, dir_x * dir_z)
    return [
        HARMONIC_ZERO + 0.0 * dir_x,
        -HARMONIC_ONE * dir_y,
        HARMONIC_ONE * dir_z,
        -HARMONIC_ONE * dir_x,
        HARMONIC_TWO[0] * prod_xy,
        HARMONIC_TWO[1] * prod_yz,
        HARMONIC_TWO[2] * (2.0 * sq_z - sq_x - sq_y),
        HARMONIC_TWO[3] * prod_xz,
        HARMONIC_TWO[4] * (sq_x - sq_y),
        HARMONIC_THREE[0] * dir_y * (3.0 * sq_x - sq_y),
        HARMONIC_THREE[1] * prod_xy * dir_z,
        HARMONIC_THREE[2] * dir_y * (4.0 * sq_z - sq_x - sq_y),
        HARMONIC_THREE[3] * dir_z * (2.0 * sq_z - 3.0 * sq_x - 3.0 * sq_y),
        HARMONIC_THREE[4] * dir_x * (4.0 * sq_z - sq_x - sq_y),
        HARMONIC_THREE[5] * dir_z * (sq_x - sq_y),
        HARMONIC_THREE[6] * dir_x * (sq_x - 3.0 * sq_y),
    ]


LANES = 128
SUBS = 8
GROUP = 8
STEP_ROWS = 16
FEATS = 8
PAIR = 2 * FEATS
COEF_ROWS = 32
DEAD = -1e30
LOG_TOP = float(np.log(0.99))
VMEM_BYTES = 48 * 1024 * 1024


def camera_table(camera):
    columns = [camera[:, entry] for entry in range(6)]
    turn = rotation(columns[0:3])
    shift = columns[3:6]
    anchor = [
        -(turn[0][c] * shift[0] + turn[1][c] * shift[1] + turn[2][c] * shift[2]) for c in range(3)
    ]
    flat = [turn[r][c] for r in range(3) for c in range(3)] + shift + anchor
    return jnp.stack(flat + [jnp.zeros_like(shift[0])], axis=1)


def shape_matrix(params):
    scales = [jnp.exp(params[3 + axis_num]) for axis_num in range(3)]
    inv_norm = 1.0 / jnp.sqrt(
        params[6] * params[6]
        + params[7] * params[7]
        + params[8] * params[8]
        + params[9] * params[9]
    )
    quat_w, quat_x, quat_y, quat_z = [params[6 + k] * inv_norm for k in range(4)]
    quat_rot = [
        [
            1.0 - 2.0 * (quat_y * quat_y + quat_z * quat_z),
            2.0 * (quat_x * quat_y - quat_w * quat_z),
            2.0 * (quat_x * quat_z + quat_w * quat_y),
        ],
        [
            2.0 * (quat_x * quat_y + quat_w * quat_z),
            1.0 - 2.0 * (quat_x * quat_x + quat_z * quat_z),
            2.0 * (quat_y * quat_z - quat_w * quat_x),
        ],
        [
            2.0 * (quat_x * quat_z - quat_w * quat_y),
            2.0 * (quat_y * quat_z + quat_w * quat_x),
            1.0 - 2.0 * (quat_x * quat_x + quat_y * quat_y),
        ],
    ]
    return [[quat_rot[r][c] * scales[c] for c in range(3)] for r in range(3)]


def view_features(params, shape, cam, image_width, image_height):
    turn = [[cam[3 * r + c] for c in range(3)] for r in range(3)]
    point = [
        turn[r][0] * params[0] + turn[r][1] * params[1] + turn[r][2] * params[2] + cam[9 + r]
        for r in range(3)
    ]
    inv_depth = 1.0 / point[2]
    ratio_x, ratio_y = point[0] * inv_depth, point[1] * inv_depth
    zoom = FOCAL * inv_depth
    row_x = [zoom * (turn[0][c] - ratio_x * turn[2][c]) for c in range(3)]
    row_y = [zoom * (turn[1][c] - ratio_y * turn[2][c]) for c in range(3)]
    proj_x = [
        row_x[0] * shape[0][c] + row_x[1] * shape[1][c] + row_x[2] * shape[2][c] for c in range(3)
    ]
    proj_y = [
        row_y[0] * shape[0][c] + row_y[1] * shape[1][c] + row_y[2] * shape[2][c] for c in range(3)
    ]
    cov_xx = proj_x[0] * proj_x[0] + proj_x[1] * proj_x[1] + proj_x[2] * proj_x[2] + LOW_PASS
    cov_xy = proj_x[0] * proj_y[0] + proj_x[1] * proj_y[1] + proj_x[2] * proj_y[2]
    cov_yy = proj_y[0] * proj_y[0] + proj_y[1] * proj_y[1] + proj_y[2] * proj_y[2] + LOW_PASS
    inv_det = 1.0 / (cov_xx * cov_yy - cov_xy * cov_xy)
    ray = [params[c] - cam[12 + c] for c in range(3)]
    inv_len = 1.0 / jnp.sqrt(ray[0] * ray[0] + ray[1] * ray[1] + ray[2] * ray[2])
    basis = harmonics(ray[0] * inv_len, ray[1] * inv_len, ray[2] * inv_len)
    colours = []
    for channel in range(3):
        summed = 0.5 + HARMONIC_ZERO * params[11 + 16 * channel]
        for harmonic in range(1, 16):
            summed = summed + basis[harmonic] * params[11 + 16 * channel + harmonic]
        colours.append(summed)
    return [
        FOCAL * ratio_x + image_width / 2.0,
        FOCAL * ratio_y + image_height / 2.0,
        cov_yy * inv_det,
        -cov_xy * inv_det,
        cov_xx * inv_det,
    ] + colours


def log_opacity(logit):
    return LOG_TOP - jnp.log(1.0 + jnp.exp(-logit))


def load_params(params_ref, tile_scr, block):
    count = params_ref.shape[0]
    for band in range(0, count, SUBS):
        high = min(band + SUBS, count)
        for j in range(SUBS):
            lane_at = pl.multiple_of(block * SUBS * LANES + j * LANES, LANES)
            tile_scr[band * SUBS + j * SUBS : band * SUBS + j * SUBS + high - band, :] = params_ref[
                band:high, pl.ds(lane_at, LANES)
            ]
    return [
        tile_scr[pl.ds((r // SUBS) * SUBS * SUBS + r % SUBS, SUBS, stride=SUBS), :]
        for r in range(count)
    ]


def source_kernel(
    sizes, cam_ref, list_ref, counts_ref, params_ref, out_ref, tile_scr, feat_scr, table, slots
):
    groups, rows, cap, lane_len, image_width, image_height = sizes
    per = params_ref.shape[1]
    parts = cap // lane_len
    views = cam_ref.shape[0]

    def project_block(block, carry):
        params = load_params(params_ref, tile_scr, block)
        shape = shape_matrix(params)
        for view in range(views):
            cam = [cam_ref[view, k] for k in range(15)]
            for num, value in enumerate(
                view_features(params, shape, cam, image_width, image_height)
            ):
                feat_scr[pl.ds(view * FEATS + num, SUBS, stride=LANES), :] = value
        feat_scr[pl.ds(views * FEATS, SUBS, stride=LANES), :] = log_opacity(params[10])
        for j in range(SUBS):
            row_at = pl.multiple_of(block * SUBS * LANES + j * LANES, LANES)
            table[pl.ds(row_at, LANES), :] = feat_scr[j * LANES : (j + 1) * LANES, :].T
        return carry

    lax.fori_loop(0, per // (SUBS * LANES), project_block, 0)

    start = jnp.int32(0)
    for group in range(groups):

        def send_block(t, start_at, group=group):
            dest = group * rows + t
            count = counts_ref[0, dest]
            base = pl.multiple_of(dest * cap, SUBS)

            def move(i, carry):
                for q in range(SUBS):
                    spot = jnp.minimum(start_at + i * SUBS + q, per - 1)
                    slots[pl.ds(base + i * SUBS + q, 1), :] = table[
                        pl.ds(list_ref[0, spot], 1), :
                    ]
                return carry

            lax.fori_loop(0, (count + SUBS - 1) // SUBS, move, 0)
            for part in range(parts):
                turned = slots[pl.ds(base + part * lane_len, lane_len), :].T
                out_ref[dest, part * PAIR : (part + 1) * PAIR, :] = turned[
                    group * PAIR : (group + 1) * PAIR
                ]
                out_ref[dest, parts * PAIR + part : parts * PAIR + part + 1, :] = turned[
                    views * FEATS : views * FEATS + 1
                ]
            return start_at + count

        start = lax.fori_loop(0, rows, send_block, start)


def split_three(value):
    first = value.astype(jnp.bfloat16).astype(jnp.float32)
    rest = value - first
    second = rest.astype(jnp.bfloat16).astype(jnp.float32)
    return [first, second, rest - second]


def swap_grain(cells):
    sub = lax.broadcasted_iota(jnp.int32, (SUBS, LANES), 0)
    lane = lax.broadcasted_iota(jnp.int32, (SUBS, LANES), 1) // TILE
    for bit in (1, 2, 4):
        sub_bit, lane_bit = (sub & bit) != 0, (lane & bit) != 0
        from_high = pltpu.roll(pltpu.roll(cells, SUBS - bit, 0), bit * TILE, 1)
        from_low = pltpu.roll(pltpu.roll(cells, bit, 0), LANES - bit * TILE, 1)
        cells = jnp.where(sub_bit == lane_bit, cells, jnp.where(lane_bit, from_high, from_low))
    return cells


def longest(lens_ref, group):
    most = lens_ref[group * GROUP]
    for t in range(1, GROUP):
        most = jnp.maximum(most, lens_ref[group * GROUP + t])
    return most


def render_kernel(
    sizes,
    row_ref,
    lists_ref,
    lens_ref,
    lens_rows_ref,
    basis_ref,
    arrived_ref,
    image_ref,
    pieces_ref,
    turn_scr,
    table,
    rows,
    feat_scr,
    mm,
):
    cap, lane_len, col_groups, list_len = sizes
    parts = cap // lane_len
    devices = arrived_ref.shape[0]
    blocks = list_len // STEP_ROWS
    turn_scr[...] = jnp.zeros_like(turn_scr)
    table[devices * cap : devices * cap + SUBS, :] = jnp.zeros((SUBS, LANES), jnp.float32)

    def unpack(source, carry):
        for part in range(parts):
            turn_scr[0:PAIR, 0:lane_len] = arrived_ref[source, part * PAIR : (part + 1) * PAIR, :]
            turn_scr[PAIR : PAIR + 1, 0:lane_len] = arrived_ref[
                source, parts * PAIR + part : parts * PAIR + part + 1, :
            ]
            row_at = pl.multiple_of(source * cap + part * lane_len, lane_len)
            table[pl.ds(row_at, lane_len), :] = turn_scr[...].T[0:lane_len]
        return carry

    lax.fori_loop(0, devices, unpack, 0)
    centre_y = (row_ref[0] * TILE).astype(jnp.float32) + (TILE - 1) / 2.0
    sub = lax.broadcasted_iota(jnp.int32, (blocks, LANES), 0)
    lane = lax.broadcasted_iota(jnp.int32, (blocks, LANES), 1)
    zero = jnp.zeros((SUBS, LANES), jnp.float32)

    def one_group(group, carry):
        view, col_group = group // col_groups, group % col_groups
        most = longest(lens_ref, group)

        def fetch(n, inner):
            for t in range(GROUP):
                slot = lists_ref[group * GROUP + t, n]
                rows[pl.ds(n * GROUP + t, 1), :] = table[pl.ds(slot, 1), :]
            return inner

        lax.fori_loop(0, most, fetch, 0)
        for block in range(blocks):
            turned = rows[block * LANES : (block + 1) * LANES, :].T
            feat_scr[block * 24 : (block + 1) * 24, :] = turned[0:24]
        feats = [
            feat_scr[pl.ds(view * FEATS + num, blocks, stride=24), :] for num in range(FEATS)
        ]
        log_o = feat_scr[pl.ds(PAIR, blocks, stride=24), :]
        live = sub * STEP_ROWS + lane // GROUP < lens_rows_ref[pl.ds(group, 1), :]
        centre_x = ((col_group * GROUP + lane % GROUP) * TILE).astype(jnp.float32) + (
            TILE - 1
        ) / 2.0
        off_x, off_y = feats[0] - centre_x, feats[1] - centre_y
        lin_x = feats[2] * off_x + feats[3] * off_y
        lin_y = feats[4] * off_y + feats[3] * off_x
        coefs = [
            log_o - 0.5 * (off_x * lin_x + off_y * lin_y),
            lin_x,
            lin_y,
            -0.5 * feats[2],
            -feats[3],
            -0.5 * feats[4],
        ]
        coefs = [
            jnp.where(live, value, DEAD if num == 0 else 0.0) for num, value in enumerate(coefs)
        ]
        lines = [None] * COEF_ROWS
        for num, value in enumerate(coefs):
            for piece, part in enumerate(split_three(value)):
                lines[piece * 6 + num] = part
        for num in range(3):
            for piece, part in enumerate(split_three(jnp.where(live, feats[5 + num], 0.0))):
                lines[18 + piece * 3 + num] = part
        lines[27] = jnp.where(live, off_x, 0.0)
        lines[28] = jnp.where(live, off_y, 0.0)
        at = group * blocks * COEF_ROWS
        for num, value in enumerate(lines):
            pieces_ref[pl.ds(at + num, blocks, stride=COEF_ROWS), :] = (
                jnp.zeros((blocks, LANES), jnp.float32) if value is None else value
            )
        expand(pieces_ref, basis_ref, mm, at, blocks)

        def entry(n, state):
            keep, colour = state
            row_at = pl.multiple_of(n * GROUP, GROUP)
            shade = [
                mm[pl.ds(row_at, GROUP), (2 + c) * LANES : (3 + c) * LANES] for c in range(3)
            ]
            new_keep, new_colour = [], []
            for half in range(2):
                alpha = jnp.exp(mm[pl.ds(row_at, GROUP), half * LANES : (half + 1) * LANES])
                weight = keep[half] * alpha
                new_keep.append(keep[half] - weight)
                new_colour.append([colour[half][c] + weight * shade[c] for c in range(3)])
            return new_keep, new_colour

        state = ([zero + 1.0] * 2, [[zero] * 3] * 2)
        _, colour = lax.fori_loop(0, most, entry, state)
        lane_at = pl.multiple_of(col_group * LANES, LANES)
        for half in range(2):
            for c in range(3):
                image_ref[view, c, half * SUBS : (half + 1) * SUBS, pl.ds(lane_at, LANES)] = (
                    swap_grain(colour[half][c])
                )
        return carry

    lax.fori_loop(0, 2 * col_groups, one_group, 0)


def expand(pieces_ref, basis_ref, mm, at, blocks):
    for block in range(blocks):
        row_at = pl.multiple_of(at + block * COEF_ROWS, COEF_ROWS)
        left = pieces_ref[pl.ds(row_at, COEF_ROWS), :].T.astype(jnp.bfloat16)
        mm[block * LANES : (block + 1) * LANES, :] = jnp.dot(
            left, basis_ref[...], preferred_element_type=jnp.float32
        )


def back_kernel(
    sizes,
    lists_ref,
    lens_ref,
    list_rows_ref,
    basis_ref,
    moment_ref,
    pieces_ref,
    grad_ref,
    out_ref,
    mm,
    weights,
    grad_scr,
    mom_scr,
    row_scr,
    rows,
    table,
):
    cap, lane_len, col_groups, list_len = sizes
    parts = cap // lane_len
    devices = out_ref.shape[0]
    blocks = list_len // STEP_ROWS
    table[...] = jnp.zeros_like(table)
    grad_scr[...] = jnp.zeros_like(grad_scr)
    row_scr[...] = jnp.zeros_like(row_scr)
    zero = jnp.zeros((SUBS, LANES), jnp.float32)
    sub = lax.broadcasted_iota(jnp.int32, (SUBS, LANES), 0)
    lane = lax.broadcasted_iota(jnp.int32, (SUBS, LANES), 1)
    own_tile = lane % GROUP == sub

    def one_group(group, carry):
        view, col_group = group // col_groups, group % col_groups
        most = longest(lens_ref, group)
        at = group * blocks * COEF_ROWS
        lane_at = pl.multiple_of(col_group * LANES, LANES)
        grads = [
            [
                swap_grain(
                    grad_ref[view, c, half * SUBS : (half + 1) * SUBS, pl.ds(lane_at, LANES)]
                )
                for c in range(3)
            ]
            for half in range(2)
        ]
        for half in range(2):
            for c in range(3):
                for piece, part in enumerate(split_three(grads[half][c])):
                    grad_scr[
                        piece * 24 + c * SUBS : piece * 24 + (c + 1) * SUBS,
                        half * LANES : (half + 1) * LANES,
                    ] = part
        expand(pieces_ref, basis_ref, mm, at, blocks)

        def ahead(n, keep):
            row_at = pl.multiple_of(n * GROUP, GROUP)
            new_keep = []
            for half in range(2):
                lanes = slice(half * LANES, (half + 1) * LANES)
                alpha = jnp.exp(mm[pl.ds(row_at, GROUP), lanes])
                weight = keep[half] * alpha
                mm[pl.ds(row_at, GROUP), lanes] = alpha
                weights[pl.ds(row_at, GROUP), lanes] = weight
                new_keep.append(keep[half] - weight)
            return new_keep

        lax.fori_loop(0, most, ahead, [zero + 1.0] * 2)

        def behind(step, seen):
            row_at = pl.multiple_of((most - 1 - step) * GROUP, GROUP)
            shade = [
                mm[pl.ds(row_at, GROUP), (2 + c) * LANES : (3 + c) * LANES] for c in range(3)
            ]
            new_seen = []
            for half in range(2):
                lanes = slice(half * LANES, (half + 1) * LANES)
                own = (
                    grads[half][0] * shade[0]
                    + grads[half][1] * shade[1]
                    + grads[half][2] * shade[2]
                )
                gap = own - seen[half]
                alpha = mm[pl.ds(row_at, GROUP), lanes]
                mm[pl.ds(row_at, GROUP), lanes] = weights[pl.ds(row_at, GROUP), lanes] * gap
                new_seen.append(seen[half] + alpha * gap)
            return new_seen

        lax.fori_loop(0, most, behind, [zero] * 2)
        grad_cols = grad_scr[...].T.astype(jnp.bfloat16)
        for block in range(blocks):
            span = slice(block * LANES, (block + 1) * LANES)
            total = jnp.zeros((LANES, LANES), jnp.float32)
            for value, right in (
                (mm[span, 0 : 2 * LANES], moment_ref[...]),
                (weights[span, :], grad_cols),
            ):
                high = value.astype(jnp.bfloat16)
                low = (value - high.astype(jnp.float32)).astype(jnp.bfloat16)
                total = total + jnp.dot(high, right, preferred_element_type=jnp.float32)
                total = total + jnp.dot(low, right, preferred_element_type=jnp.float32)
            turned = total.T
            for c in range(3):
                summed = (
                    turned[c * SUBS : (c + 1) * SUBS]
                    + turned[24 + c * SUBS : 24 + (c + 1) * SUBS]
                    + turned[48 + c * SUBS : 48 + (c + 1) * SUBS]
                )
                mom_scr[block * TILE + 8 + c : block * TILE + 9 + c, :] = jnp.sum(
                    jnp.where(own_tile, summed, 0.0), axis=0, keepdims=True
                )
            mom_scr[block * TILE : block * TILE + 8, :] = turned[96:104]
        mom = [mom_scr[pl.ds(num, blocks, stride=TILE), :] for num in range(11)]

        def piece_line(num):
            return pieces_ref[pl.ds(at + num, blocks, stride=COEF_ROWS), :]

        con_xx = -2.0 * (piece_line(3) + piece_line(9) + piece_line(15))
        con_xy = -(piece_line(4) + piece_line(10) + piece_line(16))
        con_yy = -2.0 * (piece_line(5) + piece_line(11) + piece_line(17))
        off_x, off_y = piece_line(27), piece_line(28)
        sum_x = off_x * mom[0] - mom[1]
        sum_y = off_y * mom[0] - mom[2]
        results = [
            -(con_xx * sum_x + con_xy * sum_y),
            -(con_yy * sum_y + con_xy * sum_x),
            -0.5 * (off_x * (sum_x - mom[1]) + mom[3]),
            -(off_x * sum_y - off_y * mom[1] + mom[4]),
            -0.5 * (off_y * (sum_y - mom[2]) + mom[5]),
        ] + mom[8:11]
        other = 1 - view
        for num, value in enumerate(results):
            row_scr[pl.ds(view * FEATS + num, blocks, stride=LANES), :] = value
            row_scr[pl.ds(other * FEATS + num, blocks, stride=LANES), :] = jnp.zeros_like(value)
        row_scr[pl.ds(PAIR, blocks, stride=LANES), :] = mom[0]
        for block in range(blocks):
            rows[block * LANES : (block + 1) * LANES, :] = row_scr[
                block * LANES : (block + 1) * LANES, :
            ].T
        names = list_rows_ref[pl.ds(pl.multiple_of(group * GROUP, GROUP), GROUP), :]
        twice = jnp.zeros((GROUP, LANES), jnp.float32)
        for shift in range(1, GROUP // 2 + 1):
            twice = jnp.maximum(
                twice, jnp.where(names == pltpu.roll(names, shift, 0), 1.0, 0.0)
            )
        clash = jnp.max(twice) > 0.5

        @pl.when(jnp.logical_not(clash))
        def _():
            def add(n, inner):
                spots = [lists_ref[group * GROUP + t, n] for t in range(GROUP)]
                held = [table[pl.ds(spot, 1), :] for spot in spots]
                sums = [
                    held[t] + rows[pl.ds(n * GROUP + t, 1), :] for t in range(GROUP)
                ]
                for t in range(GROUP):
                    table[pl.ds(spots[t], 1), :] = sums[t]
                return inner

            lax.fori_loop(0, most, add, 0)

        @pl.when(clash)
        def _():
            def add(n, inner):
                for t in range(GROUP):
                    spot = lists_ref[group * GROUP + t, n]
                    table[pl.ds(spot, 1), :] = (
                        table[pl.ds(spot, 1), :] + rows[pl.ds(n * GROUP + t, 1), :]
                    )
                return inner

            lax.fori_loop(0, most, add, 0)

        return carry

    lax.fori_loop(0, 2 * col_groups, one_group, 0)

    def pack(source, carry):
        for part in range(parts):
            row_at = pl.multiple_of(source * cap + part * lane_len, lane_len)
            turned = table[pl.ds(row_at, lane_len), :].T
            out_ref[source, part * PAIR : (part + 1) * PAIR, :] = turned[0:PAIR]
            out_ref[source, parts * PAIR + part : parts * PAIR + part + 1, :] = turned[
                PAIR : PAIR + 1
            ]
        return carry

    lax.fori_loop(0, devices, pack, 0)


def owner_kernel(
    sizes,
    cam_ref,
    list_ref,
    counts_ref,
    params_ref,
    back_ref,
    out_ref,
    tile_scr,
    feat_scr,
    turn_scr,
    table,
    slots,
):
    groups, rows, cap, lane_len, image_width, image_height = sizes
    count_params, per = params_ref.shape
    parts = cap // lane_len
    table[...] = jnp.zeros_like(table)
    turn_scr[...] = jnp.zeros_like(turn_scr)
    start = jnp.int32(0)
    for group in range(groups):
        turn_scr[PAIR + 1 : PAIR + 2, :] = jnp.full((1, LANES), 1.0 + group, jnp.float32)

        def take_block(t, start_at, group=group):
            dest = group * rows + t
            count = counts_ref[0, dest]
            base = pl.multiple_of(dest * cap, SUBS)
            for part in range(parts):
                turn_scr[0:PAIR, 0:lane_len] = back_ref[dest, part * PAIR : (part + 1) * PAIR, :]
                turn_scr[PAIR : PAIR + 1, 0:lane_len] = back_ref[
                    dest, parts * PAIR + part : parts * PAIR + part + 1, :
                ]
                slots[pl.ds(base + part * lane_len, lane_len), :] = turn_scr[...].T[0:lane_len]

            def move(i, carry):
                for q in range(SUBS):
                    spot = list_ref[0, start_at + i * SUBS + q]
                    table[pl.ds(spot, 1), :] = slots[pl.ds(base + i * SUBS + q, 1), :]
                return carry

            whole = count // SUBS
            lax.fori_loop(0, whole, move, 0)

            def move_one(k, carry):
                spot = list_ref[0, start_at + k]
                table[pl.ds(spot, 1), :] = slots[pl.ds(base + k, 1), :]
                return carry

            lax.fori_loop(whole * SUBS, count, move_one, 0)
            return start_at + count

        start = lax.fori_loop(0, rows, take_block, start)

    def pull_block(block, carry):
        params = load_params(params_ref, tile_scr, block)
        for j in range(SUBS):
            row_at = pl.multiple_of(block * SUBS * LANES + j * LANES, LANES)
            feat_scr[j * 24 : (j + 1) * 24, :] = table[pl.ds(row_at, LANES), :].T[0:24]
        cots = [feat_scr[pl.ds(num, SUBS, stride=24), :] for num in range(PAIR + 2)]
        home = cots[PAIR + 1]
        sent = home > 0.5
        cams = []
        for view in range(2):
            cam = []
            for k in range(15):
                value = jnp.full((SUBS, LANES), cam_ref[view, k], jnp.float32)
                for group in range(1, groups):
                    value = jnp.where(home > 0.5 + group, cam_ref[2 * group + view, k], value)
                cam.append(value)
            cams.append(cam)

        def both(*values):
            shape = shape_matrix(values)
            return (
                view_features(values, shape, cams[0], image_width, image_height)
                + view_features(values, shape, cams[1], image_width, image_height)
                + [log_opacity(values[10])]
            )

        _, pull = jax.vjp(both, *params)
        grads = pull(cots[0 : PAIR + 1])
        for num, value in enumerate(grads):
            tile_scr[pl.ds((num // SUBS) * SUBS * SUBS + num % SUBS, SUBS, stride=SUBS), :] = (
                jnp.where(sent, value, 0.0)
            )
        for band in range(0, count_params, SUBS):
            high = min(band + SUBS, count_params)
            for j in range(SUBS):
                lane_at = pl.multiple_of(block * SUBS * LANES + j * LANES, LANES)
                out_ref[band:high, pl.ds(lane_at, LANES)] = tile_scr[
                    band * SUBS + j * SUBS : band * SUBS + j * SUBS + high - band, :
                ]
        return carry

    lax.fori_loop(0, per // (SUBS * LANES), pull_block, 0)


def pixel_basis():
    pixel = np.arange(TILE * TILE)
    x = (pixel % TILE) - (TILE - 1) / 2.0
    y = (pixel // TILE) - (TILE - 1) / 2.0
    return np.stack([np.ones_like(x), x, y, x * x, x * y, y * y])


def expand_matrix():
    terms = pixel_basis()
    matrix = np.zeros((COEF_ROWS, 5 * LANES), np.float32)
    for piece in range(3):
        matrix[piece * 6 : piece * 6 + 6, 0 : 2 * LANES] = terms
        for c in range(3):
            matrix[18 + piece * 3 + c, (2 + c) * LANES : (3 + c) * LANES] = 1.0
    return jnp.asarray(matrix, jnp.bfloat16)


def moment_matrix():
    matrix = np.zeros((2 * LANES, LANES), np.float32)
    matrix[:, 96:102] = pixel_basis().T
    return jnp.asarray(matrix, jnp.bfloat16)


def smem():
    return pl.BlockSpec(memory_space=pltpu.SMEM)


def vmem():
    return pl.BlockSpec(memory_space=pltpu.VMEM)


def scratch(*shape):
    return pltpu.VMEM(shape, jnp.float32)


def run(kernel, out_shapes, in_specs, scratches, *operands):
    return pl.pallas_call(
        kernel,
        out_shape=out_shapes,
        in_specs=in_specs,
        out_specs=jax.tree.map(lambda _: vmem(), out_shapes),
        scratch_shapes=scratches,
        compiler_params=pltpu.CompilerParams(vmem_limit_bytes=VMEM_BYTES),
    )(*operands)


def shards(params, send_list, send_counts, camera, ground_truth, tile_lists, list_lengths):
    devices = lax.axis_size(("view", "tile"))
    row_devices = lax.axis_size("tile")
    groups = lax.axis_size("view")
    count_params, per_device = params.shape
    capacity = per_device // devices
    lane_len = min(capacity, LANES)
    parts = capacity // lane_len
    tile_cols, list_len = tile_lists.shape[2:]
    col_groups = tile_cols // GROUP
    blocks = list_len // STEP_ROWS
    tile_row = lax.axis_index("tile")
    image_width = float(ground_truth.shape[3])
    image_height = float(ground_truth.shape[2] * row_devices)
    table_rows = per_device + SUBS
    sent_shape = jax.ShapeDtypeStruct((devices, parts * (PAIR + 1), lane_len), jnp.float32)
    cams = camera_table(camera)

    flat_lengths = list_lengths.reshape(-1)
    entry_rank = jnp.arange(list_len, dtype=jnp.int32)
    tile_num = jnp.arange(2 * tile_cols, dtype=jnp.int32)
    lists = jnp.where(
        entry_rank[None, :] < flat_lengths[:, None],
        tile_lists.reshape(2 * tile_cols, list_len),
        per_device + tile_num[:, None] % GROUP,
    )
    lens_rows = jnp.tile(flat_lengths.reshape(-1, GROUP), (1, LANES // GROUP))

    own_sizes = (groups, row_devices, capacity, lane_len, image_width, image_height)
    sent = run(
        lambda *refs: source_kernel(own_sizes, *refs),
        sent_shape,
        [smem(), smem(), smem(), vmem()],
        [
            scratch(SUBS * SUBS * SUBS, LANES),
            scratch(SUBS * LANES, LANES),
            scratch(per_device, LANES),
            scratch(per_device, LANES),
        ],
        cams,
        send_list,
        send_counts,
        params,
    )
    arrived = lax.all_to_all(sent, ("view", "tile"), split_axis=0, concat_axis=0, tiled=True)

    tile_sizes = (capacity, lane_len, col_groups, list_len)
    rendered, pieces = run(
        lambda *refs: render_kernel(tile_sizes, *refs),
        (
            jax.ShapeDtypeStruct(ground_truth.shape, jnp.float32),
            jax.ShapeDtypeStruct((2 * col_groups * blocks * COEF_ROWS, LANES), jnp.float32),
        ),
        [smem(), smem(), smem(), vmem(), vmem(), vmem()],
        [
            scratch(LANES, LANES),
            scratch(table_rows, LANES),
            scratch(blocks * LANES, LANES),
            scratch(blocks * 24, LANES),
            scratch(blocks * LANES, 5 * LANES),
        ],
        tile_row.reshape(1),
        lists,
        flat_lengths,
        lens_rows,
        expand_matrix(),
        arrived,
    )

    stacked = jnp.stack([rendered, ground_truth])
    padded = padded_2(stacked, (("tile", 3),), 5)
    padded_truth = padded[1]

    def local_loss(padded_image):
        similarity = structure_map(padded_image, padded_truth)
        difference = padded_image[:, :, 5 : 5 + TILE] - ground_truth
        return SSIM_SHARE * jnp.sum(1.0 - similarity) + (1.0 - SSIM_SHARE) * jnp.sum(
            jnp.sqrt(difference * difference + SMOOTH_EPS)
        )

    grad_pad = jax.grad(local_loss)(padded[0])
    from_below = from_behind(grad_pad[:, :, 0:5], "tile", -1)
    from_above = from_behind(grad_pad[:, :, 5 + TILE : 10 + TILE], "tile", 1)
    grad_image = grad_pad[:, :, 5 : 5 + TILE]
    grad_image = grad_image + jnp.pad(from_above, ((0, 0), (0, 0), (0, TILE - 5), (0, 0)))
    grad_image = grad_image + jnp.pad(from_below, ((0, 0), (0, 0), (TILE - 5, 0), (0, 0)))

    grad_slots = run(
        lambda *refs: back_kernel(tile_sizes, *refs),
        sent_shape,
        [smem(), smem(), vmem(), vmem(), vmem(), vmem(), vmem()],
        [
            scratch(blocks * LANES, 5 * LANES),
            scratch(blocks * LANES, 2 * LANES),
            scratch(LANES, 2 * LANES),
            scratch(blocks * TILE, LANES),
            scratch(blocks * LANES, LANES),
            scratch(blocks * LANES, LANES),
            scratch(table_rows, LANES),
        ],
        lists,
        flat_lengths,
        lists,
        expand_matrix(),
        moment_matrix(),
        pieces,
        grad_image,
    )
    returned = lax.all_to_all(
        grad_slots, ("view", "tile"), split_axis=0, concat_axis=0, tiled=True
    )
    return run(
        lambda *refs: owner_kernel(own_sizes, *refs),
        jax.ShapeDtypeStruct(params.shape, jnp.float32),
        [smem(), smem(), smem(), vmem(), vmem()],
        [
            scratch(SUBS * SUBS * SUBS, LANES),
            scratch(SUBS * 24, LANES),
            scratch(LANES, LANES),
            scratch(per_device, LANES),
            scratch(per_device, LANES),
        ],
        cams,
        send_list,
        send_counts,
        params,
        returned,
    )


def blur_columns(images):
    col_total = images.shape[-1]
    padded_cols = jnp.pad(images, [(0, 0)] * (images.ndim - 1) + [(5, 5)])
    result = 0.0
    for shift_num, weight in enumerate(window_taps()):
        result = result + weight * padded_cols[..., shift_num : shift_num + col_total]
    return result


def blur_rows(images):
    row_total = images.shape[-2] - 10
    result = 0.0
    for shift_num, weight in enumerate(window_taps()):
        result = result + weight * images[..., shift_num : shift_num + row_total, :]
    return result


def structure_map(images, targets):

    def blurred(values):
        return blur_rows(blur_columns(values))

    mean_one = blurred(images)
    mean_two = blurred(targets)
    var_one = blurred(images * images) - mean_one * mean_one
    var_two = blurred(targets * targets) - mean_two * mean_two
    cross_var = blurred(images * targets) - mean_one * mean_two
    numerator = (2.0 * mean_one * mean_two + SSIM_ONE) * (2.0 * cross_var + SSIM_TWO)
    denominator = (mean_one * mean_one + mean_two * mean_two + SSIM_ONE) * (
        var_one + var_two + SSIM_TWO
    )
    return numerator / denominator


def solution(mesh):
    in_specs = (
        P(None, ("view", "tile")),
        P(("view", "tile"), None),
        P(("view", "tile"), None),
        P(),
        P("view", None, "tile", None),
        P("view", "tile", None, None),
        P("view", "tile", None),
    )
    out_specs = P(None, ("view", "tile"))
    return jax.shard_map(shards, mesh=mesh, in_specs=in_specs, out_specs=out_specs, check_vma=False)
```

```python
import jax
import jax.numpy as jnp
import numpy as np
from jax import lax
from jax.experimental import pallas as pl
from jax.experimental.pallas import tpu as pltpu
from jax.sharding import PartitionSpec as P

TILE = 16


FOCAL = 1000.0
LOW_PASS = 0.3
SSIM_SHARE = 0.2
SMOOTH_EPS = 1e-06
SSIM_ONE = 0.0001
SSIM_TWO = 0.0009
HARMONIC_ZERO = 0.28209479177387814
HARMONIC_ONE = 0.4886025119029199
HARMONIC_TWO = (
    1.0925484305920792,
    -1.0925484305920792,
    0.31539156525252005,
    -1.0925484305920792,
    0.5462742152960396,
)
HARMONIC_THREE = (
    -0.5900435899266435,
    2.890611442640554,
    -0.4570457994644658,
    0.3731763325901154,
    -0.4570457994644658,
    1.445305721320277,
    -0.5900435899266435,
)


def from_behind(block, axis, distance):
    devices = range(lax.axis_size(axis))
    route = [(i - distance, i) for i in devices if i - distance in devices]
    return lax.ppermute(block, axis, route)


def window_taps():
    offsets_np = np.arange(11) - 5.0
    weights = np.exp(-offsets_np * offsets_np / 4.5)
    weights = weights / weights.sum()
    return [float(weight) for weight in weights]


def matrix_product(left_side, right_side):
    return [
        [
            left_side[row_idx][0] * right_side[0][col_idx]
            + left_side[row_idx][1] * right_side[1][col_idx]
            + left_side[row_idx][2] * right_side[2][col_idx]
            for col_idx in range(3)
        ]
        for row_idx in range(3)
    ]


def rotation(angles):
    cos_a, sin_a = (jnp.cos(angles[0]), jnp.sin(angles[0]))
    cos_b, sin_b = (jnp.cos(angles[1]), jnp.sin(angles[1]))
    cos_c, sin_c = (jnp.cos(angles[2]), jnp.sin(angles[2]))
    about_x = [[1.0, 0.0, 0.0], [0.0, cos_a, -sin_a], [0.0, sin_a, cos_a]]
    about_y = [[cos_b, 0.0, sin_b], [0.0, 1.0, 0.0], [-sin_b, 0.0, cos_b]]
    about_z = [[cos_c, -sin_c, 0.0], [sin_c, cos_c, 0.0], [0.0, 0.0, 1.0]]
    return matrix_product(about_z, matrix_product(about_y, about_x))


def harmonics(dir_x, dir_y, dir_z):
    sq_x, sq_y, sq_z = (dir_x * dir_x, dir_y * dir_y, dir_z * dir_z)
    prod_xy, prod_yz, prod_xz = (dir_x * dir_y, dir_y * dir_z, dir_x * dir_z)
    return [
        HARMONIC_ZERO + 0.0 * dir_x,
        -HARMONIC_ONE * dir_y,
        HARMONIC_ONE * dir_z,
        -HARMONIC_ONE * dir_x,
        HARMONIC_TWO[0] * prod_xy,
        HARMONIC_TWO[1] * prod_yz,
        HARMONIC_TWO[2] * (2.0 * sq_z - sq_x - sq_y),
        HARMONIC_TWO[3] * prod_xz,
        HARMONIC_TWO[4] * (sq_x - sq_y),
        HARMONIC_THREE[0] * dir_y * (3.0 * sq_x - sq_y),
        HARMONIC_THREE[1] * prod_xy * dir_z,
        HARMONIC_THREE[2] * dir_y * (4.0 * sq_z - sq_x - sq_y),
        HARMONIC_THREE[3] * dir_z * (2.0 * sq_z - 3.0 * sq_x - 3.0 * sq_y),
        HARMONIC_THREE[4] * dir_x * (4.0 * sq_z - sq_x - sq_y),
        HARMONIC_THREE[5] * dir_z * (sq_x - sq_y),
        HARMONIC_THREE[6] * dir_x * (sq_x - 3.0 * sq_y),
    ]


LANES = 128
SUBS = 8
GROUP = 8
STEP_ROWS = 16
FEATS = 8
PAIR = 2 * FEATS
COEF_ROWS = 32
UNROLL = 8
MOVES = 16
TAPS = 11
DEAD = -1e30
LOG_TOP = float(np.log(0.99))
VMEM_BYTES = 48 * 1024 * 1024


def stepped(total, width, body, state):
    def step(block, held):
        for k in range(width):
            held = body(block * width + k, held)
        return held

    return lax.fori_loop(0, (total + width - 1) // width, step, state)


def camera_table(camera):
    columns = [camera[:, entry] for entry in range(6)]
    turn = rotation(columns[0:3])
    shift = columns[3:6]
    anchor = [
        -(turn[0][c] * shift[0] + turn[1][c] * shift[1] + turn[2][c] * shift[2]) for c in range(3)
    ]
    flat = [turn[r][c] for r in range(3) for c in range(3)] + shift + anchor
    return jnp.stack(flat + [jnp.zeros_like(shift[0])], axis=1)


def shape_matrix(params):
    scales = [jnp.exp(params[3 + axis_num]) for axis_num in range(3)]
    inv_norm = 1.0 / jnp.sqrt(
        params[6] * params[6]
        + params[7] * params[7]
        + params[8] * params[8]
        + params[9] * params[9]
    )
    quat_w, quat_x, quat_y, quat_z = [params[6 + k] * inv_norm for k in range(4)]
    quat_rot = [
        [
            1.0 - 2.0 * (quat_y * quat_y + quat_z * quat_z),
            2.0 * (quat_x * quat_y - quat_w * quat_z),
            2.0 * (quat_x * quat_z + quat_w * quat_y),
        ],
        [
            2.0 * (quat_x * quat_y + quat_w * quat_z),
            1.0 - 2.0 * (quat_x * quat_x + quat_z * quat_z),
            2.0 * (quat_y * quat_z - quat_w * quat_x),
        ],
        [
            2.0 * (quat_x * quat_z - quat_w * quat_y),
            2.0 * (quat_y * quat_z + quat_w * quat_x),
            1.0 - 2.0 * (quat_x * quat_x + quat_y * quat_y),
        ],
    ]
    return [[quat_rot[r][c] * scales[c] for c in range(3)] for r in range(3)]


def view_features(params, shape, cam, image_width, image_height):
    turn = [[cam[3 * r + c] for c in range(3)] for r in range(3)]
    point = [
        turn[r][0] * params[0] + turn[r][1] * params[1] + turn[r][2] * params[2] + cam[9 + r]
        for r in range(3)
    ]
    inv_depth = 1.0 / point[2]
    ratio_x, ratio_y = point[0] * inv_depth, point[1] * inv_depth
    zoom = FOCAL * inv_depth
    row_x = [zoom * (turn[0][c] - ratio_x * turn[2][c]) for c in range(3)]
    row_y = [zoom * (turn[1][c] - ratio_y * turn[2][c]) for c in range(3)]
    proj_x = [
        row_x[0] * shape[0][c] + row_x[1] * shape[1][c] + row_x[2] * shape[2][c] for c in range(3)
    ]
    proj_y = [
        row_y[0] * shape[0][c] + row_y[1] * shape[1][c] + row_y[2] * shape[2][c] for c in range(3)
    ]
    cov_xx = proj_x[0] * proj_x[0] + proj_x[1] * proj_x[1] + proj_x[2] * proj_x[2] + LOW_PASS
    cov_xy = proj_x[0] * proj_y[0] + proj_x[1] * proj_y[1] + proj_x[2] * proj_y[2]
    cov_yy = proj_y[0] * proj_y[0] + proj_y[1] * proj_y[1] + proj_y[2] * proj_y[2] + LOW_PASS
    inv_det = 1.0 / (cov_xx * cov_yy - cov_xy * cov_xy)
    ray = [params[c] - cam[12 + c] for c in range(3)]
    inv_len = 1.0 / jnp.sqrt(ray[0] * ray[0] + ray[1] * ray[1] + ray[2] * ray[2])
    basis = harmonics(ray[0] * inv_len, ray[1] * inv_len, ray[2] * inv_len)
    colours = []
    for channel in range(3):
        summed = 0.5 + HARMONIC_ZERO * params[11 + 16 * channel]
        for harmonic in range(1, 16):
            summed = summed + basis[harmonic] * params[11 + 16 * channel + harmonic]
        colours.append(summed)
    return [
        FOCAL * ratio_x + image_width / 2.0,
        FOCAL * ratio_y + image_height / 2.0,
        cov_yy * inv_det,
        -cov_xy * inv_det,
        cov_xx * inv_det,
    ] + colours


def log_opacity(logit):
    return LOG_TOP - jnp.log(1.0 + jnp.exp(-logit))


def load_params(params_ref, tile_scr, block):
    count = params_ref.shape[0]
    for band in range(0, count, SUBS):
        high = min(band + SUBS, count)
        for j in range(SUBS):
            lane_at = pl.multiple_of(block * SUBS * LANES + j * LANES, LANES)
            tile_scr[band * SUBS + j * SUBS : band * SUBS + j * SUBS + high - band, :] = params_ref[
                band:high, pl.ds(lane_at, LANES)
            ]
    return [
        tile_scr[pl.ds((r // SUBS) * SUBS * SUBS + r % SUBS, SUBS, stride=SUBS), :]
        for r in range(count)
    ]


def source_kernel(
    sizes, cam_ref, list_ref, counts_ref, params_ref, out_ref, tile_scr, feat_scr, table, slots
):
    groups, rows, cap, lane_len, image_width, image_height = sizes
    per = params_ref.shape[1]
    parts = cap // lane_len
    views = cam_ref.shape[0]

    def project_block(block, carry):
        params = load_params(params_ref, tile_scr, block)
        shape = shape_matrix(params)
        for view in range(views):
            cam = [cam_ref[view, k] for k in range(15)]
            for num, value in enumerate(
                view_features(params, shape, cam, image_width, image_height)
            ):
                feat_scr[pl.ds(view * FEATS + num, SUBS, stride=LANES), :] = value
        feat_scr[pl.ds(views * FEATS, SUBS, stride=LANES), :] = log_opacity(params[10])
        for j in range(SUBS):
            row_at = pl.multiple_of(block * SUBS * LANES + j * LANES, LANES)
            table[pl.ds(row_at, LANES), :] = feat_scr[j * LANES : (j + 1) * LANES, :].T
        return carry

    lax.fori_loop(0, per // (SUBS * LANES), project_block, 0)

    start = jnp.int32(0)
    for group in range(groups):

        def send_block(t, start_at, group=group):
            dest = group * rows + t
            count = counts_ref[0, dest]
            base = pl.multiple_of(dest * cap, SUBS)

            def move(k, carry):
                spot = jnp.minimum(start_at + k, per - 1)
                slots[pl.ds(base + k, 1), :] = table[pl.ds(list_ref[0, spot], 1), :]
                return carry

            stepped(count, MOVES, move, 0)
            for part in range(parts):
                turned = slots[pl.ds(base + part * lane_len, lane_len), :].T
                out_ref[dest, part * PAIR : (part + 1) * PAIR, :] = turned[
                    group * PAIR : (group + 1) * PAIR
                ]
                out_ref[dest, parts * PAIR + part : parts * PAIR + part + 1, :] = turned[
                    views * FEATS : views * FEATS + 1
                ]
            return start_at + count

        start = lax.fori_loop(0, rows, send_block, start)


def split_three(value):
    first = value.astype(jnp.bfloat16).astype(jnp.float32)
    rest = value - first
    second = rest.astype(jnp.bfloat16).astype(jnp.float32)
    return [first, second, rest - second]


def swap_grain(cells):
    sub = lax.broadcasted_iota(jnp.int32, (SUBS, LANES), 0)
    lane = lax.broadcasted_iota(jnp.int32, (SUBS, LANES), 1) // TILE
    for bit in (1, 2, 4):
        sub_bit, lane_bit = (sub & bit) != 0, (lane & bit) != 0
        from_high = pltpu.roll(pltpu.roll(cells, SUBS - bit, 0), bit * TILE, 1)
        from_low = pltpu.roll(pltpu.roll(cells, bit, 0), LANES - bit * TILE, 1)
        cells = jnp.where(sub_bit == lane_bit, cells, jnp.where(lane_bit, from_high, from_low))
    return cells


def longest(lens_ref, group):
    most = lens_ref[group * GROUP]
    for t in range(1, GROUP):
        most = jnp.maximum(most, lens_ref[group * GROUP + t])
    return most


def render_kernel(
    sizes,
    row_ref,
    lists_ref,
    lens_ref,
    lens_rows_ref,
    basis_ref,
    arrived_ref,
    image_ref,
    pieces_ref,
    turn_scr,
    table,
    rows,
    feat_scr,
    mm,
):
    cap, lane_len, col_groups, list_len = sizes
    parts = cap // lane_len
    devices = arrived_ref.shape[0]
    blocks = list_len // STEP_ROWS
    turn_scr[PAIR:, :] = jnp.zeros((SUBS, LANES), jnp.float32)
    table[devices * cap : devices * cap + SUBS, :] = jnp.zeros((SUBS, LANES), jnp.float32)

    def unpack(source, carry):
        for part in range(parts):
            turn_scr[0:PAIR, 0:lane_len] = arrived_ref[source, part * PAIR : (part + 1) * PAIR, :]
            turn_scr[PAIR : PAIR + 1, 0:lane_len] = arrived_ref[
                source, parts * PAIR + part : parts * PAIR + part + 1, :
            ]
            row_at = pl.multiple_of(source * cap + part * lane_len, lane_len)
            table[pl.ds(row_at, lane_len), 0:24] = turn_scr[:, 0:lane_len].T
        return carry

    lax.fori_loop(0, devices, unpack, 0)
    centre_y = (row_ref[0] * TILE).astype(jnp.float32) + (TILE - 1) / 2.0
    sub = lax.broadcasted_iota(jnp.int32, (blocks, LANES), 0)
    lane = lax.broadcasted_iota(jnp.int32, (blocks, LANES), 1)
    zero = jnp.zeros((SUBS, LANES), jnp.float32)

    def one_group(group, carry):
        view, col_group = group // col_groups, group % col_groups
        most = longest(lens_ref, group)

        def fetch(n, inner):
            for t in range(GROUP):
                slot = lists_ref[group * GROUP + t, n]
                rows[pl.ds(n * GROUP + t, 1), :] = table[pl.ds(slot, 1), :]
            return inner

        stepped(most, UNROLL, fetch, 0)
        for block in range(blocks):
            feat_scr[block * 24 : (block + 1) * 24, :] = rows[
                block * LANES : (block + 1) * LANES, 0:24
            ].T
        feats = [
            feat_scr[pl.ds(view * FEATS + num, blocks, stride=24), :] for num in range(FEATS)
        ]
        log_o = feat_scr[pl.ds(PAIR, blocks, stride=24), :]
        live = sub * STEP_ROWS + lane // GROUP < lens_rows_ref[pl.ds(group, 1), :]
        centre_x = ((col_group * GROUP + lane % GROUP) * TILE).astype(jnp.float32) + (
            TILE - 1
        ) / 2.0
        off_x, off_y = feats[0] - centre_x, feats[1] - centre_y
        lin_x = feats[2] * off_x + feats[3] * off_y
        lin_y = feats[4] * off_y + feats[3] * off_x
        coefs = [
            log_o - 0.5 * (off_x * lin_x + off_y * lin_y),
            lin_x,
            lin_y,
            -0.5 * feats[2],
            -feats[3],
            -0.5 * feats[4],
        ]
        coefs = [
            jnp.where(live, value, DEAD if num == 0 else 0.0) for num, value in enumerate(coefs)
        ]
        lines = [None] * COEF_ROWS
        for num, value in enumerate(coefs):
            for piece, part in enumerate(split_three(value)):
                lines[piece * 6 + num] = part
        for num in range(3):
            for piece, part in enumerate(split_three(jnp.where(live, feats[5 + num], 0.0))):
                lines[18 + piece * 3 + num] = part
        lines[27] = jnp.where(live, off_x, 0.0)
        lines[28] = jnp.where(live, off_y, 0.0)
        at = group * blocks * COEF_ROWS
        for num, value in enumerate(lines):
            pieces_ref[pl.ds(at + num, blocks, stride=COEF_ROWS), :] = (
                jnp.zeros((blocks, LANES), jnp.float32) if value is None else value
            )
        expand(pieces_ref, basis_ref, mm, at, blocks)

        def entry(n, state):
            keep, colour = state
            row_at = pl.multiple_of(n * GROUP, GROUP)
            shade = [
                mm[pl.ds(row_at, GROUP), (2 + c) * LANES : (3 + c) * LANES] for c in range(3)
            ]
            new_keep, new_colour = [], []
            for half in range(2):
                alpha = jnp.exp(mm[pl.ds(row_at, GROUP), half * LANES : (half + 1) * LANES])
                weight = keep[half] * alpha
                new_keep.append(keep[half] - weight)
                new_colour.append([colour[half][c] + weight * shade[c] for c in range(3)])
            return new_keep, new_colour

        state = ([zero + 1.0] * 2, [[zero] * 3] * 2)
        _, colour = stepped(most, UNROLL, entry, state)
        lane_at = pl.multiple_of(col_group * LANES, LANES)
        for half in range(2):
            for c in range(3):
                image_ref[view, c, half * SUBS : (half + 1) * SUBS, pl.ds(lane_at, LANES)] = (
                    swap_grain(colour[half][c])
                )
        return carry

    lax.fori_loop(0, 2 * col_groups, one_group, 0)


def expand(pieces_ref, basis_ref, mm, at, blocks):
    for block in range(blocks):
        row_at = pl.multiple_of(at + block * COEF_ROWS, COEF_ROWS)
        left = pieces_ref[pl.ds(row_at, COEF_ROWS), :].T.astype(jnp.bfloat16)
        mm[block * LANES : (block + 1) * LANES, :] = jnp.dot(
            left, basis_ref[...], preferred_element_type=jnp.float32
        )


def back_kernel(
    sizes,
    lists_ref,
    lens_ref,
    list_rows_ref,
    basis_ref,
    moment_ref,
    pieces_ref,
    grad_ref,
    out_ref,
    mm,
    weights,
    grad_scr,
    mom_scr,
    row_scr,
    rows,
    table,
):
    cap, lane_len, col_groups, list_len = sizes
    parts = cap // lane_len
    devices = out_ref.shape[0]
    blocks = list_len // STEP_ROWS
    table[...] = jnp.zeros_like(table)
    grad_scr[...] = jnp.zeros_like(grad_scr)
    row_scr[...] = jnp.zeros_like(row_scr)
    rows[...] = jnp.zeros_like(rows)
    zero = jnp.zeros((SUBS, LANES), jnp.float32)
    sub = lax.broadcasted_iota(jnp.int32, (SUBS, LANES), 0)
    lane = lax.broadcasted_iota(jnp.int32, (SUBS, LANES), 1)
    own_tile = lane % GROUP == sub

    def one_group(group, carry):
        view, col_group = group // col_groups, group % col_groups
        most = longest(lens_ref, group)
        at = group * blocks * COEF_ROWS
        lane_at = pl.multiple_of(col_group * LANES, LANES)
        grads = [
            [
                swap_grain(
                    grad_ref[view, c, half * SUBS : (half + 1) * SUBS, pl.ds(lane_at, LANES)]
                )
                for c in range(3)
            ]
            for half in range(2)
        ]
        for half in range(2):
            for c in range(3):
                for piece, part in enumerate(split_three(grads[half][c])):
                    grad_scr[
                        piece * 24 + c * SUBS : piece * 24 + (c + 1) * SUBS,
                        half * LANES : (half + 1) * LANES,
                    ] = part
        expand(pieces_ref, basis_ref, mm, at, blocks)

        def ahead(n, keep):
            row_at = pl.multiple_of(n * GROUP, GROUP)
            new_keep = []
            for half in range(2):
                lanes = slice(half * LANES, (half + 1) * LANES)
                alpha = jnp.exp(mm[pl.ds(row_at, GROUP), lanes])
                weight = keep[half] * alpha
                mm[pl.ds(row_at, GROUP), lanes] = alpha
                weights[pl.ds(row_at, GROUP), lanes] = weight
                new_keep.append(keep[half] - weight)
            return new_keep

        stepped(most, UNROLL, ahead, [zero + 1.0] * 2)

        last = (most + UNROLL - 1) // UNROLL * UNROLL - 1

        def behind(step, seen):
            row_at = pl.multiple_of((last - step) * GROUP, GROUP)
            shade = [
                mm[pl.ds(row_at, GROUP), (2 + c) * LANES : (3 + c) * LANES] for c in range(3)
            ]
            new_seen = []
            for half in range(2):
                lanes = slice(half * LANES, (half + 1) * LANES)
                own = (
                    grads[half][0] * shade[0]
                    + grads[half][1] * shade[1]
                    + grads[half][2] * shade[2]
                )
                gap = own - seen[half]
                alpha = mm[pl.ds(row_at, GROUP), lanes]
                mm[pl.ds(row_at, GROUP), lanes] = weights[pl.ds(row_at, GROUP), lanes] * gap
                new_seen.append(seen[half] + alpha * gap)
            return new_seen

        stepped(most, UNROLL, behind, [zero] * 2)
        grad_cols = grad_scr[...].T.astype(jnp.bfloat16)
        for block in range(blocks):
            span = slice(block * LANES, (block + 1) * LANES)
            total = jnp.zeros((LANES, LANES), jnp.float32)
            for value, right in (
                (mm[span, 0 : 2 * LANES], moment_ref[...]),
                (weights[span, :], grad_cols),
            ):
                high = value.astype(jnp.bfloat16)
                low = (value - high.astype(jnp.float32)).astype(jnp.bfloat16)
                total = total + jnp.dot(high, right, preferred_element_type=jnp.float32)
                total = total + jnp.dot(low, right, preferred_element_type=jnp.float32)
            turned = total.T
            for c in range(3):
                summed = (
                    turned[c * SUBS : (c + 1) * SUBS]
                    + turned[24 + c * SUBS : 24 + (c + 1) * SUBS]
                    + turned[48 + c * SUBS : 48 + (c + 1) * SUBS]
                )
                mom_scr[block * TILE + 8 + c : block * TILE + 9 + c, :] = jnp.sum(
                    jnp.where(own_tile, summed, 0.0), axis=0, keepdims=True
                )
            mom_scr[block * TILE : block * TILE + 8, :] = turned[96:104]
        mom = [mom_scr[pl.ds(num, blocks, stride=TILE), :] for num in range(11)]

        def piece_line(num):
            return pieces_ref[pl.ds(at + num, blocks, stride=COEF_ROWS), :]

        con_xx = -2.0 * (piece_line(3) + piece_line(9) + piece_line(15))
        con_xy = -(piece_line(4) + piece_line(10) + piece_line(16))
        con_yy = -2.0 * (piece_line(5) + piece_line(11) + piece_line(17))
        off_x, off_y = piece_line(27), piece_line(28)
        sum_x = off_x * mom[0] - mom[1]
        sum_y = off_y * mom[0] - mom[2]
        results = [
            -(con_xx * sum_x + con_xy * sum_y),
            -(con_yy * sum_y + con_xy * sum_x),
            -0.5 * (off_x * (sum_x - mom[1]) + mom[3]),
            -(off_x * sum_y - off_y * mom[1] + mom[4]),
            -0.5 * (off_y * (sum_y - mom[2]) + mom[5]),
        ] + mom[8:11]
        other = 1 - view
        for num, value in enumerate(results):
            row_scr[pl.ds(view * FEATS + num, blocks, stride=24), :] = value
            row_scr[pl.ds(other * FEATS + num, blocks, stride=24), :] = jnp.zeros_like(value)
        row_scr[pl.ds(PAIR, blocks, stride=24), :] = mom[0]
        for block in range(blocks):
            rows[block * LANES : (block + 1) * LANES, 0:24] = row_scr[
                block * 24 : (block + 1) * 24, :
            ].T
        names = list_rows_ref[pl.ds(pl.multiple_of(group * GROUP, GROUP), GROUP), :]
        twice = jnp.zeros((GROUP, LANES), jnp.float32)
        for shift in range(1, GROUP // 2 + 1):
            twice = jnp.maximum(
                twice, jnp.where(names == pltpu.roll(names, shift, 0), 1.0, 0.0)
            )
        clash = jnp.max(twice) > 0.5

        @pl.when(jnp.logical_not(clash))
        def _():
            def add(n, inner):
                spots = [lists_ref[group * GROUP + t, n] for t in range(GROUP)]
                held = [table[pl.ds(spot, 1), :] for spot in spots]
                sums = [
                    held[t] + rows[pl.ds(n * GROUP + t, 1), :] for t in range(GROUP)
                ]
                for t in range(GROUP):
                    table[pl.ds(spots[t], 1), :] = sums[t]
                return inner

            stepped(most, UNROLL, add, 0)

        @pl.when(clash)
        def _():
            def add(n, inner):
                for t in range(GROUP):
                    spot = lists_ref[group * GROUP + t, n]
                    table[pl.ds(spot, 1), :] = (
                        table[pl.ds(spot, 1), :] + rows[pl.ds(n * GROUP + t, 1), :]
                    )
                return inner

            lax.fori_loop(0, most, add, 0)

        return carry

    lax.fori_loop(0, 2 * col_groups, one_group, 0)

    def pack(source, carry):
        for part in range(parts):
            row_at = pl.multiple_of(source * cap + part * lane_len, lane_len)
            turned = table[pl.ds(row_at, lane_len), 0:24].T
            out_ref[source, part * PAIR : (part + 1) * PAIR, :] = turned[0:PAIR]
            out_ref[source, parts * PAIR + part : parts * PAIR + part + 1, :] = turned[
                PAIR : PAIR + 1
            ]
        return carry

    lax.fori_loop(0, devices, pack, 0)


def owner_kernel(
    sizes,
    cam_ref,
    list_ref,
    counts_ref,
    params_ref,
    back_ref,
    out_ref,
    tile_scr,
    feat_scr,
    turn_scr,
    table,
    slots,
):
    groups, rows, cap, lane_len, image_width, image_height = sizes
    count_params, per = params_ref.shape
    parts = cap // lane_len
    table[...] = jnp.zeros_like(table)
    turn_scr[PAIR:, :] = jnp.zeros((SUBS, LANES), jnp.float32)
    start = jnp.int32(0)
    for group in range(groups):
        turn_scr[PAIR + 1 : PAIR + 2, :] = jnp.full((1, LANES), 1.0 + group, jnp.float32)

        def take_block(t, start_at, group=group):
            dest = group * rows + t
            count = counts_ref[0, dest]
            base = pl.multiple_of(dest * cap, SUBS)
            for part in range(parts):
                turn_scr[0:PAIR, 0:lane_len] = back_ref[dest, part * PAIR : (part + 1) * PAIR, :]
                turn_scr[PAIR : PAIR + 1, 0:lane_len] = back_ref[
                    dest, parts * PAIR + part : parts * PAIR + part + 1, :
                ]
                slots[pl.ds(base + part * lane_len, lane_len), 0:24] = turn_scr[:, 0:lane_len].T

            def move(k, carry):
                spot = list_ref[0, start_at + k]
                table[pl.ds(spot, 1), :] = slots[pl.ds(base + k, 1), :]
                return carry

            rounded = (count + MOVES - 1) // MOVES * MOVES
            whole = jnp.where(start_at + rounded <= per, rounded, count // MOVES * MOVES)
            stepped(whole, MOVES, move, 0)
            lax.fori_loop(whole, count, move, 0)
            return start_at + count

        start = lax.fori_loop(0, rows, take_block, start)

    def clear(k, carry):
        table[pl.ds(list_ref[0, k], 1), :] = jnp.zeros((1, LANES), jnp.float32)
        return carry

    lax.fori_loop(start, jnp.minimum(start + MOVES, per), clear, 0)

    def pull_block(block, carry):
        params = load_params(params_ref, tile_scr, block)
        for j in range(SUBS):
            row_at = pl.multiple_of(block * SUBS * LANES + j * LANES, LANES)
            feat_scr[j * 24 : (j + 1) * 24, :] = table[pl.ds(row_at, LANES), 0:24].T
        cots = [feat_scr[pl.ds(num, SUBS, stride=24), :] for num in range(PAIR + 2)]
        home = cots[PAIR + 1]
        sent = home > 0.5
        cams = []
        for view in range(2):
            cam = []
            for k in range(15):
                value = jnp.full((SUBS, LANES), cam_ref[view, k], jnp.float32)
                for group in range(1, groups):
                    value = jnp.where(home > 0.5 + group, cam_ref[2 * group + view, k], value)
                cam.append(value)
            cams.append(cam)

        def both(*values):
            shape = shape_matrix(values)
            return (
                view_features(values, shape, cams[0], image_width, image_height)
                + view_features(values, shape, cams[1], image_width, image_height)
                + [log_opacity(values[10])]
            )

        _, pull = jax.vjp(both, *params)
        grads = pull(cots[0 : PAIR + 1])
        for num, value in enumerate(grads):
            tile_scr[pl.ds((num // SUBS) * SUBS * SUBS + num % SUBS, SUBS, stride=SUBS), :] = (
                jnp.where(sent, value, 0.0)
            )
        for band in range(0, count_params, SUBS):
            high = min(band + SUBS, count_params)
            for j in range(SUBS):
                lane_at = pl.multiple_of(block * SUBS * LANES + j * LANES, LANES)
                out_ref[band:high, pl.ds(lane_at, LANES)] = tile_scr[
                    band * SUBS + j * SUBS : band * SUBS + j * SUBS + high - band, :
                ]
        return carry

    lax.fori_loop(0, per // (SUBS * LANES), pull_block, 0)


def tap_rows(read, first, count):
    taps = window_taps()
    total = taps[5] * read(first + 5, count)
    for k in range(5):
        total = total + taps[k] * (read(first + k, count) + read(first + TAPS - 1 - k, count))
    return total


def blur_lanes(value, band):
    return jnp.dot(
        value, band, precision=lax.Precision.HIGHEST, preferred_element_type=jnp.float32
    )


def truth_kernel(band_ref, above_ref, own_ref, below_ref, out_ref, tall, mixed):
    images = own_ref.shape[0]

    def one_image(m, carry):
        whole = jnp.concatenate([above_ref[m], own_ref[m], below_ref[m]], axis=0)
        for field, value in enumerate((whole, whole * whole)):
            tall[...] = value
            row_at = pl.multiple_of((field * images + m) * 2 * TILE, 2 * TILE)
            mixed[pl.ds(row_at, 2 * TILE), :] = tap_rows(
                lambda at, count: tall[at : at + count, :], 6, 2 * TILE
            )
        return carry

    lax.fori_loop(0, images, one_image, 0)
    out_ref[...] = blur_lanes(mixed[...], band_ref[...])


def loss_kernel(
    image_rows,
    row_ref,
    band_ref,
    truth_ref,
    true_above,
    true_own,
    true_below,
    above_ref,
    own_ref,
    below_ref,
    out_ref,
    tall,
    mixed,
    blurred,
    slim,
):
    images = own_ref.shape[0]
    tall_rows = 2 * TILE
    width = own_ref.shape[2]

    def one_image(m, carry):
        whole = jnp.concatenate([above_ref[m], own_ref[m], below_ref[m]], axis=0)
        true = jnp.concatenate([true_above[m], true_own[m], true_below[m]], axis=0)
        for field, value in enumerate((whole, whole * whole, whole * true)):
            tall[field] = value
            row_at = pl.multiple_of((field * images + m) * tall_rows, tall_rows)
            mixed[pl.ds(row_at, tall_rows), :] = tap_rows(
                lambda at, count, field=field: tall[field, at : at + count, :], 6, tall_rows
            )
        return carry

    lax.fori_loop(0, images, one_image, 0)
    blurred[...] = blur_lanes(mixed[...], band_ref[...])
    sub = lax.broadcasted_iota(jnp.int32, (tall_rows, width), 0)
    image_row = row_ref[0] * TILE + sub - 5
    inside = (image_row >= 0) & (image_row < image_rows) & (sub < TILE + 10)

    def one_map(m, carry):
        def field_of(ref, field):
            row_at = pl.multiple_of((field * images + m) * tall_rows, tall_rows)
            return ref[pl.ds(row_at, tall_rows), :]

        mean_one, both_one, cross = [field_of(blurred, field) for field in range(3)]
        mean_two, both_two = field_of(truth_ref, 0), field_of(truth_ref, 1)
        square_one, square_two = mean_one * mean_one, mean_two * mean_two
        mean_cross = mean_one * mean_two
        top_one = 2.0 * mean_cross + SSIM_ONE
        top_two = 2.0 * (cross - mean_cross) + SSIM_TWO
        low_one = square_one + square_two + SSIM_ONE
        low_two = (both_one - square_one) + (both_two - square_two) + SSIM_TWO
        inv_one, inv_two = 1.0 / low_one, 1.0 / low_two
        inv_both = inv_one * inv_two
        value = top_one * top_two * inv_both
        grads = [
            2.0 * mean_two * (top_two - top_one) * inv_both
            - 2.0 * mean_one * value * (inv_one - inv_two),
            -value * inv_two,
            2.0 * top_one * inv_both,
        ]
        for field, grad in enumerate(grads):
            tall[field, 0:tall_rows] = jnp.where(inside, grad, 0.0)
            row_at = pl.multiple_of((field * images + m) * TILE, TILE)
            slim[pl.ds(row_at, TILE), :] = tap_rows(
                lambda at, count, field=field: tall[field, at : at + count, :], 0, TILE
            )
        return carry

    lax.fori_loop(0, images, one_map, 0)
    spread = blur_lanes(slim[...], band_ref[...]).reshape(3, images, TILE, width)
    own, true = own_ref[...], true_own[...]
    gap = own - true
    out_ref[...] = (1.0 - SSIM_SHARE) * gap / jnp.sqrt(gap * gap + SMOOTH_EPS) - SSIM_SHARE * (
        spread[0] + 2.0 * own * spread[1] + true * spread[2]
    )


def band_matrix(width):
    taps = window_taps()
    band = np.zeros((width, width), np.float32)
    for k in range(TAPS):
        band += np.diag(np.full(width - abs(k - 5), taps[k], np.float32), k - 5)
    return jnp.asarray(band)


def pixel_basis():
    pixel = np.arange(TILE * TILE)
    x = (pixel % TILE) - (TILE - 1) / 2.0
    y = (pixel // TILE) - (TILE - 1) / 2.0
    return np.stack([np.ones_like(x), x, y, x * x, x * y, y * y])


def expand_matrix():
    terms = pixel_basis()
    matrix = np.zeros((COEF_ROWS, 5 * LANES), np.float32)
    for piece in range(3):
        matrix[piece * 6 : piece * 6 + 6, 0 : 2 * LANES] = terms
        for c in range(3):
            matrix[18 + piece * 3 + c, (2 + c) * LANES : (3 + c) * LANES] = 1.0
    return jnp.asarray(matrix, jnp.bfloat16)


def moment_matrix():
    matrix = np.zeros((2 * LANES, LANES), np.float32)
    matrix[:, 96:102] = pixel_basis().T
    return jnp.asarray(matrix, jnp.bfloat16)


def smem():
    return pl.BlockSpec(memory_space=pltpu.SMEM)


def vmem():
    return pl.BlockSpec(memory_space=pltpu.VMEM)


def scratch(*shape):
    return pltpu.VMEM(shape, jnp.float32)


def run(kernel, out_shapes, in_specs, scratches, *operands):
    return pl.pallas_call(
        kernel,
        out_shape=out_shapes,
        in_specs=in_specs,
        out_specs=jax.tree.map(lambda _: vmem(), out_shapes),
        scratch_shapes=scratches,
        compiler_params=pltpu.CompilerParams(vmem_limit_bytes=VMEM_BYTES),
    )(*operands)


def shards(params, send_list, send_counts, camera, ground_truth, tile_lists, list_lengths):
    devices = lax.axis_size(("view", "tile"))
    row_devices = lax.axis_size("tile")
    groups = lax.axis_size("view")
    count_params, per_device = params.shape
    capacity = per_device // devices
    lane_len = min(capacity, LANES)
    parts = capacity // lane_len
    tile_cols, list_len = tile_lists.shape[2:]
    col_groups = tile_cols // GROUP
    blocks = list_len // STEP_ROWS
    tile_row = lax.axis_index("tile")
    image_width = float(ground_truth.shape[3])
    image_height = float(ground_truth.shape[2] * row_devices)
    table_rows = per_device + SUBS
    sent_shape = jax.ShapeDtypeStruct((devices, parts * (PAIR + 1), lane_len), jnp.float32)
    cams = camera_table(camera)

    flat_lengths = list_lengths.reshape(-1)
    entry_rank = jnp.arange(list_len, dtype=jnp.int32)
    tile_num = jnp.arange(2 * tile_cols, dtype=jnp.int32)
    lists = jnp.where(
        entry_rank[None, :] < flat_lengths[:, None],
        tile_lists.reshape(2 * tile_cols, list_len),
        per_device + tile_num[:, None] % GROUP,
    )
    lens_rows = jnp.tile(flat_lengths.reshape(-1, GROUP), (1, LANES // GROUP))

    width = ground_truth.shape[3]
    true_own = ground_truth.reshape(-1, TILE, width)
    true_above = from_behind(true_own, "tile", 1)
    true_below = from_behind(true_own, "tile", -1)
    band = band_matrix(width)
    truth_rows = 2 * true_own.shape[0] * 2 * TILE
    truth_blur = run(
        truth_kernel,
        jax.ShapeDtypeStruct((truth_rows, width), jnp.float32),
        [vmem()] * 4,
        [scratch(3 * TILE, width), scratch(truth_rows, width)],
        band,
        true_above,
        true_own,
        true_below,
    )

    own_sizes = (groups, row_devices, capacity, lane_len, image_width, image_height)
    sent = run(
        lambda *refs: source_kernel(own_sizes, *refs),
        sent_shape,
        [smem(), smem(), smem(), vmem()],
        [
            scratch(SUBS * SUBS * SUBS, LANES),
            scratch(SUBS * LANES, LANES),
            scratch(per_device, LANES),
            scratch(per_device, LANES),
        ],
        cams,
        send_list,
        send_counts,
        params,
    )
    arrived = lax.all_to_all(sent, ("view", "tile"), split_axis=0, concat_axis=0, tiled=True)

    tile_sizes = (capacity, lane_len, col_groups, list_len)
    rendered, pieces = run(
        lambda *refs: render_kernel(tile_sizes, *refs),
        (
            jax.ShapeDtypeStruct(ground_truth.shape, jnp.float32),
            jax.ShapeDtypeStruct((2 * col_groups * blocks * COEF_ROWS, LANES), jnp.float32),
        ),
        [smem(), smem(), smem(), vmem(), vmem(), vmem()],
        [
            scratch(24, LANES),
            scratch(table_rows, LANES),
            scratch(blocks * LANES, LANES),
            scratch(blocks * 24, LANES),
            scratch(blocks * LANES, 5 * LANES),
        ],
        tile_row.reshape(1),
        lists,
        flat_lengths,
        lens_rows,
        expand_matrix(),
        arrived,
    )

    images = rendered.reshape(true_own.shape)
    count = images.shape[0]
    grad_image = run(
        lambda *refs: loss_kernel(TILE * row_devices, *refs),
        jax.ShapeDtypeStruct(images.shape, jnp.float32),
        [smem()] + [vmem()] * 8,
        [
            scratch(3, 3 * TILE, width),
            scratch(3 * count * 2 * TILE, width),
            scratch(3 * count * 2 * TILE, width),
            scratch(3 * count * TILE, width),
        ],
        tile_row.reshape(1),
        band,
        truth_blur,
        true_above,
        true_own,
        true_below,
        from_behind(images, "tile", 1),
        images,
        from_behind(images, "tile", -1),
    ).reshape(ground_truth.shape)

    grad_slots = run(
        lambda *refs: back_kernel(tile_sizes, *refs),
        sent_shape,
        [smem(), smem(), vmem(), vmem(), vmem(), vmem(), vmem()],
        [
            scratch(blocks * LANES, 5 * LANES),
            scratch(blocks * LANES, 2 * LANES),
            scratch(LANES, 2 * LANES),
            scratch(blocks * TILE, LANES),
            scratch(blocks * 24, LANES),
            scratch(blocks * LANES, LANES),
            scratch(table_rows, LANES),
        ],
        lists,
        flat_lengths,
        lists,
        expand_matrix(),
        moment_matrix(),
        pieces,
        grad_image,
    )
    returned = lax.all_to_all(
        grad_slots, ("view", "tile"), split_axis=0, concat_axis=0, tiled=True
    )
    return run(
        lambda *refs: owner_kernel(own_sizes, *refs),
        jax.ShapeDtypeStruct(params.shape, jnp.float32),
        [smem(), smem(), smem(), vmem(), vmem()],
        [
            scratch(SUBS * SUBS * SUBS, LANES),
            scratch(SUBS * 24, LANES),
            scratch(24, LANES),
            scratch(per_device, LANES),
            scratch(per_device, LANES),
        ],
        cams,
        send_list,
        send_counts,
        params,
        returned,
    )


def solution(mesh):
    in_specs = (
        P(None, ("view", "tile")),
        P(("view", "tile"), None),
        P(("view", "tile"), None),
        P(),
        P("view", None, "tile", None),
        P("view", "tile", None, None),
        P("view", "tile", None),
    )
    out_specs = P(None, ("view", "tile"))
    return jax.shard_map(shards, mesh=mesh, in_specs=in_specs, out_specs=out_specs, check_vma=False)
```

```python
import jax
import jax.numpy as jnp
import numpy as np
from jax import lax
from jax.experimental import pallas as pl
from jax.experimental.pallas import tpu as pltpu
from jax.sharding import PartitionSpec as P

TILE = 16


FOCAL = 1000.0
LOW_PASS = 0.3
SSIM_SHARE = 0.2
SMOOTH_EPS = 1e-06
SSIM_ONE = 0.0001
SSIM_TWO = 0.0009
HARMONIC_ZERO = 0.28209479177387814
HARMONIC_ONE = 0.4886025119029199
HARMONIC_TWO = (
    1.0925484305920792,
    -1.0925484305920792,
    0.31539156525252005,
    -1.0925484305920792,
    0.5462742152960396,
)
HARMONIC_THREE = (
    -0.5900435899266435,
    2.890611442640554,
    -0.4570457994644658,
    0.3731763325901154,
    -0.4570457994644658,
    1.445305721320277,
    -0.5900435899266435,
)


def from_behind(block, axis, distance):
    devices = range(lax.axis_size(axis))
    route = [(i - distance, i) for i in devices if i - distance in devices]
    return lax.ppermute(block, axis, route)


def window_taps():
    offsets_np = np.arange(11) - 5.0
    weights = np.exp(-offsets_np * offsets_np / 4.5)
    weights = weights / weights.sum()
    return [float(weight) for weight in weights]


def matrix_product(left_side, right_side):
    return [
        [
            left_side[row_idx][0] * right_side[0][col_idx]
            + left_side[row_idx][1] * right_side[1][col_idx]
            + left_side[row_idx][2] * right_side[2][col_idx]
            for col_idx in range(3)
        ]
        for row_idx in range(3)
    ]


def rotation(angles):
    cos_a, sin_a = (jnp.cos(angles[0]), jnp.sin(angles[0]))
    cos_b, sin_b = (jnp.cos(angles[1]), jnp.sin(angles[1]))
    cos_c, sin_c = (jnp.cos(angles[2]), jnp.sin(angles[2]))
    about_x = [[1.0, 0.0, 0.0], [0.0, cos_a, -sin_a], [0.0, sin_a, cos_a]]
    about_y = [[cos_b, 0.0, sin_b], [0.0, 1.0, 0.0], [-sin_b, 0.0, cos_b]]
    about_z = [[cos_c, -sin_c, 0.0], [sin_c, cos_c, 0.0], [0.0, 0.0, 1.0]]
    return matrix_product(about_z, matrix_product(about_y, about_x))


def harmonics(dir_x, dir_y, dir_z):
    sq_x, sq_y, sq_z = (dir_x * dir_x, dir_y * dir_y, dir_z * dir_z)
    prod_xy, prod_yz, prod_xz = (dir_x * dir_y, dir_y * dir_z, dir_x * dir_z)
    return [
        HARMONIC_ZERO + 0.0 * dir_x,
        -HARMONIC_ONE * dir_y,
        HARMONIC_ONE * dir_z,
        -HARMONIC_ONE * dir_x,
        HARMONIC_TWO[0] * prod_xy,
        HARMONIC_TWO[1] * prod_yz,
        HARMONIC_TWO[2] * (2.0 * sq_z - sq_x - sq_y),
        HARMONIC_TWO[3] * prod_xz,
        HARMONIC_TWO[4] * (sq_x - sq_y),
        HARMONIC_THREE[0] * dir_y * (3.0 * sq_x - sq_y),
        HARMONIC_THREE[1] * prod_xy * dir_z,
        HARMONIC_THREE[2] * dir_y * (4.0 * sq_z - sq_x - sq_y),
        HARMONIC_THREE[3] * dir_z * (2.0 * sq_z - 3.0 * sq_x - 3.0 * sq_y),
        HARMONIC_THREE[4] * dir_x * (4.0 * sq_z - sq_x - sq_y),
        HARMONIC_THREE[5] * dir_z * (sq_x - sq_y),
        HARMONIC_THREE[6] * dir_x * (sq_x - 3.0 * sq_y),
    ]


LANES = 128
SUBS = 8
GROUP = 8
STEP_ROWS = 16
FEATS = 8
PAIR = 2 * FEATS
COEF_ROWS = 32
SLOT = PAIR + 2
PACK = LANES // SLOT
BATCH = 4
UNROLL = 8
MOVES = 16
TAPS = 11
DEAD = -1e30
LOG_TOP = float(np.log(0.99))
VMEM_BYTES = 48 * 1024 * 1024


def stepped(total, width, body, state):
    def step(block, held):
        for k in range(width):
            held = body(block * width + k, held)
        return held

    return lax.fori_loop(0, (total + width - 1) // width, step, state)


def packed_rows(cap):
    return -(-cap // (PACK * SUBS)) * SUBS


def pack_slots(read, rows, first_lane):
    lane = lax.broadcasted_iota(jnp.int32, (rows, LANES), 1)
    packed = jnp.zeros((rows, LANES), jnp.float32)
    for q in range(PACK):
        shift = (q * SLOT - first_lane) % LANES
        value = read(q * rows)
        value = pltpu.roll(value, shift, 1) if shift else value
        packed = jnp.where((lane >= q * SLOT) & (lane < (q + 1) * SLOT), value, packed)
    return packed


def unpack_slots(packed, write):
    for q in range(PACK):
        write(q * packed.shape[0], pltpu.roll(packed, LANES - q * SLOT, 1) if q else packed)


def camera_table(camera):
    columns = [camera[:, entry] for entry in range(6)]
    turn = rotation(columns[0:3])
    shift = columns[3:6]
    anchor = [
        -(turn[0][c] * shift[0] + turn[1][c] * shift[1] + turn[2][c] * shift[2]) for c in range(3)
    ]
    flat = [turn[r][c] for r in range(3) for c in range(3)] + shift + anchor
    return jnp.stack(flat + [jnp.zeros_like(shift[0])], axis=1)


def shape_matrix(params):
    scales = [jnp.exp(params[3 + axis_num]) for axis_num in range(3)]
    inv_norm = 1.0 / jnp.sqrt(
        params[6] * params[6]
        + params[7] * params[7]
        + params[8] * params[8]
        + params[9] * params[9]
    )
    quat_w, quat_x, quat_y, quat_z = [params[6 + k] * inv_norm for k in range(4)]
    quat_rot = [
        [
            1.0 - 2.0 * (quat_y * quat_y + quat_z * quat_z),
            2.0 * (quat_x * quat_y - quat_w * quat_z),
            2.0 * (quat_x * quat_z + quat_w * quat_y),
        ],
        [
            2.0 * (quat_x * quat_y + quat_w * quat_z),
            1.0 - 2.0 * (quat_x * quat_x + quat_z * quat_z),
            2.0 * (quat_y * quat_z - quat_w * quat_x),
        ],
        [
            2.0 * (quat_x * quat_z - quat_w * quat_y),
            2.0 * (quat_y * quat_z + quat_w * quat_x),
            1.0 - 2.0 * (quat_x * quat_x + quat_y * quat_y),
        ],
    ]
    return [[quat_rot[r][c] * scales[c] for c in range(3)] for r in range(3)]


def view_features(params, shape, cam, image_width, image_height):
    turn = [[cam[3 * r + c] for c in range(3)] for r in range(3)]
    point = [
        turn[r][0] * params[0] + turn[r][1] * params[1] + turn[r][2] * params[2] + cam[9 + r]
        for r in range(3)
    ]
    inv_depth = 1.0 / point[2]
    ratio_x, ratio_y = point[0] * inv_depth, point[1] * inv_depth
    zoom = FOCAL * inv_depth
    row_x = [zoom * (turn[0][c] - ratio_x * turn[2][c]) for c in range(3)]
    row_y = [zoom * (turn[1][c] - ratio_y * turn[2][c]) for c in range(3)]
    proj_x = [
        row_x[0] * shape[0][c] + row_x[1] * shape[1][c] + row_x[2] * shape[2][c] for c in range(3)
    ]
    proj_y = [
        row_y[0] * shape[0][c] + row_y[1] * shape[1][c] + row_y[2] * shape[2][c] for c in range(3)
    ]
    cov_xx = proj_x[0] * proj_x[0] + proj_x[1] * proj_x[1] + proj_x[2] * proj_x[2] + LOW_PASS
    cov_xy = proj_x[0] * proj_y[0] + proj_x[1] * proj_y[1] + proj_x[2] * proj_y[2]
    cov_yy = proj_y[0] * proj_y[0] + proj_y[1] * proj_y[1] + proj_y[2] * proj_y[2] + LOW_PASS
    inv_det = 1.0 / (cov_xx * cov_yy - cov_xy * cov_xy)
    ray = [params[c] - cam[12 + c] for c in range(3)]
    inv_len = 1.0 / jnp.sqrt(ray[0] * ray[0] + ray[1] * ray[1] + ray[2] * ray[2])
    basis = harmonics(ray[0] * inv_len, ray[1] * inv_len, ray[2] * inv_len)
    colours = []
    for channel in range(3):
        summed = 0.5 + HARMONIC_ZERO * params[11 + 16 * channel]
        for harmonic in range(1, 16):
            summed = summed + basis[harmonic] * params[11 + 16 * channel + harmonic]
        colours.append(summed)
    return [
        FOCAL * ratio_x + image_width / 2.0,
        FOCAL * ratio_y + image_height / 2.0,
        cov_yy * inv_det,
        -cov_xy * inv_det,
        cov_xx * inv_det,
    ] + colours


def log_opacity(logit):
    return LOG_TOP - jnp.log(1.0 + jnp.exp(-logit))


def load_params(params_ref, tile_scr, block):
    count = params_ref.shape[0]
    for band in range(0, count, SUBS):
        high = min(band + SUBS, count)
        for j in range(SUBS):
            lane_at = pl.multiple_of(block * SUBS * LANES + j * LANES, LANES)
            tile_scr[band * SUBS + j * SUBS : band * SUBS + j * SUBS + high - band, :] = params_ref[
                band:high, pl.ds(lane_at, LANES)
            ]
    return [
        tile_scr[pl.ds((r // SUBS) * SUBS * SUBS + r % SUBS, SUBS, stride=SUBS), :]
        for r in range(count)
    ]


def source_kernel(
    sizes, cam_ref, list_ref, counts_ref, params_ref, out_ref, tile_scr, feat_scr, table, slots
):
    groups, rows, cap, image_width, image_height = sizes
    per = params_ref.shape[1]
    views = cam_ref.shape[0]
    height = out_ref.shape[1]
    used = -(-groups * SLOT // SUBS) * SUBS

    def project_block(block, carry):
        params = load_params(params_ref, tile_scr, block)
        shape = shape_matrix(params)
        log_o = log_opacity(params[10])
        for view in range(views):
            cam = [cam_ref[view, k] for k in range(15)]
            for num, value in enumerate(
                view_features(params, shape, cam, image_width, image_height)
            ):
                line = view // 2 * SLOT + view % 2 * FEATS + num
                feat_scr[pl.ds(line, SUBS, stride=used), :] = value
        for group in range(groups):
            feat_scr[pl.ds(group * SLOT + PAIR, SUBS, stride=used), :] = log_o
        for j in range(SUBS):
            row_at = pl.multiple_of(block * SUBS * LANES + j * LANES, LANES)
            table[pl.ds(row_at, LANES), 0:used] = feat_scr[j * used : (j + 1) * used, :].T
        return carry

    lax.fori_loop(0, per // (SUBS * LANES), project_block, 0)

    start = jnp.int32(0)
    for group in range(groups):

        def send_block(t, start_at, group=group):
            dest = group * rows + t
            count = counts_ref[0, dest]

            def move(k, carry):
                spot = jnp.minimum(start_at + k, per - 1)
                slots[pl.ds(k, 1), :] = table[pl.ds(list_ref[0, spot], 1), :]
                return carry

            stepped(count, MOVES, move, 0)
            out_ref[dest] = pack_slots(
                lambda at: slots[at : at + height, :], height, group * SLOT
            )
            return start_at + count

        start = lax.fori_loop(0, rows, send_block, start)


def split_three(value):
    first = value.astype(jnp.bfloat16).astype(jnp.float32)
    rest = value - first
    second = rest.astype(jnp.bfloat16).astype(jnp.float32)
    return [first, second, rest - second]


def swap_grain(cells):
    sub = lax.broadcasted_iota(jnp.int32, (SUBS, LANES), 0)
    lane = lax.broadcasted_iota(jnp.int32, (SUBS, LANES), 1) // TILE
    for bit in (1, 2, 4):
        sub_bit, lane_bit = (sub & bit) != 0, (lane & bit) != 0
        from_high = pltpu.roll(pltpu.roll(cells, SUBS - bit, 0), bit * TILE, 1)
        from_low = pltpu.roll(pltpu.roll(cells, bit, 0), LANES - bit * TILE, 1)
        cells = jnp.where(sub_bit == lane_bit, cells, jnp.where(lane_bit, from_high, from_low))
    return cells


def longest(lens_ref, group):
    most = lens_ref[group * GROUP]
    for t in range(1, GROUP):
        most = jnp.maximum(most, lens_ref[group * GROUP + t])
    return most


def render_kernel(
    sizes,
    row_ref,
    lists_ref,
    lens_ref,
    lens_rows_ref,
    basis_ref,
    arrived_ref,
    image_ref,
    left_ref,
    shape_ref,
    table,
    rows,
    feat_scr,
    pieces,
    mm,
):
    cap, col_groups, list_len = sizes
    devices, height = arrived_ref.shape[0:2]
    blocks = list_len // STEP_ROWS
    table[devices * cap :, :] = jnp.zeros((BATCH * GROUP, LANES), jnp.float32)

    def unpack(source, carry):
        def write(at, value):
            size = min(height, cap - at)
            if size > 0:
                row_at = pl.multiple_of(source * cap + at, SUBS)
                table[pl.ds(row_at, size), :] = value[0:size]

        unpack_slots(arrived_ref[source], write)
        return carry

    lax.fori_loop(0, devices, unpack, 0)
    centre_y = (row_ref[0] * TILE).astype(jnp.float32) + (TILE - 1) / 2.0
    sub = lax.broadcasted_iota(jnp.int32, (blocks, LANES), 0)
    lane = lax.broadcasted_iota(jnp.int32, (blocks, LANES), 1)
    zero = jnp.zeros((SUBS, LANES), jnp.float32)

    def one_group(group, carry):
        view, col_group = group // col_groups, group % col_groups
        most = longest(lens_ref, group)

        def fetch(n, inner):
            for t in range(GROUP):
                slot = lists_ref[group * GROUP + t, n]
                rows[pl.ds(n * GROUP + t, 1), :] = table[pl.ds(slot, 1), :]
            return inner

        stepped(most, UNROLL, fetch, 0)
        for block in range(blocks):
            feat_scr[block * 24 : (block + 1) * 24, :] = rows[
                block * LANES : (block + 1) * LANES, 0:24
            ].T
        feats = [
            feat_scr[pl.ds(view * FEATS + num, blocks, stride=24), :] for num in range(FEATS)
        ]
        log_o = feat_scr[pl.ds(PAIR, blocks, stride=24), :]
        live = sub * STEP_ROWS + lane // GROUP < lens_rows_ref[pl.ds(group, 1), :]
        centre_x = ((col_group * GROUP + lane % GROUP) * TILE).astype(jnp.float32) + (
            TILE - 1
        ) / 2.0
        off_x, off_y = feats[0] - centre_x, feats[1] - centre_y
        lin_x = feats[2] * off_x + feats[3] * off_y
        lin_y = feats[4] * off_y + feats[3] * off_x
        coefs = [
            log_o - 0.5 * (off_x * lin_x + off_y * lin_y),
            lin_x,
            lin_y,
            -0.5 * feats[2],
            -feats[3],
            -0.5 * feats[4],
        ]
        coefs = [
            jnp.where(live, value, DEAD if num == 0 else 0.0) for num, value in enumerate(coefs)
        ]
        lines = [None] * COEF_ROWS
        for num, value in enumerate(coefs):
            for piece, part in enumerate(split_three(value)):
                lines[piece * 6 + num] = part
        for num in range(3):
            for piece, part in enumerate(split_three(jnp.where(live, feats[5 + num], 0.0))):
                lines[18 + piece * 3 + num] = part
        for num, value in enumerate(lines):
            pieces[pl.ds(num, blocks, stride=COEF_ROWS), :] = (
                jnp.zeros((blocks, LANES), jnp.float32) if value is None else value
            )
        for num, value in enumerate(feats[2:5] + [off_x, off_y]):
            shape_ref[num, pl.ds(pl.multiple_of(group * blocks, blocks), blocks), :] = jnp.where(
                live, value, 0.0
            )
        left_at = pl.multiple_of(group * blocks * LANES, LANES)
        for block in range(blocks):
            left_ref[pl.ds(left_at + block * LANES, LANES), :] = pieces[
                block * COEF_ROWS : (block + 1) * COEF_ROWS, :
            ].T.astype(jnp.bfloat16)
        expand(left_ref, basis_ref, mm, left_at)

        def entry(n, state):
            keep, colour = state
            row_at = pl.multiple_of(n * GROUP, GROUP)
            shade = [
                mm[pl.ds(row_at, GROUP), (2 + c) * LANES : (3 + c) * LANES] for c in range(3)
            ]
            new_keep, new_colour = [], []
            for half in range(2):
                alpha = jnp.exp(mm[pl.ds(row_at, GROUP), half * LANES : (half + 1) * LANES])
                weight = keep[half] * alpha
                new_keep.append(keep[half] - weight)
                new_colour.append([colour[half][c] + weight * shade[c] for c in range(3)])
            return new_keep, new_colour

        state = ([zero + 1.0] * 2, [[zero] * 3] * 2)
        _, colour = stepped(most, UNROLL, entry, state)
        lane_at = pl.multiple_of(col_group * LANES, LANES)
        for half in range(2):
            for c in range(3):
                image_ref[view, c, half * SUBS : (half + 1) * SUBS, pl.ds(lane_at, LANES)] = (
                    swap_grain(colour[half][c])
                )
        return carry

    lax.fori_loop(0, 2 * col_groups, one_group, 0)


def expand(left_ref, basis_ref, mm, left_at):
    mm[...] = jnp.dot(
        left_ref[pl.ds(left_at, mm.shape[0]), :],
        basis_ref[...],
        preferred_element_type=jnp.float32,
    )


def times_transposed(left, right):
    return lax.dot_general(
        left, right, (((1,), (1,)), ((), ())), preferred_element_type=jnp.float32
    )


def back_kernel(
    sizes,
    lists_ref,
    lens_ref,
    list_rows_ref,
    basis_ref,
    moment_ref,
    left_ref,
    shape_ref,
    grad_ref,
    out_ref,
    mm,
    weights,
    grad_scr,
    mom_scr,
    row_scr,
    rows,
    table,
):
    cap, col_groups, list_len = sizes
    devices, height = out_ref.shape[0:2]
    blocks = list_len // STEP_ROWS
    table[...] = jnp.zeros_like(table)
    row_scr[...] = jnp.zeros_like(row_scr)
    rows[...] = jnp.zeros_like(rows)
    grad_scr[...] = jnp.zeros_like(grad_scr)
    zero = jnp.zeros((SUBS, LANES), jnp.float32)
    sub = lax.broadcasted_iota(jnp.int32, (SUBS, LANES), 0)
    lane = lax.broadcasted_iota(jnp.int32, (SUBS, LANES), 1)
    own_tile = lane % GROUP == sub

    def one_group(group, carry):
        view, col_group = group // col_groups, group % col_groups
        most = longest(lens_ref, group)
        lane_at = pl.multiple_of(col_group * LANES, LANES)
        grads = [
            [
                swap_grain(
                    grad_ref[view, c, half * SUBS : (half + 1) * SUBS, pl.ds(lane_at, LANES)]
                )
                for c in range(3)
            ]
            for half in range(2)
        ]
        for half in range(2):
            for c in range(3):
                for piece, part in enumerate(split_three(grads[half][c])):
                    grad_scr[
                        piece * 24 + c * SUBS : piece * 24 + (c + 1) * SUBS,
                        half * LANES : (half + 1) * LANES,
                    ] = part
        expand(left_ref, basis_ref, mm, pl.multiple_of(group * blocks * LANES, LANES))

        def ahead(n, keep):
            row_at = pl.multiple_of(n * GROUP, GROUP)
            new_keep = []
            for half in range(2):
                lanes = slice(half * LANES, (half + 1) * LANES)
                alpha = jnp.exp(mm[pl.ds(row_at, GROUP), lanes])
                weight = keep[half] * alpha
                mm[pl.ds(row_at, GROUP), lanes] = alpha
                weights[pl.ds(row_at, GROUP), lanes] = weight
                new_keep.append(keep[half] - weight)
            return new_keep

        stepped(most, UNROLL, ahead, [zero + 1.0] * 2)

        last = (most + UNROLL - 1) // UNROLL * UNROLL - 1

        def behind(step, seen):
            row_at = pl.multiple_of((last - step) * GROUP, GROUP)
            shade = [
                mm[pl.ds(row_at, GROUP), (2 + c) * LANES : (3 + c) * LANES] for c in range(3)
            ]
            new_seen = []
            for half in range(2):
                lanes = slice(half * LANES, (half + 1) * LANES)
                own = (
                    grads[half][0] * shade[0]
                    + grads[half][1] * shade[1]
                    + grads[half][2] * shade[2]
                )
                gap = own - seen[half]
                alpha = mm[pl.ds(row_at, GROUP), lanes]
                mm[pl.ds(row_at, GROUP), lanes] = weights[pl.ds(row_at, GROUP), lanes] * gap
                new_seen.append(seen[half] + alpha * gap)
            return new_seen

        stepped(most, UNROLL, behind, [zero] * 2)
        grad_rows = grad_scr[...].astype(jnp.bfloat16)
        wide = 2 * LANES
        for part in range(blocks * LANES // wide):
            span = slice(part * wide, (part + 1) * wide)
            sums = []
            for value, left in ((mm[span, 0:wide], moment_ref[...]), (weights[span, :], grad_rows)):
                high = value.astype(jnp.bfloat16)
                low = (value - high.astype(jnp.float32)).astype(jnp.bfloat16)
                sums.append(times_transposed(left, high) + times_transposed(left, low))
            moments, colours = sums
            for k in range(wide // LANES):
                block = part * (wide // LANES) + k
                lanes = slice(k * LANES, (k + 1) * LANES)
                mom_scr[block * TILE : block * TILE + 8, :] = moments[0:8, lanes]
                for c in range(3):
                    summed = (
                        colours[c * SUBS : (c + 1) * SUBS, lanes]
                        + colours[24 + c * SUBS : 24 + (c + 1) * SUBS, lanes]
                        + colours[48 + c * SUBS : 48 + (c + 1) * SUBS, lanes]
                    )
                    mom_scr[block * TILE + 8 + c : block * TILE + 9 + c, :] = jnp.sum(
                        jnp.where(own_tile, summed, 0.0), axis=0, keepdims=True
                    )
        mom = [mom_scr[pl.ds(num, blocks, stride=TILE), :] for num in range(11)]
        con_xx, con_xy, con_yy, off_x, off_y = [
            shape_ref[num, pl.ds(pl.multiple_of(group * blocks, blocks), blocks), :]
            for num in range(5)
        ]
        sum_x = off_x * mom[0] - mom[1]
        sum_y = off_y * mom[0] - mom[2]
        results = [
            -(con_xx * sum_x + con_xy * sum_y),
            -(con_yy * sum_y + con_xy * sum_x),
            -0.5 * (off_x * (sum_x - mom[1]) + mom[3]),
            -(off_x * sum_y - off_y * mom[1] + mom[4]),
            -0.5 * (off_y * (sum_y - mom[2]) + mom[5]),
        ] + mom[8:11]
        other = 1 - view
        for num, value in enumerate(results):
            row_scr[pl.ds(view * FEATS + num, blocks, stride=24), :] = value
            row_scr[pl.ds(other * FEATS + num, blocks, stride=24), :] = jnp.zeros_like(value)
        row_scr[pl.ds(PAIR, blocks, stride=24), :] = mom[0]
        for block in range(blocks):
            rows[block * LANES : (block + 1) * LANES, 0:24] = row_scr[
                block * 24 : (block + 1) * 24, :
            ].T
        names = list_rows_ref[pl.ds(pl.multiple_of(group * GROUP, GROUP), GROUP), :]
        twice = jnp.zeros((GROUP, LANES), jnp.float32)
        for far in range(BATCH):
            moved = pltpu.roll(names, far, 1) if far else names
            for shift in range(0 if far else 1, GROUP if far else GROUP // 2 + 1):
                turned = pltpu.roll(moved, shift, 0) if shift else moved
                twice = jnp.maximum(twice, jnp.where(names == turned, 1.0, 0.0))
        clash = jnp.max(twice) > 0.5

        @pl.when(jnp.logical_not(clash))
        def _():
            def add(step, inner):
                pairs = [(step * BATCH + k, t) for k in range(BATCH) for t in range(GROUP)]
                spots = [lists_ref[group * GROUP + t, n] for n, t in pairs]
                held = [table[pl.ds(spot, 1), :] for spot in spots]
                sums = [
                    value + rows[pl.ds(n * GROUP + t, 1), :] for value, (n, t) in zip(held, pairs)
                ]
                for spot, value in zip(spots, sums):
                    table[pl.ds(spot, 1), :] = value
                return inner

            stepped((most + BATCH - 1) // BATCH, UNROLL // BATCH, add, 0)

        @pl.when(clash)
        def _():
            def add(n, inner):
                for t in range(GROUP):
                    spot = lists_ref[group * GROUP + t, n]
                    table[pl.ds(spot, 1), :] = (
                        table[pl.ds(spot, 1), :] + rows[pl.ds(n * GROUP + t, 1), :]
                    )
                return inner

            lax.fori_loop(0, most, add, 0)

        return carry

    lax.fori_loop(0, 2 * col_groups, one_group, 0)

    def pack(source, carry):
        def read(at):
            size = min(height, cap - at)
            if size <= 0:
                return jnp.zeros((height, LANES), jnp.float32)
            value = table[pl.ds(pl.multiple_of(source * cap + at, SUBS), size), :]
            if size < height:
                value = jnp.concatenate(
                    [value, jnp.zeros((height - size, LANES), jnp.float32)], axis=0
                )
            return value

        out_ref[source] = pack_slots(read, height, 0)
        return carry

    lax.fori_loop(0, devices, pack, 0)


def owner_kernel(
    sizes,
    cam_ref,
    list_ref,
    counts_ref,
    params_ref,
    back_ref,
    out_ref,
    tile_scr,
    feat_scr,
    table,
    slots,
):
    groups, rows, cap, image_width, image_height = sizes
    count_params, per = params_ref.shape
    height = back_ref.shape[1]
    table[...] = jnp.zeros_like(table)
    lane = lax.broadcasted_iota(jnp.int32, (height, LANES), 1)
    start = jnp.int32(0)
    for group in range(groups):

        def take_block(t, start_at, group=group):
            dest = group * rows + t
            count = counts_ref[0, dest]

            def write(at, value):
                slots[at : at + height, :] = jnp.where(lane == PAIR + 1, 1.0 + group, value)

            unpack_slots(back_ref[dest], write)

            def move(k, carry):
                spot = list_ref[0, start_at + k]
                table[pl.ds(spot, 1), :] = slots[pl.ds(k, 1), :]
                return carry

            rounded = (count + MOVES - 1) // MOVES * MOVES
            whole = jnp.where(start_at + rounded <= per, rounded, count // MOVES * MOVES)
            stepped(whole, MOVES, move, 0)
            lax.fori_loop(whole, count, move, 0)
            return start_at + count

        start = lax.fori_loop(0, rows, take_block, start)

    def clear(k, carry):
        table[pl.ds(list_ref[0, k], 1), :] = jnp.zeros((1, LANES), jnp.float32)
        return carry

    lax.fori_loop(start, jnp.minimum(start + MOVES, per), clear, 0)

    def pull_block(block, carry):
        params = load_params(params_ref, tile_scr, block)
        for j in range(SUBS):
            row_at = pl.multiple_of(block * SUBS * LANES + j * LANES, LANES)
            feat_scr[j * 24 : (j + 1) * 24, :] = table[pl.ds(row_at, LANES), 0:24].T
        cots = [feat_scr[pl.ds(num, SUBS, stride=24), :] for num in range(PAIR + 2)]
        home = cots[PAIR + 1]
        sent = home > 0.5
        cams = []
        for view in range(2):
            cam = []
            for k in range(15):
                value = jnp.full((SUBS, LANES), cam_ref[view, k], jnp.float32)
                for group in range(1, groups):
                    value = jnp.where(home > 0.5 + group, cam_ref[2 * group + view, k], value)
                cam.append(value)
            cams.append(cam)

        def both(*values):
            shape = shape_matrix(values)
            return (
                view_features(values, shape, cams[0], image_width, image_height)
                + view_features(values, shape, cams[1], image_width, image_height)
                + [log_opacity(values[10])]
            )

        _, pull = jax.vjp(both, *params)
        grads = pull(cots[0 : PAIR + 1])
        for num, value in enumerate(grads):
            tile_scr[pl.ds((num // SUBS) * SUBS * SUBS + num % SUBS, SUBS, stride=SUBS), :] = (
                jnp.where(sent, value, 0.0)
            )
        for band in range(0, count_params, SUBS):
            high = min(band + SUBS, count_params)
            for j in range(SUBS):
                lane_at = pl.multiple_of(block * SUBS * LANES + j * LANES, LANES)
                out_ref[band:high, pl.ds(lane_at, LANES)] = tile_scr[
                    band * SUBS + j * SUBS : band * SUBS + j * SUBS + high - band, :
                ]
        return carry

    lax.fori_loop(0, per // (SUBS * LANES), pull_block, 0)


def tap_rows(read, first, count):
    taps = window_taps()
    total = taps[5] * read(first + 5, count)
    for k in range(5):
        total = total + taps[k] * (read(first + k, count) + read(first + TAPS - 1 - k, count))
    return total


def blur_lanes(value, band):
    return jnp.dot(
        value, band, precision=lax.Precision.HIGHEST, preferred_element_type=jnp.float32
    )


def truth_kernel(band_ref, above_ref, own_ref, below_ref, out_ref, tall, mixed):
    images = own_ref.shape[0]

    def one_image(m, carry):
        whole = jnp.concatenate([above_ref[m], own_ref[m], below_ref[m]], axis=0)
        for field, value in enumerate((whole, whole * whole)):
            tall[...] = value
            row_at = pl.multiple_of((field * images + m) * 2 * TILE, 2 * TILE)
            mixed[pl.ds(row_at, 2 * TILE), :] = tap_rows(
                lambda at, count: tall[at : at + count, :], 6, 2 * TILE
            )
        return carry

    lax.fori_loop(0, images, one_image, 0)
    out_ref[...] = blur_lanes(mixed[...], band_ref[...])


def loss_kernel(
    image_rows,
    row_ref,
    band_ref,
    truth_ref,
    true_above,
    true_own,
    true_below,
    above_ref,
    own_ref,
    below_ref,
    out_ref,
    tall,
    mixed,
    blurred,
    slim,
):
    images = own_ref.shape[0]
    tall_rows = 2 * TILE
    width = own_ref.shape[2]

    def one_image(m, carry):
        whole = jnp.concatenate([above_ref[m], own_ref[m], below_ref[m]], axis=0)
        true = jnp.concatenate([true_above[m], true_own[m], true_below[m]], axis=0)
        for field, value in enumerate((whole, whole * whole, whole * true)):
            tall[field] = value
            row_at = pl.multiple_of((field * images + m) * tall_rows, tall_rows)
            mixed[pl.ds(row_at, tall_rows), :] = tap_rows(
                lambda at, count, field=field: tall[field, at : at + count, :], 6, tall_rows
            )
        return carry

    lax.fori_loop(0, images, one_image, 0)
    blurred[...] = blur_lanes(mixed[...], band_ref[...])
    sub = lax.broadcasted_iota(jnp.int32, (tall_rows, width), 0)
    image_row = row_ref[0] * TILE + sub - 5
    inside = (image_row >= 0) & (image_row < image_rows) & (sub < TILE + 10)

    def one_map(m, carry):
        def field_of(ref, field):
            row_at = pl.multiple_of((field * images + m) * tall_rows, tall_rows)
            return ref[pl.ds(row_at, tall_rows), :]

        mean_one, both_one, cross = [field_of(blurred, field) for field in range(3)]
        mean_two, both_two = field_of(truth_ref, 0), field_of(truth_ref, 1)
        square_one, square_two = mean_one * mean_one, mean_two * mean_two
        mean_cross = mean_one * mean_two
        top_one = 2.0 * mean_cross + SSIM_ONE
        top_two = 2.0 * (cross - mean_cross) + SSIM_TWO
        low_one = square_one + square_two + SSIM_ONE
        low_two = (both_one - square_one) + (both_two - square_two) + SSIM_TWO
        inv_one, inv_two = 1.0 / low_one, 1.0 / low_two
        inv_both = inv_one * inv_two
        value = top_one * top_two * inv_both
        grads = [
            2.0 * mean_two * (top_two - top_one) * inv_both
            - 2.0 * mean_one * value * (inv_one - inv_two),
            -value * inv_two,
            2.0 * top_one * inv_both,
        ]
        for field, grad in enumerate(grads):
            tall[field, 0:tall_rows] = jnp.where(inside, grad, 0.0)
            row_at = pl.multiple_of((field * images + m) * TILE, TILE)
            slim[pl.ds(row_at, TILE), :] = tap_rows(
                lambda at, count, field=field: tall[field, at : at + count, :], 0, TILE
            )
        return carry

    lax.fori_loop(0, images, one_map, 0)
    spread = blur_lanes(slim[...], band_ref[...]).reshape(3, images, TILE, width)
    own, true = own_ref[...], true_own[...]
    gap = own - true
    out_ref[...] = (1.0 - SSIM_SHARE) * gap / jnp.sqrt(gap * gap + SMOOTH_EPS) - SSIM_SHARE * (
        spread[0] + 2.0 * own * spread[1] + true * spread[2]
    )


def band_matrix(width):
    taps = window_taps()
    band = np.zeros((width, width), np.float32)
    for k in range(TAPS):
        band += np.diag(np.full(width - abs(k - 5), taps[k], np.float32), k - 5)
    return jnp.asarray(band)


def pixel_basis():
    pixel = np.arange(TILE * TILE)
    x = (pixel % TILE) - (TILE - 1) / 2.0
    y = (pixel // TILE) - (TILE - 1) / 2.0
    return np.stack([np.ones_like(x), x, y, x * x, x * y, y * y])


def expand_matrix():
    terms = pixel_basis()
    matrix = np.zeros((COEF_ROWS, 5 * LANES), np.float32)
    for piece in range(3):
        matrix[piece * 6 : piece * 6 + 6, 0 : 2 * LANES] = terms
        for c in range(3):
            matrix[18 + piece * 3 + c, (2 + c) * LANES : (3 + c) * LANES] = 1.0
    return jnp.asarray(matrix, jnp.bfloat16)


def moment_matrix():
    matrix = np.zeros((TILE, 2 * LANES), np.float32)
    matrix[0:6] = pixel_basis()
    return jnp.asarray(matrix, jnp.bfloat16)


def smem():
    return pl.BlockSpec(memory_space=pltpu.SMEM)


def vmem():
    return pl.BlockSpec(memory_space=pltpu.VMEM)


def scratch(*shape):
    return pltpu.VMEM(shape, jnp.float32)


def run(kernel, out_shapes, in_specs, scratches, *operands):
    return pl.pallas_call(
        kernel,
        out_shape=out_shapes,
        in_specs=in_specs,
        out_specs=jax.tree.map(lambda _: vmem(), out_shapes),
        scratch_shapes=scratches,
        compiler_params=pltpu.CompilerParams(vmem_limit_bytes=VMEM_BYTES),
    )(*operands)


def shards(params, send_list, send_counts, camera, ground_truth, tile_lists, list_lengths):
    devices = lax.axis_size(("view", "tile"))
    row_devices = lax.axis_size("tile")
    groups = lax.axis_size("view")
    count_params, per_device = params.shape
    capacity = per_device // devices
    tile_cols, list_len = tile_lists.shape[2:]
    col_groups = tile_cols // GROUP
    blocks = list_len // STEP_ROWS
    tile_row = lax.axis_index("tile")
    image_width = float(ground_truth.shape[3])
    image_height = float(ground_truth.shape[2] * row_devices)
    table_rows = per_device + BATCH * GROUP
    slot_rows = packed_rows(capacity)
    sent_shape = jax.ShapeDtypeStruct((devices, slot_rows, LANES), jnp.float32)
    cams = camera_table(camera)

    flat_lengths = list_lengths.reshape(-1)
    entry_rank = jnp.arange(list_len, dtype=jnp.int32)
    tile_num = jnp.arange(2 * tile_cols, dtype=jnp.int32)
    lists = jnp.where(
        entry_rank[None, :] < flat_lengths[:, None],
        tile_lists.reshape(2 * tile_cols, list_len),
        per_device + entry_rank[None, :] % BATCH * GROUP + tile_num[:, None] % GROUP,
    )
    lens_rows = jnp.tile(flat_lengths.reshape(-1, GROUP), (1, LANES // GROUP))

    width = ground_truth.shape[3]
    true_own = ground_truth.reshape(-1, TILE, width)
    true_above = from_behind(true_own, "tile", 1)
    true_below = from_behind(true_own, "tile", -1)
    band = band_matrix(width)
    truth_rows = 2 * true_own.shape[0] * 2 * TILE
    truth_blur = run(
        truth_kernel,
        jax.ShapeDtypeStruct((truth_rows, width), jnp.float32),
        [vmem()] * 4,
        [scratch(3 * TILE, width), scratch(truth_rows, width)],
        band,
        true_above,
        true_own,
        true_below,
    )

    own_sizes = (groups, row_devices, capacity, image_width, image_height)
    sent = run(
        lambda *refs: source_kernel(own_sizes, *refs),
        sent_shape,
        [smem(), smem(), smem(), vmem()],
        [
            scratch(SUBS * SUBS * SUBS, LANES),
            scratch(SUBS * LANES, LANES),
            scratch(per_device, LANES),
            scratch(PACK * slot_rows, LANES),
        ],
        cams,
        send_list,
        send_counts,
        params,
    )
    arrived = lax.all_to_all(sent, ("view", "tile"), split_axis=0, concat_axis=0, tiled=True)

    tile_sizes = (capacity, col_groups, list_len)
    entries = 2 * tile_cols * list_len
    rendered, left, shapes = run(
        lambda *refs: render_kernel(tile_sizes, *refs),
        (
            jax.ShapeDtypeStruct(ground_truth.shape, jnp.float32),
            jax.ShapeDtypeStruct((entries, COEF_ROWS), jnp.bfloat16),
            jax.ShapeDtypeStruct((5, entries // LANES, LANES), jnp.float32),
        ),
        [smem(), smem(), smem(), vmem(), vmem(), vmem()],
        [
            scratch(table_rows, LANES),
            scratch(blocks * LANES, LANES),
            scratch(blocks * 24, LANES),
            scratch(blocks * COEF_ROWS, LANES),
            scratch(blocks * LANES, 5 * LANES),
        ],
        tile_row.reshape(1),
        lists,
        flat_lengths,
        lens_rows,
        expand_matrix(),
        arrived,
    )

    images = rendered.reshape(true_own.shape)
    count = images.shape[0]
    grad_image = run(
        lambda *refs: loss_kernel(TILE * row_devices, *refs),
        jax.ShapeDtypeStruct(images.shape, jnp.float32),
        [smem()] + [vmem()] * 8,
        [
            scratch(3, 3 * TILE, width),
            scratch(3 * count * 2 * TILE, width),
            scratch(3 * count * 2 * TILE, width),
            scratch(3 * count * TILE, width),
        ],
        tile_row.reshape(1),
        band,
        truth_blur,
        true_above,
        true_own,
        true_below,
        from_behind(images, "tile", 1),
        images,
        from_behind(images, "tile", -1),
    ).reshape(ground_truth.shape)

    grad_slots = run(
        lambda *refs: back_kernel(tile_sizes, *refs),
        sent_shape,
        [smem(), smem()] + [vmem()] * 6,
        [
            scratch(blocks * LANES, 5 * LANES),
            scratch(blocks * LANES, 2 * LANES),
            scratch(80, 2 * LANES),
            scratch(blocks * TILE, LANES),
            scratch(blocks * 24, LANES),
            scratch(blocks * LANES, LANES),
            scratch(table_rows, LANES),
        ],
        lists,
        flat_lengths,
        lists,
        expand_matrix(),
        moment_matrix(),
        left,
        shapes,
        grad_image,
    )
    returned = lax.all_to_all(
        grad_slots, ("view", "tile"), split_axis=0, concat_axis=0, tiled=True
    )
    return run(
        lambda *refs: owner_kernel(own_sizes, *refs),
        jax.ShapeDtypeStruct(params.shape, jnp.float32),
        [smem(), smem(), smem(), vmem(), vmem()],
        [
            scratch(SUBS * SUBS * SUBS, LANES),
            scratch(SUBS * 24, LANES),
            scratch(per_device, LANES),
            scratch(PACK * slot_rows, LANES),
        ],
        cams,
        send_list,
        send_counts,
        params,
        returned,
    )


def solution(mesh):
    in_specs = (
        P(None, ("view", "tile")),
        P(("view", "tile"), None),
        P(("view", "tile"), None),
        P(),
        P("view", None, "tile", None),
        P("view", "tile", None, None),
        P("view", "tile", None),
    )
    out_specs = P(None, ("view", "tile"))
    return jax.shard_map(shards, mesh=mesh, in_specs=in_specs, out_specs=out_specs, check_vma=False)
```

```python
import jax
import jax.numpy as jnp
import numpy as np
from jax import lax
from jax.experimental import pallas as pl
from jax.experimental.pallas import tpu as pltpu
from jax.sharding import PartitionSpec as P

TILE = 16


FOCAL = 1000.0
LOW_PASS = 0.3
SSIM_SHARE = 0.2
SMOOTH_EPS = 1e-06
SSIM_ONE = 0.0001
SSIM_TWO = 0.0009
HARMONIC_ZERO = 0.28209479177387814
HARMONIC_ONE = 0.4886025119029199
HARMONIC_TWO = (
    1.0925484305920792,
    -1.0925484305920792,
    0.31539156525252005,
    -1.0925484305920792,
    0.5462742152960396,
)
HARMONIC_THREE = (
    -0.5900435899266435,
    2.890611442640554,
    -0.4570457994644658,
    0.3731763325901154,
    -0.4570457994644658,
    1.445305721320277,
    -0.5900435899266435,
)


def from_behind(block, axis, distance):
    devices = range(lax.axis_size(axis))
    route = [(i - distance, i) for i in devices if i - distance in devices]
    return lax.ppermute(block, axis, route)


def window_taps():
    offsets_np = np.arange(11) - 5.0
    weights = np.exp(-offsets_np * offsets_np / 4.5)
    weights = weights / weights.sum()
    return [float(weight) for weight in weights]


def matrix_product(left_side, right_side):
    return [
        [
            left_side[row_idx][0] * right_side[0][col_idx]
            + left_side[row_idx][1] * right_side[1][col_idx]
            + left_side[row_idx][2] * right_side[2][col_idx]
            for col_idx in range(3)
        ]
        for row_idx in range(3)
    ]


def rotation(angles):
    cos_a, sin_a = (jnp.cos(angles[0]), jnp.sin(angles[0]))
    cos_b, sin_b = (jnp.cos(angles[1]), jnp.sin(angles[1]))
    cos_c, sin_c = (jnp.cos(angles[2]), jnp.sin(angles[2]))
    about_x = [[1.0, 0.0, 0.0], [0.0, cos_a, -sin_a], [0.0, sin_a, cos_a]]
    about_y = [[cos_b, 0.0, sin_b], [0.0, 1.0, 0.0], [-sin_b, 0.0, cos_b]]
    about_z = [[cos_c, -sin_c, 0.0], [sin_c, cos_c, 0.0], [0.0, 0.0, 1.0]]
    return matrix_product(about_z, matrix_product(about_y, about_x))


def harmonics(dir_x, dir_y, dir_z):
    sq_x, sq_y, sq_z = (dir_x * dir_x, dir_y * dir_y, dir_z * dir_z)
    prod_xy, prod_yz, prod_xz = (dir_x * dir_y, dir_y * dir_z, dir_x * dir_z)
    return [
        HARMONIC_ZERO + 0.0 * dir_x,
        -HARMONIC_ONE * dir_y,
        HARMONIC_ONE * dir_z,
        -HARMONIC_ONE * dir_x,
        HARMONIC_TWO[0] * prod_xy,
        HARMONIC_TWO[1] * prod_yz,
        HARMONIC_TWO[2] * (2.0 * sq_z - sq_x - sq_y),
        HARMONIC_TWO[3] * prod_xz,
        HARMONIC_TWO[4] * (sq_x - sq_y),
        HARMONIC_THREE[0] * dir_y * (3.0 * sq_x - sq_y),
        HARMONIC_THREE[1] * prod_xy * dir_z,
        HARMONIC_THREE[2] * dir_y * (4.0 * sq_z - sq_x - sq_y),
        HARMONIC_THREE[3] * dir_z * (2.0 * sq_z - 3.0 * sq_x - 3.0 * sq_y),
        HARMONIC_THREE[4] * dir_x * (4.0 * sq_z - sq_x - sq_y),
        HARMONIC_THREE[5] * dir_z * (sq_x - sq_y),
        HARMONIC_THREE[6] * dir_x * (sq_x - 3.0 * sq_y),
    ]


LANES = 128
SUBS = 8
GROUP = 8
STEP_ROWS = 16
FEATS = 8
PAIR = 2 * FEATS
COEF_ROWS = 32
SLOT = PAIR + 2
PACK = LANES // SLOT
FLAG = PAIR + 1
UNROLL = 8
MOVES = 16
TAPS = 11
DEAD = -1e30
LOG_TOP = float(np.log(0.99))
VMEM_BYTES = 48 * 1024 * 1024


def stepped(total, width, body, state):
    def step(block, held):
        for k in range(width):
            held = body(block * width + k, held)
        return held

    return lax.fori_loop(0, (total + width - 1) // width, step, state)


def packed_rows(cap):
    return -(-cap // (PACK * SUBS)) * SUBS


def pack_slots(read, rows, first_lane):
    lane = lax.broadcasted_iota(jnp.int32, (rows, LANES), 1)
    packed = jnp.zeros((rows, LANES), jnp.float32)
    for q in range(PACK):
        shift = (q * SLOT - first_lane) % LANES
        value = read(q * rows)
        value = pltpu.roll(value, shift, 1) if shift else value
        packed = jnp.where((lane >= q * SLOT) & (lane < (q + 1) * SLOT), value, packed)
    return packed


def unpack_slots(packed, write):
    for q in range(PACK):
        write(q * packed.shape[0], pltpu.roll(packed, LANES - q * SLOT, 1) if q else packed)


def camera_table(camera):
    columns = [camera[:, entry] for entry in range(6)]
    turn = rotation(columns[0:3])
    shift = columns[3:6]
    anchor = [
        -(turn[0][c] * shift[0] + turn[1][c] * shift[1] + turn[2][c] * shift[2]) for c in range(3)
    ]
    flat = [turn[r][c] for r in range(3) for c in range(3)] + shift + anchor
    return jnp.stack(flat + [jnp.zeros_like(shift[0])], axis=1)


def shape_matrix(params):
    scales = [jnp.exp(params[3 + axis_num]) for axis_num in range(3)]
    inv_norm = 1.0 / jnp.sqrt(
        params[6] * params[6]
        + params[7] * params[7]
        + params[8] * params[8]
        + params[9] * params[9]
    )
    quat_w, quat_x, quat_y, quat_z = [params[6 + k] * inv_norm for k in range(4)]
    quat_rot = [
        [
            1.0 - 2.0 * (quat_y * quat_y + quat_z * quat_z),
            2.0 * (quat_x * quat_y - quat_w * quat_z),
            2.0 * (quat_x * quat_z + quat_w * quat_y),
        ],
        [
            2.0 * (quat_x * quat_y + quat_w * quat_z),
            1.0 - 2.0 * (quat_x * quat_x + quat_z * quat_z),
            2.0 * (quat_y * quat_z - quat_w * quat_x),
        ],
        [
            2.0 * (quat_x * quat_z - quat_w * quat_y),
            2.0 * (quat_y * quat_z + quat_w * quat_x),
            1.0 - 2.0 * (quat_x * quat_x + quat_y * quat_y),
        ],
    ]
    return [[quat_rot[r][c] * scales[c] for c in range(3)] for r in range(3)]


def view_features(params, shape, cam, image_width, image_height):
    turn = [[cam[3 * r + c] for c in range(3)] for r in range(3)]
    point = [
        turn[r][0] * params[0] + turn[r][1] * params[1] + turn[r][2] * params[2] + cam[9 + r]
        for r in range(3)
    ]
    inv_depth = 1.0 / point[2]
    ratio_x, ratio_y = point[0] * inv_depth, point[1] * inv_depth
    zoom = FOCAL * inv_depth
    row_x = [zoom * (turn[0][c] - ratio_x * turn[2][c]) for c in range(3)]
    row_y = [zoom * (turn[1][c] - ratio_y * turn[2][c]) for c in range(3)]
    proj_x = [
        row_x[0] * shape[0][c] + row_x[1] * shape[1][c] + row_x[2] * shape[2][c] for c in range(3)
    ]
    proj_y = [
        row_y[0] * shape[0][c] + row_y[1] * shape[1][c] + row_y[2] * shape[2][c] for c in range(3)
    ]
    cov_xx = proj_x[0] * proj_x[0] + proj_x[1] * proj_x[1] + proj_x[2] * proj_x[2] + LOW_PASS
    cov_xy = proj_x[0] * proj_y[0] + proj_x[1] * proj_y[1] + proj_x[2] * proj_y[2]
    cov_yy = proj_y[0] * proj_y[0] + proj_y[1] * proj_y[1] + proj_y[2] * proj_y[2] + LOW_PASS
    inv_det = 1.0 / (cov_xx * cov_yy - cov_xy * cov_xy)
    ray = [params[c] - cam[12 + c] for c in range(3)]
    inv_len = 1.0 / jnp.sqrt(ray[0] * ray[0] + ray[1] * ray[1] + ray[2] * ray[2])
    basis = harmonics(ray[0] * inv_len, ray[1] * inv_len, ray[2] * inv_len)
    colours = []
    for channel in range(3):
        summed = 0.5 + HARMONIC_ZERO * params[11 + 16 * channel]
        for harmonic in range(1, 16):
            summed = summed + basis[harmonic] * params[11 + 16 * channel + harmonic]
        colours.append(summed)
    return [
        FOCAL * ratio_x + image_width / 2.0,
        FOCAL * ratio_y + image_height / 2.0,
        cov_yy * inv_det,
        -cov_xy * inv_det,
        cov_xx * inv_det,
    ] + colours


def log_opacity(logit):
    return LOG_TOP - jnp.log(1.0 + jnp.exp(-logit))


def load_params(params_ref, tile_scr, block):
    count = params_ref.shape[0]
    for band in range(0, count, SUBS):
        high = min(band + SUBS, count)
        for j in range(SUBS):
            lane_at = pl.multiple_of(block * SUBS * LANES + j * LANES, LANES)
            tile_scr[band * SUBS + j * SUBS : band * SUBS + j * SUBS + high - band, :] = params_ref[
                band:high, pl.ds(lane_at, LANES)
            ]
    return [
        tile_scr[pl.ds((r // SUBS) * SUBS * SUBS + r % SUBS, SUBS, stride=SUBS), :]
        for r in range(count)
    ]


def source_kernel(
    sizes, cam_ref, list_ref, counts_ref, params_ref, out_ref, tile_scr, feat_scr, table, slots
):
    groups, rows, cap, image_width, image_height = sizes
    per = params_ref.shape[1]
    views = cam_ref.shape[0]
    height = out_ref.shape[1]
    used = -(-groups * SLOT // SUBS) * SUBS

    def project_block(block, carry):
        params = load_params(params_ref, tile_scr, block)
        shape = shape_matrix(params)
        log_o = log_opacity(params[10])
        for view in range(views):
            cam = [cam_ref[view, k] for k in range(15)]
            for num, value in enumerate(
                view_features(params, shape, cam, image_width, image_height)
            ):
                line = view // 2 * SLOT + view % 2 * FEATS + num
                feat_scr[pl.ds(line, SUBS, stride=used), :] = value
        for group in range(groups):
            feat_scr[pl.ds(group * SLOT + PAIR, SUBS, stride=used), :] = log_o
        for j in range(SUBS):
            row_at = pl.multiple_of(block * SUBS * LANES + j * LANES, LANES)
            table[pl.ds(row_at, LANES), 0:used] = feat_scr[j * used : (j + 1) * used, :].T
        return carry

    lax.fori_loop(0, per // (SUBS * LANES), project_block, 0)

    start = jnp.int32(0)
    for group in range(groups):

        def send_block(t, start_at, group=group):
            dest = group * rows + t
            count = counts_ref[0, dest]

            def move(k, carry):
                spot = jnp.minimum(start_at + k, per - 1)
                slots[pl.ds(k, 1), :] = table[pl.ds(list_ref[0, spot], 1), :]
                return carry

            stepped(count, MOVES, move, 0)
            out_ref[dest] = pack_slots(
                lambda at: slots[at : at + height, :], height, group * SLOT
            )
            return start_at + count

        start = lax.fori_loop(0, rows, send_block, start)


def split_three(value):
    first = value.astype(jnp.bfloat16).astype(jnp.float32)
    rest = value - first
    second = rest.astype(jnp.bfloat16).astype(jnp.float32)
    return [first, second, rest - second]


def swap_grain(cells):
    sub = lax.broadcasted_iota(jnp.int32, (SUBS, LANES), 0)
    lane = lax.broadcasted_iota(jnp.int32, (SUBS, LANES), 1) // TILE
    for bit in (1, 2, 4):
        sub_bit, lane_bit = (sub & bit) != 0, (lane & bit) != 0
        from_high = pltpu.roll(pltpu.roll(cells, SUBS - bit, 0), bit * TILE, 1)
        from_low = pltpu.roll(pltpu.roll(cells, bit, 0), LANES - bit * TILE, 1)
        cells = jnp.where(sub_bit == lane_bit, cells, jnp.where(lane_bit, from_high, from_low))
    return cells


def longest(lens_ref, group):
    most = lens_ref[group * GROUP]
    for t in range(1, GROUP):
        most = jnp.maximum(most, lens_ref[group * GROUP + t])
    return most


def render_kernel(
    sizes,
    row_ref,
    lists_ref,
    lens_ref,
    lens_rows_ref,
    basis_ref,
    arrived_ref,
    image_ref,
    left_ref,
    shape_ref,
    table,
    rows,
    feat_scr,
    pieces,
    mm,
):
    cap, col_groups, list_len = sizes
    devices, height = arrived_ref.shape[0:2]
    blocks = list_len // STEP_ROWS
    table[devices * cap :, :] = jnp.zeros((GROUP, LANES), jnp.float32)

    def unpack(source, carry):
        def write(at, value):
            size = min(height, cap - at)
            if size > 0:
                row_at = pl.multiple_of(source * cap + at, SUBS)
                table[pl.ds(row_at, size), :] = value[0:size]

        unpack_slots(arrived_ref[source], write)
        return carry

    lax.fori_loop(0, devices, unpack, 0)
    centre_y = (row_ref[0] * TILE).astype(jnp.float32) + (TILE - 1) / 2.0
    sub = lax.broadcasted_iota(jnp.int32, (blocks, LANES), 0)
    lane = lax.broadcasted_iota(jnp.int32, (blocks, LANES), 1)
    zero = jnp.zeros((SUBS, LANES), jnp.float32)

    def one_group(group, carry):
        view, col_group = group // col_groups, group % col_groups
        most = longest(lens_ref, group)

        def fetch(n, inner):
            for t in range(GROUP):
                slot = lists_ref[group * GROUP + t, n]
                rows[pl.ds(n * GROUP + t, 1), :] = table[pl.ds(slot, 1), :]
            return inner

        stepped(most, UNROLL, fetch, 0)
        for block in range(blocks):
            feat_scr[block * 24 : (block + 1) * 24, :] = rows[
                block * LANES : (block + 1) * LANES, 0:24
            ].T
        feats = [
            feat_scr[pl.ds(view * FEATS + num, blocks, stride=24), :] for num in range(FEATS)
        ]
        log_o = feat_scr[pl.ds(PAIR, blocks, stride=24), :]
        live = sub * STEP_ROWS + lane // GROUP < lens_rows_ref[pl.ds(group, 1), :]
        centre_x = ((col_group * GROUP + lane % GROUP) * TILE).astype(jnp.float32) + (
            TILE - 1
        ) / 2.0
        off_x, off_y = feats[0] - centre_x, feats[1] - centre_y
        lin_x = feats[2] * off_x + feats[3] * off_y
        lin_y = feats[4] * off_y + feats[3] * off_x
        coefs = [
            log_o - 0.5 * (off_x * lin_x + off_y * lin_y),
            lin_x,
            lin_y,
            -0.5 * feats[2],
            -feats[3],
            -0.5 * feats[4],
        ]
        coefs = [
            jnp.where(live, value, DEAD if num == 0 else 0.0) for num, value in enumerate(coefs)
        ]
        lines = [None] * COEF_ROWS
        for num, value in enumerate(coefs):
            for piece, part in enumerate(split_three(value)):
                lines[piece * 6 + num] = part
        for num in range(3):
            for piece, part in enumerate(split_three(jnp.where(live, feats[5 + num], 0.0))):
                lines[18 + piece * 3 + num] = part
        for num, value in enumerate(lines):
            pieces[pl.ds(num, blocks, stride=COEF_ROWS), :] = (
                jnp.zeros((blocks, LANES), jnp.float32) if value is None else value
            )
        for num, value in enumerate(feats[2:5] + [off_x, off_y]):
            shape_ref[num, pl.ds(pl.multiple_of(group * blocks, blocks), blocks), :] = jnp.where(
                live, value, 0.0
            )
        left_at = pl.multiple_of(group * blocks * LANES, LANES)
        for block in range(blocks):
            left_ref[pl.ds(left_at + block * LANES, LANES), :] = pieces[
                block * COEF_ROWS : (block + 1) * COEF_ROWS, :
            ].T.astype(jnp.bfloat16)
        expand(left_ref, basis_ref, mm, left_at)

        def entry(n, state):
            keep, colour = state
            row_at = pl.multiple_of(n * GROUP, GROUP)
            shade = [
                mm[pl.ds(row_at, GROUP), (2 + c) * LANES : (3 + c) * LANES] for c in range(3)
            ]
            new_keep, new_colour = [], []
            for half in range(2):
                alpha = jnp.exp(mm[pl.ds(row_at, GROUP), half * LANES : (half + 1) * LANES])
                weight = keep[half] * alpha
                new_keep.append(keep[half] * (1.0 - alpha))
                new_colour.append([colour[half][c] + weight * shade[c] for c in range(3)])
            return new_keep, new_colour

        state = ([zero + 1.0] * 2, [[zero] * 3] * 2)
        _, colour = stepped(most, UNROLL, entry, state)
        lane_at = pl.multiple_of(col_group * LANES, LANES)
        for half in range(2):
            for c in range(3):
                image_ref[view, c, half * SUBS : (half + 1) * SUBS, pl.ds(lane_at, LANES)] = (
                    swap_grain(colour[half][c])
                )
        return carry

    lax.fori_loop(0, 2 * col_groups, one_group, 0)


def expand(left_ref, basis_ref, mm, left_at):
    mm[...] = jnp.dot(
        left_ref[pl.ds(left_at, mm.shape[0]), :],
        basis_ref[...],
        preferred_element_type=jnp.float32,
    )


def back_kernel(
    sizes,
    lists_ref,
    lens_ref,
    basis_ref,
    moment_ref,
    left_ref,
    shape_ref,
    grad_ref,
    out_ref,
    mm,
    weights,
    grad_scr,
    mom_scr,
    row_scr,
    rows,
    table,
):
    cap, col_groups, list_len = sizes
    devices, height = out_ref.shape[0:2]
    blocks = list_len // STEP_ROWS
    table_rows = table.shape[0] // 2
    table[...] = jnp.zeros_like(table)
    row_scr[...] = jnp.zeros_like(row_scr)
    rows[...] = jnp.zeros_like(rows)
    grad_scr[...] = jnp.zeros_like(grad_scr)
    zero = jnp.zeros((SUBS, LANES), jnp.float32)
    sub = lax.broadcasted_iota(jnp.int32, (SUBS, LANES), 0)
    lane = lax.broadcasted_iota(jnp.int32, (SUBS, LANES), 1)
    own_tile = lane % GROUP == sub

    def one_group(group, carry):
        view, col_group = group // col_groups, group % col_groups
        most = longest(lens_ref, group)
        lane_at = pl.multiple_of(col_group * LANES, LANES)
        grads = [
            [
                swap_grain(
                    grad_ref[view, c, half * SUBS : (half + 1) * SUBS, pl.ds(lane_at, LANES)]
                )
                for c in range(3)
            ]
            for half in range(2)
        ]
        for half in range(2):
            for c in range(3):
                for piece, part in enumerate(split_three(grads[half][c])):
                    grad_scr[
                        piece * 24 + c * SUBS : piece * 24 + (c + 1) * SUBS,
                        half * LANES : (half + 1) * LANES,
                    ] = part
        expand(left_ref, basis_ref, mm, pl.multiple_of(group * blocks * LANES, LANES))

        def ahead(n, keep):
            row_at = pl.multiple_of(n * GROUP, GROUP)
            new_keep = []
            for half in range(2):
                lanes = slice(half * LANES, (half + 1) * LANES)
                alpha = jnp.exp(mm[pl.ds(row_at, GROUP), lanes])
                weight = keep[half] * alpha
                mm[pl.ds(row_at, GROUP), lanes] = alpha
                weights[pl.ds(row_at, GROUP), lanes] = weight
                new_keep.append(keep[half] * (1.0 - alpha))
            return new_keep

        stepped(most, UNROLL, ahead, [zero + 1.0] * 2)

        last = (most + UNROLL - 1) // UNROLL * UNROLL - 1

        def behind(step, seen):
            row_at = pl.multiple_of((last - step) * GROUP, GROUP)
            shade = [
                mm[pl.ds(row_at, GROUP), (2 + c) * LANES : (3 + c) * LANES] for c in range(3)
            ]
            new_seen = []
            for half in range(2):
                lanes = slice(half * LANES, (half + 1) * LANES)
                own = (
                    grads[half][0] * shade[0]
                    + grads[half][1] * shade[1]
                    + grads[half][2] * shade[2]
                )
                alpha = mm[pl.ds(row_at, GROUP), lanes]
                mm[pl.ds(row_at, GROUP), lanes] = weights[pl.ds(row_at, GROUP), lanes] * (
                    own - seen[half]
                )
                new_seen.append(seen[half] * (1.0 - alpha) + alpha * own)
            return new_seen

        stepped(most, UNROLL, behind, [zero] * 2)
        total = jnp.zeros((blocks * LANES, LANES), jnp.float32)
        for value, right in (
            (mm[:, 0 : 2 * LANES], moment_ref[...]),
            (weights[...], grad_scr[...].T.astype(jnp.bfloat16)),
        ):
            high = value.astype(jnp.bfloat16)
            low = (value - high.astype(jnp.float32)).astype(jnp.bfloat16)
            total = total + jnp.dot(high, right, preferred_element_type=jnp.float32)
            total = total + jnp.dot(low, right, preferred_element_type=jnp.float32)
        for block in range(blocks):
            turned = total[block * LANES : (block + 1) * LANES].T
            mom_scr[block * TILE : block * TILE + 8, :] = turned[96:104]
            for c in range(3):
                summed = (
                    turned[c * SUBS : (c + 1) * SUBS]
                    + turned[24 + c * SUBS : 24 + (c + 1) * SUBS]
                    + turned[48 + c * SUBS : 48 + (c + 1) * SUBS]
                )
                mom_scr[block * TILE + 8 + c : block * TILE + 9 + c, :] = jnp.sum(
                    jnp.where(own_tile, summed, 0.0), axis=0, keepdims=True
                )
        mom = [mom_scr[pl.ds(num, blocks, stride=TILE), :] for num in range(11)]
        con_xx, con_xy, con_yy, off_x, off_y = [
            shape_ref[num, pl.ds(pl.multiple_of(group * blocks, blocks), blocks), :]
            for num in range(5)
        ]
        sum_x = off_x * mom[0] - mom[1]
        sum_y = off_y * mom[0] - mom[2]
        results = [
            -(con_xx * sum_x + con_xy * sum_y),
            -(con_yy * sum_y + con_xy * sum_x),
            -0.5 * (off_x * (sum_x - mom[1]) + mom[3]),
            -(off_x * sum_y - off_y * mom[1] + mom[4]),
            -0.5 * (off_y * (sum_y - mom[2]) + mom[5]),
        ] + mom[8:11]
        other = 1 - view
        for num, value in enumerate(results):
            row_scr[pl.ds(view * FEATS + num, blocks, stride=24), :] = value
            row_scr[pl.ds(other * FEATS + num, blocks, stride=24), :] = jnp.zeros_like(value)
        row_scr[pl.ds(PAIR, blocks, stride=24), :] = mom[0]
        row_scr[pl.ds(FLAG, blocks, stride=24), :] = jnp.ones((blocks, LANES), jnp.float32)
        first = pl.multiple_of(group * blocks * LANES, LANES)
        for block in range(blocks):
            rows[pl.ds(first + block * LANES, LANES), 0:24] = row_scr[
                block * 24 : (block + 1) * 24, :
            ].T

        def put(n, inner):
            for t in range(GROUP):
                spot = view * table_rows + lists_ref[group * GROUP + t, n]
                table[pl.ds(spot, 1), :] = rows[pl.ds(first + n * GROUP + t, 1), :]
            return inner

        stepped(most, UNROLL, put, 0)
        return carry

    lax.fori_loop(0, 2 * col_groups, one_group, 0)

    def pack(source, count):
        found = [count]

        def read(at):
            size = min(height, cap - at)
            if size <= 0:
                return jnp.zeros((height, LANES), jnp.float32)
            row_at = pl.multiple_of(source * cap + at, SUBS)
            value = table[pl.ds(row_at, size), :] + table[pl.ds(table_rows + row_at, size), :]
            found[0] = found[0] + value.reshape(size // SUBS, SUBS, LANES).sum(axis=0)
            if size < height:
                value = jnp.concatenate(
                    [value, jnp.zeros((height - size, LANES), jnp.float32)], axis=0
                )
            return value

        out_ref[source] = pack_slots(read, height, 0)
        return found[0]

    count = lax.fori_loop(0, devices, pack, zero)
    stored = jnp.sum(jnp.where(lane == FLAG, count, 0.0))
    named = lens_ref[0]
    for tile in range(1, 2 * col_groups * GROUP):
        named = named + lens_ref[tile]

    @pl.when(stored < named.astype(jnp.float32) - 0.5)
    def _():
        table[...] = jnp.zeros_like(table)

        def add_group(group, carry):
            def add(n, inner):
                for t in range(GROUP):
                    spot = lists_ref[group * GROUP + t, n]
                    row_at = group * blocks * LANES + n * GROUP + t
                    table[pl.ds(spot, 1), :] = table[pl.ds(spot, 1), :] + rows[pl.ds(row_at, 1), :]
                return inner

            return lax.fori_loop(0, longest(lens_ref, group), add, carry)

        lax.fori_loop(0, 2 * col_groups, add_group, 0)
        lax.fori_loop(0, devices, pack, zero)


def owner_kernel(
    sizes,
    cam_ref,
    list_ref,
    counts_ref,
    params_ref,
    back_ref,
    out_ref,
    tile_scr,
    feat_scr,
    table,
    slots,
):
    groups, rows, cap, image_width, image_height = sizes
    count_params, per = params_ref.shape
    height = back_ref.shape[1]
    table[...] = jnp.zeros_like(table)
    lane = lax.broadcasted_iota(jnp.int32, (height, LANES), 1)
    start = jnp.int32(0)
    for group in range(groups):

        def take_block(t, start_at, group=group):
            dest = group * rows + t
            count = counts_ref[0, dest]

            def write(at, value):
                slots[at : at + height, :] = jnp.where(lane == PAIR + 1, 1.0 + group, value)

            unpack_slots(back_ref[dest], write)

            def move(k, carry):
                spot = list_ref[0, start_at + k]
                table[pl.ds(spot, 1), :] = slots[pl.ds(k, 1), :]
                return carry

            rounded = (count + MOVES - 1) // MOVES * MOVES
            whole = jnp.where(start_at + rounded <= per, rounded, count // MOVES * MOVES)
            stepped(whole, MOVES, move, 0)
            lax.fori_loop(whole, count, move, 0)
            return start_at + count

        start = lax.fori_loop(0, rows, take_block, start)

    def clear(k, carry):
        table[pl.ds(list_ref[0, k], 1), :] = jnp.zeros((1, LANES), jnp.float32)
        return carry

    lax.fori_loop(start, jnp.minimum(start + MOVES, per), clear, 0)

    def pull_block(block, carry):
        params = load_params(params_ref, tile_scr, block)
        for j in range(SUBS):
            row_at = pl.multiple_of(block * SUBS * LANES + j * LANES, LANES)
            feat_scr[j * 24 : (j + 1) * 24, :] = table[pl.ds(row_at, LANES), 0:24].T
        cots = [feat_scr[pl.ds(num, SUBS, stride=24), :] for num in range(PAIR + 2)]
        home = cots[PAIR + 1]
        sent = home > 0.5
        cams = []
        for view in range(2):
            cam = []
            for k in range(15):
                value = jnp.full((SUBS, LANES), cam_ref[view, k], jnp.float32)
                for group in range(1, groups):
                    value = jnp.where(home > 0.5 + group, cam_ref[2 * group + view, k], value)
                cam.append(value)
            cams.append(cam)

        def both(*values):
            shape = shape_matrix(values)
            return (
                view_features(values, shape, cams[0], image_width, image_height)
                + view_features(values, shape, cams[1], image_width, image_height)
                + [log_opacity(values[10])]
            )

        _, pull = jax.vjp(both, *params)
        grads = pull(cots[0 : PAIR + 1])
        for num, value in enumerate(grads):
            tile_scr[pl.ds((num // SUBS) * SUBS * SUBS + num % SUBS, SUBS, stride=SUBS), :] = (
                jnp.where(sent, value, 0.0)
            )
        for band in range(0, count_params, SUBS):
            high = min(band + SUBS, count_params)
            for j in range(SUBS):
                lane_at = pl.multiple_of(block * SUBS * LANES + j * LANES, LANES)
                out_ref[band:high, pl.ds(lane_at, LANES)] = tile_scr[
                    band * SUBS + j * SUBS : band * SUBS + j * SUBS + high - band, :
                ]
        return carry

    lax.fori_loop(0, per // (SUBS * LANES), pull_block, 0)


def tap_rows(read, first, count):
    taps = window_taps()
    total = taps[5] * read(first + 5, count)
    for k in range(5):
        total = total + taps[k] * (read(first + k, count) + read(first + TAPS - 1 - k, count))
    return total


def blur_lanes(value, band):
    return jnp.dot(
        value, band, precision=lax.Precision.HIGHEST, preferred_element_type=jnp.float32
    )


def truth_kernel(band_ref, above_ref, own_ref, below_ref, out_ref, tall, mixed):
    images = own_ref.shape[0]

    def one_image(m, carry):
        whole = jnp.concatenate([above_ref[m], own_ref[m], below_ref[m]], axis=0)
        for field, value in enumerate((whole, whole * whole)):
            tall[...] = value
            row_at = pl.multiple_of((field * images + m) * 2 * TILE, 2 * TILE)
            mixed[pl.ds(row_at, 2 * TILE), :] = tap_rows(
                lambda at, count: tall[at : at + count, :], 6, 2 * TILE
            )
        return carry

    lax.fori_loop(0, images, one_image, 0)
    out_ref[...] = blur_lanes(mixed[...], band_ref[...])


def loss_kernel(
    image_rows,
    row_ref,
    band_ref,
    truth_ref,
    true_above,
    true_own,
    true_below,
    above_ref,
    own_ref,
    below_ref,
    out_ref,
    tall,
    mixed,
    blurred,
    slim,
):
    images = own_ref.shape[0]
    tall_rows = 2 * TILE
    width = own_ref.shape[2]

    def one_image(m, carry):
        whole = jnp.concatenate([above_ref[m], own_ref[m], below_ref[m]], axis=0)
        true = jnp.concatenate([true_above[m], true_own[m], true_below[m]], axis=0)
        for field, value in enumerate((whole, whole * whole, whole * true)):
            tall[field] = value
            row_at = pl.multiple_of((field * images + m) * tall_rows, tall_rows)
            mixed[pl.ds(row_at, tall_rows), :] = tap_rows(
                lambda at, count, field=field: tall[field, at : at + count, :], 6, tall_rows
            )
        return carry

    lax.fori_loop(0, images, one_image, 0)
    blurred[...] = blur_lanes(mixed[...], band_ref[...])
    sub = lax.broadcasted_iota(jnp.int32, (tall_rows, width), 0)
    image_row = row_ref[0] * TILE + sub - 5
    inside = (image_row >= 0) & (image_row < image_rows) & (sub < TILE + 10)

    def one_map(m, carry):
        def field_of(ref, field):
            row_at = pl.multiple_of((field * images + m) * tall_rows, tall_rows)
            return ref[pl.ds(row_at, tall_rows), :]

        mean_one, both_one, cross = [field_of(blurred, field) for field in range(3)]
        mean_two, both_two = field_of(truth_ref, 0), field_of(truth_ref, 1)
        square_one, square_two = mean_one * mean_one, mean_two * mean_two
        mean_cross = mean_one * mean_two
        top_one = 2.0 * mean_cross + SSIM_ONE
        top_two = 2.0 * (cross - mean_cross) + SSIM_TWO
        low_one = square_one + square_two + SSIM_ONE
        low_two = (both_one - square_one) + (both_two - square_two) + SSIM_TWO
        inv_one, inv_two = 1.0 / low_one, 1.0 / low_two
        inv_both = inv_one * inv_two
        value = top_one * top_two * inv_both
        grads = [
            2.0 * mean_two * (top_two - top_one) * inv_both
            - 2.0 * mean_one * value * (inv_one - inv_two),
            -value * inv_two,
            2.0 * top_one * inv_both,
        ]
        for field, grad in enumerate(grads):
            tall[field, 0:tall_rows] = jnp.where(inside, grad, 0.0)
            row_at = pl.multiple_of((field * images + m) * TILE, TILE)
            slim[pl.ds(row_at, TILE), :] = tap_rows(
                lambda at, count, field=field: tall[field, at : at + count, :], 0, TILE
            )
        return carry

    lax.fori_loop(0, images, one_map, 0)
    spread = blur_lanes(slim[...], band_ref[...]).reshape(3, images, TILE, width)
    own, true = own_ref[...], true_own[...]
    gap = own - true
    out_ref[...] = (1.0 - SSIM_SHARE) * gap / jnp.sqrt(gap * gap + SMOOTH_EPS) - SSIM_SHARE * (
        spread[0] + 2.0 * own * spread[1] + true * spread[2]
    )


def band_matrix(width):
    taps = window_taps()
    band = np.zeros((width, width), np.float32)
    for k in range(TAPS):
        band += np.diag(np.full(width - abs(k - 5), taps[k], np.float32), k - 5)
    return jnp.asarray(band)


def pixel_basis():
    pixel = np.arange(TILE * TILE)
    x = (pixel % TILE) - (TILE - 1) / 2.0
    y = (pixel // TILE) - (TILE - 1) / 2.0
    return np.stack([np.ones_like(x), x, y, x * x, x * y, y * y])


def expand_matrix():
    terms = pixel_basis()
    matrix = np.zeros((COEF_ROWS, 5 * LANES), np.float32)
    for piece in range(3):
        matrix[piece * 6 : piece * 6 + 6, 0 : 2 * LANES] = terms
        for c in range(3):
            matrix[18 + piece * 3 + c, (2 + c) * LANES : (3 + c) * LANES] = 1.0
    return jnp.asarray(matrix, jnp.bfloat16)


def moment_matrix():
    matrix = np.zeros((2 * LANES, LANES), np.float32)
    matrix[:, 96:102] = pixel_basis().T
    return jnp.asarray(matrix, jnp.bfloat16)


def smem():
    return pl.BlockSpec(memory_space=pltpu.SMEM)


def vmem():
    return pl.BlockSpec(memory_space=pltpu.VMEM)


def scratch(*shape):
    return pltpu.VMEM(shape, jnp.float32)


def run(kernel, out_shapes, in_specs, scratches, *operands):
    return pl.pallas_call(
        kernel,
        out_shape=out_shapes,
        in_specs=in_specs,
        out_specs=jax.tree.map(lambda _: vmem(), out_shapes),
        scratch_shapes=scratches,
        compiler_params=pltpu.CompilerParams(vmem_limit_bytes=VMEM_BYTES),
    )(*operands)


def shards(params, send_list, send_counts, camera, ground_truth, tile_lists, list_lengths):
    devices = lax.axis_size(("view", "tile"))
    row_devices = lax.axis_size("tile")
    groups = lax.axis_size("view")
    count_params, per_device = params.shape
    capacity = per_device // devices
    tile_cols, list_len = tile_lists.shape[2:]
    col_groups = tile_cols // GROUP
    blocks = list_len // STEP_ROWS
    tile_row = lax.axis_index("tile")
    image_width = float(ground_truth.shape[3])
    image_height = float(ground_truth.shape[2] * row_devices)
    table_rows = per_device + GROUP
    slot_rows = packed_rows(capacity)
    sent_shape = jax.ShapeDtypeStruct((devices, slot_rows, LANES), jnp.float32)
    cams = camera_table(camera)

    flat_lengths = list_lengths.reshape(-1)
    entry_rank = jnp.arange(list_len, dtype=jnp.int32)
    tile_num = jnp.arange(2 * tile_cols, dtype=jnp.int32)
    lists = jnp.where(
        entry_rank[None, :] < flat_lengths[:, None],
        tile_lists.reshape(2 * tile_cols, list_len),
        per_device + tile_num[:, None] % GROUP,
    )
    lens_rows = jnp.tile(flat_lengths.reshape(-1, GROUP), (1, LANES // GROUP))

    width = ground_truth.shape[3]
    true_own = ground_truth.reshape(-1, TILE, width)
    true_above = from_behind(true_own, "tile", 1)
    true_below = from_behind(true_own, "tile", -1)
    band = band_matrix(width)
    truth_rows = 2 * true_own.shape[0] * 2 * TILE
    truth_blur = run(
        truth_kernel,
        jax.ShapeDtypeStruct((truth_rows, width), jnp.float32),
        [vmem()] * 4,
        [scratch(3 * TILE, width), scratch(truth_rows, width)],
        band,
        true_above,
        true_own,
        true_below,
    )

    own_sizes = (groups, row_devices, capacity, image_width, image_height)
    sent = run(
        lambda *refs: source_kernel(own_sizes, *refs),
        sent_shape,
        [smem(), smem(), smem(), vmem()],
        [
            scratch(SUBS * SUBS * SUBS, LANES),
            scratch(SUBS * LANES, LANES),
            scratch(per_device, LANES),
            scratch(PACK * slot_rows, LANES),
        ],
        cams,
        send_list,
        send_counts,
        params,
    )
    arrived = lax.all_to_all(sent, ("view", "tile"), split_axis=0, concat_axis=0, tiled=True)

    tile_sizes = (capacity, col_groups, list_len)
    entries = 2 * tile_cols * list_len
    rendered, left, shapes = run(
        lambda *refs: render_kernel(tile_sizes, *refs),
        (
            jax.ShapeDtypeStruct(ground_truth.shape, jnp.float32),
            jax.ShapeDtypeStruct((entries, COEF_ROWS), jnp.bfloat16),
            jax.ShapeDtypeStruct((5, entries // LANES, LANES), jnp.float32),
        ),
        [smem(), smem(), smem(), vmem(), vmem(), vmem()],
        [
            scratch(table_rows, LANES),
            scratch(blocks * LANES, LANES),
            scratch(blocks * 24, LANES),
            scratch(blocks * COEF_ROWS, LANES),
            scratch(blocks * LANES, 5 * LANES),
        ],
        tile_row.reshape(1),
        lists,
        flat_lengths,
        lens_rows,
        expand_matrix(),
        arrived,
    )

    images = rendered.reshape(true_own.shape)
    count = images.shape[0]
    grad_image = run(
        lambda *refs: loss_kernel(TILE * row_devices, *refs),
        jax.ShapeDtypeStruct(images.shape, jnp.float32),
        [smem()] + [vmem()] * 8,
        [
            scratch(3, 3 * TILE, width),
            scratch(3 * count * 2 * TILE, width),
            scratch(3 * count * 2 * TILE, width),
            scratch(3 * count * TILE, width),
        ],
        tile_row.reshape(1),
        band,
        truth_blur,
        true_above,
        true_own,
        true_below,
        from_behind(images, "tile", 1),
        images,
        from_behind(images, "tile", -1),
    ).reshape(ground_truth.shape)

    grad_slots = run(
        lambda *refs: back_kernel(tile_sizes, *refs),
        sent_shape,
        [smem(), smem()] + [vmem()] * 5,
        [
            scratch(blocks * LANES, 5 * LANES),
            scratch(blocks * LANES, 2 * LANES),
            scratch(LANES, 2 * LANES),
            scratch(blocks * TILE, LANES),
            scratch(blocks * 24, LANES),
            scratch(entries, LANES),
            scratch(2 * table_rows, LANES),
        ],
        lists,
        flat_lengths,
        expand_matrix(),
        moment_matrix(),
        left,
        shapes,
        grad_image,
    )
    returned = lax.all_to_all(
        grad_slots, ("view", "tile"), split_axis=0, concat_axis=0, tiled=True
    )
    return run(
        lambda *refs: owner_kernel(own_sizes, *refs),
        jax.ShapeDtypeStruct(params.shape, jnp.float32),
        [smem(), smem(), smem(), vmem(), vmem()],
        [
            scratch(SUBS * SUBS * SUBS, LANES),
            scratch(SUBS * 24, LANES),
            scratch(per_device, LANES),
            scratch(PACK * slot_rows, LANES),
        ],
        cams,
        send_list,
        send_counts,
        params,
        returned,
    )


def solution(mesh):
    in_specs = (
        P(None, ("view", "tile")),
        P(("view", "tile"), None),
        P(("view", "tile"), None),
        P(),
        P("view", None, "tile", None),
        P("view", "tile", None, None),
        P("view", "tile", None),
    )
    out_specs = P(None, ("view", "tile"))
    return jax.shard_map(shards, mesh=mesh, in_specs=in_specs, out_specs=out_specs, check_vma=False)
```

```python
import jax
import jax.numpy as jnp
import numpy as np
from jax import lax
from jax.experimental import pallas as pl
from jax.experimental.pallas import tpu as pltpu
from jax.sharding import PartitionSpec as P

TILE = 16


FOCAL = 1000.0
LOW_PASS = 0.3
SSIM_SHARE = 0.2
SMOOTH_EPS = 1e-06
SSIM_ONE = 0.0001
SSIM_TWO = 0.0009
HARMONIC_ZERO = 0.28209479177387814
HARMONIC_ONE = 0.4886025119029199
HARMONIC_TWO = (
    1.0925484305920792,
    -1.0925484305920792,
    0.31539156525252005,
    -1.0925484305920792,
    0.5462742152960396,
)
HARMONIC_THREE = (
    -0.5900435899266435,
    2.890611442640554,
    -0.4570457994644658,
    0.3731763325901154,
    -0.4570457994644658,
    1.445305721320277,
    -0.5900435899266435,
)


def from_behind(block, axis, distance):
    devices = range(lax.axis_size(axis))
    route = [(i - distance, i) for i in devices if i - distance in devices]
    return lax.ppermute(block, axis, route)


def window_taps():
    offsets_np = np.arange(11) - 5.0
    weights = np.exp(-offsets_np * offsets_np / 4.5)
    weights = weights / weights.sum()
    return [float(weight) for weight in weights]


def matrix_product(left_side, right_side):
    return [
        [
            left_side[row_idx][0] * right_side[0][col_idx]
            + left_side[row_idx][1] * right_side[1][col_idx]
            + left_side[row_idx][2] * right_side[2][col_idx]
            for col_idx in range(3)
        ]
        for row_idx in range(3)
    ]


def rotation(angles):
    cos_a, sin_a = (jnp.cos(angles[0]), jnp.sin(angles[0]))
    cos_b, sin_b = (jnp.cos(angles[1]), jnp.sin(angles[1]))
    cos_c, sin_c = (jnp.cos(angles[2]), jnp.sin(angles[2]))
    about_x = [[1.0, 0.0, 0.0], [0.0, cos_a, -sin_a], [0.0, sin_a, cos_a]]
    about_y = [[cos_b, 0.0, sin_b], [0.0, 1.0, 0.0], [-sin_b, 0.0, cos_b]]
    about_z = [[cos_c, -sin_c, 0.0], [sin_c, cos_c, 0.0], [0.0, 0.0, 1.0]]
    return matrix_product(about_z, matrix_product(about_y, about_x))


def harmonics(dir_x, dir_y, dir_z):
    sq_x, sq_y, sq_z = (dir_x * dir_x, dir_y * dir_y, dir_z * dir_z)
    prod_xy, prod_yz, prod_xz = (dir_x * dir_y, dir_y * dir_z, dir_x * dir_z)
    return [
        HARMONIC_ZERO + 0.0 * dir_x,
        -HARMONIC_ONE * dir_y,
        HARMONIC_ONE * dir_z,
        -HARMONIC_ONE * dir_x,
        HARMONIC_TWO[0] * prod_xy,
        HARMONIC_TWO[1] * prod_yz,
        HARMONIC_TWO[2] * (2.0 * sq_z - sq_x - sq_y),
        HARMONIC_TWO[3] * prod_xz,
        HARMONIC_TWO[4] * (sq_x - sq_y),
        HARMONIC_THREE[0] * dir_y * (3.0 * sq_x - sq_y),
        HARMONIC_THREE[1] * prod_xy * dir_z,
        HARMONIC_THREE[2] * dir_y * (4.0 * sq_z - sq_x - sq_y),
        HARMONIC_THREE[3] * dir_z * (2.0 * sq_z - 3.0 * sq_x - 3.0 * sq_y),
        HARMONIC_THREE[4] * dir_x * (4.0 * sq_z - sq_x - sq_y),
        HARMONIC_THREE[5] * dir_z * (sq_x - sq_y),
        HARMONIC_THREE[6] * dir_x * (sq_x - 3.0 * sq_y),
    ]


LANES = 128
SUBS = 8
GROUP = 8
STEP_ROWS = 16
FEATS = 8
PAIR = 2 * FEATS
COEF_ROWS = 32
SLOT = PAIR + 2
PACK = LANES // SLOT
FLAG = PAIR + 1
UNROLL = 8
MOVES = 16
TAPS = 11
DEAD = -1e30
LOG_TOP = float(np.log(0.99))
VMEM_BYTES = 48 * 1024 * 1024


def stepped(total, width, body, state):
    def step(block, held):
        for k in range(width):
            held = body(block * width + k, held)
        return held

    return lax.fori_loop(0, (total + width - 1) // width, step, state)


def packed_rows(cap):
    return -(-cap // (PACK * SUBS)) * SUBS


def pack_slots(read, rows, first_lane):
    lane = lax.broadcasted_iota(jnp.int32, (rows, LANES), 1)
    packed = jnp.zeros((rows, LANES), jnp.float32)
    for q in range(PACK):
        shift = (q * SLOT - first_lane) % LANES
        value = read(q * rows)
        value = pltpu.roll(value, shift, 1) if shift else value
        packed = jnp.where((lane >= q * SLOT) & (lane < (q + 1) * SLOT), value, packed)
    return packed


def unpack_slots(packed, write):
    for q in range(PACK):
        write(q * packed.shape[0], pltpu.roll(packed, LANES - q * SLOT, 1) if q else packed)


def camera_table(camera):
    columns = [camera[:, entry] for entry in range(6)]
    turn = rotation(columns[0:3])
    shift = columns[3:6]
    anchor = [
        -(turn[0][c] * shift[0] + turn[1][c] * shift[1] + turn[2][c] * shift[2]) for c in range(3)
    ]
    flat = [turn[r][c] for r in range(3) for c in range(3)] + shift + anchor
    return jnp.stack(flat + [jnp.zeros_like(shift[0])], axis=1)


def shape_matrix(params):
    scales = [jnp.exp(params[3 + axis_num]) for axis_num in range(3)]
    inv_norm = 1.0 / jnp.sqrt(
        params[6] * params[6]
        + params[7] * params[7]
        + params[8] * params[8]
        + params[9] * params[9]
    )
    quat_w, quat_x, quat_y, quat_z = [params[6 + k] * inv_norm for k in range(4)]
    quat_rot = [
        [
            1.0 - 2.0 * (quat_y * quat_y + quat_z * quat_z),
            2.0 * (quat_x * quat_y - quat_w * quat_z),
            2.0 * (quat_x * quat_z + quat_w * quat_y),
        ],
        [
            2.0 * (quat_x * quat_y + quat_w * quat_z),
            1.0 - 2.0 * (quat_x * quat_x + quat_z * quat_z),
            2.0 * (quat_y * quat_z - quat_w * quat_x),
        ],
        [
            2.0 * (quat_x * quat_z - quat_w * quat_y),
            2.0 * (quat_y * quat_z + quat_w * quat_x),
            1.0 - 2.0 * (quat_x * quat_x + quat_y * quat_y),
        ],
    ]
    return [[quat_rot[r][c] * scales[c] for c in range(3)] for r in range(3)]


def view_features(params, shape, cam, image_width, image_height):
    turn = [[cam[3 * r + c] for c in range(3)] for r in range(3)]
    point = [
        turn[r][0] * params[0] + turn[r][1] * params[1] + turn[r][2] * params[2] + cam[9 + r]
        for r in range(3)
    ]
    inv_depth = 1.0 / point[2]
    ratio_x, ratio_y = point[0] * inv_depth, point[1] * inv_depth
    zoom = FOCAL * inv_depth
    row_x = [zoom * (turn[0][c] - ratio_x * turn[2][c]) for c in range(3)]
    row_y = [zoom * (turn[1][c] - ratio_y * turn[2][c]) for c in range(3)]
    proj_x = [
        row_x[0] * shape[0][c] + row_x[1] * shape[1][c] + row_x[2] * shape[2][c] for c in range(3)
    ]
    proj_y = [
        row_y[0] * shape[0][c] + row_y[1] * shape[1][c] + row_y[2] * shape[2][c] for c in range(3)
    ]
    cov_xx = proj_x[0] * proj_x[0] + proj_x[1] * proj_x[1] + proj_x[2] * proj_x[2] + LOW_PASS
    cov_xy = proj_x[0] * proj_y[0] + proj_x[1] * proj_y[1] + proj_x[2] * proj_y[2]
    cov_yy = proj_y[0] * proj_y[0] + proj_y[1] * proj_y[1] + proj_y[2] * proj_y[2] + LOW_PASS
    inv_det = 1.0 / (cov_xx * cov_yy - cov_xy * cov_xy)
    ray = [params[c] - cam[12 + c] for c in range(3)]
    inv_len = 1.0 / jnp.sqrt(ray[0] * ray[0] + ray[1] * ray[1] + ray[2] * ray[2])
    basis = harmonics(ray[0] * inv_len, ray[1] * inv_len, ray[2] * inv_len)
    colours = []
    for channel in range(3):
        summed = 0.5 + HARMONIC_ZERO * params[11 + 16 * channel]
        for harmonic in range(1, 16):
            summed = summed + basis[harmonic] * params[11 + 16 * channel + harmonic]
        colours.append(summed)
    return [
        FOCAL * ratio_x + image_width / 2.0,
        FOCAL * ratio_y + image_height / 2.0,
        cov_yy * inv_det,
        -cov_xy * inv_det,
        cov_xx * inv_det,
    ] + colours


def log_opacity(logit):
    return LOG_TOP - jnp.log(1.0 + jnp.exp(-logit))


def load_params(params_ref, tile_scr, block):
    count = params_ref.shape[0]
    for band in range(0, count, SUBS):
        high = min(band + SUBS, count)
        for j in range(SUBS):
            lane_at = pl.multiple_of(block * SUBS * LANES + j * LANES, LANES)
            tile_scr[band * SUBS + j * SUBS : band * SUBS + j * SUBS + high - band, :] = params_ref[
                band:high, pl.ds(lane_at, LANES)
            ]
    return [
        tile_scr[pl.ds((r // SUBS) * SUBS * SUBS + r % SUBS, SUBS, stride=SUBS), :]
        for r in range(count)
    ]


def source_kernel(
    sizes, cam_ref, list_ref, counts_ref, params_ref, out_ref, tile_scr, feat_scr, table, slots
):
    groups, rows, cap, image_width, image_height = sizes
    per = params_ref.shape[1]
    views = cam_ref.shape[0]
    height = out_ref.shape[1]
    used = -(-groups * SLOT // SUBS) * SUBS

    def project_block(block, carry):
        params = load_params(params_ref, tile_scr, block)
        shape = shape_matrix(params)
        log_o = log_opacity(params[10])
        for view in range(views):
            cam = [cam_ref[view, k] for k in range(15)]
            for num, value in enumerate(
                view_features(params, shape, cam, image_width, image_height)
            ):
                line = view // 2 * SLOT + view % 2 * FEATS + num
                feat_scr[pl.ds(line, SUBS, stride=used), :] = value
        for group in range(groups):
            feat_scr[pl.ds(group * SLOT + PAIR, SUBS, stride=used), :] = log_o
        for j in range(SUBS):
            row_at = pl.multiple_of(block * SUBS * LANES + j * LANES, LANES)
            table[pl.ds(row_at, LANES), 0:used] = feat_scr[j * used : (j + 1) * used, :].T
        return carry

    lax.fori_loop(0, per // (SUBS * LANES), project_block, 0)

    start = jnp.int32(0)
    for group in range(groups):

        def send_block(t, start_at, group=group):
            dest = group * rows + t
            count = counts_ref[0, dest]

            def move(k, carry):
                spot = jnp.minimum(start_at + k, per - 1)
                slots[pl.ds(k, 1), :] = table[pl.ds(list_ref[0, spot], 1), :]
                return carry

            stepped(count, MOVES, move, 0)
            out_ref[dest] = pack_slots(
                lambda at: slots[at : at + height, :], height, group * SLOT
            )
            return start_at + count

        start = lax.fori_loop(0, rows, send_block, start)


def split_three(value):
    first = value.astype(jnp.bfloat16).astype(jnp.float32)
    rest = value - first
    second = rest.astype(jnp.bfloat16).astype(jnp.float32)
    return [first, second, rest - second]


def swap_grain(cells):
    sub = lax.broadcasted_iota(jnp.int32, (SUBS, LANES), 0)
    lane = lax.broadcasted_iota(jnp.int32, (SUBS, LANES), 1) // TILE
    for bit in (1, 2, 4):
        sub_bit, lane_bit = (sub & bit) != 0, (lane & bit) != 0
        from_high = pltpu.roll(pltpu.roll(cells, SUBS - bit, 0), bit * TILE, 1)
        from_low = pltpu.roll(pltpu.roll(cells, bit, 0), LANES - bit * TILE, 1)
        cells = jnp.where(sub_bit == lane_bit, cells, jnp.where(lane_bit, from_high, from_low))
    return cells


def longest(lens_ref, group):
    most = lens_ref[group * GROUP]
    for t in range(1, GROUP):
        most = jnp.maximum(most, lens_ref[group * GROUP + t])
    return most


def render_kernel(
    sizes,
    row_ref,
    lists_ref,
    lens_ref,
    lens_rows_ref,
    basis_ref,
    arrived_ref,
    image_ref,
    left_ref,
    shape_ref,
    table,
    rows,
    feat_scr,
    pieces,
    mm,
):
    cap, col_groups, list_len = sizes
    devices, height = arrived_ref.shape[0:2]
    blocks = list_len // STEP_ROWS
    table[devices * cap :, :] = jnp.zeros((GROUP, LANES), jnp.float32)

    def unpack(source, carry):
        def write(at, value):
            size = min(height, cap - at)
            if size > 0:
                row_at = pl.multiple_of(source * cap + at, SUBS)
                table[pl.ds(row_at, size), :] = value[0:size]

        unpack_slots(arrived_ref[source], write)
        return carry

    lax.fori_loop(0, devices, unpack, 0)
    centre_y = (row_ref[0] * TILE).astype(jnp.float32) + (TILE - 1) / 2.0
    sub = lax.broadcasted_iota(jnp.int32, (blocks, LANES), 0)
    lane = lax.broadcasted_iota(jnp.int32, (blocks, LANES), 1)
    zero = jnp.zeros((SUBS, LANES), jnp.float32)

    def one_group(group, carry):
        view, col_group = group // col_groups, group % col_groups
        most = longest(lens_ref, group)

        def fetch(n, inner):
            for t in range(GROUP):
                slot = lists_ref[group * GROUP + t, n]
                rows[pl.ds(n * GROUP + t, 1), :] = table[pl.ds(slot, 1), :]
            return inner

        stepped(most, UNROLL, fetch, 0)
        for block in range(blocks):
            feat_scr[block * 24 : (block + 1) * 24, :] = rows[
                block * LANES : (block + 1) * LANES, 0:24
            ].T
        feats = [
            feat_scr[pl.ds(view * FEATS + num, blocks, stride=24), :] for num in range(FEATS)
        ]
        log_o = feat_scr[pl.ds(PAIR, blocks, stride=24), :]
        live = sub * STEP_ROWS + lane // GROUP < lens_rows_ref[pl.ds(group, 1), :]
        centre_x = ((col_group * GROUP + lane % GROUP) * TILE).astype(jnp.float32) + (
            TILE - 1
        ) / 2.0
        off_x, off_y = feats[0] - centre_x, feats[1] - centre_y
        lin_x = feats[2] * off_x + feats[3] * off_y
        lin_y = feats[4] * off_y + feats[3] * off_x
        coefs = [
            log_o - 0.5 * (off_x * lin_x + off_y * lin_y),
            lin_x,
            lin_y,
            -0.5 * feats[2],
            -feats[3],
            -0.5 * feats[4],
        ]
        coefs = [
            jnp.where(live, value, DEAD if num == 0 else 0.0) for num, value in enumerate(coefs)
        ]
        lines = [None] * COEF_ROWS
        for num, value in enumerate(coefs):
            for piece, part in enumerate(split_three(value)):
                lines[piece * 6 + num] = part
        for num in range(3):
            for piece, part in enumerate(split_three(jnp.where(live, feats[5 + num], 0.0))):
                lines[18 + piece * 3 + num] = part
        for num, value in enumerate(lines):
            pieces[pl.ds(num, blocks, stride=COEF_ROWS), :] = (
                jnp.zeros((blocks, LANES), jnp.float32) if value is None else value
            )
        for num, value in enumerate(feats[2:5] + [off_x, off_y]):
            shape_ref[num, pl.ds(pl.multiple_of(group * blocks, blocks), blocks), :] = jnp.where(
                live, value, 0.0
            )
        left_at = pl.multiple_of(group * blocks * LANES, LANES)
        for block in range(blocks):
            left_ref[pl.ds(left_at + block * LANES, LANES), :] = pieces[
                block * COEF_ROWS : (block + 1) * COEF_ROWS, :
            ].T.astype(jnp.bfloat16)
        expand(left_ref, basis_ref, mm, left_at)

        def entry(n, state):
            keep, colour = state
            row_at = pl.multiple_of(n * GROUP, GROUP)
            shade = [
                mm[pl.ds(row_at, GROUP), (2 + c) * LANES : (3 + c) * LANES] for c in range(3)
            ]
            new_keep, new_colour = [], []
            for half in range(2):
                alpha = jnp.exp(mm[pl.ds(row_at, GROUP), half * LANES : (half + 1) * LANES])
                weight = keep[half] * alpha
                new_keep.append(keep[half] * (1.0 - alpha))
                new_colour.append([colour[half][c] + weight * shade[c] for c in range(3)])
            return new_keep, new_colour

        state = ([zero + 1.0] * 2, [[zero] * 3] * 2)
        _, colour = stepped(most, UNROLL, entry, state)
        lane_at = pl.multiple_of(col_group * LANES, LANES)
        for half in range(2):
            for c in range(3):
                image_ref[view, c, half * SUBS : (half + 1) * SUBS, pl.ds(lane_at, LANES)] = (
                    swap_grain(colour[half][c])
                )
        return carry

    lax.fori_loop(0, 2 * col_groups, one_group, 0)


def expand(left_ref, basis_ref, mm, left_at):
    mm[...] = jnp.dot(
        left_ref[pl.ds(left_at, mm.shape[0]), :],
        basis_ref[...],
        preferred_element_type=jnp.float32,
    )


def back_kernel(
    sizes,
    lists_ref,
    lens_ref,
    basis_ref,
    moment_ref,
    left_ref,
    shape_ref,
    grad_ref,
    out_ref,
    mm,
    alphas,
    weights,
    slopes,
    grad_scr,
    mom_scr,
    row_scr,
    rows,
    table,
):
    cap, col_groups, list_len = sizes
    devices, height = out_ref.shape[0:2]
    blocks = list_len // STEP_ROWS
    table_rows = table.shape[0] // 2
    table[...] = jnp.zeros_like(table)
    grad_scr[...] = jnp.zeros_like(grad_scr)
    zero = jnp.zeros((SUBS, LANES), jnp.float32)
    sub = lax.broadcasted_iota(jnp.int32, (SUBS, LANES), 0)
    lane = lax.broadcasted_iota(jnp.int32, (SUBS, LANES), 1)
    own_tile = lane % GROUP == sub

    def one_group(group, carry):
        view, col_group = group // col_groups, group % col_groups
        most = longest(lens_ref, group)
        lane_at = pl.multiple_of(col_group * LANES, LANES)
        grads = [
            [
                swap_grain(
                    grad_ref[view, c, half * SUBS : (half + 1) * SUBS, pl.ds(lane_at, LANES)]
                )
                for c in range(3)
            ]
            for half in range(2)
        ]
        for half in range(2):
            for c in range(3):
                for piece, part in enumerate(split_three(grads[half][c])):
                    grad_scr[
                        piece * 24 + c * SUBS : piece * 24 + (c + 1) * SUBS,
                        half * LANES : (half + 1) * LANES,
                    ] = part
        expand(left_ref, basis_ref, mm, pl.multiple_of(group * blocks * LANES, LANES))

        def ahead(n, keep):
            row_at = pl.multiple_of(n * GROUP, GROUP)
            new_keep = []
            for half in range(2):
                lanes = slice(half * LANES, (half + 1) * LANES)
                alpha = jnp.exp(mm[pl.ds(row_at, GROUP), lanes])
                weight = keep[half] * alpha
                alphas[pl.ds(row_at, GROUP), lanes] = alpha
                weights[pl.ds(row_at, GROUP), lanes] = weight
                new_keep.append(keep[half] * (1.0 - alpha))
            return new_keep

        stepped(most, UNROLL, ahead, [zero + 1.0] * 2)

        last = (most + UNROLL - 1) // UNROLL * UNROLL - 1

        def behind(step, seen):
            row_at = pl.multiple_of((last - step) * GROUP, GROUP)
            shade = [
                mm[pl.ds(row_at, GROUP), (2 + c) * LANES : (3 + c) * LANES] for c in range(3)
            ]
            new_seen = []
            for half in range(2):
                lanes = slice(half * LANES, (half + 1) * LANES)
                own = (
                    grads[half][0] * shade[0]
                    + grads[half][1] * shade[1]
                    + grads[half][2] * shade[2]
                )
                alpha = alphas[pl.ds(row_at, GROUP), lanes]
                slopes[pl.ds(row_at, GROUP), lanes] = weights[pl.ds(row_at, GROUP), lanes] * (
                    own - seen[half]
                )
                new_seen.append(seen[half] * (1.0 - alpha) + alpha * own)
            return new_seen

        stepped(most, UNROLL, behind, [zero] * 2)
        total = jnp.zeros((blocks * LANES, LANES), jnp.float32)
        for value, right in (
            (slopes[...], moment_ref[...]),
            (weights[...], grad_scr[...].T.astype(jnp.bfloat16)),
        ):
            high = value.astype(jnp.bfloat16)
            low = (value - high.astype(jnp.float32)).astype(jnp.bfloat16)
            total = total + jnp.dot(high, right, preferred_element_type=jnp.float32)
            total = total + jnp.dot(low, right, preferred_element_type=jnp.float32)
        for block in range(blocks):
            turned = total[block * LANES : (block + 1) * LANES].T
            mom_scr[block * TILE : block * TILE + 8, :] = turned[96:104]
            for c in range(3):
                summed = (
                    turned[c * SUBS : (c + 1) * SUBS]
                    + turned[24 + c * SUBS : 24 + (c + 1) * SUBS]
                    + turned[48 + c * SUBS : 48 + (c + 1) * SUBS]
                )
                mom_scr[block * TILE + 8 + c : block * TILE + 9 + c, :] = jnp.sum(
                    jnp.where(own_tile, summed, 0.0), axis=0, keepdims=True
                )
        mom = [mom_scr[pl.ds(num, blocks, stride=TILE), :] for num in range(11)]
        con_xx, con_xy, con_yy, off_x, off_y = [
            shape_ref[num, pl.ds(pl.multiple_of(group * blocks, blocks), blocks), :]
            for num in range(5)
        ]
        sum_x = off_x * mom[0] - mom[1]
        sum_y = off_y * mom[0] - mom[2]
        results = [
            -(con_xx * sum_x + con_xy * sum_y),
            -(con_yy * sum_y + con_xy * sum_x),
            -0.5 * (off_x * (sum_x - mom[1]) + mom[3]),
            -(off_x * sum_y - off_y * mom[1] + mom[4]),
            -0.5 * (off_y * (sum_y - mom[2]) + mom[5]),
        ] + mom[8:11]
        other = 1 - view
        for num, value in enumerate(results):
            row_scr[pl.ds(view * FEATS + num, blocks, stride=24), :] = value
            row_scr[pl.ds(other * FEATS + num, blocks, stride=24), :] = jnp.zeros_like(value)
        row_scr[pl.ds(PAIR, blocks, stride=24), :] = mom[0]
        row_scr[pl.ds(FLAG, blocks, stride=24), :] = jnp.ones((blocks, LANES), jnp.float32)
        first = pl.multiple_of(group * blocks * LANES, LANES)
        for block in range(blocks):
            rows[pl.ds(first + block * LANES, LANES), 0:24] = row_scr[
                block * 24 : (block + 1) * 24, :
            ].T

        def put(n, inner):
            for t in range(GROUP):
                spot = view * table_rows + lists_ref[group * GROUP + t, n]
                table[pl.ds(spot, 1), :] = rows[pl.ds(first + n * GROUP + t, 1), :]
            return inner

        stepped(most, UNROLL, put, 0)
        return carry

    lax.fori_loop(0, 2 * col_groups, one_group, 0)

    def pack(source, count):
        found = [count]

        def read(at):
            size = min(height, cap - at)
            if size <= 0:
                return jnp.zeros((height, LANES), jnp.float32)
            row_at = pl.multiple_of(source * cap + at, SUBS)
            value = table[pl.ds(row_at, size), :] + table[pl.ds(table_rows + row_at, size), :]
            found[0] = found[0] + value.reshape(size // SUBS, SUBS, LANES).sum(axis=0)
            if size < height:
                value = jnp.concatenate(
                    [value, jnp.zeros((height - size, LANES), jnp.float32)], axis=0
                )
            return value

        out_ref[source] = pack_slots(read, height, 0)
        return found[0]

    count = lax.fori_loop(0, devices, pack, zero)
    stored = jnp.sum(jnp.where(lane == FLAG, count, 0.0))
    named = lens_ref[0]
    for tile in range(1, 2 * col_groups * GROUP):
        named = named + lens_ref[tile]

    @pl.when(stored < named.astype(jnp.float32) - 0.5)
    def _():
        table[...] = jnp.zeros_like(table)

        def add_group(group, carry):
            def add(n, inner):
                for t in range(GROUP):
                    spot = lists_ref[group * GROUP + t, n]
                    row_at = group * blocks * LANES + n * GROUP + t
                    table[pl.ds(spot, 1), :] = table[pl.ds(spot, 1), :] + rows[pl.ds(row_at, 1), :]
                return inner

            return lax.fori_loop(0, longest(lens_ref, group), add, carry)

        lax.fori_loop(0, 2 * col_groups, add_group, 0)
        lax.fori_loop(0, devices, pack, zero)


def owner_kernel(
    sizes,
    cam_ref,
    list_ref,
    counts_ref,
    params_ref,
    back_ref,
    out_ref,
    tile_scr,
    feat_scr,
    table,
    slots,
):
    groups, rows, cap, image_width, image_height = sizes
    count_params, per = params_ref.shape
    height = back_ref.shape[1]
    table[...] = jnp.zeros_like(table)
    lane = lax.broadcasted_iota(jnp.int32, (height, LANES), 1)
    start = jnp.int32(0)
    for group in range(groups):

        def take_block(t, start_at, group=group):
            dest = group * rows + t
            count = counts_ref[0, dest]

            def write(at, value):
                slots[at : at + height, :] = jnp.where(lane == PAIR + 1, 1.0 + group, value)

            unpack_slots(back_ref[dest], write)

            def move(k, carry):
                spot = list_ref[0, start_at + k]
                table[pl.ds(spot, 1), :] = slots[pl.ds(k, 1), :]
                return carry

            rounded = (count + MOVES - 1) // MOVES * MOVES
            whole = jnp.where(start_at + rounded <= per, rounded, count // MOVES * MOVES)
            stepped(whole, MOVES, move, 0)
            lax.fori_loop(whole, count, move, 0)
            return start_at + count

        start = lax.fori_loop(0, rows, take_block, start)

    def clear(k, carry):
        table[pl.ds(list_ref[0, k], 1), :] = jnp.zeros((1, LANES), jnp.float32)
        return carry

    lax.fori_loop(start, jnp.minimum(start + MOVES, per), clear, 0)

    def pull_block(block, carry):
        params = load_params(params_ref, tile_scr, block)
        for j in range(SUBS):
            row_at = pl.multiple_of(block * SUBS * LANES + j * LANES, LANES)
            feat_scr[j * 24 : (j + 1) * 24, :] = table[pl.ds(row_at, LANES), 0:24].T
        cots = [feat_scr[pl.ds(num, SUBS, stride=24), :] for num in range(PAIR + 2)]
        home = cots[PAIR + 1]
        sent = home > 0.5
        cams = []
        for view in range(2):
            cam = []
            for k in range(15):
                value = jnp.full((SUBS, LANES), cam_ref[view, k], jnp.float32)
                for group in range(1, groups):
                    value = jnp.where(home > 0.5 + group, cam_ref[2 * group + view, k], value)
                cam.append(value)
            cams.append(cam)

        def both(*values):
            shape = shape_matrix(values)
            return (
                view_features(values, shape, cams[0], image_width, image_height)
                + view_features(values, shape, cams[1], image_width, image_height)
                + [log_opacity(values[10])]
            )

        _, pull = jax.vjp(both, *params)
        grads = pull(cots[0 : PAIR + 1])
        for num, value in enumerate(grads):
            tile_scr[pl.ds((num // SUBS) * SUBS * SUBS + num % SUBS, SUBS, stride=SUBS), :] = (
                jnp.where(sent, value, 0.0)
            )
        for band in range(0, count_params, SUBS):
            high = min(band + SUBS, count_params)
            for j in range(SUBS):
                lane_at = pl.multiple_of(block * SUBS * LANES + j * LANES, LANES)
                out_ref[band:high, pl.ds(lane_at, LANES)] = tile_scr[
                    band * SUBS + j * SUBS : band * SUBS + j * SUBS + high - band, :
                ]
        return carry

    lax.fori_loop(0, per // (SUBS * LANES), pull_block, 0)


def tap_rows(read, first, count):
    taps = window_taps()
    total = taps[5] * read(first + 5, count)
    for k in range(5):
        total = total + taps[k] * (read(first + k, count) + read(first + TAPS - 1 - k, count))
    return total


def blur_lanes(value, band):
    return jnp.dot(
        value, band, precision=lax.Precision.HIGHEST, preferred_element_type=jnp.float32
    )


def truth_kernel(band_ref, above_ref, own_ref, below_ref, out_ref, tall, mixed):
    images = own_ref.shape[0]

    def one_image(m, carry):
        whole = jnp.concatenate([above_ref[m], own_ref[m], below_ref[m]], axis=0)
        for field, value in enumerate((whole, whole * whole)):
            tall[...] = value
            row_at = pl.multiple_of((field * images + m) * 2 * TILE, 2 * TILE)
            mixed[pl.ds(row_at, 2 * TILE), :] = tap_rows(
                lambda at, count: tall[at : at + count, :], 6, 2 * TILE
            )
        return carry

    lax.fori_loop(0, images, one_image, 0)
    out_ref[...] = blur_lanes(mixed[...], band_ref[...])


def loss_kernel(
    image_rows,
    row_ref,
    band_ref,
    truth_ref,
    true_above,
    true_own,
    true_below,
    above_ref,
    own_ref,
    below_ref,
    out_ref,
    tall,
    mixed,
    blurred,
    slim,
):
    images = own_ref.shape[0]
    tall_rows = 2 * TILE
    width = own_ref.shape[2]

    def one_image(m, carry):
        whole = jnp.concatenate([above_ref[m], own_ref[m], below_ref[m]], axis=0)
        true = jnp.concatenate([true_above[m], true_own[m], true_below[m]], axis=0)
        for field, value in enumerate((whole, whole * whole, whole * true)):
            tall[field] = value
            row_at = pl.multiple_of((field * images + m) * tall_rows, tall_rows)
            mixed[pl.ds(row_at, tall_rows), :] = tap_rows(
                lambda at, count, field=field: tall[field, at : at + count, :], 6, tall_rows
            )
        return carry

    lax.fori_loop(0, images, one_image, 0)
    blurred[...] = blur_lanes(mixed[...], band_ref[...])
    sub = lax.broadcasted_iota(jnp.int32, (tall_rows, width), 0)
    image_row = row_ref[0] * TILE + sub - 5
    inside = (image_row >= 0) & (image_row < image_rows) & (sub < TILE + 10)

    def one_map(m, carry):
        def field_of(ref, field):
            row_at = pl.multiple_of((field * images + m) * tall_rows, tall_rows)
            return ref[pl.ds(row_at, tall_rows), :]

        mean_one, both_one, cross = [field_of(blurred, field) for field in range(3)]
        mean_two, both_two = field_of(truth_ref, 0), field_of(truth_ref, 1)
        square_one, square_two = mean_one * mean_one, mean_two * mean_two
        mean_cross = mean_one * mean_two
        top_one = 2.0 * mean_cross + SSIM_ONE
        top_two = 2.0 * (cross - mean_cross) + SSIM_TWO
        low_one = square_one + square_two + SSIM_ONE
        low_two = (both_one - square_one) + (both_two - square_two) + SSIM_TWO
        inv_one, inv_two = 1.0 / low_one, 1.0 / low_two
        inv_both = inv_one * inv_two
        value = top_one * top_two * inv_both
        grads = [
            2.0 * mean_two * (top_two - top_one) * inv_both
            - 2.0 * mean_one * value * (inv_one - inv_two),
            -value * inv_two,
            2.0 * top_one * inv_both,
        ]
        for field, grad in enumerate(grads):
            tall[field, 0:tall_rows] = jnp.where(inside, grad, 0.0)
            row_at = pl.multiple_of((field * images + m) * TILE, TILE)
            slim[pl.ds(row_at, TILE), :] = tap_rows(
                lambda at, count, field=field: tall[field, at : at + count, :], 0, TILE
            )
        return carry

    lax.fori_loop(0, images, one_map, 0)
    spread = blur_lanes(slim[...], band_ref[...]).reshape(3, images, TILE, width)
    own, true = own_ref[...], true_own[...]
    gap = own - true
    out_ref[...] = (1.0 - SSIM_SHARE) * gap / jnp.sqrt(gap * gap + SMOOTH_EPS) - SSIM_SHARE * (
        spread[0] + 2.0 * own * spread[1] + true * spread[2]
    )


def band_matrix(width):
    taps = window_taps()
    band = np.zeros((width, width), np.float32)
    for k in range(TAPS):
        band += np.diag(np.full(width - abs(k - 5), taps[k], np.float32), k - 5)
    return jnp.asarray(band)


def pixel_basis():
    pixel = np.arange(TILE * TILE)
    x = (pixel % TILE) - (TILE - 1) / 2.0
    y = (pixel // TILE) - (TILE - 1) / 2.0
    return np.stack([np.ones_like(x), x, y, x * x, x * y, y * y])


def expand_matrix():
    terms = pixel_basis()
    matrix = np.zeros((COEF_ROWS, 5 * LANES), np.float32)
    for piece in range(3):
        matrix[piece * 6 : piece * 6 + 6, 0 : 2 * LANES] = terms
        for c in range(3):
            matrix[18 + piece * 3 + c, (2 + c) * LANES : (3 + c) * LANES] = 1.0
    return jnp.asarray(matrix, jnp.bfloat16)


def moment_matrix():
    matrix = np.zeros((2 * LANES, LANES), np.float32)
    matrix[:, 96:102] = pixel_basis().T
    return jnp.asarray(matrix, jnp.bfloat16)


def smem():
    return pl.BlockSpec(memory_space=pltpu.SMEM)


def vmem():
    return pl.BlockSpec(memory_space=pltpu.VMEM)


def scratch(*shape):
    return pltpu.VMEM(shape, jnp.float32)


def run(kernel, out_shapes, in_specs, scratches, *operands):
    return pl.pallas_call(
        kernel,
        out_shape=out_shapes,
        in_specs=in_specs,
        out_specs=jax.tree.map(lambda _: vmem(), out_shapes),
        scratch_shapes=scratches,
        compiler_params=pltpu.CompilerParams(vmem_limit_bytes=VMEM_BYTES),
    )(*operands)


def shards(params, send_list, send_counts, camera, ground_truth, tile_lists, list_lengths):
    devices = lax.axis_size(("view", "tile"))
    row_devices = lax.axis_size("tile")
    groups = lax.axis_size("view")
    count_params, per_device = params.shape
    capacity = per_device // devices
    tile_cols, list_len = tile_lists.shape[2:]
    col_groups = tile_cols // GROUP
    blocks = list_len // STEP_ROWS
    tile_row = lax.axis_index("tile")
    image_width = float(ground_truth.shape[3])
    image_height = float(ground_truth.shape[2] * row_devices)
    table_rows = per_device + GROUP
    slot_rows = packed_rows(capacity)
    sent_shape = jax.ShapeDtypeStruct((devices, slot_rows, LANES), jnp.float32)
    cams = camera_table(camera)

    flat_lengths = list_lengths.reshape(-1)
    entry_rank = jnp.arange(list_len, dtype=jnp.int32)
    tile_num = jnp.arange(2 * tile_cols, dtype=jnp.int32)
    lists = jnp.where(
        entry_rank[None, :] < flat_lengths[:, None],
        tile_lists.reshape(2 * tile_cols, list_len),
        per_device + tile_num[:, None] % GROUP,
    )
    lens_rows = jnp.tile(flat_lengths.reshape(-1, GROUP), (1, LANES // GROUP))

    width = ground_truth.shape[3]
    true_own = ground_truth.reshape(-1, TILE, width)
    true_above = from_behind(true_own, "tile", 1)
    true_below = from_behind(true_own, "tile", -1)
    band = band_matrix(width)
    truth_rows = 2 * true_own.shape[0] * 2 * TILE
    truth_blur = run(
        truth_kernel,
        jax.ShapeDtypeStruct((truth_rows, width), jnp.float32),
        [vmem()] * 4,
        [scratch(3 * TILE, width), scratch(truth_rows, width)],
        band,
        true_above,
        true_own,
        true_below,
    )

    own_sizes = (groups, row_devices, capacity, image_width, image_height)
    sent = run(
        lambda *refs: source_kernel(own_sizes, *refs),
        sent_shape,
        [smem(), smem(), smem(), vmem()],
        [
            scratch(SUBS * SUBS * SUBS, LANES),
            scratch(SUBS * LANES, LANES),
            scratch(per_device, LANES),
            scratch(PACK * slot_rows, LANES),
        ],
        cams,
        send_list,
        send_counts,
        params,
    )
    arrived = lax.all_to_all(sent, ("view", "tile"), split_axis=0, concat_axis=0, tiled=True)

    tile_sizes = (capacity, col_groups, list_len)
    entries = 2 * tile_cols * list_len
    rendered, left, shapes = run(
        lambda *refs: render_kernel(tile_sizes, *refs),
        (
            jax.ShapeDtypeStruct(ground_truth.shape, jnp.float32),
            jax.ShapeDtypeStruct((entries, COEF_ROWS), jnp.bfloat16),
            jax.ShapeDtypeStruct((5, entries // LANES, LANES), jnp.float32),
        ),
        [smem(), smem(), smem(), vmem(), vmem(), vmem()],
        [
            scratch(table_rows, LANES),
            scratch(blocks * LANES, LANES),
            scratch(blocks * 24, LANES),
            scratch(blocks * COEF_ROWS, LANES),
            scratch(blocks * LANES, 5 * LANES),
        ],
        tile_row.reshape(1),
        lists,
        flat_lengths,
        lens_rows,
        expand_matrix(),
        arrived,
    )

    images = rendered.reshape(true_own.shape)
    count = images.shape[0]
    grad_image = run(
        lambda *refs: loss_kernel(TILE * row_devices, *refs),
        jax.ShapeDtypeStruct(images.shape, jnp.float32),
        [smem()] + [vmem()] * 8,
        [
            scratch(3, 3 * TILE, width),
            scratch(3 * count * 2 * TILE, width),
            scratch(3 * count * 2 * TILE, width),
            scratch(3 * count * TILE, width),
        ],
        tile_row.reshape(1),
        band,
        truth_blur,
        true_above,
        true_own,
        true_below,
        from_behind(images, "tile", 1),
        images,
        from_behind(images, "tile", -1),
    ).reshape(ground_truth.shape)

    grad_slots = run(
        lambda *refs: back_kernel(tile_sizes, *refs),
        sent_shape,
        [smem(), smem()] + [vmem()] * 5,
        [
            scratch(blocks * LANES, 5 * LANES),
            scratch(blocks * LANES, 2 * LANES),
            scratch(blocks * LANES, 2 * LANES),
            scratch(blocks * LANES, 2 * LANES),
            scratch(LANES, 2 * LANES),
            scratch(blocks * TILE, LANES),
            scratch(blocks * 24, LANES),
            scratch(entries, LANES),
            scratch(2 * table_rows, LANES),
        ],
        lists,
        flat_lengths,
        expand_matrix(),
        moment_matrix(),
        left,
        shapes,
        grad_image,
    )
    returned = lax.all_to_all(
        grad_slots, ("view", "tile"), split_axis=0, concat_axis=0, tiled=True
    )
    return run(
        lambda *refs: owner_kernel(own_sizes, *refs),
        jax.ShapeDtypeStruct(params.shape, jnp.float32),
        [smem(), smem(), smem(), vmem(), vmem()],
        [
            scratch(SUBS * SUBS * SUBS, LANES),
            scratch(SUBS * 24, LANES),
            scratch(per_device, LANES),
            scratch(PACK * slot_rows, LANES),
        ],
        cams,
        send_list,
        send_counts,
        params,
        returned,
    )


def solution(mesh):
    in_specs = (
        P(None, ("view", "tile")),
        P(("view", "tile"), None),
        P(("view", "tile"), None),
        P(),
        P("view", None, "tile", None),
        P("view", "tile", None, None),
        P("view", "tile", None),
    )
    out_specs = P(None, ("view", "tile"))
    return jax.shard_map(shards, mesh=mesh, in_specs=in_specs, out_specs=out_specs, check_vma=False)
```

```python
import jax
import jax.numpy as jnp
import numpy as np
from jax import lax
from jax.experimental import pallas as pl
from jax.experimental.pallas import tpu as pltpu
from jax.sharding import PartitionSpec as P

TILE = 16


FOCAL = 1000.0
LOW_PASS = 0.3
SSIM_SHARE = 0.2
SMOOTH_EPS = 1e-06
SSIM_ONE = 0.0001
SSIM_TWO = 0.0009
HARMONIC_ZERO = 0.28209479177387814
HARMONIC_ONE = 0.4886025119029199
HARMONIC_TWO = (
    1.0925484305920792,
    -1.0925484305920792,
    0.31539156525252005,
    -1.0925484305920792,
    0.5462742152960396,
)
HARMONIC_THREE = (
    -0.5900435899266435,
    2.890611442640554,
    -0.4570457994644658,
    0.3731763325901154,
    -0.4570457994644658,
    1.445305721320277,
    -0.5900435899266435,
)


def from_behind(block, axis, distance):
    devices = range(lax.axis_size(axis))
    route = [(i - distance, i) for i in devices if i - distance in devices]
    return lax.ppermute(block, axis, route)


def window_taps():
    offsets_np = np.arange(11) - 5.0
    weights = np.exp(-offsets_np * offsets_np / 4.5)
    weights = weights / weights.sum()
    return [float(weight) for weight in weights]


def matrix_product(left_side, right_side):
    return [
        [
            left_side[row_idx][0] * right_side[0][col_idx]
            + left_side[row_idx][1] * right_side[1][col_idx]
            + left_side[row_idx][2] * right_side[2][col_idx]
            for col_idx in range(3)
        ]
        for row_idx in range(3)
    ]


def rotation(angles):
    cos_a, sin_a = (jnp.cos(angles[0]), jnp.sin(angles[0]))
    cos_b, sin_b = (jnp.cos(angles[1]), jnp.sin(angles[1]))
    cos_c, sin_c = (jnp.cos(angles[2]), jnp.sin(angles[2]))
    about_x = [[1.0, 0.0, 0.0], [0.0, cos_a, -sin_a], [0.0, sin_a, cos_a]]
    about_y = [[cos_b, 0.0, sin_b], [0.0, 1.0, 0.0], [-sin_b, 0.0, cos_b]]
    about_z = [[cos_c, -sin_c, 0.0], [sin_c, cos_c, 0.0], [0.0, 0.0, 1.0]]
    return matrix_product(about_z, matrix_product(about_y, about_x))


def harmonics(dir_x, dir_y, dir_z):
    sq_x, sq_y, sq_z = (dir_x * dir_x, dir_y * dir_y, dir_z * dir_z)
    prod_xy, prod_yz, prod_xz = (dir_x * dir_y, dir_y * dir_z, dir_x * dir_z)
    return [
        HARMONIC_ZERO + 0.0 * dir_x,
        -HARMONIC_ONE * dir_y,
        HARMONIC_ONE * dir_z,
        -HARMONIC_ONE * dir_x,
        HARMONIC_TWO[0] * prod_xy,
        HARMONIC_TWO[1] * prod_yz,
        HARMONIC_TWO[2] * (2.0 * sq_z - sq_x - sq_y),
        HARMONIC_TWO[3] * prod_xz,
        HARMONIC_TWO[4] * (sq_x - sq_y),
        HARMONIC_THREE[0] * dir_y * (3.0 * sq_x - sq_y),
        HARMONIC_THREE[1] * prod_xy * dir_z,
        HARMONIC_THREE[2] * dir_y * (4.0 * sq_z - sq_x - sq_y),
        HARMONIC_THREE[3] * dir_z * (2.0 * sq_z - 3.0 * sq_x - 3.0 * sq_y),
        HARMONIC_THREE[4] * dir_x * (4.0 * sq_z - sq_x - sq_y),
        HARMONIC_THREE[5] * dir_z * (sq_x - sq_y),
        HARMONIC_THREE[6] * dir_x * (sq_x - 3.0 * sq_y),
    ]


LANES = 128
SUBS = 8
GROUP = 16
STEP_ROWS = LANES // GROUP
FEATS = 8
PAIR = 2 * FEATS
COEF_ROWS = 32
SLOT = PAIR + 2
PACK = LANES // SLOT
FLAG = PAIR + 1
UNROLL = 8
MOVES = 16
TAPS = 11
DEAD = -1e30
LOG_TOP = float(np.log(0.99))
VMEM_BYTES = 48 * 1024 * 1024


def stepped(total, width, body, state):
    def step(block, held):
        for k in range(width):
            held = body(block * width + k, held)
        return held

    return lax.fori_loop(0, (total + width - 1) // width, step, state)


def packed_rows(cap):
    return -(-cap // (PACK * SUBS)) * SUBS


def pack_slots(read, rows, first_lane):
    lane = lax.broadcasted_iota(jnp.int32, (rows, LANES), 1)
    packed = jnp.zeros((rows, LANES), jnp.float32)
    for q in range(PACK):
        shift = (q * SLOT - first_lane) % LANES
        value = read(q * rows)
        value = pltpu.roll(value, shift, 1) if shift else value
        packed = jnp.where((lane >= q * SLOT) & (lane < (q + 1) * SLOT), value, packed)
    return packed


def unpack_slots(packed, write):
    for q in range(PACK):
        write(q * packed.shape[0], pltpu.roll(packed, LANES - q * SLOT, 1) if q else packed)


def camera_table(camera):
    columns = [camera[:, entry] for entry in range(6)]
    turn = rotation(columns[0:3])
    shift = columns[3:6]
    anchor = [
        -(turn[0][c] * shift[0] + turn[1][c] * shift[1] + turn[2][c] * shift[2]) for c in range(3)
    ]
    flat = [turn[r][c] for r in range(3) for c in range(3)] + shift + anchor
    return jnp.stack(flat + [jnp.zeros_like(shift[0])], axis=1)


def shape_matrix(params):
    scales = [jnp.exp(params[3 + axis_num]) for axis_num in range(3)]
    inv_norm = 1.0 / jnp.sqrt(
        params[6] * params[6]
        + params[7] * params[7]
        + params[8] * params[8]
        + params[9] * params[9]
    )
    quat_w, quat_x, quat_y, quat_z = [params[6 + k] * inv_norm for k in range(4)]
    quat_rot = [
        [
            1.0 - 2.0 * (quat_y * quat_y + quat_z * quat_z),
            2.0 * (quat_x * quat_y - quat_w * quat_z),
            2.0 * (quat_x * quat_z + quat_w * quat_y),
        ],
        [
            2.0 * (quat_x * quat_y + quat_w * quat_z),
            1.0 - 2.0 * (quat_x * quat_x + quat_z * quat_z),
            2.0 * (quat_y * quat_z - quat_w * quat_x),
        ],
        [
            2.0 * (quat_x * quat_z - quat_w * quat_y),
            2.0 * (quat_y * quat_z + quat_w * quat_x),
            1.0 - 2.0 * (quat_x * quat_x + quat_y * quat_y),
        ],
    ]
    return [[quat_rot[r][c] * scales[c] for c in range(3)] for r in range(3)]


def view_features(params, shape, cam, image_width, image_height):
    turn = [[cam[3 * r + c] for c in range(3)] for r in range(3)]
    point = [
        turn[r][0] * params[0] + turn[r][1] * params[1] + turn[r][2] * params[2] + cam[9 + r]
        for r in range(3)
    ]
    inv_depth = 1.0 / point[2]
    ratio_x, ratio_y = point[0] * inv_depth, point[1] * inv_depth
    zoom = FOCAL * inv_depth
    row_x = [zoom * (turn[0][c] - ratio_x * turn[2][c]) for c in range(3)]
    row_y = [zoom * (turn[1][c] - ratio_y * turn[2][c]) for c in range(3)]
    proj_x = [
        row_x[0] * shape[0][c] + row_x[1] * shape[1][c] + row_x[2] * shape[2][c] for c in range(3)
    ]
    proj_y = [
        row_y[0] * shape[0][c] + row_y[1] * shape[1][c] + row_y[2] * shape[2][c] for c in range(3)
    ]
    cov_xx = proj_x[0] * proj_x[0] + proj_x[1] * proj_x[1] + proj_x[2] * proj_x[2] + LOW_PASS
    cov_xy = proj_x[0] * proj_y[0] + proj_x[1] * proj_y[1] + proj_x[2] * proj_y[2]
    cov_yy = proj_y[0] * proj_y[0] + proj_y[1] * proj_y[1] + proj_y[2] * proj_y[2] + LOW_PASS
    inv_det = 1.0 / (cov_xx * cov_yy - cov_xy * cov_xy)
    ray = [params[c] - cam[12 + c] for c in range(3)]
    inv_len = 1.0 / jnp.sqrt(ray[0] * ray[0] + ray[1] * ray[1] + ray[2] * ray[2])
    basis = harmonics(ray[0] * inv_len, ray[1] * inv_len, ray[2] * inv_len)
    colours = []
    for channel in range(3):
        summed = 0.5 + HARMONIC_ZERO * params[11 + 16 * channel]
        for harmonic in range(1, 16):
            summed = summed + basis[harmonic] * params[11 + 16 * channel + harmonic]
        colours.append(summed)
    return [
        FOCAL * ratio_x + image_width / 2.0,
        FOCAL * ratio_y + image_height / 2.0,
        cov_yy * inv_det,
        -cov_xy * inv_det,
        cov_xx * inv_det,
    ] + colours


def log_opacity(logit):
    return LOG_TOP - jnp.log(1.0 + jnp.exp(-logit))


def load_params(params_ref, tile_scr, block):
    count = params_ref.shape[0]
    for band in range(0, count, SUBS):
        high = min(band + SUBS, count)
        for j in range(SUBS):
            lane_at = pl.multiple_of(block * SUBS * LANES + j * LANES, LANES)
            tile_scr[band * SUBS + j * SUBS : band * SUBS + j * SUBS + high - band, :] = params_ref[
                band:high, pl.ds(lane_at, LANES)
            ]
    return [
        tile_scr[pl.ds((r // SUBS) * SUBS * SUBS + r % SUBS, SUBS, stride=SUBS), :]
        for r in range(count)
    ]


def source_kernel(
    sizes, cam_ref, list_ref, counts_ref, params_ref, out_ref, tile_scr, feat_scr, table, slots
):
    groups, rows, cap, image_width, image_height = sizes
    per = params_ref.shape[1]
    views = cam_ref.shape[0]
    height = out_ref.shape[1]
    used = -(-groups * SLOT // SUBS) * SUBS

    def project_block(block, carry):
        params = load_params(params_ref, tile_scr, block)
        shape = shape_matrix(params)
        log_o = log_opacity(params[10])
        for view in range(views):
            cam = [cam_ref[view, k] for k in range(15)]
            for num, value in enumerate(
                view_features(params, shape, cam, image_width, image_height)
            ):
                line = view // 2 * SLOT + view % 2 * FEATS + num
                feat_scr[pl.ds(line, SUBS, stride=used), :] = value
        for group in range(groups):
            feat_scr[pl.ds(group * SLOT + PAIR, SUBS, stride=used), :] = log_o
        for j in range(SUBS):
            row_at = pl.multiple_of(block * SUBS * LANES + j * LANES, LANES)
            table[pl.ds(row_at, LANES), 0:used] = feat_scr[j * used : (j + 1) * used, :].T
        return carry

    lax.fori_loop(0, per // (SUBS * LANES), project_block, 0)

    start = jnp.int32(0)
    for group in range(groups):

        def send_block(t, start_at, group=group):
            dest = group * rows + t
            count = counts_ref[0, dest]

            def move(k, carry):
                spot = jnp.minimum(start_at + k, per - 1)
                slots[pl.ds(k, 1), :] = table[pl.ds(list_ref[0, spot], 1), :]
                return carry

            stepped(count, MOVES, move, 0)
            out_ref[dest] = pack_slots(
                lambda at: slots[at : at + height, :], height, group * SLOT
            )
            return start_at + count

        start = lax.fori_loop(0, rows, send_block, start)


def split_three(value):
    first = value.astype(jnp.bfloat16).astype(jnp.float32)
    rest = value - first
    second = rest.astype(jnp.bfloat16).astype(jnp.float32)
    return [first, second, rest - second]


def swap_grain(cells):
    sub = lax.broadcasted_iota(jnp.int32, (SUBS, LANES), 0)
    lane = lax.broadcasted_iota(jnp.int32, (SUBS, LANES), 1) // TILE
    for bit in (1, 2, 4):
        sub_bit, lane_bit = (sub & bit) != 0, (lane & bit) != 0
        from_high = pltpu.roll(pltpu.roll(cells, SUBS - bit, 0), bit * TILE, 1)
        from_low = pltpu.roll(pltpu.roll(cells, bit, 0), LANES - bit * TILE, 1)
        cells = jnp.where(sub_bit == lane_bit, cells, jnp.where(lane_bit, from_high, from_low))
    return cells


def longest(lens_ref, group):
    most = lens_ref[group * GROUP]
    for t in range(1, GROUP):
        most = jnp.maximum(most, lens_ref[group * GROUP + t])
    return most


def render_kernel(
    sizes,
    row_ref,
    lists_ref,
    lens_ref,
    lens_rows_ref,
    basis_ref,
    arrived_ref,
    image_ref,
    left_ref,
    shape_ref,
    table,
    rows,
    feat_scr,
    pieces,
    mm,
):
    cap, col_groups, list_len = sizes
    devices, height = arrived_ref.shape[0:2]
    blocks = list_len // STEP_ROWS
    table[devices * cap :, :] = jnp.zeros((GROUP, LANES), jnp.float32)

    def unpack(source, carry):
        def write(at, value):
            size = min(height, cap - at)
            if size > 0:
                row_at = pl.multiple_of(source * cap + at, SUBS)
                table[pl.ds(row_at, size), :] = value[0:size]

        unpack_slots(arrived_ref[source], write)
        return carry

    lax.fori_loop(0, devices, unpack, 0)
    centre_y = (row_ref[0] * TILE).astype(jnp.float32) + (TILE - 1) / 2.0
    sub = lax.broadcasted_iota(jnp.int32, (blocks, LANES), 0)
    lane = lax.broadcasted_iota(jnp.int32, (blocks, LANES), 1)
    zero = jnp.zeros((GROUP, LANES), jnp.float32)

    def one_group(group, carry):
        view, col_group = group // col_groups, group % col_groups
        most = longest(lens_ref, group)

        def fetch(n, inner):
            for t in range(GROUP):
                slot = lists_ref[group * GROUP + t, n]
                rows[pl.ds(n * GROUP + t, 1), :] = table[pl.ds(slot, 1), :]
            return inner

        stepped(most, UNROLL, fetch, 0)
        for block in range(blocks):
            feat_scr[block * 24 : (block + 1) * 24, :] = rows[
                block * LANES : (block + 1) * LANES, 0:24
            ].T
        feats = [
            feat_scr[pl.ds(view * FEATS + num, blocks, stride=24), :] for num in range(FEATS)
        ]
        log_o = feat_scr[pl.ds(PAIR, blocks, stride=24), :]
        live = sub * STEP_ROWS + lane // GROUP < lens_rows_ref[pl.ds(group, 1), :]
        centre_x = ((col_group * GROUP + lane % GROUP) * TILE).astype(jnp.float32) + (
            TILE - 1
        ) / 2.0
        off_x, off_y = feats[0] - centre_x, feats[1] - centre_y
        lin_x = feats[2] * off_x + feats[3] * off_y
        lin_y = feats[4] * off_y + feats[3] * off_x
        coefs = [
            log_o - 0.5 * (off_x * lin_x + off_y * lin_y),
            lin_x,
            lin_y,
            -0.5 * feats[2],
            -feats[3],
            -0.5 * feats[4],
        ]
        coefs = [
            jnp.where(live, value, DEAD if num == 0 else 0.0) for num, value in enumerate(coefs)
        ]
        lines = [None] * COEF_ROWS
        for num, value in enumerate(coefs):
            for piece, part in enumerate(split_three(value)):
                lines[piece * 6 + num] = part
        for num in range(3):
            for piece, part in enumerate(split_three(jnp.where(live, feats[5 + num], 0.0))):
                lines[18 + piece * 3 + num] = part
        for num, value in enumerate(lines):
            pieces[pl.ds(num, blocks, stride=COEF_ROWS), :] = (
                jnp.zeros((blocks, LANES), jnp.float32) if value is None else value
            )
        for num, value in enumerate(feats[2:5] + [off_x, off_y]):
            shape_ref[num, pl.ds(pl.multiple_of(group * blocks, blocks), blocks), :] = jnp.where(
                live, value, 0.0
            )
        left_at = pl.multiple_of(group * blocks * LANES, LANES)
        for block in range(blocks):
            left_ref[pl.ds(left_at + block * LANES, LANES), :] = pieces[
                block * COEF_ROWS : (block + 1) * COEF_ROWS, :
            ].T.astype(jnp.bfloat16)
        expand(left_ref, basis_ref, mm, left_at)

        def entry(n, state):
            keep, colour = state
            row_at = pl.multiple_of(n * GROUP, GROUP)
            shade = [
                mm[pl.ds(row_at, GROUP), (2 + c) * LANES : (3 + c) * LANES] for c in range(3)
            ]
            new_keep, new_colour = [], []
            for half in range(2):
                alpha = jnp.exp(mm[pl.ds(row_at, GROUP), half * LANES : (half + 1) * LANES])
                weight = keep[half] * alpha
                new_keep.append(keep[half] * (1.0 - alpha))
                new_colour.append([colour[half][c] + weight * shade[c] for c in range(3)])
            return new_keep, new_colour

        state = ([zero + 1.0] * 2, [[zero] * 3] * 2)
        _, colour = stepped(most, UNROLL, entry, state)
        for side in range(GROUP // SUBS):
            lane_at = pl.multiple_of(col_group * GROUP * TILE + side * LANES, LANES)
            for half in range(2):
                for c in range(3):
                    image_ref[view, c, half * SUBS : (half + 1) * SUBS, pl.ds(lane_at, LANES)] = (
                        swap_grain(colour[half][c][side * SUBS : (side + 1) * SUBS])
                    )
        return carry

    lax.fori_loop(0, 2 * col_groups, one_group, 0)


def expand(left_ref, basis_ref, mm, left_at):
    mm[...] = jnp.dot(
        left_ref[pl.ds(left_at, mm.shape[0]), :],
        basis_ref[...],
        preferred_element_type=jnp.float32,
    )


def back_kernel(
    sizes,
    lists_ref,
    lens_ref,
    basis_ref,
    moment_ref,
    left_ref,
    shape_ref,
    grad_ref,
    out_ref,
    mm,
    alphas,
    weights,
    slopes,
    grad_scr,
    mom_scr,
    row_scr,
    rows,
    table,
):
    cap, col_groups, list_len = sizes
    devices, height = out_ref.shape[0:2]
    blocks = list_len // STEP_ROWS
    table_rows = table.shape[0] // 2
    table[...] = jnp.zeros_like(table)
    grad_scr[...] = jnp.zeros_like(grad_scr)
    zero = jnp.zeros((GROUP, LANES), jnp.float32)
    sub = lax.broadcasted_iota(jnp.int32, (GROUP, LANES), 0)
    lane = lax.broadcasted_iota(jnp.int32, (GROUP, LANES), 1)
    own_tile = lane % GROUP == sub

    def one_group(group, carry):
        view, col_group = group // col_groups, group % col_groups
        most = longest(lens_ref, group)
        lane_at = pl.multiple_of(col_group * GROUP * TILE, LANES)
        grads = [
            [
                jnp.concatenate(
                    [
                        swap_grain(
                            grad_ref[
                                view,
                                c,
                                half * SUBS : (half + 1) * SUBS,
                                pl.ds(lane_at + side * LANES, LANES),
                            ]
                        )
                        for side in range(GROUP // SUBS)
                    ],
                    axis=0,
                )
                for c in range(3)
            ]
            for half in range(2)
        ]
        for half in range(2):
            for c in range(3):
                high = grads[half][c].astype(jnp.bfloat16).astype(jnp.float32)
                for piece, part in enumerate((high, grads[half][c] - high)):
                    line = (piece * 3 + c) * GROUP
                    grad_scr[line : line + GROUP, half * LANES : (half + 1) * LANES] = part
        expand(left_ref, basis_ref, mm, pl.multiple_of(group * blocks * LANES, LANES))

        def ahead(n, keep):
            row_at = pl.multiple_of(n * GROUP, GROUP)
            new_keep = []
            for half in range(2):
                lanes = slice(half * LANES, (half + 1) * LANES)
                alpha = jnp.exp(mm[pl.ds(row_at, GROUP), lanes])
                weight = keep[half] * alpha
                alphas[pl.ds(row_at, GROUP), lanes] = alpha
                weights[pl.ds(row_at, GROUP), lanes] = weight
                new_keep.append(keep[half] * (1.0 - alpha))
            return new_keep

        stepped(most, UNROLL, ahead, [zero + 1.0] * 2)

        last = (most + UNROLL - 1) // UNROLL * UNROLL - 1

        def behind(step, seen):
            row_at = pl.multiple_of((last - step) * GROUP, GROUP)
            shade = [
                mm[pl.ds(row_at, GROUP), (2 + c) * LANES : (3 + c) * LANES] for c in range(3)
            ]
            new_seen = []
            for half in range(2):
                lanes = slice(half * LANES, (half + 1) * LANES)
                own = (
                    grads[half][0] * shade[0]
                    + grads[half][1] * shade[1]
                    + grads[half][2] * shade[2]
                )
                alpha = alphas[pl.ds(row_at, GROUP), lanes]
                slopes[pl.ds(row_at, GROUP), lanes] = weights[pl.ds(row_at, GROUP), lanes] * (
                    own - seen[half]
                )
                new_seen.append(seen[half] * (1.0 - alpha) + alpha * own)
            return new_seen

        stepped(most, UNROLL, behind, [zero] * 2)
        total = jnp.zeros((blocks * LANES, LANES), jnp.float32)
        for value, right in (
            (slopes[...], moment_ref[...]),
            (weights[...], grad_scr[...].T.astype(jnp.bfloat16)),
        ):
            high = value.astype(jnp.bfloat16)
            low = (value - high.astype(jnp.float32)).astype(jnp.bfloat16)
            total = total + jnp.dot(high, right, preferred_element_type=jnp.float32)
            total = total + jnp.dot(low, right, preferred_element_type=jnp.float32)
        for block in range(blocks):
            turned = total[block * LANES : (block + 1) * LANES].T
            mom_scr[block * TILE : block * TILE + 8, :] = turned[6 * GROUP : 6 * GROUP + 8]
            for c in range(3):
                summed = (
                    turned[c * GROUP : (c + 1) * GROUP]
                    + turned[(3 + c) * GROUP : (4 + c) * GROUP]
                )
                mom_scr[block * TILE + 8 + c : block * TILE + 9 + c, :] = jnp.sum(
                    jnp.where(own_tile, summed, 0.0), axis=0, keepdims=True
                )
        mom = [mom_scr[pl.ds(num, blocks, stride=TILE), :] for num in range(11)]
        con_xx, con_xy, con_yy, off_x, off_y = [
            shape_ref[num, pl.ds(pl.multiple_of(group * blocks, blocks), blocks), :]
            for num in range(5)
        ]
        sum_x = off_x * mom[0] - mom[1]
        sum_y = off_y * mom[0] - mom[2]
        results = [
            -(con_xx * sum_x + con_xy * sum_y),
            -(con_yy * sum_y + con_xy * sum_x),
            -0.5 * (off_x * (sum_x - mom[1]) + mom[3]),
            -(off_x * sum_y - off_y * mom[1] + mom[4]),
            -0.5 * (off_y * (sum_y - mom[2]) + mom[5]),
        ] + mom[8:11]
        other = 1 - view
        for num, value in enumerate(results):
            row_scr[pl.ds(view * FEATS + num, blocks, stride=24), :] = value
            row_scr[pl.ds(other * FEATS + num, blocks, stride=24), :] = jnp.zeros_like(value)
        row_scr[pl.ds(PAIR, blocks, stride=24), :] = mom[0]
        row_scr[pl.ds(FLAG, blocks, stride=24), :] = jnp.ones((blocks, LANES), jnp.float32)
        first = pl.multiple_of(group * blocks * LANES, LANES)
        for block in range(blocks):
            rows[pl.ds(first + block * LANES, LANES), 0:24] = row_scr[
                block * 24 : (block + 1) * 24, :
            ].T

        def put(n, inner):
            for t in range(GROUP):
                spot = view * table_rows + lists_ref[group * GROUP + t, n]
                table[pl.ds(spot, 1), :] = rows[pl.ds(first + n * GROUP + t, 1), :]
            return inner

        stepped(most, UNROLL, put, 0)
        return carry

    lax.fori_loop(0, 2 * col_groups, one_group, 0)

    def pack(source, count):
        found = [count]

        def read(at):
            size = min(height, cap - at)
            if size <= 0:
                return jnp.zeros((height, LANES), jnp.float32)
            row_at = pl.multiple_of(source * cap + at, SUBS)
            value = table[pl.ds(row_at, size), :] + table[pl.ds(table_rows + row_at, size), :]
            found[0] = found[0] + value.reshape(size // SUBS, SUBS, LANES).sum(axis=0)
            if size < height:
                value = jnp.concatenate(
                    [value, jnp.zeros((height - size, LANES), jnp.float32)], axis=0
                )
            return value

        out_ref[source] = pack_slots(read, height, 0)
        return found[0]

    none = jnp.zeros((SUBS, LANES), jnp.float32)
    count = lax.fori_loop(0, devices, pack, none)
    stored = jnp.sum(jnp.where(lane[0:SUBS] == FLAG, count, 0.0))
    named = lens_ref[0]
    for tile in range(1, 2 * col_groups * GROUP):
        named = named + lens_ref[tile]

    @pl.when(stored < named.astype(jnp.float32) - 0.5)
    def _():
        table[...] = jnp.zeros_like(table)

        def add_group(group, carry):
            def add(n, inner):
                for t in range(GROUP):
                    spot = lists_ref[group * GROUP + t, n]
                    row_at = group * blocks * LANES + n * GROUP + t
                    table[pl.ds(spot, 1), :] = table[pl.ds(spot, 1), :] + rows[pl.ds(row_at, 1), :]
                return inner

            return lax.fori_loop(0, longest(lens_ref, group), add, carry)

        lax.fori_loop(0, 2 * col_groups, add_group, 0)
        lax.fori_loop(0, devices, pack, none)


def owner_kernel(
    sizes,
    cam_ref,
    list_ref,
    counts_ref,
    params_ref,
    back_ref,
    out_ref,
    tile_scr,
    feat_scr,
    table,
    slots,
):
    groups, rows, cap, image_width, image_height = sizes
    count_params, per = params_ref.shape
    height = back_ref.shape[1]
    table[...] = jnp.zeros_like(table)
    lane = lax.broadcasted_iota(jnp.int32, (height, LANES), 1)
    start = jnp.int32(0)
    for group in range(groups):

        def take_block(t, start_at, group=group):
            dest = group * rows + t
            count = counts_ref[0, dest]

            def write(at, value):
                slots[at : at + height, :] = jnp.where(lane == PAIR + 1, 1.0 + group, value)

            unpack_slots(back_ref[dest], write)

            def move(k, carry):
                spot = list_ref[0, start_at + k]
                table[pl.ds(spot, 1), :] = slots[pl.ds(k, 1), :]
                return carry

            rounded = (count + MOVES - 1) // MOVES * MOVES
            whole = jnp.where(start_at + rounded <= per, rounded, count // MOVES * MOVES)
            stepped(whole, MOVES, move, 0)
            lax.fori_loop(whole, count, move, 0)
            return start_at + count

        start = lax.fori_loop(0, rows, take_block, start)

    def clear(k, carry):
        table[pl.ds(list_ref[0, k], 1), :] = jnp.zeros((1, LANES), jnp.float32)
        return carry

    lax.fori_loop(start, jnp.minimum(start + MOVES, per), clear, 0)

    def pull_block(block, carry):
        params = load_params(params_ref, tile_scr, block)
        for j in range(SUBS):
            row_at = pl.multiple_of(block * SUBS * LANES + j * LANES, LANES)
            feat_scr[j * 24 : (j + 1) * 24, :] = table[pl.ds(row_at, LANES), 0:24].T
        cots = [feat_scr[pl.ds(num, SUBS, stride=24), :] for num in range(PAIR + 2)]
        home = cots[PAIR + 1]
        sent = home > 0.5
        cams = []
        for view in range(2):
            cam = []
            for k in range(15):
                value = jnp.full((SUBS, LANES), cam_ref[view, k], jnp.float32)
                for group in range(1, groups):
                    value = jnp.where(home > 0.5 + group, cam_ref[2 * group + view, k], value)
                cam.append(value)
            cams.append(cam)

        def both(*values):
            shape = shape_matrix(values)
            return (
                view_features(values, shape, cams[0], image_width, image_height)
                + view_features(values, shape, cams[1], image_width, image_height)
                + [log_opacity(values[10])]
            )

        _, pull = jax.vjp(both, *params)
        grads = pull(cots[0 : PAIR + 1])
        for num, value in enumerate(grads):
            tile_scr[pl.ds((num // SUBS) * SUBS * SUBS + num % SUBS, SUBS, stride=SUBS), :] = (
                jnp.where(sent, value, 0.0)
            )
        for band in range(0, count_params, SUBS):
            high = min(band + SUBS, count_params)
            for j in range(SUBS):
                lane_at = pl.multiple_of(block * SUBS * LANES + j * LANES, LANES)
                out_ref[band:high, pl.ds(lane_at, LANES)] = tile_scr[
                    band * SUBS + j * SUBS : band * SUBS + j * SUBS + high - band, :
                ]
        return carry

    lax.fori_loop(0, per // (SUBS * LANES), pull_block, 0)


def tap_rows(read, first, count):
    taps = window_taps()
    total = taps[5] * read(first + 5, count)
    for k in range(5):
        total = total + taps[k] * (read(first + k, count) + read(first + TAPS - 1 - k, count))
    return total


def blur_lanes(value, band):
    return jnp.dot(
        value, band, precision=lax.Precision.HIGHEST, preferred_element_type=jnp.float32
    )


def truth_kernel(band_ref, above_ref, own_ref, below_ref, out_ref, tall, mixed):
    images = own_ref.shape[0]

    def one_image(m, carry):
        whole = jnp.concatenate([above_ref[m], own_ref[m], below_ref[m]], axis=0)
        for field, value in enumerate((whole, whole * whole)):
            tall[...] = value
            row_at = pl.multiple_of((field * images + m) * 2 * TILE, 2 * TILE)
            mixed[pl.ds(row_at, 2 * TILE), :] = tap_rows(
                lambda at, count: tall[at : at + count, :], 6, 2 * TILE
            )
        return carry

    lax.fori_loop(0, images, one_image, 0)
    out_ref[...] = blur_lanes(mixed[...], band_ref[...])


def loss_kernel(
    image_rows,
    row_ref,
    band_ref,
    truth_ref,
    true_above,
    true_own,
    true_below,
    above_ref,
    own_ref,
    below_ref,
    out_ref,
    tall,
    mixed,
    blurred,
    slim,
):
    images = own_ref.shape[0]
    tall_rows = 2 * TILE
    width = own_ref.shape[2]

    def one_image(m, carry):
        whole = jnp.concatenate([above_ref[m], own_ref[m], below_ref[m]], axis=0)
        true = jnp.concatenate([true_above[m], true_own[m], true_below[m]], axis=0)
        for field, value in enumerate((whole, whole * whole, whole * true)):
            tall[field] = value
            row_at = pl.multiple_of((field * images + m) * tall_rows, tall_rows)
            mixed[pl.ds(row_at, tall_rows), :] = tap_rows(
                lambda at, count, field=field: tall[field, at : at + count, :], 6, tall_rows
            )
        return carry

    lax.fori_loop(0, images, one_image, 0)
    blurred[...] = blur_lanes(mixed[...], band_ref[...])
    sub = lax.broadcasted_iota(jnp.int32, (tall_rows, width), 0)
    image_row = row_ref[0] * TILE + sub - 5
    inside = (image_row >= 0) & (image_row < image_rows) & (sub < TILE + 10)

    def one_map(m, carry):
        def field_of(ref, field):
            row_at = pl.multiple_of((field * images + m) * tall_rows, tall_rows)
            return ref[pl.ds(row_at, tall_rows), :]

        mean_one, both_one, cross = [field_of(blurred, field) for field in range(3)]
        mean_two, both_two = field_of(truth_ref, 0), field_of(truth_ref, 1)
        square_one, square_two = mean_one * mean_one, mean_two * mean_two
        mean_cross = mean_one * mean_two
        top_one = 2.0 * mean_cross + SSIM_ONE
        top_two = 2.0 * (cross - mean_cross) + SSIM_TWO
        low_one = square_one + square_two + SSIM_ONE
        low_two = (both_one - square_one) + (both_two - square_two) + SSIM_TWO
        inv_one, inv_two = 1.0 / low_one, 1.0 / low_two
        inv_both = inv_one * inv_two
        value = top_one * top_two * inv_both
        grads = [
            2.0 * mean_two * (top_two - top_one) * inv_both
            - 2.0 * mean_one * value * (inv_one - inv_two),
            -value * inv_two,
            2.0 * top_one * inv_both,
        ]
        for field, grad in enumerate(grads):
            tall[field, 0:tall_rows] = jnp.where(inside, grad, 0.0)
            row_at = pl.multiple_of((field * images + m) * TILE, TILE)
            slim[pl.ds(row_at, TILE), :] = tap_rows(
                lambda at, count, field=field: tall[field, at : at + count, :], 0, TILE
            )
        return carry

    lax.fori_loop(0, images, one_map, 0)
    spread = blur_lanes(slim[...], band_ref[...]).reshape(3, images, TILE, width)
    own, true = own_ref[...], true_own[...]
    gap = own - true
    out_ref[...] = (1.0 - SSIM_SHARE) * gap / jnp.sqrt(gap * gap + SMOOTH_EPS) - SSIM_SHARE * (
        spread[0] + 2.0 * own * spread[1] + true * spread[2]
    )


def band_matrix(width):
    taps = window_taps()
    band = np.zeros((width, width), np.float32)
    for k in range(TAPS):
        band += np.diag(np.full(width - abs(k - 5), taps[k], np.float32), k - 5)
    return jnp.asarray(band)


def pixel_basis():
    pixel = np.arange(TILE * TILE)
    x = (pixel % TILE) - (TILE - 1) / 2.0
    y = (pixel // TILE) - (TILE - 1) / 2.0
    return np.stack([np.ones_like(x), x, y, x * x, x * y, y * y])


def expand_matrix():
    terms = pixel_basis()
    matrix = np.zeros((COEF_ROWS, 5 * LANES), np.float32)
    for piece in range(3):
        matrix[piece * 6 : piece * 6 + 6, 0 : 2 * LANES] = terms
        for c in range(3):
            matrix[18 + piece * 3 + c, (2 + c) * LANES : (3 + c) * LANES] = 1.0
    return jnp.asarray(matrix, jnp.bfloat16)


def moment_matrix():
    matrix = np.zeros((2 * LANES, LANES), np.float32)
    matrix[:, 6 * GROUP : 6 * GROUP + 6] = pixel_basis().T
    return jnp.asarray(matrix, jnp.bfloat16)


def smem():
    return pl.BlockSpec(memory_space=pltpu.SMEM)


def vmem():
    return pl.BlockSpec(memory_space=pltpu.VMEM)


def scratch(*shape):
    return pltpu.VMEM(shape, jnp.float32)


def run(kernel, out_shapes, in_specs, scratches, *operands):
    return pl.pallas_call(
        kernel,
        out_shape=out_shapes,
        in_specs=in_specs,
        out_specs=jax.tree.map(lambda _: vmem(), out_shapes),
        scratch_shapes=scratches,
        compiler_params=pltpu.CompilerParams(vmem_limit_bytes=VMEM_BYTES),
    )(*operands)


def shards(params, send_list, send_counts, camera, ground_truth, tile_lists, list_lengths):
    devices = lax.axis_size(("view", "tile"))
    row_devices = lax.axis_size("tile")
    groups = lax.axis_size("view")
    count_params, per_device = params.shape
    capacity = per_device // devices
    tile_cols, list_len = tile_lists.shape[2:]
    col_groups = tile_cols // GROUP
    blocks = list_len // STEP_ROWS
    tile_row = lax.axis_index("tile")
    image_width = float(ground_truth.shape[3])
    image_height = float(ground_truth.shape[2] * row_devices)
    table_rows = per_device + GROUP
    slot_rows = packed_rows(capacity)
    sent_shape = jax.ShapeDtypeStruct((devices, slot_rows, LANES), jnp.float32)
    cams = camera_table(camera)

    flat_lengths = list_lengths.reshape(-1)
    entry_rank = jnp.arange(list_len, dtype=jnp.int32)
    tile_num = jnp.arange(2 * tile_cols, dtype=jnp.int32)
    lists = jnp.where(
        entry_rank[None, :] < flat_lengths[:, None],
        tile_lists.reshape(2 * tile_cols, list_len),
        per_device + tile_num[:, None] % GROUP,
    )
    lens_rows = jnp.tile(flat_lengths.reshape(-1, GROUP), (1, LANES // GROUP))

    width = ground_truth.shape[3]
    true_own = ground_truth.reshape(-1, TILE, width)
    true_above = from_behind(true_own, "tile", 1)
    true_below = from_behind(true_own, "tile", -1)
    band = band_matrix(width)
    truth_rows = 2 * true_own.shape[0] * 2 * TILE
    truth_blur = run(
        truth_kernel,
        jax.ShapeDtypeStruct((truth_rows, width), jnp.float32),
        [vmem()] * 4,
        [scratch(3 * TILE, width), scratch(truth_rows, width)],
        band,
        true_above,
        true_own,
        true_below,
    )

    own_sizes = (groups, row_devices, capacity, image_width, image_height)
    sent = run(
        lambda *refs: source_kernel(own_sizes, *refs),
        sent_shape,
        [smem(), smem(), smem(), vmem()],
        [
            scratch(SUBS * SUBS * SUBS, LANES),
            scratch(SUBS * LANES, LANES),
            scratch(per_device, LANES),
            scratch(PACK * slot_rows, LANES),
        ],
        cams,
        send_list,
        send_counts,
        params,
    )
    arrived = lax.all_to_all(sent, ("view", "tile"), split_axis=0, concat_axis=0, tiled=True)

    tile_sizes = (capacity, col_groups, list_len)
    entries = 2 * tile_cols * list_len
    rendered, left, shapes = run(
        lambda *refs: render_kernel(tile_sizes, *refs),
        (
            jax.ShapeDtypeStruct(ground_truth.shape, jnp.float32),
            jax.ShapeDtypeStruct((entries, COEF_ROWS), jnp.bfloat16),
            jax.ShapeDtypeStruct((5, entries // LANES, LANES), jnp.float32),
        ),
        [smem(), smem(), smem(), vmem(), vmem(), vmem()],
        [
            scratch(table_rows, LANES),
            scratch(blocks * LANES, LANES),
            scratch(blocks * 24, LANES),
            scratch(blocks * COEF_ROWS, LANES),
            scratch(blocks * LANES, 5 * LANES),
        ],
        tile_row.reshape(1),
        lists,
        flat_lengths,
        lens_rows,
        expand_matrix(),
        arrived,
    )

    images = rendered.reshape(true_own.shape)
    count = images.shape[0]
    grad_image = run(
        lambda *refs: loss_kernel(TILE * row_devices, *refs),
        jax.ShapeDtypeStruct(images.shape, jnp.float32),
        [smem()] + [vmem()] * 8,
        [
            scratch(3, 3 * TILE, width),
            scratch(3 * count * 2 * TILE, width),
            scratch(3 * count * 2 * TILE, width),
            scratch(3 * count * TILE, width),
        ],
        tile_row.reshape(1),
        band,
        truth_blur,
        true_above,
        true_own,
        true_below,
        from_behind(images, "tile", 1),
        images,
        from_behind(images, "tile", -1),
    ).reshape(ground_truth.shape)

    grad_slots = run(
        lambda *refs: back_kernel(tile_sizes, *refs),
        sent_shape,
        [smem(), smem()] + [vmem()] * 5,
        [
            scratch(blocks * LANES, 5 * LANES),
            scratch(blocks * LANES, 2 * LANES),
            scratch(blocks * LANES, 2 * LANES),
            scratch(blocks * LANES, 2 * LANES),
            scratch(LANES, 2 * LANES),
            scratch(blocks * TILE, LANES),
            scratch(blocks * 24, LANES),
            scratch(entries, LANES),
            scratch(2 * table_rows, LANES),
        ],
        lists,
        flat_lengths,
        expand_matrix(),
        moment_matrix(),
        left,
        shapes,
        grad_image,
    )
    returned = lax.all_to_all(
        grad_slots, ("view", "tile"), split_axis=0, concat_axis=0, tiled=True
    )
    return run(
        lambda *refs: owner_kernel(own_sizes, *refs),
        jax.ShapeDtypeStruct(params.shape, jnp.float32),
        [smem(), smem(), smem(), vmem(), vmem()],
        [
            scratch(SUBS * SUBS * SUBS, LANES),
            scratch(SUBS * 24, LANES),
            scratch(per_device, LANES),
            scratch(PACK * slot_rows, LANES),
        ],
        cams,
        send_list,
        send_counts,
        params,
        returned,
    )


def solution(mesh):
    in_specs = (
        P(None, ("view", "tile")),
        P(("view", "tile"), None),
        P(("view", "tile"), None),
        P(),
        P("view", None, "tile", None),
        P("view", "tile", None, None),
        P("view", "tile", None),
    )
    out_specs = P(None, ("view", "tile"))
    return jax.shard_map(shards, mesh=mesh, in_specs=in_specs, out_specs=out_specs, check_vma=False)
```

```python
import jax
import jax.numpy as jnp
import numpy as np
from jax import lax
from jax.experimental import pallas as pl
from jax.experimental.pallas import tpu as pltpu
from jax.sharding import PartitionSpec as P

TILE = 16


FOCAL = 1000.0
LOW_PASS = 0.3
SSIM_SHARE = 0.2
SMOOTH_EPS = 1e-06
SSIM_ONE = 0.0001
SSIM_TWO = 0.0009
HARMONIC_ZERO = 0.28209479177387814
HARMONIC_ONE = 0.4886025119029199
HARMONIC_TWO = (
    1.0925484305920792,
    -1.0925484305920792,
    0.31539156525252005,
    -1.0925484305920792,
    0.5462742152960396,
)
HARMONIC_THREE = (
    -0.5900435899266435,
    2.890611442640554,
    -0.4570457994644658,
    0.3731763325901154,
    -0.4570457994644658,
    1.445305721320277,
    -0.5900435899266435,
)


def from_behind(block, axis, distance):
    devices = range(lax.axis_size(axis))
    route = [(i - distance, i) for i in devices if i - distance in devices]
    return lax.ppermute(block, axis, route)


def window_taps():
    offsets_np = np.arange(11) - 5.0
    weights = np.exp(-offsets_np * offsets_np / 4.5)
    weights = weights / weights.sum()
    return [float(weight) for weight in weights]


def matrix_product(left_side, right_side):
    return [
        [
            left_side[row_idx][0] * right_side[0][col_idx]
            + left_side[row_idx][1] * right_side[1][col_idx]
            + left_side[row_idx][2] * right_side[2][col_idx]
            for col_idx in range(3)
        ]
        for row_idx in range(3)
    ]


def rotation(angles):
    cos_a, sin_a = (jnp.cos(angles[0]), jnp.sin(angles[0]))
    cos_b, sin_b = (jnp.cos(angles[1]), jnp.sin(angles[1]))
    cos_c, sin_c = (jnp.cos(angles[2]), jnp.sin(angles[2]))
    about_x = [[1.0, 0.0, 0.0], [0.0, cos_a, -sin_a], [0.0, sin_a, cos_a]]
    about_y = [[cos_b, 0.0, sin_b], [0.0, 1.0, 0.0], [-sin_b, 0.0, cos_b]]
    about_z = [[cos_c, -sin_c, 0.0], [sin_c, cos_c, 0.0], [0.0, 0.0, 1.0]]
    return matrix_product(about_z, matrix_product(about_y, about_x))


def harmonics(dir_x, dir_y, dir_z):
    sq_x, sq_y, sq_z = (dir_x * dir_x, dir_y * dir_y, dir_z * dir_z)
    prod_xy, prod_yz, prod_xz = (dir_x * dir_y, dir_y * dir_z, dir_x * dir_z)
    return [
        HARMONIC_ZERO + 0.0 * dir_x,
        -HARMONIC_ONE * dir_y,
        HARMONIC_ONE * dir_z,
        -HARMONIC_ONE * dir_x,
        HARMONIC_TWO[0] * prod_xy,
        HARMONIC_TWO[1] * prod_yz,
        HARMONIC_TWO[2] * (2.0 * sq_z - sq_x - sq_y),
        HARMONIC_TWO[3] * prod_xz,
        HARMONIC_TWO[4] * (sq_x - sq_y),
        HARMONIC_THREE[0] * dir_y * (3.0 * sq_x - sq_y),
        HARMONIC_THREE[1] * prod_xy * dir_z,
        HARMONIC_THREE[2] * dir_y * (4.0 * sq_z - sq_x - sq_y),
        HARMONIC_THREE[3] * dir_z * (2.0 * sq_z - 3.0 * sq_x - 3.0 * sq_y),
        HARMONIC_THREE[4] * dir_x * (4.0 * sq_z - sq_x - sq_y),
        HARMONIC_THREE[5] * dir_z * (sq_x - sq_y),
        HARMONIC_THREE[6] * dir_x * (sq_x - 3.0 * sq_y),
    ]


LANES = 128
SUBS = 8
GROUP = 16
STEP_ROWS = LANES // GROUP
FEATS = 8
PAIR = 2 * FEATS
COEF_ROWS = 32
FLAG = PAIR + 1
UNROLL = 8
MOVES = 16
TAPS = 11
DEAD = -1e30
LOG_TOP = float(np.log(0.99))
VMEM_BYTES = 48 * 1024 * 1024


def stepped(total, width, body, state):
    def step(block, held):
        for k in range(width):
            held = body(block * width + k, held)
        return held

    return lax.fori_loop(0, (total + width - 1) // width, step, state)


def lane_spread(index):
    return index // LANES, index % LANES


def take_blocks(read, count, block, place):
    result = jnp.zeros(place.shape, jnp.float32)
    for num in range(count):
        taken = jnp.take_along_axis(read(num), place, axis=1, mode="promise_in_bounds")
        result = jnp.where(block == num, taken, result)
    return result


def take_line(read, count, block, place):
    sub = lax.broadcasted_iota(jnp.int32, (SUBS, LANES), 0)
    result = take_blocks(read, -(-count // SUBS), block // SUBS, place)
    return jnp.sum(jnp.where(sub == block % SUBS, result, 0.0), axis=0, keepdims=True)


def camera_table(camera):
    columns = [camera[:, entry] for entry in range(6)]
    turn = rotation(columns[0:3])
    shift = columns[3:6]
    anchor = [
        -(turn[0][c] * shift[0] + turn[1][c] * shift[1] + turn[2][c] * shift[2]) for c in range(3)
    ]
    flat = [turn[r][c] for r in range(3) for c in range(3)] + shift + anchor
    return jnp.stack(flat + [jnp.zeros_like(shift[0])], axis=1)


def shape_matrix(params):
    scales = [jnp.exp(params[3 + axis_num]) for axis_num in range(3)]
    inv_norm = 1.0 / jnp.sqrt(
        params[6] * params[6]
        + params[7] * params[7]
        + params[8] * params[8]
        + params[9] * params[9]
    )
    quat_w, quat_x, quat_y, quat_z = [params[6 + k] * inv_norm for k in range(4)]
    quat_rot = [
        [
            1.0 - 2.0 * (quat_y * quat_y + quat_z * quat_z),
            2.0 * (quat_x * quat_y - quat_w * quat_z),
            2.0 * (quat_x * quat_z + quat_w * quat_y),
        ],
        [
            2.0 * (quat_x * quat_y + quat_w * quat_z),
            1.0 - 2.0 * (quat_x * quat_x + quat_z * quat_z),
            2.0 * (quat_y * quat_z - quat_w * quat_x),
        ],
        [
            2.0 * (quat_x * quat_z - quat_w * quat_y),
            2.0 * (quat_y * quat_z + quat_w * quat_x),
            1.0 - 2.0 * (quat_x * quat_x + quat_y * quat_y),
        ],
    ]
    return [[quat_rot[r][c] * scales[c] for c in range(3)] for r in range(3)]


def view_features(params, shape, cam, image_width, image_height):
    turn = [[cam[3 * r + c] for c in range(3)] for r in range(3)]
    point = [
        turn[r][0] * params[0] + turn[r][1] * params[1] + turn[r][2] * params[2] + cam[9 + r]
        for r in range(3)
    ]
    inv_depth = 1.0 / point[2]
    ratio_x, ratio_y = point[0] * inv_depth, point[1] * inv_depth
    zoom = FOCAL * inv_depth
    row_x = [zoom * (turn[0][c] - ratio_x * turn[2][c]) for c in range(3)]
    row_y = [zoom * (turn[1][c] - ratio_y * turn[2][c]) for c in range(3)]
    proj_x = [
        row_x[0] * shape[0][c] + row_x[1] * shape[1][c] + row_x[2] * shape[2][c] for c in range(3)
    ]
    proj_y = [
        row_y[0] * shape[0][c] + row_y[1] * shape[1][c] + row_y[2] * shape[2][c] for c in range(3)
    ]
    cov_xx = proj_x[0] * proj_x[0] + proj_x[1] * proj_x[1] + proj_x[2] * proj_x[2] + LOW_PASS
    cov_xy = proj_x[0] * proj_y[0] + proj_x[1] * proj_y[1] + proj_x[2] * proj_y[2]
    cov_yy = proj_y[0] * proj_y[0] + proj_y[1] * proj_y[1] + proj_y[2] * proj_y[2] + LOW_PASS
    inv_det = 1.0 / (cov_xx * cov_yy - cov_xy * cov_xy)
    ray = [params[c] - cam[12 + c] for c in range(3)]
    inv_len = 1.0 / jnp.sqrt(ray[0] * ray[0] + ray[1] * ray[1] + ray[2] * ray[2])
    basis = harmonics(ray[0] * inv_len, ray[1] * inv_len, ray[2] * inv_len)
    colours = []
    for channel in range(3):
        summed = 0.5 + HARMONIC_ZERO * params[11 + 16 * channel]
        for harmonic in range(1, 16):
            summed = summed + basis[harmonic] * params[11 + 16 * channel + harmonic]
        colours.append(summed)
    return [
        FOCAL * ratio_x + image_width / 2.0,
        FOCAL * ratio_y + image_height / 2.0,
        cov_yy * inv_det,
        -cov_xy * inv_det,
        cov_xx * inv_det,
    ] + colours


def log_opacity(logit):
    return LOG_TOP - jnp.log(1.0 + jnp.exp(-logit))


def load_params(params_ref, tile_scr, block):
    count = params_ref.shape[0]
    for band in range(0, count, SUBS):
        high = min(band + SUBS, count)
        for j in range(SUBS):
            lane_at = pl.multiple_of(block * SUBS * LANES + j * LANES, LANES)
            tile_scr[band * SUBS + j * SUBS : band * SUBS + j * SUBS + high - band, :] = params_ref[
                band:high, pl.ds(lane_at, LANES)
            ]
    return [
        tile_scr[pl.ds((r // SUBS) * SUBS * SUBS + r % SUBS, SUBS, stride=SUBS), :]
        for r in range(count)
    ]


def source_kernel(
    sizes, cam_ref, counts_ref, list_ref, params_ref, out_ref, tile_scr, table, logs
):
    groups, rows, cap, lane_len, image_width, image_height = sizes
    per = params_ref.shape[1]
    views = cam_ref.shape[0]
    parts = cap // lane_len
    used = views * FEATS
    count_blocks = per // LANES

    def project_block(block, carry):
        params = load_params(params_ref, tile_scr, block)
        shape = shape_matrix(params)
        at = block * SUBS * used
        for view in range(views):
            cam = [cam_ref[view, k] for k in range(15)]
            for num, value in enumerate(
                view_features(params, shape, cam, image_width, image_height)
            ):
                table[pl.ds(at + view * FEATS + num, SUBS, stride=used), :] = value
        logs[pl.ds(pl.multiple_of(block * SUBS, SUBS), SUBS), :] = log_opacity(params[10])
        return carry

    lax.fori_loop(0, per // (SUBS * LANES), project_block, 0)
    lane = lax.broadcasted_iota(jnp.int32, (SUBS, LANES), 1)

    def send_block(dest, start_at):
        count = counts_ref[0, dest]
        line = pl.multiple_of(dest // rows * PAIR, SUBS)
        for part in range(parts):

            @pl.when(count > part * lane_len)
            def _(part=part):
                first = start_at + part * lane_len
                block, turn = first // LANES, first % LANES
                pieces = []
                for step in range(2):
                    at = jnp.minimum(block + step, count_blocks - 1) * LANES
                    names = list_ref[0:1, pl.ds(pl.multiple_of(at, LANES), LANES)]
                    pieces.append(
                        pltpu.roll(jnp.broadcast_to(names, (SUBS, LANES)), LANES - turn, 1)
                    )
                index = jnp.where(lane < LANES - turn, pieces[0], pieces[1])
                home, place = lane_spread(index)
                twice = [jnp.concatenate([value, value], axis=0) for value in (home, place)]
                taken = take_blocks(
                    lambda num: table[pl.ds(num * used + line, PAIR), :], count_blocks, *twice
                )
                log_o = take_line(
                    lambda num: logs[num * SUBS : (num + 1) * SUBS, :], count_blocks, home, place
                )
                out_ref[dest, part * PAIR : (part + 1) * PAIR, :] = taken[:, 0:lane_len]
                out_ref[dest, parts * PAIR + part : parts * PAIR + part + 1, :] = log_o[
                    :, 0:lane_len
                ]

        return start_at + count

    lax.fori_loop(0, groups * rows, send_block, jnp.int32(0))


def split_three(value):
    first = value.astype(jnp.bfloat16).astype(jnp.float32)
    rest = value - first
    second = rest.astype(jnp.bfloat16).astype(jnp.float32)
    return [first, second, rest - second]


def swap_grain(cells):
    sub = lax.broadcasted_iota(jnp.int32, (SUBS, LANES), 0)
    lane = lax.broadcasted_iota(jnp.int32, (SUBS, LANES), 1) // TILE
    for bit in (1, 2, 4):
        sub_bit, lane_bit = (sub & bit) != 0, (lane & bit) != 0
        from_high = pltpu.roll(pltpu.roll(cells, SUBS - bit, 0), bit * TILE, 1)
        from_low = pltpu.roll(pltpu.roll(cells, bit, 0), LANES - bit * TILE, 1)
        cells = jnp.where(sub_bit == lane_bit, cells, jnp.where(lane_bit, from_high, from_low))
    return cells


def longest(lens_ref, group):
    most = lens_ref[group * GROUP]
    for t in range(1, GROUP):
        most = jnp.maximum(most, lens_ref[group * GROUP + t])
    return most


def render_kernel(
    sizes,
    row_ref,
    lens_ref,
    lens_rows_ref,
    names_ref,
    basis_ref,
    arrived_ref,
    image_ref,
    left_ref,
    shape_ref,
    table,
    logs,
    feat_scr,
    pieces,
    mm,
):
    cap, lane_len, col_groups, list_len = sizes
    devices = arrived_ref.shape[0]
    blocks = list_len // STEP_ROWS
    count_blocks = devices * cap // LANES
    parts = cap // lane_len
    joined = LANES // lane_len

    def unpack(block, carry):
        for k in range(joined):
            source = block * joined // parts + k
            part = block * joined % parts
            lanes = slice(k * lane_len, (k + 1) * lane_len)
            at = pl.multiple_of(part * PAIR, PAIR)
            for view in range(2):
                row_at = pl.multiple_of((view * count_blocks + block) * FEATS, FEATS)
                table[pl.ds(row_at, FEATS), lanes] = arrived_ref[
                    source, pl.ds(at + view * FEATS, FEATS), :
                ]
            logs[pl.ds(block, 1), lanes] = arrived_ref[source, pl.ds(parts * PAIR + part, 1), :]
        return carry

    lax.fori_loop(0, count_blocks, unpack, 0)
    centre_y = (row_ref[0] * TILE).astype(jnp.float32) + (TILE - 1) / 2.0
    sub = lax.broadcasted_iota(jnp.int32, (blocks, LANES), 0)
    lane = lax.broadcasted_iota(jnp.int32, (blocks, LANES), 1)
    zero = jnp.zeros((GROUP, LANES), jnp.float32)

    def one_group(group, carry):
        view, col_group = group // col_groups, group % col_groups
        most = longest(lens_ref, group)

        def fetch(block, inner):
            names = names_ref[pl.ds(group * blocks + block, 1), :]
            home, place = lane_spread(jnp.broadcast_to(names, (SUBS, LANES)))
            feat_at = pl.multiple_of(block * PAIR, PAIR)
            feat_scr[pl.ds(feat_at, FEATS), :] = take_blocks(
                lambda num: table[
                    pl.ds(pl.multiple_of((view * count_blocks + num) * FEATS, FEATS), FEATS), :
                ],
                count_blocks,
                home,
                place,
            )
            feat_scr[pl.ds(feat_at + FEATS, 1), :] = take_line(
                lambda num: logs[num * SUBS : (num + 1) * SUBS, :], count_blocks, home, place
            )
            return inner

        stepped((most + STEP_ROWS - 1) // STEP_ROWS, 2, fetch, 0)
        feats = [feat_scr[pl.ds(num, blocks, stride=PAIR), :] for num in range(FEATS)]
        log_o = feat_scr[pl.ds(FEATS, blocks, stride=PAIR), :]
        live = sub * STEP_ROWS + lane // GROUP < lens_rows_ref[pl.ds(group, 1), :]
        centre_x = ((col_group * GROUP + lane % GROUP) * TILE).astype(jnp.float32) + (
            TILE - 1
        ) / 2.0
        off_x, off_y = feats[0] - centre_x, feats[1] - centre_y
        lin_x = feats[2] * off_x + feats[3] * off_y
        lin_y = feats[4] * off_y + feats[3] * off_x
        coefs = [
            log_o - 0.5 * (off_x * lin_x + off_y * lin_y),
            lin_x,
            lin_y,
            -0.5 * feats[2],
            -feats[3],
            -0.5 * feats[4],
        ]
        coefs = [
            jnp.where(live, value, DEAD if num == 0 else 0.0) for num, value in enumerate(coefs)
        ]
        lines = [None] * COEF_ROWS
        for num, value in enumerate(coefs):
            for piece, part in enumerate(split_three(value)):
                lines[piece * 6 + num] = part
        for num in range(3):
            for piece, part in enumerate(split_three(jnp.where(live, feats[5 + num], 0.0))):
                lines[18 + piece * 3 + num] = part
        for num, value in enumerate(lines):
            pieces[pl.ds(num, blocks, stride=COEF_ROWS), :] = (
                jnp.zeros((blocks, LANES), jnp.float32) if value is None else value
            )
        for num, value in enumerate(feats[2:5] + [off_x, off_y]):
            shape_ref[num, pl.ds(pl.multiple_of(group * blocks, blocks), blocks), :] = jnp.where(
                live, value, 0.0
            )
        left_at = pl.multiple_of(group * blocks * LANES, LANES)
        for block in range(blocks):
            left_ref[pl.ds(left_at + block * LANES, LANES), :] = pieces[
                block * COEF_ROWS : (block + 1) * COEF_ROWS, :
            ].T.astype(jnp.bfloat16)
        expand(left_ref, basis_ref, mm, left_at)

        def entry(n, state):
            keep, colour = state
            row_at = pl.multiple_of(n * GROUP, GROUP)
            shade = [
                mm[pl.ds(row_at, GROUP), (2 + c) * LANES : (3 + c) * LANES] for c in range(3)
            ]
            new_keep, new_colour = [], []
            for half in range(2):
                alpha = jnp.exp(mm[pl.ds(row_at, GROUP), half * LANES : (half + 1) * LANES])
                weight = keep[half] * alpha
                new_keep.append(keep[half] * (1.0 - alpha))
                new_colour.append([colour[half][c] + weight * shade[c] for c in range(3)])
            return new_keep, new_colour

        state = ([zero + 1.0] * 2, [[zero] * 3] * 2)
        _, colour = stepped(most, UNROLL, entry, state)
        for side in range(GROUP // SUBS):
            lane_at = pl.multiple_of(col_group * GROUP * TILE + side * LANES, LANES)
            for half in range(2):
                for c in range(3):
                    image_ref[view, c, half * SUBS : (half + 1) * SUBS, pl.ds(lane_at, LANES)] = (
                        swap_grain(colour[half][c][side * SUBS : (side + 1) * SUBS])
                    )
        return carry

    lax.fori_loop(0, 2 * col_groups, one_group, 0)


def expand(left_ref, basis_ref, mm, left_at):
    mm[...] = jnp.dot(
        left_ref[pl.ds(left_at, mm.shape[0]), :],
        basis_ref[...],
        preferred_element_type=jnp.float32,
    )


def back_kernel(
    sizes,
    lists_ref,
    lens_ref,
    basis_ref,
    moment_ref,
    left_ref,
    shape_ref,
    grad_ref,
    out_ref,
    mm,
    alphas,
    weights,
    slopes,
    grad_scr,
    mom_scr,
    row_scr,
    rows,
    table,
):
    cap, lane_len, col_groups, list_len = sizes
    devices = out_ref.shape[0]
    parts = cap // lane_len
    blocks = list_len // STEP_ROWS
    table_rows = table.shape[0] // 2
    table[...] = jnp.zeros_like(table)
    grad_scr[...] = jnp.zeros_like(grad_scr)
    zero = jnp.zeros((GROUP, LANES), jnp.float32)
    sub = lax.broadcasted_iota(jnp.int32, (GROUP, LANES), 0)
    lane = lax.broadcasted_iota(jnp.int32, (GROUP, LANES), 1)
    own_tile = lane % GROUP == sub

    def one_group(group, carry):
        view, col_group = group // col_groups, group % col_groups
        most = longest(lens_ref, group)
        lane_at = pl.multiple_of(col_group * GROUP * TILE, LANES)
        grads = [
            [
                jnp.concatenate(
                    [
                        swap_grain(
                            grad_ref[
                                view,
                                c,
                                half * SUBS : (half + 1) * SUBS,
                                pl.ds(lane_at + side * LANES, LANES),
                            ]
                        )
                        for side in range(GROUP // SUBS)
                    ],
                    axis=0,
                )
                for c in range(3)
            ]
            for half in range(2)
        ]
        for half in range(2):
            for c in range(3):
                high = grads[half][c].astype(jnp.bfloat16).astype(jnp.float32)
                for piece, part in enumerate((high, grads[half][c] - high)):
                    line = (piece * 3 + c) * GROUP
                    grad_scr[line : line + GROUP, half * LANES : (half + 1) * LANES] = part
        expand(left_ref, basis_ref, mm, pl.multiple_of(group * blocks * LANES, LANES))

        def ahead(n, keep):
            row_at = pl.multiple_of(n * GROUP, GROUP)
            new_keep = []
            for half in range(2):
                lanes = slice(half * LANES, (half + 1) * LANES)
                alpha = jnp.exp(mm[pl.ds(row_at, GROUP), lanes])
                weight = keep[half] * alpha
                alphas[pl.ds(row_at, GROUP), lanes] = alpha
                weights[pl.ds(row_at, GROUP), lanes] = weight
                new_keep.append(keep[half] * (1.0 - alpha))
            return new_keep

        stepped(most, UNROLL, ahead, [zero + 1.0] * 2)

        last = (most + UNROLL - 1) // UNROLL * UNROLL - 1

        def behind(step, seen):
            row_at = pl.multiple_of((last - step) * GROUP, GROUP)
            shade = [
                mm[pl.ds(row_at, GROUP), (2 + c) * LANES : (3 + c) * LANES] for c in range(3)
            ]
            new_seen = []
            for half in range(2):
                lanes = slice(half * LANES, (half + 1) * LANES)
                own = (
                    grads[half][0] * shade[0]
                    + grads[half][1] * shade[1]
                    + grads[half][2] * shade[2]
                )
                alpha = alphas[pl.ds(row_at, GROUP), lanes]
                slopes[pl.ds(row_at, GROUP), lanes] = weights[pl.ds(row_at, GROUP), lanes] * (
                    own - seen[half]
                )
                new_seen.append(seen[half] * (1.0 - alpha) + alpha * own)
            return new_seen

        stepped(most, UNROLL, behind, [zero] * 2)
        total = jnp.zeros((blocks * LANES, LANES), jnp.float32)
        for value, right in (
            (slopes[...], moment_ref[...]),
            (weights[...], grad_scr[...].T.astype(jnp.bfloat16)),
        ):
            high = value.astype(jnp.bfloat16)
            low = (value - high.astype(jnp.float32)).astype(jnp.bfloat16)
            total = total + jnp.dot(high, right, preferred_element_type=jnp.float32)
            total = total + jnp.dot(low, right, preferred_element_type=jnp.float32)
        for block in range(blocks):
            turned = total[block * LANES : (block + 1) * LANES].T
            mom_scr[block * TILE : block * TILE + 8, :] = turned[6 * GROUP : 6 * GROUP + 8]
            for c in range(3):
                summed = (
                    turned[c * GROUP : (c + 1) * GROUP]
                    + turned[(3 + c) * GROUP : (4 + c) * GROUP]
                )
                mom_scr[block * TILE + 8 + c : block * TILE + 9 + c, :] = jnp.sum(
                    jnp.where(own_tile, summed, 0.0), axis=0, keepdims=True
                )
        mom = [mom_scr[pl.ds(num, blocks, stride=TILE), :] for num in range(11)]
        con_xx, con_xy, con_yy, off_x, off_y = [
            shape_ref[num, pl.ds(pl.multiple_of(group * blocks, blocks), blocks), :]
            for num in range(5)
        ]
        sum_x = off_x * mom[0] - mom[1]
        sum_y = off_y * mom[0] - mom[2]
        results = [
            -(con_xx * sum_x + con_xy * sum_y),
            -(con_yy * sum_y + con_xy * sum_x),
            -0.5 * (off_x * (sum_x - mom[1]) + mom[3]),
            -(off_x * sum_y - off_y * mom[1] + mom[4]),
            -0.5 * (off_y * (sum_y - mom[2]) + mom[5]),
        ] + mom[8:11]
        other = 1 - view
        for num, value in enumerate(results):
            row_scr[pl.ds(view * FEATS + num, blocks, stride=24), :] = value
            row_scr[pl.ds(other * FEATS + num, blocks, stride=24), :] = jnp.zeros_like(value)
        row_scr[pl.ds(PAIR, blocks, stride=24), :] = mom[0]
        row_scr[pl.ds(FLAG, blocks, stride=24), :] = jnp.ones((blocks, LANES), jnp.float32)
        first = pl.multiple_of(group * blocks * LANES, LANES)
        for block in range(blocks):
            rows[pl.ds(first + block * LANES, LANES), 0:24] = row_scr[
                block * 24 : (block + 1) * 24, :
            ].T

        def put(n, inner):
            for t in range(GROUP):
                spot = view * table_rows + lists_ref[group * GROUP + t, n]
                table[pl.ds(spot, 1), :] = rows[pl.ds(first + n * GROUP + t, 1), :]
            return inner

        stepped(most, UNROLL, put, 0)
        return carry

    lax.fori_loop(0, 2 * col_groups, one_group, 0)

    def pack(source, count):
        for part in range(parts):
            row_at = pl.multiple_of(source * cap + part * lane_len, lane_len)
            value = (
                table[pl.ds(row_at, lane_len), :]
                + table[pl.ds(pl.multiple_of(table_rows + row_at, SUBS), lane_len), :]
            )
            count = count + value.reshape(lane_len // SUBS, SUBS, LANES).sum(axis=0)
            turned = value[:, 0:24].T
            out_ref[source, part * PAIR : (part + 1) * PAIR, :] = turned[0:PAIR]
            out_ref[source, parts * PAIR + part : parts * PAIR + part + 1, :] = turned[
                PAIR : PAIR + 1
            ]
        return count

    none = jnp.zeros((SUBS, LANES), jnp.float32)
    count = lax.fori_loop(0, devices, pack, none)
    stored = jnp.sum(jnp.where(lane[0:SUBS] == FLAG, count, 0.0))
    named = lens_ref[0]
    for tile in range(1, 2 * col_groups * GROUP):
        named = named + lens_ref[tile]

    @pl.when(stored < named.astype(jnp.float32) - 0.5)
    def _():
        table[...] = jnp.zeros_like(table)

        def add_group(group, carry):
            def add(n, inner):
                for t in range(GROUP):
                    spot = lists_ref[group * GROUP + t, n]
                    row_at = group * blocks * LANES + n * GROUP + t
                    table[pl.ds(spot, 1), :] = table[pl.ds(spot, 1), :] + rows[pl.ds(row_at, 1), :]
                return inner

            return lax.fori_loop(0, longest(lens_ref, group), add, carry)

        lax.fori_loop(0, 2 * col_groups, add_group, 0)
        lax.fori_loop(0, devices, pack, none)


def owner_kernel(
    sizes,
    cam_ref,
    list_ref,
    counts_ref,
    params_ref,
    back_ref,
    out_ref,
    tile_scr,
    feat_scr,
    turn_scr,
    table,
    slots,
):
    groups, rows, cap, lane_len, image_width, image_height = sizes
    count_params, per = params_ref.shape
    parts = cap // lane_len
    table[...] = jnp.zeros_like(table)
    turn_scr[...] = jnp.zeros_like(turn_scr)
    start = jnp.int32(0)
    for group in range(groups):
        turn_scr[PAIR + 1 : PAIR + 2, :] = jnp.full((1, LANES), 1.0 + group, jnp.float32)

        def take_block(t, start_at, group=group):
            dest = group * rows + t
            count = counts_ref[0, dest]

            for part in range(parts):
                turn_scr[0:PAIR, 0:lane_len] = back_ref[dest, part * PAIR : (part + 1) * PAIR, :]
                turn_scr[PAIR : PAIR + 1, 0:lane_len] = back_ref[
                    dest, parts * PAIR + part : parts * PAIR + part + 1, :
                ]
                slots[part * lane_len : (part + 1) * lane_len, 0:24] = turn_scr[
                    :, 0:lane_len
                ].T

            def move(k, carry):
                spot = list_ref[0, start_at + k]
                table[pl.ds(spot, 1), :] = slots[pl.ds(k, 1), :]
                return carry

            rounded = (count + MOVES - 1) // MOVES * MOVES
            whole = jnp.where(start_at + rounded <= per, rounded, count // MOVES * MOVES)
            stepped(whole, MOVES, move, 0)
            lax.fori_loop(whole, count, move, 0)
            return start_at + count

        start = lax.fori_loop(0, rows, take_block, start)

    def clear(k, carry):
        table[pl.ds(list_ref[0, k], 1), :] = jnp.zeros((1, LANES), jnp.float32)
        return carry

    lax.fori_loop(start, jnp.minimum(start + MOVES, per), clear, 0)

    def pull_block(block, carry):
        params = load_params(params_ref, tile_scr, block)
        for j in range(SUBS):
            row_at = pl.multiple_of(block * SUBS * LANES + j * LANES, LANES)
            feat_scr[j * 24 : (j + 1) * 24, :] = table[pl.ds(row_at, LANES), 0:24].T
        cots = [feat_scr[pl.ds(num, SUBS, stride=24), :] for num in range(PAIR + 2)]
        home = cots[PAIR + 1]
        sent = home > 0.5
        cams = []
        for view in range(2):
            cam = []
            for k in range(15):
                value = jnp.full((SUBS, LANES), cam_ref[view, k], jnp.float32)
                for group in range(1, groups):
                    value = jnp.where(home > 0.5 + group, cam_ref[2 * group + view, k], value)
                cam.append(value)
            cams.append(cam)

        def both(*values):
            shape = shape_matrix(values)
            return (
                view_features(values, shape, cams[0], image_width, image_height)
                + view_features(values, shape, cams[1], image_width, image_height)
                + [log_opacity(values[10])]
            )

        _, pull = jax.vjp(both, *params)
        grads = pull(cots[0 : PAIR + 1])
        for num, value in enumerate(grads):
            tile_scr[pl.ds((num // SUBS) * SUBS * SUBS + num % SUBS, SUBS, stride=SUBS), :] = (
                jnp.where(sent, value, 0.0)
            )
        for band in range(0, count_params, SUBS):
            high = min(band + SUBS, count_params)
            for j in range(SUBS):
                lane_at = pl.multiple_of(block * SUBS * LANES + j * LANES, LANES)
                out_ref[band:high, pl.ds(lane_at, LANES)] = tile_scr[
                    band * SUBS + j * SUBS : band * SUBS + j * SUBS + high - band, :
                ]
        return carry

    lax.fori_loop(0, per // (SUBS * LANES), pull_block, 0)


def tap_rows(read, first, count):
    taps = window_taps()
    total = taps[5] * read(first + 5, count)
    for k in range(5):
        total = total + taps[k] * (read(first + k, count) + read(first + TAPS - 1 - k, count))
    return total


def blur_lanes(value, band):
    return jnp.dot(
        value, band, precision=lax.Precision.HIGHEST, preferred_element_type=jnp.float32
    )


def truth_kernel(band_ref, above_ref, own_ref, below_ref, out_ref, tall, mixed):
    images = own_ref.shape[0]

    def one_image(m, carry):
        whole = jnp.concatenate([above_ref[m], own_ref[m], below_ref[m]], axis=0)
        for field, value in enumerate((whole, whole * whole)):
            tall[...] = value
            row_at = pl.multiple_of((field * images + m) * 2 * TILE, 2 * TILE)
            mixed[pl.ds(row_at, 2 * TILE), :] = tap_rows(
                lambda at, count: tall[at : at + count, :], 6, 2 * TILE
            )
        return carry

    lax.fori_loop(0, images, one_image, 0)
    out_ref[...] = blur_lanes(mixed[...], band_ref[...])


def loss_kernel(
    image_rows,
    row_ref,
    band_ref,
    truth_ref,
    true_above,
    true_own,
    true_below,
    above_ref,
    own_ref,
    below_ref,
    out_ref,
    tall,
    mixed,
    blurred,
    slim,
):
    images = own_ref.shape[0]
    tall_rows = 2 * TILE
    width = own_ref.shape[2]

    def one_image(m, carry):
        whole = jnp.concatenate([above_ref[m], own_ref[m], below_ref[m]], axis=0)
        true = jnp.concatenate([true_above[m], true_own[m], true_below[m]], axis=0)
        for field, value in enumerate((whole, whole * whole, whole * true)):
            tall[field] = value
            row_at = pl.multiple_of((field * images + m) * tall_rows, tall_rows)
            mixed[pl.ds(row_at, tall_rows), :] = tap_rows(
                lambda at, count, field=field: tall[field, at : at + count, :], 6, tall_rows
            )
        return carry

    lax.fori_loop(0, images, one_image, 0)
    blurred[...] = blur_lanes(mixed[...], band_ref[...])
    sub = lax.broadcasted_iota(jnp.int32, (tall_rows, width), 0)
    image_row = row_ref[0] * TILE + sub - 5
    inside = (image_row >= 0) & (image_row < image_rows) & (sub < TILE + 10)

    def one_map(m, carry):
        def field_of(ref, field):
            row_at = pl.multiple_of((field * images + m) * tall_rows, tall_rows)
            return ref[pl.ds(row_at, tall_rows), :]

        mean_one, both_one, cross = [field_of(blurred, field) for field in range(3)]
        mean_two, both_two = field_of(truth_ref, 0), field_of(truth_ref, 1)
        square_one, square_two = mean_one * mean_one, mean_two * mean_two
        mean_cross = mean_one * mean_two
        top_one = 2.0 * mean_cross + SSIM_ONE
        top_two = 2.0 * (cross - mean_cross) + SSIM_TWO
        low_one = square_one + square_two + SSIM_ONE
        low_two = (both_one - square_one) + (both_two - square_two) + SSIM_TWO
        inv_one, inv_two = 1.0 / low_one, 1.0 / low_two
        inv_both = inv_one * inv_two
        value = top_one * top_two * inv_both
        grads = [
            2.0 * mean_two * (top_two - top_one) * inv_both
            - 2.0 * mean_one * value * (inv_one - inv_two),
            -value * inv_two,
            2.0 * top_one * inv_both,
        ]
        for field, grad in enumerate(grads):
            tall[field, 0:tall_rows] = jnp.where(inside, grad, 0.0)
            row_at = pl.multiple_of((field * images + m) * TILE, TILE)
            slim[pl.ds(row_at, TILE), :] = tap_rows(
                lambda at, count, field=field: tall[field, at : at + count, :], 0, TILE
            )
        return carry

    lax.fori_loop(0, images, one_map, 0)
    spread = blur_lanes(slim[...], band_ref[...]).reshape(3, images, TILE, width)
    own, true = own_ref[...], true_own[...]
    gap = own - true
    out_ref[...] = (1.0 - SSIM_SHARE) * gap / jnp.sqrt(gap * gap + SMOOTH_EPS) - SSIM_SHARE * (
        spread[0] + 2.0 * own * spread[1] + true * spread[2]
    )


def band_matrix(width):
    taps = window_taps()
    band = np.zeros((width, width), np.float32)
    for k in range(TAPS):
        band += np.diag(np.full(width - abs(k - 5), taps[k], np.float32), k - 5)
    return jnp.asarray(band)


def pixel_basis():
    pixel = np.arange(TILE * TILE)
    x = (pixel % TILE) - (TILE - 1) / 2.0
    y = (pixel // TILE) - (TILE - 1) / 2.0
    return np.stack([np.ones_like(x), x, y, x * x, x * y, y * y])


def expand_matrix():
    terms = pixel_basis()
    matrix = np.zeros((COEF_ROWS, 5 * LANES), np.float32)
    for piece in range(3):
        matrix[piece * 6 : piece * 6 + 6, 0 : 2 * LANES] = terms
        for c in range(3):
            matrix[18 + piece * 3 + c, (2 + c) * LANES : (3 + c) * LANES] = 1.0
    return jnp.asarray(matrix, jnp.bfloat16)


def moment_matrix():
    matrix = np.zeros((2 * LANES, LANES), np.float32)
    matrix[:, 6 * GROUP : 6 * GROUP + 6] = pixel_basis().T
    return jnp.asarray(matrix, jnp.bfloat16)


def smem():
    return pl.BlockSpec(memory_space=pltpu.SMEM)


def vmem():
    return pl.BlockSpec(memory_space=pltpu.VMEM)


def scratch(*shape):
    return pltpu.VMEM(shape, jnp.float32)


def run(kernel, out_shapes, in_specs, scratches, *operands):
    return pl.pallas_call(
        kernel,
        out_shape=out_shapes,
        in_specs=in_specs,
        out_specs=jax.tree.map(lambda _: vmem(), out_shapes),
        scratch_shapes=scratches,
        compiler_params=pltpu.CompilerParams(vmem_limit_bytes=VMEM_BYTES),
    )(*operands)


def shards(params, send_list, send_counts, camera, ground_truth, tile_lists, list_lengths):
    devices = lax.axis_size(("view", "tile"))
    row_devices = lax.axis_size("tile")
    groups = lax.axis_size("view")
    count_params, per_device = params.shape
    capacity = per_device // devices
    tile_cols, list_len = tile_lists.shape[2:]
    col_groups = tile_cols // GROUP
    blocks = list_len // STEP_ROWS
    tile_row = lax.axis_index("tile")
    image_width = float(ground_truth.shape[3])
    image_height = float(ground_truth.shape[2] * row_devices)
    table_rows = per_device + GROUP
    lane_len = min(capacity, LANES)
    sent_shape = jax.ShapeDtypeStruct(
        (devices, capacity // lane_len * (PAIR + 1), lane_len), jnp.float32
    )
    count_blocks = per_device // LANES
    cams = camera_table(camera)

    flat_lengths = list_lengths.reshape(-1)
    entry_rank = jnp.arange(list_len, dtype=jnp.int32)
    tile_num = jnp.arange(2 * tile_cols, dtype=jnp.int32)
    lists = jnp.where(
        entry_rank[None, :] < flat_lengths[:, None],
        tile_lists.reshape(2 * tile_cols, list_len),
        per_device + tile_num[:, None] % GROUP,
    )
    lens_rows = jnp.tile(flat_lengths.reshape(-1, GROUP), (1, LANES // GROUP))

    width = ground_truth.shape[3]
    true_own = ground_truth.reshape(-1, TILE, width)
    true_above = from_behind(true_own, "tile", 1)
    true_below = from_behind(true_own, "tile", -1)
    band = band_matrix(width)
    truth_rows = 2 * true_own.shape[0] * 2 * TILE
    truth_blur = run(
        truth_kernel,
        jax.ShapeDtypeStruct((truth_rows, width), jnp.float32),
        [vmem()] * 4,
        [scratch(3 * TILE, width), scratch(truth_rows, width)],
        band,
        true_above,
        true_own,
        true_below,
    )

    own_sizes = (groups, row_devices, capacity, lane_len, image_width, image_height)
    sent = run(
        lambda *refs: source_kernel(own_sizes, *refs),
        sent_shape,
        [smem(), smem(), vmem(), vmem()],
        [
            scratch(SUBS * SUBS * SUBS, LANES),
            scratch(count_blocks * camera.shape[0] * FEATS, LANES),
            scratch(count_blocks, LANES),
        ],
        cams,
        send_counts,
        send_list,
        params,
    )
    arrived = lax.all_to_all(sent, ("view", "tile"), split_axis=0, concat_axis=0, tiled=True)

    tile_sizes = (capacity, lane_len, col_groups, list_len)
    entries = 2 * tile_cols * list_len
    rendered, left, shapes = run(
        lambda *refs: render_kernel(tile_sizes, *refs),
        (
            jax.ShapeDtypeStruct(ground_truth.shape, jnp.float32),
            jax.ShapeDtypeStruct((entries, COEF_ROWS), jnp.bfloat16),
            jax.ShapeDtypeStruct((5, entries // LANES, LANES), jnp.float32),
        ),
        [smem(), smem(), vmem(), vmem(), vmem(), vmem()],
        [
            scratch(2 * per_device // LANES * FEATS, LANES),
            scratch(count_blocks, LANES),
            scratch(blocks * PAIR, LANES),
            scratch(blocks * COEF_ROWS, LANES),
            scratch(blocks * LANES, 5 * LANES),
        ],
        tile_row.reshape(1),
        flat_lengths,
        lens_rows,
        lists.reshape(-1, GROUP, list_len).transpose(0, 2, 1).reshape(-1, LANES),
        expand_matrix(),
        arrived,
    )

    images = rendered.reshape(true_own.shape)
    count = images.shape[0]
    grad_image = run(
        lambda *refs: loss_kernel(TILE * row_devices, *refs),
        jax.ShapeDtypeStruct(images.shape, jnp.float32),
        [smem()] + [vmem()] * 8,
        [
            scratch(3, 3 * TILE, width),
            scratch(3 * count * 2 * TILE, width),
            scratch(3 * count * 2 * TILE, width),
            scratch(3 * count * TILE, width),
        ],
        tile_row.reshape(1),
        band,
        truth_blur,
        true_above,
        true_own,
        true_below,
        from_behind(images, "tile", 1),
        images,
        from_behind(images, "tile", -1),
    ).reshape(ground_truth.shape)

    grad_slots = run(
        lambda *refs: back_kernel(tile_sizes, *refs),
        sent_shape,
        [smem(), smem()] + [vmem()] * 5,
        [
            scratch(blocks * LANES, 5 * LANES),
            scratch(blocks * LANES, 2 * LANES),
            scratch(blocks * LANES, 2 * LANES),
            scratch(blocks * LANES, 2 * LANES),
            scratch(LANES, 2 * LANES),
            scratch(blocks * TILE, LANES),
            scratch(blocks * 24, LANES),
            scratch(entries, LANES),
            scratch(2 * table_rows, LANES),
        ],
        lists,
        flat_lengths,
        expand_matrix(),
        moment_matrix(),
        left,
        shapes,
        grad_image,
    )
    returned = lax.all_to_all(
        grad_slots, ("view", "tile"), split_axis=0, concat_axis=0, tiled=True
    )
    return run(
        lambda *refs: owner_kernel(own_sizes, *refs),
        jax.ShapeDtypeStruct(params.shape, jnp.float32),
        [smem(), smem(), smem(), vmem(), vmem()],
        [
            scratch(SUBS * SUBS * SUBS, LANES),
            scratch(SUBS * 24, LANES),
            scratch(24, LANES),
            scratch(per_device, LANES),
            scratch(capacity, LANES),
        ],
        cams,
        send_list,
        send_counts,
        params,
        returned,
    )


def solution(mesh):
    in_specs = (
        P(None, ("view", "tile")),
        P(("view", "tile"), None),
        P(("view", "tile"), None),
        P(),
        P("view", None, "tile", None),
        P("view", "tile", None, None),
        P("view", "tile", None),
    )
    out_specs = P(None, ("view", "tile"))
    return jax.shard_map(shards, mesh=mesh, in_specs=in_specs, out_specs=out_specs, check_vma=False)
```

```python
import jax
import jax.numpy as jnp
import numpy as np
from jax import lax
from jax.experimental import pallas as pl
from jax.experimental.pallas import tpu as pltpu
from jax.sharding import PartitionSpec as P

TILE = 16


FOCAL = 1000.0
LOW_PASS = 0.3
SSIM_SHARE = 0.2
SMOOTH_EPS = 1e-06
SSIM_ONE = 0.0001
SSIM_TWO = 0.0009
HARMONIC_ZERO = 0.28209479177387814
HARMONIC_ONE = 0.4886025119029199
HARMONIC_TWO = (
    1.0925484305920792,
    -1.0925484305920792,
    0.31539156525252005,
    -1.0925484305920792,
    0.5462742152960396,
)
HARMONIC_THREE = (
    -0.5900435899266435,
    2.890611442640554,
    -0.4570457994644658,
    0.3731763325901154,
    -0.4570457994644658,
    1.445305721320277,
    -0.5900435899266435,
)


def from_behind(block, axis, distance):
    devices = range(lax.axis_size(axis))
    route = [(i - distance, i) for i in devices if i - distance in devices]
    return lax.ppermute(block, axis, route)


def window_taps():
    offsets_np = np.arange(11) - 5.0
    weights = np.exp(-offsets_np * offsets_np / 4.5)
    weights = weights / weights.sum()
    return [float(weight) for weight in weights]


def matrix_product(left_side, right_side):
    return [
        [
            left_side[row_idx][0] * right_side[0][col_idx]
            + left_side[row_idx][1] * right_side[1][col_idx]
            + left_side[row_idx][2] * right_side[2][col_idx]
            for col_idx in range(3)
        ]
        for row_idx in range(3)
    ]


def rotation(angles):
    cos_a, sin_a = (jnp.cos(angles[0]), jnp.sin(angles[0]))
    cos_b, sin_b = (jnp.cos(angles[1]), jnp.sin(angles[1]))
    cos_c, sin_c = (jnp.cos(angles[2]), jnp.sin(angles[2]))
    about_x = [[1.0, 0.0, 0.0], [0.0, cos_a, -sin_a], [0.0, sin_a, cos_a]]
    about_y = [[cos_b, 0.0, sin_b], [0.0, 1.0, 0.0], [-sin_b, 0.0, cos_b]]
    about_z = [[cos_c, -sin_c, 0.0], [sin_c, cos_c, 0.0], [0.0, 0.0, 1.0]]
    return matrix_product(about_z, matrix_product(about_y, about_x))


def harmonics(dir_x, dir_y, dir_z):
    sq_x, sq_y, sq_z = (dir_x * dir_x, dir_y * dir_y, dir_z * dir_z)
    prod_xy, prod_yz, prod_xz = (dir_x * dir_y, dir_y * dir_z, dir_x * dir_z)
    return [
        HARMONIC_ZERO + 0.0 * dir_x,
        -HARMONIC_ONE * dir_y,
        HARMONIC_ONE * dir_z,
        -HARMONIC_ONE * dir_x,
        HARMONIC_TWO[0] * prod_xy,
        HARMONIC_TWO[1] * prod_yz,
        HARMONIC_TWO[2] * (2.0 * sq_z - sq_x - sq_y),
        HARMONIC_TWO[3] * prod_xz,
        HARMONIC_TWO[4] * (sq_x - sq_y),
        HARMONIC_THREE[0] * dir_y * (3.0 * sq_x - sq_y),
        HARMONIC_THREE[1] * prod_xy * dir_z,
        HARMONIC_THREE[2] * dir_y * (4.0 * sq_z - sq_x - sq_y),
        HARMONIC_THREE[3] * dir_z * (2.0 * sq_z - 3.0 * sq_x - 3.0 * sq_y),
        HARMONIC_THREE[4] * dir_x * (4.0 * sq_z - sq_x - sq_y),
        HARMONIC_THREE[5] * dir_z * (sq_x - sq_y),
        HARMONIC_THREE[6] * dir_x * (sq_x - 3.0 * sq_y),
    ]


LANES = 128
SUBS = 8
GROUP = 16
STEP_ROWS = LANES // GROUP
FEATS = 8
PAIR = 2 * FEATS
COEF_ROWS = 32
JOIN = 4
UNROLL = 8
MOVES = 16
TAPS = 11
DEAD = -1e30
LOG_TOP = float(np.log(0.99))
VMEM_BYTES = 48 * 1024 * 1024


def stepped(total, width, body, state):
    def step(block, held):
        for k in range(width):
            held = body(block * width + k, held)
        return held

    return lax.fori_loop(0, (total + width - 1) // width, step, state)


def lane_spread(index):
    return index // LANES, index % LANES


def take_blocks(read, count, block, place):
    result = jnp.zeros(place.shape, jnp.float32)
    for num in range(count):
        taken = jnp.take_along_axis(read(num), place, axis=1, mode="promise_in_bounds")
        result = jnp.where(block == num, taken, result)
    return result


def take_line(read, count, block, place):
    sub = lax.broadcasted_iota(jnp.int32, (SUBS, LANES), 0)
    result = take_blocks(read, -(-count // SUBS), block // SUBS, place)
    return jnp.sum(jnp.where(sub == block % SUBS, result, 0.0), axis=0, keepdims=True)


def camera_table(camera):
    columns = [camera[:, entry] for entry in range(6)]
    turn = rotation(columns[0:3])
    shift = columns[3:6]
    anchor = [
        -(turn[0][c] * shift[0] + turn[1][c] * shift[1] + turn[2][c] * shift[2]) for c in range(3)
    ]
    flat = [turn[r][c] for r in range(3) for c in range(3)] + shift + anchor
    return jnp.stack(flat + [jnp.zeros_like(shift[0])], axis=1)


def shape_matrix(params):
    scales = [jnp.exp(params[3 + axis_num]) for axis_num in range(3)]
    inv_norm = 1.0 / jnp.sqrt(
        params[6] * params[6]
        + params[7] * params[7]
        + params[8] * params[8]
        + params[9] * params[9]
    )
    quat_w, quat_x, quat_y, quat_z = [params[6 + k] * inv_norm for k in range(4)]
    quat_rot = [
        [
            1.0 - 2.0 * (quat_y * quat_y + quat_z * quat_z),
            2.0 * (quat_x * quat_y - quat_w * quat_z),
            2.0 * (quat_x * quat_z + quat_w * quat_y),
        ],
        [
            2.0 * (quat_x * quat_y + quat_w * quat_z),
            1.0 - 2.0 * (quat_x * quat_x + quat_z * quat_z),
            2.0 * (quat_y * quat_z - quat_w * quat_x),
        ],
        [
            2.0 * (quat_x * quat_z - quat_w * quat_y),
            2.0 * (quat_y * quat_z + quat_w * quat_x),
            1.0 - 2.0 * (quat_x * quat_x + quat_y * quat_y),
        ],
    ]
    return [[quat_rot[r][c] * scales[c] for c in range(3)] for r in range(3)]


def view_features(params, shape, cam, image_width, image_height):
    turn = [[cam[3 * r + c] for c in range(3)] for r in range(3)]
    point = [
        turn[r][0] * params[0] + turn[r][1] * params[1] + turn[r][2] * params[2] + cam[9 + r]
        for r in range(3)
    ]
    inv_depth = 1.0 / point[2]
    ratio_x, ratio_y = point[0] * inv_depth, point[1] * inv_depth
    zoom = FOCAL * inv_depth
    row_x = [zoom * (turn[0][c] - ratio_x * turn[2][c]) for c in range(3)]
    row_y = [zoom * (turn[1][c] - ratio_y * turn[2][c]) for c in range(3)]
    proj_x = [
        row_x[0] * shape[0][c] + row_x[1] * shape[1][c] + row_x[2] * shape[2][c] for c in range(3)
    ]
    proj_y = [
        row_y[0] * shape[0][c] + row_y[1] * shape[1][c] + row_y[2] * shape[2][c] for c in range(3)
    ]
    cov_xx = proj_x[0] * proj_x[0] + proj_x[1] * proj_x[1] + proj_x[2] * proj_x[2] + LOW_PASS
    cov_xy = proj_x[0] * proj_y[0] + proj_x[1] * proj_y[1] + proj_x[2] * proj_y[2]
    cov_yy = proj_y[0] * proj_y[0] + proj_y[1] * proj_y[1] + proj_y[2] * proj_y[2] + LOW_PASS
    inv_det = 1.0 / (cov_xx * cov_yy - cov_xy * cov_xy)
    ray = [params[c] - cam[12 + c] for c in range(3)]
    inv_len = 1.0 / jnp.sqrt(ray[0] * ray[0] + ray[1] * ray[1] + ray[2] * ray[2])
    basis = harmonics(ray[0] * inv_len, ray[1] * inv_len, ray[2] * inv_len)
    colours = []
    for channel in range(3):
        summed = 0.5 + HARMONIC_ZERO * params[11 + 16 * channel]
        for harmonic in range(1, 16):
            summed = summed + basis[harmonic] * params[11 + 16 * channel + harmonic]
        colours.append(summed)
    return [
        FOCAL * ratio_x + image_width / 2.0,
        FOCAL * ratio_y + image_height / 2.0,
        cov_yy * inv_det,
        -cov_xy * inv_det,
        cov_xx * inv_det,
    ] + colours


def log_opacity(logit):
    return LOG_TOP - jnp.log(1.0 + jnp.exp(-logit))


def load_params(params_ref, tile_scr, block):
    count = params_ref.shape[0]
    for band in range(0, count, SUBS):
        high = min(band + SUBS, count)
        for j in range(SUBS):
            lane_at = pl.multiple_of(block * SUBS * LANES + j * LANES, LANES)
            tile_scr[band * SUBS + j * SUBS : band * SUBS + j * SUBS + high - band, :] = params_ref[
                band:high, pl.ds(lane_at, LANES)
            ]
    return [
        tile_scr[pl.ds((r // SUBS) * SUBS * SUBS + r % SUBS, SUBS, stride=SUBS), :]
        for r in range(count)
    ]


def source_kernel(
    sizes, cam_ref, counts_ref, list_ref, params_ref, out_ref, tile_scr, table, logs
):
    groups, rows, cap, lane_len, image_width, image_height = sizes
    per = params_ref.shape[1]
    views = cam_ref.shape[0]
    parts = cap // lane_len
    used = views * FEATS
    count_blocks = per // LANES

    def project_block(block, carry):
        params = load_params(params_ref, tile_scr, block)
        shape = shape_matrix(params)
        at = block * SUBS * used
        for view in range(views):
            cam = [cam_ref[view, k] for k in range(15)]
            for num, value in enumerate(
                view_features(params, shape, cam, image_width, image_height)
            ):
                table[pl.ds(at + view * FEATS + num, SUBS, stride=used), :] = value
        logs[pl.ds(pl.multiple_of(block * SUBS, SUBS), SUBS), :] = log_opacity(params[10])
        return carry

    lax.fori_loop(0, per // (SUBS * LANES), project_block, 0)
    lane = lax.broadcasted_iota(jnp.int32, (SUBS, LANES), 1)

    def send_block(dest, start_at):
        count = counts_ref[0, dest]
        line = pl.multiple_of(dest // rows * PAIR, SUBS)
        for part in range(parts):

            @pl.when(count > part * lane_len)
            def _(part=part):
                first = start_at + part * lane_len
                block, turn = first // LANES, first % LANES
                pieces = []
                for step in range(2):
                    at = jnp.minimum(block + step, count_blocks - 1) * LANES
                    names = list_ref[0:1, pl.ds(pl.multiple_of(at, LANES), LANES)]
                    pieces.append(
                        pltpu.roll(jnp.broadcast_to(names, (SUBS, LANES)), LANES - turn, 1)
                    )
                index = jnp.where(lane < LANES - turn, pieces[0], pieces[1])
                home, place = lane_spread(index)
                twice = [jnp.concatenate([value, value], axis=0) for value in (home, place)]
                taken = take_blocks(
                    lambda num: table[pl.ds(num * used + line, PAIR), :], count_blocks, *twice
                )
                log_o = take_line(
                    lambda num: logs[num * SUBS : (num + 1) * SUBS, :], count_blocks, home, place
                )
                out_ref[dest, part * PAIR : (part + 1) * PAIR, :] = taken[:, 0:lane_len]
                out_ref[dest, parts * PAIR + part : parts * PAIR + part + 1, :] = log_o[
                    :, 0:lane_len
                ]

        return start_at + count

    lax.fori_loop(0, groups * rows, send_block, jnp.int32(0))


def split_three(value):
    first = value.astype(jnp.bfloat16).astype(jnp.float32)
    rest = value - first
    second = rest.astype(jnp.bfloat16).astype(jnp.float32)
    return [first, second, rest - second]


def in_two(value):
    high = value.astype(jnp.bfloat16).astype(jnp.float32)
    return [high, value - high]


def swap_grain(cells):
    sub = lax.broadcasted_iota(jnp.int32, (SUBS, LANES), 0)
    lane = lax.broadcasted_iota(jnp.int32, (SUBS, LANES), 1) // TILE
    for bit in (1, 2, 4):
        sub_bit, lane_bit = (sub & bit) != 0, (lane & bit) != 0
        from_high = pltpu.roll(pltpu.roll(cells, SUBS - bit, 0), bit * TILE, 1)
        from_low = pltpu.roll(pltpu.roll(cells, bit, 0), LANES - bit * TILE, 1)
        cells = jnp.where(sub_bit == lane_bit, cells, jnp.where(lane_bit, from_high, from_low))
    return cells


def longest(lens_ref, group):
    most = lens_ref[group * GROUP]
    for t in range(1, GROUP):
        most = jnp.maximum(most, lens_ref[group * GROUP + t])
    return most


def render_kernel(
    sizes,
    row_ref,
    lens_ref,
    lens_rows_ref,
    names_ref,
    basis_ref,
    arrived_ref,
    image_ref,
    left_ref,
    shape_ref,
    table,
    logs,
    feat_scr,
    pieces,
    mm,
):
    cap, lane_len, col_groups, list_len = sizes
    devices = arrived_ref.shape[0]
    blocks = list_len // STEP_ROWS
    count_blocks = devices * cap // LANES
    parts = cap // lane_len
    joined = LANES // lane_len

    def unpack(block, carry):
        for k in range(joined):
            source = block * joined // parts + k
            part = block * joined % parts
            lanes = slice(k * lane_len, (k + 1) * lane_len)
            at = pl.multiple_of(part * PAIR, PAIR)
            for view in range(2):
                row_at = pl.multiple_of((view * count_blocks + block) * FEATS, FEATS)
                table[pl.ds(row_at, FEATS), lanes] = arrived_ref[
                    source, pl.ds(at + view * FEATS, FEATS), :
                ]
            logs[pl.ds(block, 1), lanes] = arrived_ref[source, pl.ds(parts * PAIR + part, 1), :]
        return carry

    lax.fori_loop(0, count_blocks, unpack, 0)
    centre_y = (row_ref[0] * TILE).astype(jnp.float32) + (TILE - 1) / 2.0
    sub = lax.broadcasted_iota(jnp.int32, (blocks, LANES), 0)
    lane = lax.broadcasted_iota(jnp.int32, (blocks, LANES), 1)
    zero = jnp.zeros((GROUP, LANES), jnp.float32)

    def one_group(group, carry):
        view, col_group = group // col_groups, group % col_groups
        most = longest(lens_ref, group)

        def fetch(block, inner):
            names = names_ref[pl.ds(group * blocks + block, 1), :]
            home, place = lane_spread(jnp.broadcast_to(names, (SUBS, LANES)))
            feat_at = pl.multiple_of(block * PAIR, PAIR)
            feat_scr[pl.ds(feat_at, FEATS), :] = take_blocks(
                lambda num: table[
                    pl.ds(pl.multiple_of((view * count_blocks + num) * FEATS, FEATS), FEATS), :
                ],
                count_blocks,
                home,
                place,
            )
            feat_scr[pl.ds(feat_at + FEATS, 1), :] = take_line(
                lambda num: logs[num * SUBS : (num + 1) * SUBS, :], count_blocks, home, place
            )
            return inner

        stepped((most + STEP_ROWS - 1) // STEP_ROWS, 2, fetch, 0)
        feats = [feat_scr[pl.ds(num, blocks, stride=PAIR), :] for num in range(FEATS)]
        log_o = feat_scr[pl.ds(FEATS, blocks, stride=PAIR), :]
        live = sub * STEP_ROWS + lane // GROUP < lens_rows_ref[pl.ds(group, 1), :]
        centre_x = ((col_group * GROUP + lane % GROUP) * TILE).astype(jnp.float32) + (
            TILE - 1
        ) / 2.0
        off_x, off_y = feats[0] - centre_x, feats[1] - centre_y
        lin_x = feats[2] * off_x + feats[3] * off_y
        lin_y = feats[4] * off_y + feats[3] * off_x
        coefs = [
            log_o - 0.5 * (off_x * lin_x + off_y * lin_y),
            lin_x,
            lin_y,
            -0.5 * feats[2],
            -feats[3],
            -0.5 * feats[4],
        ]
        coefs = [
            jnp.where(live, value, DEAD if num == 0 else 0.0) for num, value in enumerate(coefs)
        ]
        lines = [None] * COEF_ROWS
        for num, value in enumerate(coefs):
            for piece, part in enumerate(split_three(value)):
                lines[piece * 6 + num] = part
        for num in range(3):
            for piece, part in enumerate(split_three(jnp.where(live, feats[5 + num], 0.0))):
                lines[18 + piece * 3 + num] = part
        for num, value in enumerate(lines):
            pieces[pl.ds(num, blocks, stride=COEF_ROWS), :] = (
                jnp.zeros((blocks, LANES), jnp.float32) if value is None else value
            )
        for num, value in enumerate(feats[2:5] + [off_x, off_y]):
            shape_ref[num, pl.ds(pl.multiple_of(group * blocks, blocks), blocks), :] = jnp.where(
                live, value, 0.0
            )
        left_at = pl.multiple_of(group * blocks * LANES, LANES)
        for block in range(blocks):
            left_ref[pl.ds(left_at + block * LANES, LANES), :] = pieces[
                block * COEF_ROWS : (block + 1) * COEF_ROWS, :
            ].T.astype(jnp.bfloat16)
        expand(left_ref, basis_ref, mm, left_at)

        def entry(n, state):
            keep, colour = state
            row_at = pl.multiple_of(n * GROUP, GROUP)
            shade = [
                mm[pl.ds(row_at, GROUP), (2 + c) * LANES : (3 + c) * LANES] for c in range(3)
            ]
            new_keep, new_colour = [], []
            for half in range(2):
                alpha = jnp.exp(mm[pl.ds(row_at, GROUP), half * LANES : (half + 1) * LANES])
                weight = keep[half] * alpha
                new_keep.append(keep[half] * (1.0 - alpha))
                new_colour.append([colour[half][c] + weight * shade[c] for c in range(3)])
            return new_keep, new_colour

        state = ([zero + 1.0] * 2, [[zero] * 3] * 2)
        _, colour = stepped(most, UNROLL, entry, state)
        for side in range(GROUP // SUBS):
            lane_at = pl.multiple_of(col_group * GROUP * TILE + side * LANES, LANES)
            for half in range(2):
                for c in range(3):
                    image_ref[view, c, half * SUBS : (half + 1) * SUBS, pl.ds(lane_at, LANES)] = (
                        swap_grain(colour[half][c][side * SUBS : (side + 1) * SUBS])
                    )
        return carry

    lax.fori_loop(0, 2 * col_groups, one_group, 0)


def expand(left_ref, basis_ref, mm, left_at):
    mm[...] = jnp.dot(
        left_ref[pl.ds(left_at, mm.shape[0]), :],
        basis_ref[...],
        preferred_element_type=jnp.float32,
    )


def back_kernel(
    sizes,
    lens_ref,
    names_ref,
    basis_ref,
    moment_ref,
    left_ref,
    shape_ref,
    grad_ref,
    out_ref,
    mm,
    alphas,
    weights,
    slopes,
    grad_scr,
    mom_scr,
    line_scr,
    masked,
    places,
    total_scr,
):
    cap, lane_len, col_groups, list_len = sizes
    devices = out_ref.shape[0]
    parts = cap // lane_len
    blocks = list_len // STEP_ROWS
    count_blocks = devices * cap // LANES
    joined = LANES // lane_len
    value_rows = count_blocks * 2 * FEATS
    total_scr[...] = jnp.zeros_like(total_scr)
    line_scr[...] = jnp.zeros_like(line_scr)
    grad_scr[...] = jnp.zeros_like(grad_scr)
    zero = jnp.zeros((GROUP, LANES), jnp.float32)
    sub = lax.broadcasted_iota(jnp.int32, (GROUP, LANES), 0)
    lane = lax.broadcasted_iota(jnp.int32, (GROUP, LANES), 1)
    own_tile = lane % GROUP == sub

    def one_group(group, carry):
        view, col_group = group // col_groups, group % col_groups
        most = longest(lens_ref, group)
        lane_at = pl.multiple_of(col_group * GROUP * TILE, LANES)
        grads = [
            [
                jnp.concatenate(
                    [
                        swap_grain(
                            grad_ref[
                                view,
                                c,
                                half * SUBS : (half + 1) * SUBS,
                                pl.ds(lane_at + side * LANES, LANES),
                            ]
                        )
                        for side in range(GROUP // SUBS)
                    ],
                    axis=0,
                )
                for c in range(3)
            ]
            for half in range(2)
        ]
        for half in range(2):
            for c in range(3):
                for piece, part in enumerate(in_two(grads[half][c])):
                    line = (piece * 3 + c) * GROUP
                    grad_scr[line : line + GROUP, half * LANES : (half + 1) * LANES] = part
        expand(left_ref, basis_ref, mm, pl.multiple_of(group * blocks * LANES, LANES))

        def ahead(n, keep):
            row_at = pl.multiple_of(n * GROUP, GROUP)
            new_keep = []
            for half in range(2):
                lanes = slice(half * LANES, (half + 1) * LANES)
                alpha = jnp.exp(mm[pl.ds(row_at, GROUP), lanes])
                weight = keep[half] * alpha
                alphas[pl.ds(row_at, GROUP), lanes] = alpha
                weights[pl.ds(row_at, GROUP), lanes] = weight
                new_keep.append(keep[half] * (1.0 - alpha))
            return new_keep

        stepped(most, UNROLL, ahead, [zero + 1.0] * 2)

        last = (most + UNROLL - 1) // UNROLL * UNROLL - 1

        def behind(step, seen):
            row_at = pl.multiple_of((last - step) * GROUP, GROUP)
            shade = [
                mm[pl.ds(row_at, GROUP), (2 + c) * LANES : (3 + c) * LANES] for c in range(3)
            ]
            new_seen = []
            for half in range(2):
                lanes = slice(half * LANES, (half + 1) * LANES)
                own = (
                    grads[half][0] * shade[0]
                    + grads[half][1] * shade[1]
                    + grads[half][2] * shade[2]
                )
                alpha = alphas[pl.ds(row_at, GROUP), lanes]
                slopes[pl.ds(row_at, GROUP), lanes] = weights[pl.ds(row_at, GROUP), lanes] * (
                    own - seen[half]
                )
                new_seen.append(seen[half] * (1.0 - alpha) + alpha * own)
            return new_seen

        stepped(most, UNROLL, behind, [zero] * 2)
        total = jnp.zeros((blocks * LANES, LANES), jnp.float32)
        for value, right in (
            (slopes[...], moment_ref[...]),
            (weights[...], grad_scr[...].T.astype(jnp.bfloat16)),
        ):
            high = value.astype(jnp.bfloat16)
            low = (value - high.astype(jnp.float32)).astype(jnp.bfloat16)
            total = total + jnp.dot(high, right, preferred_element_type=jnp.float32)
            total = total + jnp.dot(low, right, preferred_element_type=jnp.float32)
        for block in range(blocks):
            turned = total[block * LANES : (block + 1) * LANES].T
            mom_scr[block * TILE : block * TILE + 8, :] = turned[6 * GROUP : 6 * GROUP + 8]
            for c in range(3):
                summed = (
                    turned[c * GROUP : (c + 1) * GROUP]
                    + turned[(3 + c) * GROUP : (4 + c) * GROUP]
                )
                mom_scr[block * TILE + 8 + c : block * TILE + 9 + c, :] = jnp.sum(
                    jnp.where(own_tile, summed, 0.0), axis=0, keepdims=True
                )
        mom = [mom_scr[pl.ds(num, blocks, stride=TILE), :] for num in range(11)]
        con_xx, con_xy, con_yy, off_x, off_y = [
            shape_ref[num, pl.ds(pl.multiple_of(group * blocks, blocks), blocks), :]
            for num in range(5)
        ]
        sum_x = off_x * mom[0] - mom[1]
        sum_y = off_y * mom[0] - mom[2]
        results = [
            -(con_xx * sum_x + con_xy * sum_y),
            -(con_yy * sum_y + con_xy * sum_x),
            -0.5 * (off_x * (sum_x - mom[1]) + mom[3]),
            -(off_x * sum_y - off_y * mom[1] + mom[4]),
            -0.5 * (off_y * (sum_y - mom[2]) + mom[5]),
        ] + mom[8:11]
        for num, value in enumerate(results + [mom[0]]):
            line_scr[pl.ds(num, blocks, stride=PAIR), :] = value

        def spread(step, inner):
            for k in range(JOIN):
                block = step * JOIN + k
                lanes = slice(k * LANES, (k + 1) * LANES)
                names = names_ref[pl.ds(group * blocks + block, 1), :]
                home, place = names // LANES, names % LANES
                line_at = pl.multiple_of(block * PAIR, PAIR)
                values = in_two(line_scr[pl.ds(line_at, FEATS), :])
                logs = in_two(line_scr[pl.ds(line_at + FEATS, 1), :])
                home_wide = jnp.broadcast_to(home, (2 * FEATS, LANES)).astype(jnp.bfloat16)
                pair = jnp.concatenate(values, axis=0).astype(jnp.bfloat16)
                for num in range(count_blocks):
                    masked[num * 2 * FEATS : (num + 1) * 2 * FEATS, lanes] = jnp.where(
                        home_wide == jnp.bfloat16(num), pair, jnp.bfloat16(0)
                    )
                rank = lax.broadcasted_iota(jnp.int32, (count_blocks, LANES), 0)
                for piece, value in enumerate(logs):
                    first = value_rows + piece * count_blocks
                    masked[first : first + count_blocks, lanes] = jnp.where(
                        rank == home, value, 0.0
                    ).astype(jnp.bfloat16)
                seat = lax.broadcasted_iota(jnp.int32, (LANES, LANES), 0)
                places[:, lanes] = jnp.where(seat == place, 1.0, 0.0).astype(jnp.bfloat16)
            total_scr[view] += lax.dot_general(
                masked[...],
                places[...],
                (((1,), (1,)), ((), ())),
                preferred_element_type=jnp.float32,
            )
            return inner

        width = JOIN * STEP_ROWS
        lax.fori_loop(0, (most + width - 1) // width, spread, 0)
        return carry

    lax.fori_loop(0, 2 * col_groups, one_group, 0)

    def pack(block, carry):
        for k in range(joined):
            source = block * joined // parts + k
            part = block * joined % parts
            lanes = slice(k * lane_len, (k + 1) * lane_len)
            at = pl.multiple_of(part * PAIR, PAIR)
            log_sum = jnp.zeros((1, LANES), jnp.float32)
            for view in range(2):
                row_at = pl.multiple_of(block * 2 * FEATS, 2 * FEATS)
                both = total_scr[view, pl.ds(row_at, 2 * FEATS), :]
                out_ref[source, pl.ds(at + view * FEATS, FEATS), :] = (
                    both[0:FEATS, lanes] + both[FEATS:, lanes]
                )
                for piece in range(2):
                    row = value_rows + piece * count_blocks + block
                    log_sum = log_sum + total_scr[view, pl.ds(row, 1), :]
            out_ref[source, pl.ds(parts * PAIR + part, 1), :] = log_sum[:, lanes]
        return carry

    lax.fori_loop(0, count_blocks, pack, 0)


def owner_kernel(
    sizes,
    cam_ref,
    list_ref,
    counts_ref,
    params_ref,
    back_ref,
    out_ref,
    tile_scr,
    feat_scr,
    turn_scr,
    table,
    slots,
):
    groups, rows, cap, lane_len, image_width, image_height = sizes
    count_params, per = params_ref.shape
    parts = cap // lane_len
    table[...] = jnp.zeros_like(table)
    turn_scr[...] = jnp.zeros_like(turn_scr)
    start = jnp.int32(0)
    for group in range(groups):
        turn_scr[PAIR + 1 : PAIR + 2, :] = jnp.full((1, LANES), 1.0 + group, jnp.float32)

        def take_block(t, start_at, group=group):
            dest = group * rows + t
            count = counts_ref[0, dest]

            for part in range(parts):
                turn_scr[0:PAIR, 0:lane_len] = back_ref[dest, part * PAIR : (part + 1) * PAIR, :]
                turn_scr[PAIR : PAIR + 1, 0:lane_len] = back_ref[
                    dest, parts * PAIR + part : parts * PAIR + part + 1, :
                ]
                slots[part * lane_len : (part + 1) * lane_len, 0:24] = turn_scr[
                    :, 0:lane_len
                ].T

            def move(k, carry):
                spot = list_ref[0, start_at + k]
                table[pl.ds(spot, 1), :] = slots[pl.ds(k, 1), :]
                return carry

            rounded = (count + MOVES - 1) // MOVES * MOVES
            whole = jnp.where(start_at + rounded <= per, rounded, count // MOVES * MOVES)
            stepped(whole, MOVES, move, 0)
            lax.fori_loop(whole, count, move, 0)
            return start_at + count

        start = lax.fori_loop(0, rows, take_block, start)

    def clear(k, carry):
        table[pl.ds(list_ref[0, k], 1), :] = jnp.zeros((1, LANES), jnp.float32)
        return carry

    lax.fori_loop(start, jnp.minimum(start + MOVES, per), clear, 0)

    def pull_block(block, carry):
        params = load_params(params_ref, tile_scr, block)
        for j in range(SUBS):
            row_at = pl.multiple_of(block * SUBS * LANES + j * LANES, LANES)
            feat_scr[j * 24 : (j + 1) * 24, :] = table[pl.ds(row_at, LANES), 0:24].T
        cots = [feat_scr[pl.ds(num, SUBS, stride=24), :] for num in range(PAIR + 2)]
        home = cots[PAIR + 1]
        sent = home > 0.5
        cams = []
        for view in range(2):
            cam = []
            for k in range(15):
                value = jnp.full((SUBS, LANES), cam_ref[view, k], jnp.float32)
                for group in range(1, groups):
                    value = jnp.where(home > 0.5 + group, cam_ref[2 * group + view, k], value)
                cam.append(value)
            cams.append(cam)

        def both(*values):
            shape = shape_matrix(values)
            return (
                view_features(values, shape, cams[0], image_width, image_height)
                + view_features(values, shape, cams[1], image_width, image_height)
                + [log_opacity(values[10])]
            )

        _, pull = jax.vjp(both, *params)
        grads = pull(cots[0 : PAIR + 1])
        for num, value in enumerate(grads):
            tile_scr[pl.ds((num // SUBS) * SUBS * SUBS + num % SUBS, SUBS, stride=SUBS), :] = (
                jnp.where(sent, value, 0.0)
            )
        for band in range(0, count_params, SUBS):
            high = min(band + SUBS, count_params)
            for j in range(SUBS):
                lane_at = pl.multiple_of(block * SUBS * LANES + j * LANES, LANES)
                out_ref[band:high, pl.ds(lane_at, LANES)] = tile_scr[
                    band * SUBS + j * SUBS : band * SUBS + j * SUBS + high - band, :
                ]
        return carry

    lax.fori_loop(0, per // (SUBS * LANES), pull_block, 0)


def tap_rows(read, first, count):
    taps = window_taps()
    total = taps[5] * read(first + 5, count)
    for k in range(5):
        total = total + taps[k] * (read(first + k, count) + read(first + TAPS - 1 - k, count))
    return total


def blur_lanes(value, band):
    return jnp.dot(
        value, band, precision=lax.Precision.HIGHEST, preferred_element_type=jnp.float32
    )


def truth_kernel(band_ref, above_ref, own_ref, below_ref, out_ref, tall, mixed):
    images = own_ref.shape[0]

    def one_image(m, carry):
        whole = jnp.concatenate([above_ref[m], own_ref[m], below_ref[m]], axis=0)
        for field, value in enumerate((whole, whole * whole)):
            tall[...] = value
            row_at = pl.multiple_of((field * images + m) * 2 * TILE, 2 * TILE)
            mixed[pl.ds(row_at, 2 * TILE), :] = tap_rows(
                lambda at, count: tall[at : at + count, :], 6, 2 * TILE
            )
        return carry

    lax.fori_loop(0, images, one_image, 0)
    out_ref[...] = blur_lanes(mixed[...], band_ref[...])


def loss_kernel(
    image_rows,
    row_ref,
    band_ref,
    truth_ref,
    true_above,
    true_own,
    true_below,
    above_ref,
    own_ref,
    below_ref,
    out_ref,
    tall,
    mixed,
    blurred,
    slim,
):
    images = own_ref.shape[0]
    tall_rows = 2 * TILE
    width = own_ref.shape[2]

    def one_image(m, carry):
        whole = jnp.concatenate([above_ref[m], own_ref[m], below_ref[m]], axis=0)
        true = jnp.concatenate([true_above[m], true_own[m], true_below[m]], axis=0)
        for field, value in enumerate((whole, whole * whole, whole * true)):
            tall[field] = value
            row_at = pl.multiple_of((field * images + m) * tall_rows, tall_rows)
            mixed[pl.ds(row_at, tall_rows), :] = tap_rows(
                lambda at, count, field=field: tall[field, at : at + count, :], 6, tall_rows
            )
        return carry

    lax.fori_loop(0, images, one_image, 0)
    blurred[...] = blur_lanes(mixed[...], band_ref[...])
    sub = lax.broadcasted_iota(jnp.int32, (tall_rows, width), 0)
    image_row = row_ref[0] * TILE + sub - 5
    inside = (image_row >= 0) & (image_row < image_rows) & (sub < TILE + 10)

    def one_map(m, carry):
        def field_of(ref, field):
            row_at = pl.multiple_of((field * images + m) * tall_rows, tall_rows)
            return ref[pl.ds(row_at, tall_rows), :]

        mean_one, both_one, cross = [field_of(blurred, field) for field in range(3)]
        mean_two, both_two = field_of(truth_ref, 0), field_of(truth_ref, 1)
        square_one, square_two = mean_one * mean_one, mean_two * mean_two
        mean_cross = mean_one * mean_two
        top_one = 2.0 * mean_cross + SSIM_ONE
        top_two = 2.0 * (cross - mean_cross) + SSIM_TWO
        low_one = square_one + square_two + SSIM_ONE
        low_two = (both_one - square_one) + (both_two - square_two) + SSIM_TWO
        inv_one, inv_two = 1.0 / low_one, 1.0 / low_two
        inv_both = inv_one * inv_two
        value = top_one * top_two * inv_both
        grads = [
            2.0 * mean_two * (top_two - top_one) * inv_both
            - 2.0 * mean_one * value * (inv_one - inv_two),
            -value * inv_two,
            2.0 * top_one * inv_both,
        ]
        for field, grad in enumerate(grads):
            tall[field, 0:tall_rows] = jnp.where(inside, grad, 0.0)
            row_at = pl.multiple_of((field * images + m) * TILE, TILE)
            slim[pl.ds(row_at, TILE), :] = tap_rows(
                lambda at, count, field=field: tall[field, at : at + count, :], 0, TILE
            )
        return carry

    lax.fori_loop(0, images, one_map, 0)
    spread = blur_lanes(slim[...], band_ref[...]).reshape(3, images, TILE, width)
    own, true = own_ref[...], true_own[...]
    gap = own - true
    out_ref[...] = (1.0 - SSIM_SHARE) * gap / jnp.sqrt(gap * gap + SMOOTH_EPS) - SSIM_SHARE * (
        spread[0] + 2.0 * own * spread[1] + true * spread[2]
    )


def band_matrix(width):
    taps = window_taps()
    band = np.zeros((width, width), np.float32)
    for k in range(TAPS):
        band += np.diag(np.full(width - abs(k - 5), taps[k], np.float32), k - 5)
    return jnp.asarray(band)


def pixel_basis():
    pixel = np.arange(TILE * TILE)
    x = (pixel % TILE) - (TILE - 1) / 2.0
    y = (pixel // TILE) - (TILE - 1) / 2.0
    return np.stack([np.ones_like(x), x, y, x * x, x * y, y * y])


def expand_matrix():
    terms = pixel_basis()
    matrix = np.zeros((COEF_ROWS, 5 * LANES), np.float32)
    for piece in range(3):
        matrix[piece * 6 : piece * 6 + 6, 0 : 2 * LANES] = terms
        for c in range(3):
            matrix[18 + piece * 3 + c, (2 + c) * LANES : (3 + c) * LANES] = 1.0
    return jnp.asarray(matrix, jnp.bfloat16)


def moment_matrix():
    matrix = np.zeros((2 * LANES, LANES), np.float32)
    matrix[:, 6 * GROUP : 6 * GROUP + 6] = pixel_basis().T
    return jnp.asarray(matrix, jnp.bfloat16)


def smem():
    return pl.BlockSpec(memory_space=pltpu.SMEM)


def vmem():
    return pl.BlockSpec(memory_space=pltpu.VMEM)


def scratch(*shape):
    return pltpu.VMEM(shape, jnp.float32)


def run(kernel, out_shapes, in_specs, scratches, *operands):
    return pl.pallas_call(
        kernel,
        out_shape=out_shapes,
        in_specs=in_specs,
        out_specs=jax.tree.map(lambda _: vmem(), out_shapes),
        scratch_shapes=scratches,
        compiler_params=pltpu.CompilerParams(vmem_limit_bytes=VMEM_BYTES),
    )(*operands)


def shards(params, send_list, send_counts, camera, ground_truth, tile_lists, list_lengths):
    devices = lax.axis_size(("view", "tile"))
    row_devices = lax.axis_size("tile")
    groups = lax.axis_size("view")
    count_params, per_device = params.shape
    capacity = per_device // devices
    tile_cols, list_len = tile_lists.shape[2:]
    col_groups = tile_cols // GROUP
    blocks = list_len // STEP_ROWS
    tile_row = lax.axis_index("tile")
    image_width = float(ground_truth.shape[3])
    image_height = float(ground_truth.shape[2] * row_devices)
    lane_len = min(capacity, LANES)
    sent_shape = jax.ShapeDtypeStruct(
        (devices, capacity // lane_len * (PAIR + 1), lane_len), jnp.float32
    )
    count_blocks = per_device // LANES
    cams = camera_table(camera)

    flat_lengths = list_lengths.reshape(-1)
    entry_rank = jnp.arange(list_len, dtype=jnp.int32)
    tile_num = jnp.arange(2 * tile_cols, dtype=jnp.int32)
    lists = jnp.where(
        entry_rank[None, :] < flat_lengths[:, None],
        tile_lists.reshape(2 * tile_cols, list_len),
        per_device + tile_num[:, None] % GROUP,
    )
    lens_rows = jnp.tile(flat_lengths.reshape(-1, GROUP), (1, LANES // GROUP))

    width = ground_truth.shape[3]
    true_own = ground_truth.reshape(-1, TILE, width)
    true_above = from_behind(true_own, "tile", 1)
    true_below = from_behind(true_own, "tile", -1)
    band = band_matrix(width)
    truth_rows = 2 * true_own.shape[0] * 2 * TILE
    truth_blur = run(
        truth_kernel,
        jax.ShapeDtypeStruct((truth_rows, width), jnp.float32),
        [vmem()] * 4,
        [scratch(3 * TILE, width), scratch(truth_rows, width)],
        band,
        true_above,
        true_own,
        true_below,
    )

    own_sizes = (groups, row_devices, capacity, lane_len, image_width, image_height)
    sent = run(
        lambda *refs: source_kernel(own_sizes, *refs),
        sent_shape,
        [smem(), smem(), vmem(), vmem()],
        [
            scratch(SUBS * SUBS * SUBS, LANES),
            scratch(count_blocks * camera.shape[0] * FEATS, LANES),
            scratch(count_blocks, LANES),
        ],
        cams,
        send_counts,
        send_list,
        params,
    )
    arrived = lax.all_to_all(sent, ("view", "tile"), split_axis=0, concat_axis=0, tiled=True)

    tile_sizes = (capacity, lane_len, col_groups, list_len)
    entries = 2 * tile_cols * list_len
    names = lists.reshape(-1, GROUP, list_len).transpose(0, 2, 1).reshape(-1, LANES)
    rendered, left, shapes = run(
        lambda *refs: render_kernel(tile_sizes, *refs),
        (
            jax.ShapeDtypeStruct(ground_truth.shape, jnp.float32),
            jax.ShapeDtypeStruct((entries, COEF_ROWS), jnp.bfloat16),
            jax.ShapeDtypeStruct((5, entries // LANES, LANES), jnp.float32),
        ),
        [smem(), smem(), vmem(), vmem(), vmem(), vmem()],
        [
            scratch(2 * per_device // LANES * FEATS, LANES),
            scratch(count_blocks, LANES),
            scratch(blocks * PAIR, LANES),
            scratch(blocks * COEF_ROWS, LANES),
            scratch(blocks * LANES, 5 * LANES),
        ],
        tile_row.reshape(1),
        flat_lengths,
        lens_rows,
        names,
        expand_matrix(),
        arrived,
    )

    images = rendered.reshape(true_own.shape)
    count = images.shape[0]
    grad_image = run(
        lambda *refs: loss_kernel(TILE * row_devices, *refs),
        jax.ShapeDtypeStruct(images.shape, jnp.float32),
        [smem()] + [vmem()] * 8,
        [
            scratch(3, 3 * TILE, width),
            scratch(3 * count * 2 * TILE, width),
            scratch(3 * count * 2 * TILE, width),
            scratch(3 * count * TILE, width),
        ],
        tile_row.reshape(1),
        band,
        truth_blur,
        true_above,
        true_own,
        true_below,
        from_behind(images, "tile", 1),
        images,
        from_behind(images, "tile", -1),
    ).reshape(ground_truth.shape)

    spread_rows = count_blocks * (2 * FEATS + 2)
    grad_slots = run(
        lambda *refs: back_kernel(tile_sizes, *refs),
        sent_shape,
        [smem()] + [vmem()] * 6,
        [
            scratch(blocks * LANES, 5 * LANES),
            scratch(blocks * LANES, 2 * LANES),
            scratch(blocks * LANES, 2 * LANES),
            scratch(blocks * LANES, 2 * LANES),
            scratch(LANES, 2 * LANES),
            scratch(blocks * TILE, LANES),
            scratch(blocks * PAIR, LANES),
            pltpu.VMEM((spread_rows, JOIN * LANES), jnp.bfloat16),
            pltpu.VMEM((LANES, JOIN * LANES), jnp.bfloat16),
            scratch(2, spread_rows, LANES),
        ],
        flat_lengths,
        names,
        expand_matrix(),
        moment_matrix(),
        left,
        shapes,
        grad_image,
    )
    returned = lax.all_to_all(
        grad_slots, ("view", "tile"), split_axis=0, concat_axis=0, tiled=True
    )
    return run(
        lambda *refs: owner_kernel(own_sizes, *refs),
        jax.ShapeDtypeStruct(params.shape, jnp.float32),
        [smem(), smem(), smem(), vmem(), vmem()],
        [
            scratch(SUBS * SUBS * SUBS, LANES),
            scratch(SUBS * 24, LANES),
            scratch(24, LANES),
            scratch(per_device, LANES),
            scratch(capacity, LANES),
        ],
        cams,
        send_list,
        send_counts,
        params,
        returned,
    )


def solution(mesh):
    in_specs = (
        P(None, ("view", "tile")),
        P(("view", "tile"), None),
        P(("view", "tile"), None),
        P(),
        P("view", None, "tile", None),
        P("view", "tile", None, None),
        P("view", "tile", None),
    )
    out_specs = P(None, ("view", "tile"))
    return jax.shard_map(shards, mesh=mesh, in_specs=in_specs, out_specs=out_specs, check_vma=False)
```

```python
import jax
import jax.numpy as jnp
import numpy as np
from jax import lax
from jax.experimental import pallas as pl
from jax.experimental.pallas import tpu as pltpu
from jax.sharding import PartitionSpec as P

TILE = 16


FOCAL = 1000.0
LOW_PASS = 0.3
SSIM_SHARE = 0.2
SMOOTH_EPS = 1e-06
SSIM_ONE = 0.0001
SSIM_TWO = 0.0009
HARMONIC_ZERO = 0.28209479177387814
HARMONIC_ONE = 0.4886025119029199
HARMONIC_TWO = (
    1.0925484305920792,
    -1.0925484305920792,
    0.31539156525252005,
    -1.0925484305920792,
    0.5462742152960396,
)
HARMONIC_THREE = (
    -0.5900435899266435,
    2.890611442640554,
    -0.4570457994644658,
    0.3731763325901154,
    -0.4570457994644658,
    1.445305721320277,
    -0.5900435899266435,
)


def from_behind(block, axis, distance):
    devices = range(lax.axis_size(axis))
    route = [(i - distance, i) for i in devices if i - distance in devices]
    return lax.ppermute(block, axis, route)


def window_taps():
    offsets_np = np.arange(11) - 5.0
    weights = np.exp(-offsets_np * offsets_np / 4.5)
    weights = weights / weights.sum()
    return [float(weight) for weight in weights]


def matrix_product(left_side, right_side):
    return [
        [
            left_side[row_idx][0] * right_side[0][col_idx]
            + left_side[row_idx][1] * right_side[1][col_idx]
            + left_side[row_idx][2] * right_side[2][col_idx]
            for col_idx in range(3)
        ]
        for row_idx in range(3)
    ]


def rotation(angles):
    cos_a, sin_a = (jnp.cos(angles[0]), jnp.sin(angles[0]))
    cos_b, sin_b = (jnp.cos(angles[1]), jnp.sin(angles[1]))
    cos_c, sin_c = (jnp.cos(angles[2]), jnp.sin(angles[2]))
    about_x = [[1.0, 0.0, 0.0], [0.0, cos_a, -sin_a], [0.0, sin_a, cos_a]]
    about_y = [[cos_b, 0.0, sin_b], [0.0, 1.0, 0.0], [-sin_b, 0.0, cos_b]]
    about_z = [[cos_c, -sin_c, 0.0], [sin_c, cos_c, 0.0], [0.0, 0.0, 1.0]]
    return matrix_product(about_z, matrix_product(about_y, about_x))


def harmonics(dir_x, dir_y, dir_z):
    sq_x, sq_y, sq_z = (dir_x * dir_x, dir_y * dir_y, dir_z * dir_z)
    prod_xy, prod_yz, prod_xz = (dir_x * dir_y, dir_y * dir_z, dir_x * dir_z)
    return [
        HARMONIC_ZERO + 0.0 * dir_x,
        -HARMONIC_ONE * dir_y,
        HARMONIC_ONE * dir_z,
        -HARMONIC_ONE * dir_x,
        HARMONIC_TWO[0] * prod_xy,
        HARMONIC_TWO[1] * prod_yz,
        HARMONIC_TWO[2] * (2.0 * sq_z - sq_x - sq_y),
        HARMONIC_TWO[3] * prod_xz,
        HARMONIC_TWO[4] * (sq_x - sq_y),
        HARMONIC_THREE[0] * dir_y * (3.0 * sq_x - sq_y),
        HARMONIC_THREE[1] * prod_xy * dir_z,
        HARMONIC_THREE[2] * dir_y * (4.0 * sq_z - sq_x - sq_y),
        HARMONIC_THREE[3] * dir_z * (2.0 * sq_z - 3.0 * sq_x - 3.0 * sq_y),
        HARMONIC_THREE[4] * dir_x * (4.0 * sq_z - sq_x - sq_y),
        HARMONIC_THREE[5] * dir_z * (sq_x - sq_y),
        HARMONIC_THREE[6] * dir_x * (sq_x - 3.0 * sq_y),
    ]


LANES = 128
SUBS = 8
GROUP = 16
STEP_ROWS = LANES // GROUP
FEATS = 8
PAIR = 2 * FEATS
OPACITY, COLOUR = 9, 10
COEF_ROWS = 32
JOIN = 4
UNROLL = 8
MOVES = 16
TAPS = 11
DEAD = -1e30
LOG_TOP = float(np.log(0.99))
VMEM_BYTES = 48 * 1024 * 1024


def stepped(total, width, body, state):
    def step(block, held):
        for k in range(width):
            held = body(block * width + k, held)
        return held

    return lax.fori_loop(0, (total + width - 1) // width, step, state)


def lane_spread(index):
    return index // LANES, index % LANES


def take_blocks(read, count, block, place):
    result = jnp.zeros(place.shape, jnp.float32)
    for num in range(count):
        taken = jnp.take_along_axis(read(num), place, axis=1, mode="promise_in_bounds")
        result = jnp.where(block == num, taken, result)
    return result


def take_line(read, count, block, place):
    sub = lax.broadcasted_iota(jnp.int32, (SUBS, LANES), 0)
    result = take_blocks(read, -(-count // SUBS), block // SUBS, place)
    return jnp.sum(jnp.where(sub == block % SUBS, result, 0.0), axis=0, keepdims=True)


def camera_table(camera):
    columns = [camera[:, entry] for entry in range(6)]
    turn = rotation(columns[0:3])
    shift = columns[3:6]
    anchor = [
        -(turn[0][c] * shift[0] + turn[1][c] * shift[1] + turn[2][c] * shift[2]) for c in range(3)
    ]
    flat = [turn[r][c] for r in range(3) for c in range(3)] + shift + anchor
    return jnp.stack(flat + [jnp.zeros_like(shift[0])], axis=1)


def covariance(params):
    scales = [jnp.exp(params[3 + axis_num]) for axis_num in range(3)]
    inv_norm = 1.0 / jnp.sqrt(
        params[6] * params[6]
        + params[7] * params[7]
        + params[8] * params[8]
        + params[9] * params[9]
    )
    quat_w, quat_x, quat_y, quat_z = [params[6 + k] * inv_norm for k in range(4)]
    quat_rot = [
        [
            1.0 - 2.0 * (quat_y * quat_y + quat_z * quat_z),
            2.0 * (quat_x * quat_y - quat_w * quat_z),
            2.0 * (quat_x * quat_z + quat_w * quat_y),
        ],
        [
            2.0 * (quat_x * quat_y + quat_w * quat_z),
            1.0 - 2.0 * (quat_x * quat_x + quat_z * quat_z),
            2.0 * (quat_y * quat_z - quat_w * quat_x),
        ],
        [
            2.0 * (quat_x * quat_z - quat_w * quat_y),
            2.0 * (quat_y * quat_z + quat_w * quat_x),
            1.0 - 2.0 * (quat_x * quat_x + quat_y * quat_y),
        ],
    ]
    root = [[quat_rot[r][c] * scales[c] for c in range(3)] for r in range(3)]
    return [
        root[r][0] * root[k][0] + root[r][1] * root[k][1] + root[r][2] * root[k][2]
        for r, k in ((0, 0), (0, 1), (0, 2), (1, 1), (1, 2), (2, 2))
    ]


def view_colours(params, cam):
    ray = [params[c] - cam[12 + c] for c in range(3)]
    inv_len = 1.0 / jnp.sqrt(ray[0] * ray[0] + ray[1] * ray[1] + ray[2] * ray[2])
    basis = harmonics(ray[0] * inv_len, ray[1] * inv_len, ray[2] * inv_len)
    colours = []
    for channel in range(3):
        summed = 0.5 + HARMONIC_ZERO * params[11 + 16 * channel]
        for harmonic in range(1, 16):
            summed = summed + basis[harmonic] * params[11 + 16 * channel + harmonic]
        colours.append(summed)
    return colours


def footprint(mean, cov, cam, image_width, image_height):
    turn = [[cam[3 * r + c] for c in range(3)] for r in range(3)]
    point = [
        turn[r][0] * mean[0] + turn[r][1] * mean[1] + turn[r][2] * mean[2] + cam[9 + r]
        for r in range(3)
    ]
    inv_depth = 1.0 / point[2]
    ratio_x, ratio_y = point[0] * inv_depth, point[1] * inv_depth
    zoom = FOCAL * inv_depth
    row_x = [zoom * (turn[0][c] - ratio_x * turn[2][c]) for c in range(3)]
    row_y = [zoom * (turn[1][c] - ratio_y * turn[2][c]) for c in range(3)]
    full = [[cov[0], cov[1], cov[2]], [cov[1], cov[3], cov[4]], [cov[2], cov[4], cov[5]]]
    spread_x = [
        row_x[0] * full[0][c] + row_x[1] * full[1][c] + row_x[2] * full[2][c] for c in range(3)
    ]
    spread_y = [
        row_y[0] * full[0][c] + row_y[1] * full[1][c] + row_y[2] * full[2][c] for c in range(3)
    ]
    cov_xx = spread_x[0] * row_x[0] + spread_x[1] * row_x[1] + spread_x[2] * row_x[2] + LOW_PASS
    cov_xy = spread_x[0] * row_y[0] + spread_x[1] * row_y[1] + spread_x[2] * row_y[2]
    cov_yy = spread_y[0] * row_y[0] + spread_y[1] * row_y[1] + spread_y[2] * row_y[2] + LOW_PASS
    inv_det = 1.0 / (cov_xx * cov_yy - cov_xy * cov_xy)
    return [
        FOCAL * ratio_x + image_width / 2.0,
        FOCAL * ratio_y + image_height / 2.0,
        cov_yy * inv_det,
        -cov_xy * inv_det,
        cov_xx * inv_det,
    ]


def log_opacity(logit):
    return LOG_TOP - jnp.log(1.0 + jnp.exp(-logit))


def load_params(params_ref, tile_scr, block):
    count = params_ref.shape[0]
    for band in range(0, count, SUBS):
        high = min(band + SUBS, count)
        for j in range(SUBS):
            lane_at = pl.multiple_of(block * SUBS * LANES + j * LANES, LANES)
            tile_scr[band * SUBS + j * SUBS : band * SUBS + j * SUBS + high - band, :] = params_ref[
                band:high, pl.ds(lane_at, LANES)
            ]
    return [
        tile_scr[pl.ds((r // SUBS) * SUBS * SUBS + r % SUBS, SUBS, stride=SUBS), :]
        for r in range(count)
    ]


def source_kernel(
    sizes, cam_ref, counts_ref, list_ref, params_ref, out_ref, tile_scr, table
):
    groups, rows, cap, lane_len = sizes
    per = params_ref.shape[1]
    parts = cap // lane_len
    used = (1 + groups) * FEATS
    count_blocks = per // LANES

    def project_block(block, carry):
        params = load_params(params_ref, tile_scr, block)
        at = block * SUBS * used
        shared = params[0:3] + covariance(params) + [log_opacity(params[10])]
        for num, value in enumerate(shared[0:FEATS]):
            table[pl.ds(at + num, SUBS, stride=used), :] = value
        for group in range(groups):
            lines = shared[FEATS:]
            for view in range(2):
                lines = lines + view_colours(
                    params, [cam_ref[2 * group + view, k] for k in range(15)]
                )
            for num, value in enumerate(lines):
                table[pl.ds(at + (1 + group) * FEATS + num, SUBS, stride=used), :] = value
        return carry

    lax.fori_loop(0, per // (SUBS * LANES), project_block, 0)
    lane = lax.broadcasted_iota(jnp.int32, (SUBS, LANES), 1)

    def send_block(dest, start_at):
        count = counts_ref[0, dest]
        line = pl.multiple_of((1 + dest // rows) * FEATS, FEATS)
        for part in range(parts):

            @pl.when(count > part * lane_len)
            def _(part=part):
                first = start_at + part * lane_len
                block, turn = first // LANES, first % LANES
                pieces = []
                for step in range(2):
                    at = jnp.minimum(block + step, count_blocks - 1) * LANES
                    names = list_ref[0:1, pl.ds(pl.multiple_of(at, LANES), LANES)]
                    pieces.append(
                        pltpu.roll(jnp.broadcast_to(names, (SUBS, LANES)), LANES - turn, 1)
                    )
                index = jnp.where(lane < LANES - turn, pieces[0], pieces[1])
                home, place = lane_spread(index)
                for side in range(2):
                    at = line if side else 0
                    taken = take_blocks(
                        lambda num, at=at: table[pl.ds(num * used + at, FEATS), :],
                        count_blocks,
                        home,
                        place,
                    )
                    line_at = part * PAIR + side * FEATS
                    out_ref[dest, line_at : line_at + FEATS, :] = taken[:, 0:lane_len]

        return start_at + count

    lax.fori_loop(0, groups * rows, send_block, jnp.int32(0))


def split_three(value):
    first = value.astype(jnp.bfloat16).astype(jnp.float32)
    rest = value - first
    second = rest.astype(jnp.bfloat16).astype(jnp.float32)
    return [first, second, rest - second]


def in_two(value):
    high = value.astype(jnp.bfloat16).astype(jnp.float32)
    return [high, value - high]


def swap_grain(cells):
    sub = lax.broadcasted_iota(jnp.int32, (SUBS, LANES), 0)
    lane = lax.broadcasted_iota(jnp.int32, (SUBS, LANES), 1) // TILE
    for bit in (1, 2, 4):
        sub_bit, lane_bit = (sub & bit) != 0, (lane & bit) != 0
        from_high = pltpu.roll(pltpu.roll(cells, SUBS - bit, 0), bit * TILE, 1)
        from_low = pltpu.roll(pltpu.roll(cells, bit, 0), LANES - bit * TILE, 1)
        cells = jnp.where(sub_bit == lane_bit, cells, jnp.where(lane_bit, from_high, from_low))
    return cells


def longest(lens_ref, group):
    most = lens_ref[group * GROUP]
    for t in range(1, GROUP):
        most = jnp.maximum(most, lens_ref[group * GROUP + t])
    return most


def gather_slots(arrived_ref, slot_scr, lane_len):
    parts = arrived_ref.shape[1] // PAIR
    joined = LANES // lane_len

    def unpack(block, carry):
        line_at = pl.multiple_of(block * PAIR, PAIR)
        for k in range(joined):
            source = block * joined // parts + k
            part_at = pl.multiple_of(block * joined % parts * PAIR, PAIR)
            slot_scr[pl.ds(line_at, PAIR), k * lane_len : (k + 1) * lane_len] = arrived_ref[
                source, pl.ds(part_at, PAIR), :
            ]
        return carry

    lax.fori_loop(0, slot_scr.shape[0] // PAIR, unpack, 0)


def slot_lines(slot_scr, first):
    return [slot_scr[pl.ds(first * PAIR + num, SUBS, stride=PAIR), :] for num in range(PAIR)]


def render_kernel(
    sizes,
    place_ref,
    cam_ref,
    lens_ref,
    lens_rows_ref,
    names_ref,
    basis_ref,
    arrived_ref,
    image_ref,
    left_ref,
    shape_ref,
    slot_scr,
    table,
    logs,
    feat_scr,
    pieces,
    mm,
):
    cap, lane_len, col_groups, list_len, image_width, image_height = sizes
    devices = arrived_ref.shape[0]
    blocks = list_len // STEP_ROWS
    count_blocks = devices * cap // LANES
    gather_slots(arrived_ref, slot_scr, lane_len)

    def project_block(step, carry):
        first = step * SUBS
        lines = slot_lines(slot_scr, first)
        logs[pl.ds(pl.multiple_of(first, SUBS), SUBS), :] = lines[OPACITY]
        for view in range(2):
            cam = [cam_ref[2 * place_ref[1] + view, k] for k in range(15)]
            feats = footprint(lines[0:3], lines[3:9], cam, image_width, image_height)
            feats = feats + lines[COLOUR + 3 * view : COLOUR + 3 * view + 3]
            for num, value in enumerate(feats):
                row_at = (view * count_blocks + first) * FEATS + num
                table[pl.ds(row_at, SUBS, stride=FEATS), :] = value
        return carry

    lax.fori_loop(0, count_blocks // SUBS, project_block, 0)
    centre_y = (place_ref[0] * TILE).astype(jnp.float32) + (TILE - 1) / 2.0
    sub = lax.broadcasted_iota(jnp.int32, (blocks, LANES), 0)
    lane = lax.broadcasted_iota(jnp.int32, (blocks, LANES), 1)
    zero = jnp.zeros((GROUP, LANES), jnp.float32)

    def one_group(group, carry):
        view, col_group = group // col_groups, group % col_groups
        most = longest(lens_ref, group)

        def fetch(block, inner):
            names = names_ref[pl.ds(group * blocks + block, 1), :]
            home, place = lane_spread(jnp.broadcast_to(names, (SUBS, LANES)))
            feat_at = pl.multiple_of(block * PAIR, PAIR)
            feat_scr[pl.ds(feat_at, FEATS), :] = take_blocks(
                lambda num: table[
                    pl.ds(pl.multiple_of((view * count_blocks + num) * FEATS, FEATS), FEATS), :
                ],
                count_blocks,
                home,
                place,
            )
            feat_scr[pl.ds(feat_at + FEATS, 1), :] = take_line(
                lambda num: logs[num * SUBS : (num + 1) * SUBS, :], count_blocks, home, place
            )
            return inner

        stepped((most + STEP_ROWS - 1) // STEP_ROWS, 2, fetch, 0)
        feats = [feat_scr[pl.ds(num, blocks, stride=PAIR), :] for num in range(FEATS)]
        log_o = feat_scr[pl.ds(FEATS, blocks, stride=PAIR), :]
        live = sub * STEP_ROWS + lane // GROUP < lens_rows_ref[pl.ds(group, 1), :]
        centre_x = ((col_group * GROUP + lane % GROUP) * TILE).astype(jnp.float32) + (
            TILE - 1
        ) / 2.0
        off_x, off_y = feats[0] - centre_x, feats[1] - centre_y
        lin_x = feats[2] * off_x + feats[3] * off_y
        lin_y = feats[4] * off_y + feats[3] * off_x
        coefs = [
            log_o - 0.5 * (off_x * lin_x + off_y * lin_y),
            lin_x,
            lin_y,
            -0.5 * feats[2],
            -feats[3],
            -0.5 * feats[4],
        ]
        coefs = [
            jnp.where(live, value, DEAD if num == 0 else 0.0) for num, value in enumerate(coefs)
        ]
        lines = [None] * COEF_ROWS
        for num, value in enumerate(coefs):
            for piece, part in enumerate(split_three(value)):
                lines[piece * 6 + num] = part
        for num in range(3):
            for piece, part in enumerate(split_three(jnp.where(live, feats[5 + num], 0.0))):
                lines[18 + piece * 3 + num] = part
        for num, value in enumerate(lines):
            pieces[pl.ds(num, blocks, stride=COEF_ROWS), :] = (
                jnp.zeros((blocks, LANES), jnp.float32) if value is None else value
            )
        for num, value in enumerate(feats[2:5] + [off_x, off_y]):
            shape_ref[num, pl.ds(pl.multiple_of(group * blocks, blocks), blocks), :] = jnp.where(
                live, value, 0.0
            )
        left_at = pl.multiple_of(group * blocks * LANES, LANES)
        for block in range(blocks):
            left_ref[pl.ds(left_at + block * LANES, LANES), :] = pieces[
                block * COEF_ROWS : (block + 1) * COEF_ROWS, :
            ].T.astype(jnp.bfloat16)
        expand(left_ref, basis_ref, mm, left_at)

        def entry(n, state):
            keep, colour = state
            row_at = pl.multiple_of(n * GROUP, GROUP)
            shade = [
                mm[pl.ds(row_at, GROUP), (2 + c) * LANES : (3 + c) * LANES] for c in range(3)
            ]
            new_keep, new_colour = [], []
            for half in range(2):
                alpha = jnp.exp(mm[pl.ds(row_at, GROUP), half * LANES : (half + 1) * LANES])
                weight = keep[half] * alpha
                new_keep.append(keep[half] * (1.0 - alpha))
                new_colour.append([colour[half][c] + weight * shade[c] for c in range(3)])
            return new_keep, new_colour

        state = ([zero + 1.0] * 2, [[zero] * 3] * 2)
        _, colour = stepped(most, UNROLL, entry, state)
        for side in range(GROUP // SUBS):
            lane_at = pl.multiple_of(col_group * GROUP * TILE + side * LANES, LANES)
            for half in range(2):
                for c in range(3):
                    image_ref[view, c, half * SUBS : (half + 1) * SUBS, pl.ds(lane_at, LANES)] = (
                        swap_grain(colour[half][c][side * SUBS : (side + 1) * SUBS])
                    )
        return carry

    lax.fori_loop(0, 2 * col_groups, one_group, 0)


def expand(left_ref, basis_ref, mm, left_at):
    mm[...] = jnp.dot(
        left_ref[pl.ds(left_at, mm.shape[0]), :],
        basis_ref[...],
        preferred_element_type=jnp.float32,
    )


def back_kernel(
    sizes,
    place_ref,
    cam_ref,
    lens_ref,
    names_ref,
    basis_ref,
    moment_ref,
    left_ref,
    shape_ref,
    arrived_ref,
    grad_ref,
    out_ref,
    mm,
    alphas,
    weights,
    slopes,
    grad_scr,
    mom_scr,
    line_scr,
    masked,
    places,
    total_scr,
    slot_scr,
):
    cap, lane_len, col_groups, list_len, image_width, image_height = sizes
    devices = out_ref.shape[0]
    parts = cap // lane_len
    blocks = list_len // STEP_ROWS
    count_blocks = devices * cap // LANES
    joined = LANES // lane_len
    value_rows = count_blocks * 2 * FEATS
    total_scr[...] = jnp.zeros_like(total_scr)
    line_scr[...] = jnp.zeros_like(line_scr)
    grad_scr[...] = jnp.zeros_like(grad_scr)
    zero = jnp.zeros((GROUP, LANES), jnp.float32)
    sub = lax.broadcasted_iota(jnp.int32, (GROUP, LANES), 0)
    lane = lax.broadcasted_iota(jnp.int32, (GROUP, LANES), 1)
    own_tile = lane % GROUP == sub

    def one_group(group, carry):
        view, col_group = group // col_groups, group % col_groups
        most = longest(lens_ref, group)
        lane_at = pl.multiple_of(col_group * GROUP * TILE, LANES)
        grads = [
            [
                jnp.concatenate(
                    [
                        swap_grain(
                            grad_ref[
                                view,
                                c,
                                half * SUBS : (half + 1) * SUBS,
                                pl.ds(lane_at + side * LANES, LANES),
                            ]
                        )
                        for side in range(GROUP // SUBS)
                    ],
                    axis=0,
                )
                for c in range(3)
            ]
            for half in range(2)
        ]
        for half in range(2):
            for c in range(3):
                for piece, part in enumerate(in_two(grads[half][c])):
                    line = (piece * 3 + c) * GROUP
                    grad_scr[line : line + GROUP, half * LANES : (half + 1) * LANES] = part
        expand(left_ref, basis_ref, mm, pl.multiple_of(group * blocks * LANES, LANES))

        def ahead(n, keep):
            row_at = pl.multiple_of(n * GROUP, GROUP)
            new_keep = []
            for half in range(2):
                lanes = slice(half * LANES, (half + 1) * LANES)
                alpha = jnp.exp(mm[pl.ds(row_at, GROUP), lanes])
                weight = keep[half] * alpha
                alphas[pl.ds(row_at, GROUP), lanes] = alpha
                weights[pl.ds(row_at, GROUP), lanes] = weight
                new_keep.append(keep[half] * (1.0 - alpha))
            return new_keep

        stepped(most, UNROLL, ahead, [zero + 1.0] * 2)

        last = (most + UNROLL - 1) // UNROLL * UNROLL - 1

        def behind(step, seen):
            row_at = pl.multiple_of((last - step) * GROUP, GROUP)
            shade = [
                mm[pl.ds(row_at, GROUP), (2 + c) * LANES : (3 + c) * LANES] for c in range(3)
            ]
            new_seen = []
            for half in range(2):
                lanes = slice(half * LANES, (half + 1) * LANES)
                own = (
                    grads[half][0] * shade[0]
                    + grads[half][1] * shade[1]
                    + grads[half][2] * shade[2]
                )
                alpha = alphas[pl.ds(row_at, GROUP), lanes]
                slopes[pl.ds(row_at, GROUP), lanes] = weights[pl.ds(row_at, GROUP), lanes] * (
                    own - seen[half]
                )
                new_seen.append(seen[half] * (1.0 - alpha) + alpha * own)
            return new_seen

        stepped(most, UNROLL, behind, [zero] * 2)
        total = jnp.zeros((blocks * LANES, LANES), jnp.float32)
        for value, right in (
            (slopes[...], moment_ref[...]),
            (weights[...], grad_scr[...].T.astype(jnp.bfloat16)),
        ):
            high = value.astype(jnp.bfloat16)
            low = (value - high.astype(jnp.float32)).astype(jnp.bfloat16)
            total = total + jnp.dot(high, right, preferred_element_type=jnp.float32)
            total = total + jnp.dot(low, right, preferred_element_type=jnp.float32)
        for block in range(blocks):
            turned = total[block * LANES : (block + 1) * LANES].T
            mom_scr[block * TILE : block * TILE + 8, :] = turned[6 * GROUP : 6 * GROUP + 8]
            for c in range(3):
                summed = (
                    turned[c * GROUP : (c + 1) * GROUP]
                    + turned[(3 + c) * GROUP : (4 + c) * GROUP]
                )
                mom_scr[block * TILE + 8 + c : block * TILE + 9 + c, :] = jnp.sum(
                    jnp.where(own_tile, summed, 0.0), axis=0, keepdims=True
                )
        mom = [mom_scr[pl.ds(num, blocks, stride=TILE), :] for num in range(11)]
        con_xx, con_xy, con_yy, off_x, off_y = [
            shape_ref[num, pl.ds(pl.multiple_of(group * blocks, blocks), blocks), :]
            for num in range(5)
        ]
        sum_x = off_x * mom[0] - mom[1]
        sum_y = off_y * mom[0] - mom[2]
        results = [
            -(con_xx * sum_x + con_xy * sum_y),
            -(con_yy * sum_y + con_xy * sum_x),
            -0.5 * (off_x * (sum_x - mom[1]) + mom[3]),
            -(off_x * sum_y - off_y * mom[1] + mom[4]),
            -0.5 * (off_y * (sum_y - mom[2]) + mom[5]),
        ] + mom[8:11]
        for num, value in enumerate(results + [mom[0]]):
            line_scr[pl.ds(num, blocks, stride=PAIR), :] = value

        def spread(step, inner):
            for k in range(JOIN):
                block = step * JOIN + k
                lanes = slice(k * LANES, (k + 1) * LANES)
                names = names_ref[pl.ds(group * blocks + block, 1), :]
                home, place = names // LANES, names % LANES
                line_at = pl.multiple_of(block * PAIR, PAIR)
                values = in_two(line_scr[pl.ds(line_at, FEATS), :])
                logs = in_two(line_scr[pl.ds(line_at + FEATS, 1), :])
                home_wide = jnp.broadcast_to(home, (2 * FEATS, LANES)).astype(jnp.bfloat16)
                pair = jnp.concatenate(values, axis=0).astype(jnp.bfloat16)
                for num in range(count_blocks):
                    masked[num * 2 * FEATS : (num + 1) * 2 * FEATS, lanes] = jnp.where(
                        home_wide == jnp.bfloat16(num), pair, jnp.bfloat16(0)
                    )
                rank = lax.broadcasted_iota(jnp.int32, (count_blocks, LANES), 0)
                for piece, value in enumerate(logs):
                    first = value_rows + piece * count_blocks
                    masked[first : first + count_blocks, lanes] = jnp.where(
                        rank == home, value, 0.0
                    ).astype(jnp.bfloat16)
                seat = lax.broadcasted_iota(jnp.int32, (LANES, LANES), 0)
                places[:, lanes] = jnp.where(seat == place, 1.0, 0.0).astype(jnp.bfloat16)
            total_scr[view] += lax.dot_general(
                masked[...],
                places[...],
                (((1,), (1,)), ((), ())),
                preferred_element_type=jnp.float32,
            )
            return inner

        width = JOIN * STEP_ROWS
        lax.fori_loop(0, (most + width - 1) // width, spread, 0)
        return carry

    lax.fori_loop(0, 2 * col_groups, one_group, 0)

    gather_slots(arrived_ref, slot_scr, lane_len)

    def pull_block(step, carry):
        first = step * SUBS
        lines = slot_lines(slot_scr, first)
        cams = [[cam_ref[2 * place_ref[1] + view, k] for k in range(15)] for view in range(2)]

        def both(*values):
            return [
                footprint(values[0:3], values[3:9], cam, image_width, image_height)
                for cam in cams
            ]

        cots = []
        log_sum = jnp.zeros((SUBS, LANES), jnp.float32)
        for view in range(2):
            row_at = first * 2 * FEATS
            cots.append(
                [
                    total_scr[view, pl.ds(row_at + num, SUBS, stride=2 * FEATS), :]
                    + total_scr[view, pl.ds(row_at + FEATS + num, SUBS, stride=2 * FEATS), :]
                    for num in range(FEATS)
                ]
            )
            for piece in range(2):
                row = pl.multiple_of(value_rows + piece * count_blocks + first, SUBS)
                log_sum = log_sum + total_scr[view, pl.ds(row, SUBS), :]
        _, pull = jax.vjp(both, *lines[0:9])
        results = list(pull([cot[0:5] for cot in cots])) + [log_sum] + cots[0][5:] + cots[1][5:]
        for num, value in enumerate(results):
            slot_scr[pl.ds(first * PAIR + num, SUBS, stride=PAIR), :] = value
        return carry

    lax.fori_loop(0, count_blocks // SUBS, pull_block, 0)

    def pack(block, carry):
        line_at = pl.multiple_of(block * PAIR, PAIR)
        for k in range(joined):
            source = block * joined // parts + k
            part_at = pl.multiple_of(block * joined % parts * PAIR, PAIR)
            out_ref[source, pl.ds(part_at, PAIR), :] = slot_scr[
                pl.ds(line_at, PAIR), k * lane_len : (k + 1) * lane_len
            ]
        return carry

    lax.fori_loop(0, count_blocks, pack, 0)


def owner_kernel(
    sizes,
    cam_ref,
    list_ref,
    counts_ref,
    params_ref,
    back_ref,
    out_ref,
    tile_scr,
    feat_scr,
    turn_scr,
    table,
    slots,
):
    groups, rows, cap, lane_len = sizes
    count_params, per = params_ref.shape
    parts = cap // lane_len
    table[...] = jnp.zeros_like(table)
    turn_scr[...] = jnp.zeros_like(turn_scr)
    start = jnp.int32(0)
    for group in range(groups):
        turn_scr[PAIR : PAIR + 1, :] = jnp.full((1, LANES), 1.0 + group, jnp.float32)

        def take_block(t, start_at, group=group):
            dest = group * rows + t
            count = counts_ref[0, dest]

            for part in range(parts):
                turn_scr[0:PAIR, 0:lane_len] = back_ref[dest, part * PAIR : (part + 1) * PAIR, :]
                slots[part * lane_len : (part + 1) * lane_len, 0:24] = turn_scr[
                    :, 0:lane_len
                ].T

            def move(k, carry):
                spot = list_ref[0, start_at + k]
                table[pl.ds(spot, 1), :] = slots[pl.ds(k, 1), :]
                return carry

            rounded = (count + MOVES - 1) // MOVES * MOVES
            whole = jnp.where(start_at + rounded <= per, rounded, count // MOVES * MOVES)
            stepped(whole, MOVES, move, 0)
            lax.fori_loop(whole, count, move, 0)
            return start_at + count

        start = lax.fori_loop(0, rows, take_block, start)

    def clear(k, carry):
        table[pl.ds(list_ref[0, k], 1), :] = jnp.zeros((1, LANES), jnp.float32)
        return carry

    lax.fori_loop(start, jnp.minimum(start + MOVES, per), clear, 0)

    def pull_block(block, carry):
        params = load_params(params_ref, tile_scr, block)
        for j in range(SUBS):
            row_at = pl.multiple_of(block * SUBS * LANES + j * LANES, LANES)
            feat_scr[j * 24 : (j + 1) * 24, :] = table[pl.ds(row_at, LANES), 0:24].T
        cots = [feat_scr[pl.ds(num, SUBS, stride=24), :] for num in range(PAIR + 1)]
        home = cots[PAIR]
        sent = home > 0.5
        cams = []
        for view in range(2):
            cam = []
            for k in range(15):
                value = jnp.full((SUBS, LANES), cam_ref[view, k], jnp.float32)
                for group in range(1, groups):
                    value = jnp.where(home > 0.5 + group, cam_ref[2 * group + view, k], value)
                cam.append(value)
            cams.append(cam)

        def both(*values):
            return (
                covariance(values)
                + [log_opacity(values[10])]
                + view_colours(values, cams[0])
                + view_colours(values, cams[1])
            )

        _, pull = jax.vjp(both, *params)
        grads = list(pull(cots[3:PAIR]))
        for num in range(3):
            grads[num] = grads[num] + cots[num]
        for num, value in enumerate(grads):
            tile_scr[pl.ds((num // SUBS) * SUBS * SUBS + num % SUBS, SUBS, stride=SUBS), :] = (
                jnp.where(sent, value, 0.0)
            )
        for band in range(0, count_params, SUBS):
            high = min(band + SUBS, count_params)
            for j in range(SUBS):
                lane_at = pl.multiple_of(block * SUBS * LANES + j * LANES, LANES)
                out_ref[band:high, pl.ds(lane_at, LANES)] = tile_scr[
                    band * SUBS + j * SUBS : band * SUBS + j * SUBS + high - band, :
                ]
        return carry

    lax.fori_loop(0, per // (SUBS * LANES), pull_block, 0)


def tap_rows(read, first, count):
    taps = window_taps()
    total = taps[5] * read(first + 5, count)
    for k in range(5):
        total = total + taps[k] * (read(first + k, count) + read(first + TAPS - 1 - k, count))
    return total


def blur_lanes(value, band):
    return jnp.dot(
        value, band, precision=lax.Precision.HIGHEST, preferred_element_type=jnp.float32
    )


def truth_kernel(band_ref, above_ref, own_ref, below_ref, out_ref, tall, mixed):
    images = own_ref.shape[0]

    def one_image(m, carry):
        whole = jnp.concatenate([above_ref[m], own_ref[m], below_ref[m]], axis=0)
        for field, value in enumerate((whole, whole * whole)):
            tall[...] = value
            row_at = pl.multiple_of((field * images + m) * 2 * TILE, 2 * TILE)
            mixed[pl.ds(row_at, 2 * TILE), :] = tap_rows(
                lambda at, count: tall[at : at + count, :], 6, 2 * TILE
            )
        return carry

    lax.fori_loop(0, images, one_image, 0)
    out_ref[...] = blur_lanes(mixed[...], band_ref[...])


def loss_kernel(
    image_rows,
    row_ref,
    band_ref,
    truth_ref,
    true_above,
    true_own,
    true_below,
    above_ref,
    own_ref,
    below_ref,
    out_ref,
    tall,
    mixed,
    blurred,
    slim,
):
    images = own_ref.shape[0]
    tall_rows = 2 * TILE
    width = own_ref.shape[2]

    def one_image(m, carry):
        whole = jnp.concatenate([above_ref[m], own_ref[m], below_ref[m]], axis=0)
        true = jnp.concatenate([true_above[m], true_own[m], true_below[m]], axis=0)
        for field, value in enumerate((whole, whole * whole, whole * true)):
            tall[field] = value
            row_at = pl.multiple_of((field * images + m) * tall_rows, tall_rows)
            mixed[pl.ds(row_at, tall_rows), :] = tap_rows(
                lambda at, count, field=field: tall[field, at : at + count, :], 6, tall_rows
            )
        return carry

    lax.fori_loop(0, images, one_image, 0)
    blurred[...] = blur_lanes(mixed[...], band_ref[...])
    sub = lax.broadcasted_iota(jnp.int32, (tall_rows, width), 0)
    image_row = row_ref[0] * TILE + sub - 5
    inside = (image_row >= 0) & (image_row < image_rows) & (sub < TILE + 10)

    def one_map(m, carry):
        def field_of(ref, field):
            row_at = pl.multiple_of((field * images + m) * tall_rows, tall_rows)
            return ref[pl.ds(row_at, tall_rows), :]

        mean_one, both_one, cross = [field_of(blurred, field) for field in range(3)]
        mean_two, both_two = field_of(truth_ref, 0), field_of(truth_ref, 1)
        square_one, square_two = mean_one * mean_one, mean_two * mean_two
        mean_cross = mean_one * mean_two
        top_one = 2.0 * mean_cross + SSIM_ONE
        top_two = 2.0 * (cross - mean_cross) + SSIM_TWO
        low_one = square_one + square_two + SSIM_ONE
        low_two = (both_one - square_one) + (both_two - square_two) + SSIM_TWO
        inv_one, inv_two = 1.0 / low_one, 1.0 / low_two
        inv_both = inv_one * inv_two
        value = top_one * top_two * inv_both
        grads = [
            2.0 * mean_two * (top_two - top_one) * inv_both
            - 2.0 * mean_one * value * (inv_one - inv_two),
            -value * inv_two,
            2.0 * top_one * inv_both,
        ]
        for field, grad in enumerate(grads):
            tall[field, 0:tall_rows] = jnp.where(inside, grad, 0.0)
            row_at = pl.multiple_of((field * images + m) * TILE, TILE)
            slim[pl.ds(row_at, TILE), :] = tap_rows(
                lambda at, count, field=field: tall[field, at : at + count, :], 0, TILE
            )
        return carry

    lax.fori_loop(0, images, one_map, 0)
    spread = blur_lanes(slim[...], band_ref[...]).reshape(3, images, TILE, width)
    own, true = own_ref[...], true_own[...]
    gap = own - true
    out_ref[...] = (1.0 - SSIM_SHARE) * gap / jnp.sqrt(gap * gap + SMOOTH_EPS) - SSIM_SHARE * (
        spread[0] + 2.0 * own * spread[1] + true * spread[2]
    )


def band_matrix(width):
    taps = window_taps()
    band = np.zeros((width, width), np.float32)
    for k in range(TAPS):
        band += np.diag(np.full(width - abs(k - 5), taps[k], np.float32), k - 5)
    return jnp.asarray(band)


def pixel_basis():
    pixel = np.arange(TILE * TILE)
    x = (pixel % TILE) - (TILE - 1) / 2.0
    y = (pixel // TILE) - (TILE - 1) / 2.0
    return np.stack([np.ones_like(x), x, y, x * x, x * y, y * y])


def expand_matrix():
    terms = pixel_basis()
    matrix = np.zeros((COEF_ROWS, 5 * LANES), np.float32)
    for piece in range(3):
        matrix[piece * 6 : piece * 6 + 6, 0 : 2 * LANES] = terms
        for c in range(3):
            matrix[18 + piece * 3 + c, (2 + c) * LANES : (3 + c) * LANES] = 1.0
    return jnp.asarray(matrix, jnp.bfloat16)


def moment_matrix():
    matrix = np.zeros((2 * LANES, LANES), np.float32)
    matrix[:, 6 * GROUP : 6 * GROUP + 6] = pixel_basis().T
    return jnp.asarray(matrix, jnp.bfloat16)


def smem():
    return pl.BlockSpec(memory_space=pltpu.SMEM)


def vmem():
    return pl.BlockSpec(memory_space=pltpu.VMEM)


def scratch(*shape):
    return pltpu.VMEM(shape, jnp.float32)


def run(kernel, out_shapes, in_specs, scratches, *operands):
    return pl.pallas_call(
        kernel,
        out_shape=out_shapes,
        in_specs=in_specs,
        out_specs=jax.tree.map(lambda _: vmem(), out_shapes),
        scratch_shapes=scratches,
        compiler_params=pltpu.CompilerParams(vmem_limit_bytes=VMEM_BYTES),
    )(*operands)


def shards(params, send_list, send_counts, camera, ground_truth, tile_lists, list_lengths):
    devices = lax.axis_size(("view", "tile"))
    row_devices = lax.axis_size("tile")
    groups = lax.axis_size("view")
    count_params, per_device = params.shape
    capacity = per_device // devices
    tile_cols, list_len = tile_lists.shape[2:]
    col_groups = tile_cols // GROUP
    blocks = list_len // STEP_ROWS
    tile_row = lax.axis_index("tile")
    image_width = float(ground_truth.shape[3])
    image_height = float(ground_truth.shape[2] * row_devices)
    lane_len = min(capacity, LANES)
    sent_shape = jax.ShapeDtypeStruct(
        (devices, capacity // lane_len * PAIR, lane_len), jnp.float32
    )
    count_blocks = per_device // LANES
    cams = camera_table(camera)

    flat_lengths = list_lengths.reshape(-1)
    entry_rank = jnp.arange(list_len, dtype=jnp.int32)
    tile_num = jnp.arange(2 * tile_cols, dtype=jnp.int32)
    lists = jnp.where(
        entry_rank[None, :] < flat_lengths[:, None],
        tile_lists.reshape(2 * tile_cols, list_len),
        per_device + tile_num[:, None] % GROUP,
    )
    lens_rows = jnp.tile(flat_lengths.reshape(-1, GROUP), (1, LANES // GROUP))

    width = ground_truth.shape[3]
    true_own = ground_truth.reshape(-1, TILE, width)
    true_above = from_behind(true_own, "tile", 1)
    true_below = from_behind(true_own, "tile", -1)
    band = band_matrix(width)
    truth_rows = 2 * true_own.shape[0] * 2 * TILE
    truth_blur = run(
        truth_kernel,
        jax.ShapeDtypeStruct((truth_rows, width), jnp.float32),
        [vmem()] * 4,
        [scratch(3 * TILE, width), scratch(truth_rows, width)],
        band,
        true_above,
        true_own,
        true_below,
    )

    own_sizes = (groups, row_devices, capacity, lane_len)
    sent = run(
        lambda *refs: source_kernel(own_sizes, *refs),
        sent_shape,
        [smem(), smem(), vmem(), vmem()],
        [
            scratch(SUBS * SUBS * SUBS, LANES),
            scratch(count_blocks * (1 + groups) * FEATS, LANES),
        ],
        cams,
        send_counts,
        send_list,
        params,
    )
    arrived = lax.all_to_all(sent, ("view", "tile"), split_axis=0, concat_axis=0, tiled=True)

    arrived, truth_blur = lax.optimization_barrier((arrived, truth_blur))
    tile_sizes = (capacity, lane_len, col_groups, list_len, image_width, image_height)
    place = jnp.stack([tile_row, lax.axis_index("view")])
    entries = 2 * tile_cols * list_len
    names = lists.reshape(-1, GROUP, list_len).transpose(0, 2, 1).reshape(-1, LANES)
    rendered, left, shapes = run(
        lambda *refs: render_kernel(tile_sizes, *refs),
        (
            jax.ShapeDtypeStruct(ground_truth.shape, jnp.float32),
            jax.ShapeDtypeStruct((entries, COEF_ROWS), jnp.bfloat16),
            jax.ShapeDtypeStruct((5, entries // LANES, LANES), jnp.float32),
        ),
        [smem(), smem(), smem(), vmem(), vmem(), vmem(), vmem()],
        [
            scratch(count_blocks * PAIR, LANES),
            scratch(2 * per_device // LANES * FEATS, LANES),
            scratch(count_blocks, LANES),
            scratch(blocks * PAIR, LANES),
            scratch(blocks * COEF_ROWS, LANES),
            scratch(blocks * LANES, 5 * LANES),
        ],
        place,
        cams,
        flat_lengths,
        lens_rows,
        names,
        expand_matrix(),
        arrived,
    )

    images = rendered.reshape(true_own.shape)
    count = images.shape[0]
    grad_image = run(
        lambda *refs: loss_kernel(TILE * row_devices, *refs),
        jax.ShapeDtypeStruct(images.shape, jnp.float32),
        [smem()] + [vmem()] * 8,
        [
            scratch(3, 3 * TILE, width),
            scratch(3 * count * 2 * TILE, width),
            scratch(3 * count * 2 * TILE, width),
            scratch(3 * count * TILE, width),
        ],
        place,
        band,
        truth_blur,
        true_above,
        true_own,
        true_below,
        from_behind(images, "tile", 1),
        images,
        from_behind(images, "tile", -1),
    ).reshape(ground_truth.shape)

    spread_rows = count_blocks * (2 * FEATS + 2)
    grad_slots = run(
        lambda *refs: back_kernel(tile_sizes, *refs),
        sent_shape,
        [smem()] * 3 + [vmem()] * 7,
        [
            scratch(blocks * LANES, 5 * LANES),
            scratch(blocks * LANES, 2 * LANES),
            scratch(blocks * LANES, 2 * LANES),
            scratch(blocks * LANES, 2 * LANES),
            scratch(LANES, 2 * LANES),
            scratch(blocks * TILE, LANES),
            scratch(blocks * PAIR, LANES),
            pltpu.VMEM((spread_rows, JOIN * LANES), jnp.bfloat16),
            pltpu.VMEM((LANES, JOIN * LANES), jnp.bfloat16),
            scratch(2, spread_rows, LANES),
            scratch(count_blocks * PAIR, LANES),
        ],
        place,
        cams,
        flat_lengths,
        names,
        expand_matrix(),
        moment_matrix(),
        left,
        shapes,
        arrived,
        grad_image,
    )
    returned = lax.all_to_all(
        grad_slots, ("view", "tile"), split_axis=0, concat_axis=0, tiled=True
    )
    return run(
        lambda *refs: owner_kernel(own_sizes, *refs),
        jax.ShapeDtypeStruct(params.shape, jnp.float32),
        [smem(), smem(), smem(), vmem(), vmem()],
        [
            scratch(SUBS * SUBS * SUBS, LANES),
            scratch(SUBS * 24, LANES),
            scratch(24, LANES),
            scratch(per_device, LANES),
            scratch(capacity, LANES),
        ],
        cams,
        send_list,
        send_counts,
        params,
        returned,
    )


def solution(mesh):
    in_specs = (
        P(None, ("view", "tile")),
        P(("view", "tile"), None),
        P(("view", "tile"), None),
        P(),
        P("view", None, "tile", None),
        P("view", "tile", None, None),
        P("view", "tile", None),
    )
    out_specs = P(None, ("view", "tile"))
    return jax.shard_map(shards, mesh=mesh, in_specs=in_specs, out_specs=out_specs, check_vma=False)
```

```python
import jax
import jax.numpy as jnp
import numpy as np
from jax import lax
from jax.experimental import pallas as pl
from jax.experimental.pallas import tpu as pltpu
from jax.sharding import PartitionSpec as P

TILE = 16


FOCAL = 1000.0
LOW_PASS = 0.3
SSIM_SHARE = 0.2
SMOOTH_EPS = 1e-06
SSIM_ONE = 0.0001
SSIM_TWO = 0.0009
HARMONIC_ZERO = 0.28209479177387814
HARMONIC_ONE = 0.4886025119029199
HARMONIC_TWO = (
    1.0925484305920792,
    -1.0925484305920792,
    0.31539156525252005,
    -1.0925484305920792,
    0.5462742152960396,
)
HARMONIC_THREE = (
    -0.5900435899266435,
    2.890611442640554,
    -0.4570457994644658,
    0.3731763325901154,
    -0.4570457994644658,
    1.445305721320277,
    -0.5900435899266435,
)


def from_behind(block, axis, distance):
    devices = range(lax.axis_size(axis))
    route = [(i - distance, i) for i in devices if i - distance in devices]
    return lax.ppermute(block, axis, route)


def window_taps():
    offsets_np = np.arange(11) - 5.0
    weights = np.exp(-offsets_np * offsets_np / 4.5)
    weights = weights / weights.sum()
    return [float(weight) for weight in weights]


def matrix_product(left_side, right_side):
    return [
        [
            left_side[row_idx][0] * right_side[0][col_idx]
            + left_side[row_idx][1] * right_side[1][col_idx]
            + left_side[row_idx][2] * right_side[2][col_idx]
            for col_idx in range(3)
        ]
        for row_idx in range(3)
    ]


def rotation(angles):
    cos_a, sin_a = (jnp.cos(angles[0]), jnp.sin(angles[0]))
    cos_b, sin_b = (jnp.cos(angles[1]), jnp.sin(angles[1]))
    cos_c, sin_c = (jnp.cos(angles[2]), jnp.sin(angles[2]))
    about_x = [[1.0, 0.0, 0.0], [0.0, cos_a, -sin_a], [0.0, sin_a, cos_a]]
    about_y = [[cos_b, 0.0, sin_b], [0.0, 1.0, 0.0], [-sin_b, 0.0, cos_b]]
    about_z = [[cos_c, -sin_c, 0.0], [sin_c, cos_c, 0.0], [0.0, 0.0, 1.0]]
    return matrix_product(about_z, matrix_product(about_y, about_x))


def harmonics(dir_x, dir_y, dir_z):
    sq_x, sq_y, sq_z = (dir_x * dir_x, dir_y * dir_y, dir_z * dir_z)
    prod_xy, prod_yz, prod_xz = (dir_x * dir_y, dir_y * dir_z, dir_x * dir_z)
    return [
        HARMONIC_ZERO + 0.0 * dir_x,
        -HARMONIC_ONE * dir_y,
        HARMONIC_ONE * dir_z,
        -HARMONIC_ONE * dir_x,
        HARMONIC_TWO[0] * prod_xy,
        HARMONIC_TWO[1] * prod_yz,
        HARMONIC_TWO[2] * (2.0 * sq_z - sq_x - sq_y),
        HARMONIC_TWO[3] * prod_xz,
        HARMONIC_TWO[4] * (sq_x - sq_y),
        HARMONIC_THREE[0] * dir_y * (3.0 * sq_x - sq_y),
        HARMONIC_THREE[1] * prod_xy * dir_z,
        HARMONIC_THREE[2] * dir_y * (4.0 * sq_z - sq_x - sq_y),
        HARMONIC_THREE[3] * dir_z * (2.0 * sq_z - 3.0 * sq_x - 3.0 * sq_y),
        HARMONIC_THREE[4] * dir_x * (4.0 * sq_z - sq_x - sq_y),
        HARMONIC_THREE[5] * dir_z * (sq_x - sq_y),
        HARMONIC_THREE[6] * dir_x * (sq_x - 3.0 * sq_y),
    ]


LANES = 128
SUBS = 8
GROUP = 16
STEP_ROWS = LANES // GROUP
FEATS = 8
PAIR = 2 * FEATS
OPACITY, COLOUR = 9, 10
COEF_ROWS = 32
JOIN = 4
UNROLL = 8
TAPS = 11
DEAD = -1e30
LOG_TOP = float(np.log(0.99))
VMEM_BYTES = 48 * 1024 * 1024


def stepped(total, width, body, state):
    def step(block, held):
        for k in range(width):
            held = body(block * width + k, held)
        return held

    return lax.fori_loop(0, (total + width - 1) // width, step, state)


def lane_spread(index):
    return index // LANES, index % LANES


def take_blocks(read, count, block, place):
    result = jnp.zeros(place.shape, jnp.float32)
    for num in range(count):
        taken = jnp.take_along_axis(read(num), place, axis=1, mode="promise_in_bounds")
        result = jnp.where(block == num, taken, result)
    return result


def take_line(read, count, block, place):
    sub = lax.broadcasted_iota(jnp.int32, (SUBS, LANES), 0)
    result = take_blocks(read, -(-count // SUBS), block // SUBS, place)
    return jnp.sum(jnp.where(sub == block % SUBS, result, 0.0), axis=0, keepdims=True)


def camera_table(camera):
    columns = [camera[:, entry] for entry in range(6)]
    turn = rotation(columns[0:3])
    shift = columns[3:6]
    anchor = [
        -(turn[0][c] * shift[0] + turn[1][c] * shift[1] + turn[2][c] * shift[2]) for c in range(3)
    ]
    flat = [turn[r][c] for r in range(3) for c in range(3)] + shift + anchor
    return jnp.stack(flat + [jnp.zeros_like(shift[0])], axis=1)


def covariance(params):
    scales = [jnp.exp(params[3 + axis_num]) for axis_num in range(3)]
    inv_norm = 1.0 / jnp.sqrt(
        params[6] * params[6]
        + params[7] * params[7]
        + params[8] * params[8]
        + params[9] * params[9]
    )
    quat_w, quat_x, quat_y, quat_z = [params[6 + k] * inv_norm for k in range(4)]
    quat_rot = [
        [
            1.0 - 2.0 * (quat_y * quat_y + quat_z * quat_z),
            2.0 * (quat_x * quat_y - quat_w * quat_z),
            2.0 * (quat_x * quat_z + quat_w * quat_y),
        ],
        [
            2.0 * (quat_x * quat_y + quat_w * quat_z),
            1.0 - 2.0 * (quat_x * quat_x + quat_z * quat_z),
            2.0 * (quat_y * quat_z - quat_w * quat_x),
        ],
        [
            2.0 * (quat_x * quat_z - quat_w * quat_y),
            2.0 * (quat_y * quat_z + quat_w * quat_x),
            1.0 - 2.0 * (quat_x * quat_x + quat_y * quat_y),
        ],
    ]
    root = [[quat_rot[r][c] * scales[c] for c in range(3)] for r in range(3)]
    return [
        root[r][0] * root[k][0] + root[r][1] * root[k][1] + root[r][2] * root[k][2]
        for r, k in ((0, 0), (0, 1), (0, 2), (1, 1), (1, 2), (2, 2))
    ]


def view_basis(mean, cam):
    ray = [mean[c] - cam[12 + c] for c in range(3)]
    inv_len = 1.0 / jnp.sqrt(ray[0] * ray[0] + ray[1] * ray[1] + ray[2] * ray[2])
    return harmonics(ray[0] * inv_len, ray[1] * inv_len, ray[2] * inv_len)[1:]


def view_colours(params, cam):
    basis = [HARMONIC_ZERO] + view_basis(params[0:3], cam)
    colours = []
    for channel in range(3):
        summed = 0.5 + HARMONIC_ZERO * params[11 + 16 * channel]
        for harmonic in range(1, 16):
            summed = summed + basis[harmonic] * params[11 + 16 * channel + harmonic]
        colours.append(summed)
    return colours


def footprint(mean, cov, cam, image_width, image_height):
    turn = [[cam[3 * r + c] for c in range(3)] for r in range(3)]
    point = [
        turn[r][0] * mean[0] + turn[r][1] * mean[1] + turn[r][2] * mean[2] + cam[9 + r]
        for r in range(3)
    ]
    inv_depth = 1.0 / point[2]
    ratio_x, ratio_y = point[0] * inv_depth, point[1] * inv_depth
    zoom = FOCAL * inv_depth
    row_x = [zoom * (turn[0][c] - ratio_x * turn[2][c]) for c in range(3)]
    row_y = [zoom * (turn[1][c] - ratio_y * turn[2][c]) for c in range(3)]
    full = [[cov[0], cov[1], cov[2]], [cov[1], cov[3], cov[4]], [cov[2], cov[4], cov[5]]]
    spread_x = [
        row_x[0] * full[0][c] + row_x[1] * full[1][c] + row_x[2] * full[2][c] for c in range(3)
    ]
    spread_y = [
        row_y[0] * full[0][c] + row_y[1] * full[1][c] + row_y[2] * full[2][c] for c in range(3)
    ]
    cov_xx = spread_x[0] * row_x[0] + spread_x[1] * row_x[1] + spread_x[2] * row_x[2] + LOW_PASS
    cov_xy = spread_x[0] * row_y[0] + spread_x[1] * row_y[1] + spread_x[2] * row_y[2]
    cov_yy = spread_y[0] * row_y[0] + spread_y[1] * row_y[1] + spread_y[2] * row_y[2] + LOW_PASS
    inv_det = 1.0 / (cov_xx * cov_yy - cov_xy * cov_xy)
    return [
        FOCAL * ratio_x + image_width / 2.0,
        FOCAL * ratio_y + image_height / 2.0,
        cov_yy * inv_det,
        -cov_xy * inv_det,
        cov_xx * inv_det,
    ]


def log_opacity(logit):
    return LOG_TOP - jnp.log(1.0 + jnp.exp(-logit))


def load_params(params_ref, tile_scr, block, count):
    for band in range(0, count, SUBS):
        high = min(band + SUBS, count)
        for j in range(SUBS):
            lane_at = pl.multiple_of(block * SUBS * LANES + j * LANES, LANES)
            tile_scr[band * SUBS + j * SUBS : band * SUBS + j * SUBS + high - band, :] = params_ref[
                band:high, pl.ds(lane_at, LANES)
            ]
    return [
        tile_scr[pl.ds((r // SUBS) * SUBS * SUBS + r % SUBS, SUBS, stride=SUBS), :]
        for r in range(count)
    ]


def source_kernel(
    sizes, cam_ref, counts_ref, list_ref, params_ref, out_ref, tile_scr, table
):
    groups, rows, cap, lane_len = sizes
    per = params_ref.shape[1]
    parts = cap // lane_len
    used = (1 + groups) * FEATS
    count_blocks = per // LANES

    def project_block(block, carry):
        params = load_params(params_ref, tile_scr, block, params_ref.shape[0])
        at = block * SUBS * used
        shared = params[0:3] + covariance(params) + [log_opacity(params[10])]
        for num, value in enumerate(shared[0:FEATS]):
            table[pl.ds(at + num, SUBS, stride=used), :] = value
        for group in range(groups):
            lines = shared[FEATS:]
            for view in range(2):
                lines = lines + view_colours(
                    params, [cam_ref[2 * group + view, k] for k in range(15)]
                )
            for num, value in enumerate(lines):
                table[pl.ds(at + (1 + group) * FEATS + num, SUBS, stride=used), :] = value
        return carry

    lax.fori_loop(0, per // (SUBS * LANES), project_block, 0)
    lane = lax.broadcasted_iota(jnp.int32, (SUBS, LANES), 1)

    def send_block(dest, start_at):
        count = counts_ref[0, dest]
        line = pl.multiple_of((1 + dest // rows) * FEATS, FEATS)
        for part in range(parts):

            @pl.when(count > part * lane_len)
            def _(part=part):
                first = start_at + part * lane_len
                block, turn = first // LANES, first % LANES
                pieces = []
                for step in range(2):
                    at = jnp.minimum(block + step, count_blocks - 1) * LANES
                    names = list_ref[0:1, pl.ds(pl.multiple_of(at, LANES), LANES)]
                    pieces.append(
                        pltpu.roll(jnp.broadcast_to(names, (SUBS, LANES)), LANES - turn, 1)
                    )
                index = jnp.where(lane < LANES - turn, pieces[0], pieces[1])
                home, place = lane_spread(index)
                for side in range(2):
                    at = line if side else 0
                    taken = take_blocks(
                        lambda num, at=at: table[pl.ds(num * used + at, FEATS), :],
                        count_blocks,
                        home,
                        place,
                    )
                    line_at = part * PAIR + side * FEATS
                    out_ref[dest, line_at : line_at + FEATS, :] = taken[:, 0:lane_len]

        return start_at + count

    lax.fori_loop(0, groups * rows, send_block, jnp.int32(0))


def split_three(value):
    first = value.astype(jnp.bfloat16).astype(jnp.float32)
    rest = value - first
    second = rest.astype(jnp.bfloat16).astype(jnp.float32)
    return [first, second, rest - second]


def in_two(value):
    high = value.astype(jnp.bfloat16).astype(jnp.float32)
    return [high, value - high]


def swap_grain(cells):
    sub = lax.broadcasted_iota(jnp.int32, (SUBS, LANES), 0)
    lane = lax.broadcasted_iota(jnp.int32, (SUBS, LANES), 1) // TILE
    for bit in (1, 2, 4):
        sub_bit, lane_bit = (sub & bit) != 0, (lane & bit) != 0
        from_high = pltpu.roll(pltpu.roll(cells, SUBS - bit, 0), bit * TILE, 1)
        from_low = pltpu.roll(pltpu.roll(cells, bit, 0), LANES - bit * TILE, 1)
        cells = jnp.where(sub_bit == lane_bit, cells, jnp.where(lane_bit, from_high, from_low))
    return cells


def longest(lens_ref, group):
    most = lens_ref[group * GROUP]
    for t in range(1, GROUP):
        most = jnp.maximum(most, lens_ref[group * GROUP + t])
    return most


def gather_slots(arrived_ref, slot_scr, lane_len):
    parts = arrived_ref.shape[1] // PAIR
    joined = LANES // lane_len

    def unpack(block, carry):
        line_at = pl.multiple_of(block * PAIR, PAIR)
        for k in range(joined):
            source = block * joined // parts + k
            part_at = pl.multiple_of(block * joined % parts * PAIR, PAIR)
            slot_scr[pl.ds(line_at, PAIR), k * lane_len : (k + 1) * lane_len] = arrived_ref[
                source, pl.ds(part_at, PAIR), :
            ]
        return carry

    lax.fori_loop(0, slot_scr.shape[0] // PAIR, unpack, 0)


def slot_lines(slot_scr, first):
    return [slot_scr[pl.ds(first * PAIR + num, SUBS, stride=PAIR), :] for num in range(PAIR)]


def render_kernel(
    sizes,
    place_ref,
    cam_ref,
    lens_ref,
    lens_rows_ref,
    names_ref,
    basis_ref,
    arrived_ref,
    image_ref,
    left_ref,
    shape_ref,
    slot_scr,
    table,
    logs,
    feat_scr,
    pieces,
    mm,
):
    cap, lane_len, col_groups, list_len, image_width, image_height = sizes
    devices = arrived_ref.shape[0]
    blocks = list_len // STEP_ROWS
    count_blocks = devices * cap // LANES
    gather_slots(arrived_ref, slot_scr, lane_len)

    def project_block(step, carry):
        first = step * SUBS
        lines = slot_lines(slot_scr, first)
        logs[pl.ds(pl.multiple_of(first, SUBS), SUBS), :] = lines[OPACITY]
        for view in range(2):
            cam = [cam_ref[2 * place_ref[1] + view, k] for k in range(15)]
            feats = footprint(lines[0:3], lines[3:9], cam, image_width, image_height)
            feats = feats + lines[COLOUR + 3 * view : COLOUR + 3 * view + 3]
            for num, value in enumerate(feats):
                row_at = (view * count_blocks + first) * FEATS + num
                table[pl.ds(row_at, SUBS, stride=FEATS), :] = value
        return carry

    lax.fori_loop(0, count_blocks // SUBS, project_block, 0)
    centre_y = (place_ref[0] * TILE).astype(jnp.float32) + (TILE - 1) / 2.0
    sub = lax.broadcasted_iota(jnp.int32, (blocks, LANES), 0)
    lane = lax.broadcasted_iota(jnp.int32, (blocks, LANES), 1)
    zero = jnp.zeros((GROUP, LANES), jnp.float32)

    def one_group(group, carry):
        view, col_group = group // col_groups, group % col_groups
        most = longest(lens_ref, group)

        def fetch(block, inner):
            names = names_ref[pl.ds(group * blocks + block, 1), :]
            home, place = lane_spread(jnp.broadcast_to(names, (SUBS, LANES)))
            feat_at = pl.multiple_of(block * PAIR, PAIR)
            feat_scr[pl.ds(feat_at, FEATS), :] = take_blocks(
                lambda num: table[
                    pl.ds(pl.multiple_of((view * count_blocks + num) * FEATS, FEATS), FEATS), :
                ],
                count_blocks,
                home,
                place,
            )
            feat_scr[pl.ds(feat_at + FEATS, 1), :] = take_line(
                lambda num: logs[num * SUBS : (num + 1) * SUBS, :], count_blocks, home, place
            )
            return inner

        stepped((most + STEP_ROWS - 1) // STEP_ROWS, 2, fetch, 0)
        feats = [feat_scr[pl.ds(num, blocks, stride=PAIR), :] for num in range(FEATS)]
        log_o = feat_scr[pl.ds(FEATS, blocks, stride=PAIR), :]
        live = sub * STEP_ROWS + lane // GROUP < lens_rows_ref[pl.ds(group, 1), :]
        centre_x = ((col_group * GROUP + lane % GROUP) * TILE).astype(jnp.float32) + (
            TILE - 1
        ) / 2.0
        off_x, off_y = feats[0] - centre_x, feats[1] - centre_y
        lin_x = feats[2] * off_x + feats[3] * off_y
        lin_y = feats[4] * off_y + feats[3] * off_x
        coefs = [
            log_o - 0.5 * (off_x * lin_x + off_y * lin_y),
            lin_x,
            lin_y,
            -0.5 * feats[2],
            -feats[3],
            -0.5 * feats[4],
        ]
        coefs = [
            jnp.where(live, value, DEAD if num == 0 else 0.0) for num, value in enumerate(coefs)
        ]
        lines = [None] * COEF_ROWS
        for num, value in enumerate(coefs):
            for piece, part in enumerate(split_three(value)):
                lines[piece * 6 + num] = part
        for num in range(3):
            for piece, part in enumerate(split_three(jnp.where(live, feats[5 + num], 0.0))):
                lines[18 + piece * 3 + num] = part
        for num, value in enumerate(lines):
            pieces[pl.ds(num, blocks, stride=COEF_ROWS), :] = (
                jnp.zeros((blocks, LANES), jnp.float32) if value is None else value
            )
        for num, value in enumerate(feats[2:5] + [off_x, off_y]):
            shape_ref[num, pl.ds(pl.multiple_of(group * blocks, blocks), blocks), :] = jnp.where(
                live, value, 0.0
            )
        left_at = pl.multiple_of(group * blocks * LANES, LANES)
        for block in range(blocks):
            left_ref[pl.ds(left_at + block * LANES, LANES), :] = pieces[
                block * COEF_ROWS : (block + 1) * COEF_ROWS, :
            ].T.astype(jnp.bfloat16)
        expand(left_ref, basis_ref, mm, left_at)

        def entry(n, state):
            keep, colour = state
            row_at = pl.multiple_of(n * GROUP, GROUP)
            shade = [
                mm[pl.ds(row_at, GROUP), (2 + c) * LANES : (3 + c) * LANES] for c in range(3)
            ]
            new_keep, new_colour = [], []
            for half in range(2):
                alpha = jnp.exp(mm[pl.ds(row_at, GROUP), half * LANES : (half + 1) * LANES])
                weight = keep[half] * alpha
                new_keep.append(keep[half] * (1.0 - alpha))
                new_colour.append([colour[half][c] + weight * shade[c] for c in range(3)])
            return new_keep, new_colour

        state = ([zero + 1.0] * 2, [[zero] * 3] * 2)
        _, colour = stepped(most, UNROLL, entry, state)
        for side in range(GROUP // SUBS):
            lane_at = pl.multiple_of(col_group * GROUP * TILE + side * LANES, LANES)
            for half in range(2):
                for c in range(3):
                    image_ref[view, c, half * SUBS : (half + 1) * SUBS, pl.ds(lane_at, LANES)] = (
                        swap_grain(colour[half][c][side * SUBS : (side + 1) * SUBS])
                    )
        return carry

    lax.fori_loop(0, 2 * col_groups, one_group, 0)


def expand(left_ref, basis_ref, mm, left_at):
    mm[...] = jnp.dot(
        left_ref[pl.ds(left_at, mm.shape[0]), :],
        basis_ref[...],
        preferred_element_type=jnp.float32,
    )


def back_kernel(
    sizes,
    place_ref,
    cam_ref,
    lens_ref,
    names_ref,
    basis_ref,
    moment_ref,
    left_ref,
    shape_ref,
    arrived_ref,
    grad_ref,
    out_ref,
    mm,
    alphas,
    weights,
    slopes,
    grad_scr,
    mom_scr,
    line_scr,
    masked,
    places,
    total_scr,
    slot_scr,
):
    cap, lane_len, col_groups, list_len, image_width, image_height = sizes
    devices = out_ref.shape[0]
    parts = cap // lane_len
    blocks = list_len // STEP_ROWS
    count_blocks = devices * cap // LANES
    joined = LANES // lane_len
    value_rows = count_blocks * 2 * FEATS
    total_scr[...] = jnp.zeros_like(total_scr)
    line_scr[...] = jnp.zeros_like(line_scr)
    grad_scr[...] = jnp.zeros_like(grad_scr)
    zero = jnp.zeros((GROUP, LANES), jnp.float32)
    sub = lax.broadcasted_iota(jnp.int32, (GROUP, LANES), 0)
    lane = lax.broadcasted_iota(jnp.int32, (GROUP, LANES), 1)
    own_tile = lane % GROUP == sub

    def one_group(group, carry):
        view, col_group = group // col_groups, group % col_groups
        most = longest(lens_ref, group)
        lane_at = pl.multiple_of(col_group * GROUP * TILE, LANES)
        grads = [
            [
                jnp.concatenate(
                    [
                        swap_grain(
                            grad_ref[
                                view,
                                c,
                                half * SUBS : (half + 1) * SUBS,
                                pl.ds(lane_at + side * LANES, LANES),
                            ]
                        )
                        for side in range(GROUP // SUBS)
                    ],
                    axis=0,
                )
                for c in range(3)
            ]
            for half in range(2)
        ]
        for half in range(2):
            for c in range(3):
                for piece, part in enumerate(in_two(grads[half][c])):
                    line = (piece * 3 + c) * GROUP
                    grad_scr[line : line + GROUP, half * LANES : (half + 1) * LANES] = part
        expand(left_ref, basis_ref, mm, pl.multiple_of(group * blocks * LANES, LANES))

        def ahead(n, keep):
            row_at = pl.multiple_of(n * GROUP, GROUP)
            new_keep = []
            for half in range(2):
                lanes = slice(half * LANES, (half + 1) * LANES)
                alpha = jnp.exp(mm[pl.ds(row_at, GROUP), lanes])
                weight = keep[half] * alpha
                alphas[pl.ds(row_at, GROUP), lanes] = alpha
                weights[pl.ds(row_at, GROUP), lanes] = weight
                new_keep.append(keep[half] * (1.0 - alpha))
            return new_keep

        stepped(most, UNROLL, ahead, [zero + 1.0] * 2)

        last = (most + UNROLL - 1) // UNROLL * UNROLL - 1

        def behind(step, seen):
            row_at = pl.multiple_of((last - step) * GROUP, GROUP)
            shade = [
                mm[pl.ds(row_at, GROUP), (2 + c) * LANES : (3 + c) * LANES] for c in range(3)
            ]
            new_seen = []
            for half in range(2):
                lanes = slice(half * LANES, (half + 1) * LANES)
                own = (
                    grads[half][0] * shade[0]
                    + grads[half][1] * shade[1]
                    + grads[half][2] * shade[2]
                )
                alpha = alphas[pl.ds(row_at, GROUP), lanes]
                slopes[pl.ds(row_at, GROUP), lanes] = weights[pl.ds(row_at, GROUP), lanes] * (
                    own - seen[half]
                )
                new_seen.append(seen[half] * (1.0 - alpha) + alpha * own)
            return new_seen

        stepped(most, UNROLL, behind, [zero] * 2)
        total = jnp.zeros((blocks * LANES, LANES), jnp.float32)
        for value, right in (
            (slopes[...], moment_ref[...]),
            (weights[...], grad_scr[...].T.astype(jnp.bfloat16)),
        ):
            high = value.astype(jnp.bfloat16)
            low = (value - high.astype(jnp.float32)).astype(jnp.bfloat16)
            total = total + jnp.dot(high, right, preferred_element_type=jnp.float32)
            total = total + jnp.dot(low, right, preferred_element_type=jnp.float32)
        for block in range(blocks):
            turned = total[block * LANES : (block + 1) * LANES].T
            mom_scr[block * TILE : block * TILE + 8, :] = turned[6 * GROUP : 6 * GROUP + 8]
            for c in range(3):
                summed = (
                    turned[c * GROUP : (c + 1) * GROUP]
                    + turned[(3 + c) * GROUP : (4 + c) * GROUP]
                )
                mom_scr[block * TILE + 8 + c : block * TILE + 9 + c, :] = jnp.sum(
                    jnp.where(own_tile, summed, 0.0), axis=0, keepdims=True
                )
        mom = [mom_scr[pl.ds(num, blocks, stride=TILE), :] for num in range(11)]
        con_xx, con_xy, con_yy, off_x, off_y = [
            shape_ref[num, pl.ds(pl.multiple_of(group * blocks, blocks), blocks), :]
            for num in range(5)
        ]
        sum_x = off_x * mom[0] - mom[1]
        sum_y = off_y * mom[0] - mom[2]
        results = [
            -(con_xx * sum_x + con_xy * sum_y),
            -(con_yy * sum_y + con_xy * sum_x),
            -0.5 * (off_x * (sum_x - mom[1]) + mom[3]),
            -(off_x * sum_y - off_y * mom[1] + mom[4]),
            -0.5 * (off_y * (sum_y - mom[2]) + mom[5]),
        ] + mom[8:11]
        for num, value in enumerate(results + [mom[0]]):
            line_scr[pl.ds(num, blocks, stride=PAIR), :] = value

        def spread(step, inner):
            for k in range(JOIN):
                block = step * JOIN + k
                lanes = slice(k * LANES, (k + 1) * LANES)
                names = names_ref[pl.ds(group * blocks + block, 1), :]
                home, place = names // LANES, names % LANES
                line_at = pl.multiple_of(block * PAIR, PAIR)
                values = in_two(line_scr[pl.ds(line_at, FEATS), :])
                logs = in_two(line_scr[pl.ds(line_at + FEATS, 1), :])
                home_wide = jnp.broadcast_to(home, (2 * FEATS, LANES)).astype(jnp.bfloat16)
                pair = jnp.concatenate(values, axis=0).astype(jnp.bfloat16)
                for num in range(count_blocks):
                    masked[num * 2 * FEATS : (num + 1) * 2 * FEATS, lanes] = jnp.where(
                        home_wide == jnp.bfloat16(num), pair, jnp.bfloat16(0)
                    )
                rank = lax.broadcasted_iota(jnp.int32, (count_blocks, LANES), 0)
                for piece, value in enumerate(logs):
                    first = value_rows + piece * count_blocks
                    masked[first : first + count_blocks, lanes] = jnp.where(
                        rank == home, value, 0.0
                    ).astype(jnp.bfloat16)
                seat = lax.broadcasted_iota(jnp.int32, (LANES, LANES), 0)
                places[:, lanes] = jnp.where(seat == place, 1.0, 0.0).astype(jnp.bfloat16)
            total_scr[view] += lax.dot_general(
                masked[...],
                places[...],
                (((1,), (1,)), ((), ())),
                preferred_element_type=jnp.float32,
            )
            return inner

        width = JOIN * STEP_ROWS
        lax.fori_loop(0, (most + width - 1) // width, spread, 0)
        return carry

    lax.fori_loop(0, 2 * col_groups, one_group, 0)

    gather_slots(arrived_ref, slot_scr, lane_len)

    def pull_block(step, carry):
        first = step * SUBS
        lines = slot_lines(slot_scr, first)
        cams = [[cam_ref[2 * place_ref[1] + view, k] for k in range(15)] for view in range(2)]

        def both(*values):
            return [
                footprint(values[0:3], values[3:9], cam, image_width, image_height)
                for cam in cams
            ]

        cots = []
        log_sum = jnp.zeros((SUBS, LANES), jnp.float32)
        for view in range(2):
            row_at = first * 2 * FEATS
            cots.append(
                [
                    total_scr[view, pl.ds(row_at + num, SUBS, stride=2 * FEATS), :]
                    + total_scr[view, pl.ds(row_at + FEATS + num, SUBS, stride=2 * FEATS), :]
                    for num in range(FEATS)
                ]
            )
            for piece in range(2):
                row = pl.multiple_of(value_rows + piece * count_blocks + first, SUBS)
                log_sum = log_sum + total_scr[view, pl.ds(row, SUBS), :]
        _, pull = jax.vjp(both, *lines[0:9])
        results = list(pull([cot[0:5] for cot in cots])) + [log_sum] + cots[0][5:] + cots[1][5:]
        for num, value in enumerate(results):
            slot_scr[pl.ds(first * PAIR + num, SUBS, stride=PAIR), :] = value
        return carry

    lax.fori_loop(0, count_blocks // SUBS, pull_block, 0)

    def pack(block, carry):
        line_at = pl.multiple_of(block * PAIR, PAIR)
        for k in range(joined):
            source = block * joined // parts + k
            part_at = pl.multiple_of(block * joined % parts * PAIR, PAIR)
            out_ref[source, pl.ds(part_at, PAIR), :] = slot_scr[
                pl.ds(line_at, PAIR), k * lane_len : (k + 1) * lane_len
            ]
        return carry

    lax.fori_loop(0, count_blocks, pack, 0)


def prepare_kernel(
    sizes, cam_ref, counts_ref, list_ref, params_ref, slot_ref, parts_ref, tile_scr, rows_scr
):
    groups, rows, cap = sizes
    per = params_ref.shape[1]
    blocks = per // LANES
    devices = groups * rows
    rank = lax.broadcasted_iota(jnp.int32, (blocks, LANES), 0)
    lane = lax.broadcasted_iota(jnp.int32, (blocks, LANES), 1)
    spot = rank * LANES + lane

    def shift(dest, state):
        start, slots = state
        slack = cap - counts_ref[0, dest - 1]
        start = start + counts_ref[0, dest - 1]
        return start, slots + jnp.where(spot >= start, slack, 0)

    start, slots = lax.fori_loop(1, devices, shift, (jnp.int32(0), spot))
    live = spot < start + counts_ref[0, devices - 1]
    for num, value in enumerate((slots // LANES, slots % LANES, jnp.ones_like(slots))):
        rows_scr[num] = jnp.where(live, value, 0).astype(jnp.float32)

    def place_names(step, total):
        masked, places = [], []
        for k in range(JOIN):
            block = step * JOIN + k
            names = list_ref[0:1, pl.ds(pl.multiple_of(block * LANES, LANES), LANES)]
            home, place = names // LANES, names % LANES
            masked.append(
                jnp.concatenate(
                    [
                        jnp.where(rank == home, rows_scr[num, pl.ds(block, 1), :], 0.0)
                        for num in range(3)
                    ],
                    axis=0,
                ).astype(jnp.bfloat16)
            )
            seat = lax.broadcasted_iota(jnp.int32, (LANES, LANES), 0)
            places.append(jnp.where(seat == place, 1.0, 0.0).astype(jnp.bfloat16))
        return total + lax.dot_general(
            jnp.concatenate(masked, axis=1),
            jnp.concatenate(places, axis=1),
            (((1,), (1,)), ((), ())),
            preferred_element_type=jnp.float32,
        )

    total = lax.fori_loop(
        0, blocks // JOIN, place_names, jnp.zeros((3 * blocks, LANES), jnp.float32)
    )
    own = (total[0:blocks] * LANES + total[blocks : 2 * blocks]).astype(jnp.int32)
    slot_ref[...] = jnp.where(total[2 * blocks :] > 0.5, own, devices * cap)

    def one_block(block, carry):
        params = load_params(params_ref, tile_scr, block, params_ref.shape[0])
        at = pl.multiple_of(block * SUBS, SUBS)
        home = slot_ref[pl.ds(at, SUBS), :] // (rows * cap)
        one, none = jnp.ones((SUBS, LANES), jnp.float32), jnp.zeros((SUBS, LANES), jnp.float32)
        for view in range(2):
            cam = []
            for k in range(15):
                value = jnp.full((SUBS, LANES), cam_ref[view, k], jnp.float32)
                for group in range(1, groups):
                    value = jnp.where(home == group, cam_ref[2 * group + view, k], value)
                cam.append(value)
            first = view * (TILE - 1 + 9)
            for axis in range(3):
                toward = [one if k == axis else none for k in range(3)]
                basis, slopes = jax.jvp(
                    lambda *mean, cam=cam: view_basis(mean, cam), tuple(params[0:3]), tuple(toward)
                )
                if axis == 0:
                    for k in range(15):
                        parts_ref[first + k, pl.ds(at, SUBS), :] = basis[k]
                for channel in range(3):
                    summed = none
                    for k in range(15):
                        summed = summed + slopes[k] * params[12 + 16 * channel + k]
                    parts_ref[first + 15 + 3 * channel + axis, pl.ds(at, SUBS), :] = summed
        return carry

    lax.fori_loop(0, blocks // SUBS, one_block, 0)


def owner_kernel(
    lane_len,
    slot_ref,
    parts_ref,
    params_ref,
    back_ref,
    out_ref,
    tile_scr,
    line_scr,
    slot_scr,
):
    count_params, per = params_ref.shape
    count_blocks = per // LANES
    gather_slots(back_ref, slot_scr, lane_len)

    def pull_block(block, carry):
        at = pl.multiple_of(block * SUBS, SUBS)
        own = slot_ref[pl.ds(at, SUBS), :]

        def fetch(j, inner):
            names = slot_ref[pl.ds(at + j, 1), :]
            home, place = lane_spread(jnp.broadcast_to(names, (SUBS, LANES)))
            for side in range(2):
                line_at = pl.multiple_of(j * PAIR + side * FEATS, FEATS)
                line_scr[pl.ds(line_at, FEATS), :] = take_blocks(
                    lambda num, side=side: slot_scr[
                        num * PAIR + side * FEATS : num * PAIR + (side + 1) * FEATS, :
                    ],
                    count_blocks,
                    home,
                    place,
                )
            return inner

        stepped(SUBS, 2, fetch, 0)
        cots = [line_scr[pl.ds(num, SUBS, stride=PAIR), :] for num in range(PAIR)]
        sent = own < count_blocks * LANES
        params = load_params(params_ref, tile_scr, block, PAIR)

        def both(*values):
            every = params[0:3] + list(values)
            return covariance(every) + [log_opacity(every[10])]

        _, pull = jax.vjp(both, *params[3:11])
        grads = cots[0:3] + list(pull(cots[3:COLOUR])) + [None] * 48
        for channel in range(3):
            tints = [cots[COLOUR + 3 * view + channel] for view in range(2)]
            grads[11 + 16 * channel] = HARMONIC_ZERO * (tints[0] + tints[1])
            for k in range(15):
                grads[12 + 16 * channel + k] = (
                    tints[0] * parts_ref[k, pl.ds(at, SUBS), :]
                    + tints[1] * parts_ref[24 + k, pl.ds(at, SUBS), :]
                )
            for axis in range(3):
                for view in range(2):
                    line = 24 * view + 15 + 3 * channel + axis
                    grads[axis] = grads[axis] + tints[view] * parts_ref[line, pl.ds(at, SUBS), :]
        for num, value in enumerate(grads):
            tile_scr[pl.ds((num // SUBS) * SUBS * SUBS + num % SUBS, SUBS, stride=SUBS), :] = (
                jnp.where(sent, value, 0.0)
            )
        for band in range(0, count_params, SUBS):
            high = min(band + SUBS, count_params)
            for j in range(SUBS):
                lane_at = pl.multiple_of(block * SUBS * LANES + j * LANES, LANES)
                out_ref[band:high, pl.ds(lane_at, LANES)] = tile_scr[
                    band * SUBS + j * SUBS : band * SUBS + j * SUBS + high - band, :
                ]
        return carry

    lax.fori_loop(0, count_blocks // SUBS, pull_block, 0)


def tap_rows(read, first, count):
    taps = window_taps()
    total = taps[5] * read(first + 5, count)
    for k in range(5):
        total = total + taps[k] * (read(first + k, count) + read(first + TAPS - 1 - k, count))
    return total


def blur_lanes(value, band):
    return jnp.dot(
        value, band, precision=lax.Precision.HIGHEST, preferred_element_type=jnp.float32
    )


def truth_kernel(band_ref, above_ref, own_ref, below_ref, out_ref, tall, mixed):
    images = own_ref.shape[0]

    def one_image(m, carry):
        whole = jnp.concatenate([above_ref[m], own_ref[m], below_ref[m]], axis=0)
        for field, value in enumerate((whole, whole * whole)):
            tall[...] = value
            row_at = pl.multiple_of((field * images + m) * 2 * TILE, 2 * TILE)
            mixed[pl.ds(row_at, 2 * TILE), :] = tap_rows(
                lambda at, count: tall[at : at + count, :], 6, 2 * TILE
            )
        return carry

    lax.fori_loop(0, images, one_image, 0)
    out_ref[...] = blur_lanes(mixed[...], band_ref[...])


def loss_kernel(
    image_rows,
    row_ref,
    band_ref,
    truth_ref,
    true_above,
    true_own,
    true_below,
    above_ref,
    own_ref,
    below_ref,
    out_ref,
    tall,
    mixed,
    blurred,
    slim,
):
    images = own_ref.shape[0]
    tall_rows = 2 * TILE
    width = own_ref.shape[2]

    def one_image(m, carry):
        whole = jnp.concatenate([above_ref[m], own_ref[m], below_ref[m]], axis=0)
        true = jnp.concatenate([true_above[m], true_own[m], true_below[m]], axis=0)
        for field, value in enumerate((whole, whole * whole, whole * true)):
            tall[field] = value
            row_at = pl.multiple_of((field * images + m) * tall_rows, tall_rows)
            mixed[pl.ds(row_at, tall_rows), :] = tap_rows(
                lambda at, count, field=field: tall[field, at : at + count, :], 6, tall_rows
            )
        return carry

    lax.fori_loop(0, images, one_image, 0)
    blurred[...] = blur_lanes(mixed[...], band_ref[...])
    sub = lax.broadcasted_iota(jnp.int32, (tall_rows, width), 0)
    image_row = row_ref[0] * TILE + sub - 5
    inside = (image_row >= 0) & (image_row < image_rows) & (sub < TILE + 10)

    def one_map(m, carry):
        def field_of(ref, field):
            row_at = pl.multiple_of((field * images + m) * tall_rows, tall_rows)
            return ref[pl.ds(row_at, tall_rows), :]

        mean_one, both_one, cross = [field_of(blurred, field) for field in range(3)]
        mean_two, both_two = field_of(truth_ref, 0), field_of(truth_ref, 1)
        square_one, square_two = mean_one * mean_one, mean_two * mean_two
        mean_cross = mean_one * mean_two
        top_one = 2.0 * mean_cross + SSIM_ONE
        top_two = 2.0 * (cross - mean_cross) + SSIM_TWO
        low_one = square_one + square_two + SSIM_ONE
        low_two = (both_one - square_one) + (both_two - square_two) + SSIM_TWO
        inv_one, inv_two = 1.0 / low_one, 1.0 / low_two
        inv_both = inv_one * inv_two
        value = top_one * top_two * inv_both
        grads = [
            2.0 * mean_two * (top_two - top_one) * inv_both
            - 2.0 * mean_one * value * (inv_one - inv_two),
            -value * inv_two,
            2.0 * top_one * inv_both,
        ]
        for field, grad in enumerate(grads):
            tall[field, 0:tall_rows] = jnp.where(inside, grad, 0.0)
            row_at = pl.multiple_of((field * images + m) * TILE, TILE)
            slim[pl.ds(row_at, TILE), :] = tap_rows(
                lambda at, count, field=field: tall[field, at : at + count, :], 0, TILE
            )
        return carry

    lax.fori_loop(0, images, one_map, 0)
    spread = blur_lanes(slim[...], band_ref[...]).reshape(3, images, TILE, width)
    own, true = own_ref[...], true_own[...]
    gap = own - true
    out_ref[...] = (1.0 - SSIM_SHARE) * gap / jnp.sqrt(gap * gap + SMOOTH_EPS) - SSIM_SHARE * (
        spread[0] + 2.0 * own * spread[1] + true * spread[2]
    )


def band_matrix(width):
    taps = window_taps()
    band = np.zeros((width, width), np.float32)
    for k in range(TAPS):
        band += np.diag(np.full(width - abs(k - 5), taps[k], np.float32), k - 5)
    return jnp.asarray(band)


def pixel_basis():
    pixel = np.arange(TILE * TILE)
    x = (pixel % TILE) - (TILE - 1) / 2.0
    y = (pixel // TILE) - (TILE - 1) / 2.0
    return np.stack([np.ones_like(x), x, y, x * x, x * y, y * y])


def expand_matrix():
    terms = pixel_basis()
    matrix = np.zeros((COEF_ROWS, 5 * LANES), np.float32)
    for piece in range(3):
        matrix[piece * 6 : piece * 6 + 6, 0 : 2 * LANES] = terms
        for c in range(3):
            matrix[18 + piece * 3 + c, (2 + c) * LANES : (3 + c) * LANES] = 1.0
    return jnp.asarray(matrix, jnp.bfloat16)


def moment_matrix():
    matrix = np.zeros((2 * LANES, LANES), np.float32)
    matrix[:, 6 * GROUP : 6 * GROUP + 6] = pixel_basis().T
    return jnp.asarray(matrix, jnp.bfloat16)


def smem():
    return pl.BlockSpec(memory_space=pltpu.SMEM)


def vmem():
    return pl.BlockSpec(memory_space=pltpu.VMEM)


def scratch(*shape):
    return pltpu.VMEM(shape, jnp.float32)


def run(kernel, out_shapes, in_specs, scratches, *operands):
    return pl.pallas_call(
        kernel,
        out_shape=out_shapes,
        in_specs=in_specs,
        out_specs=jax.tree.map(lambda _: vmem(), out_shapes),
        scratch_shapes=scratches,
        compiler_params=pltpu.CompilerParams(vmem_limit_bytes=VMEM_BYTES),
    )(*operands)


def shards(params, send_list, send_counts, camera, ground_truth, tile_lists, list_lengths):
    devices = lax.axis_size(("view", "tile"))
    row_devices = lax.axis_size("tile")
    groups = lax.axis_size("view")
    count_params, per_device = params.shape
    capacity = per_device // devices
    tile_cols, list_len = tile_lists.shape[2:]
    col_groups = tile_cols // GROUP
    blocks = list_len // STEP_ROWS
    tile_row = lax.axis_index("tile")
    image_width = float(ground_truth.shape[3])
    image_height = float(ground_truth.shape[2] * row_devices)
    lane_len = min(capacity, LANES)
    sent_shape = jax.ShapeDtypeStruct(
        (devices, capacity // lane_len * PAIR, lane_len), jnp.float32
    )
    count_blocks = per_device // LANES
    cams = camera_table(camera)

    flat_lengths = list_lengths.reshape(-1)
    entry_rank = jnp.arange(list_len, dtype=jnp.int32)
    tile_num = jnp.arange(2 * tile_cols, dtype=jnp.int32)
    lists = jnp.where(
        entry_rank[None, :] < flat_lengths[:, None],
        tile_lists.reshape(2 * tile_cols, list_len),
        per_device + tile_num[:, None] % GROUP,
    )
    lens_rows = jnp.tile(flat_lengths.reshape(-1, GROUP), (1, LANES // GROUP))

    width = ground_truth.shape[3]
    true_own = ground_truth.reshape(-1, TILE, width)
    true_above = from_behind(true_own, "tile", 1)
    true_below = from_behind(true_own, "tile", -1)
    band = band_matrix(width)
    truth_rows = 2 * true_own.shape[0] * 2 * TILE
    truth_blur = run(
        truth_kernel,
        jax.ShapeDtypeStruct((truth_rows, width), jnp.float32),
        [vmem()] * 4,
        [scratch(3 * TILE, width), scratch(truth_rows, width)],
        band,
        true_above,
        true_own,
        true_below,
    )

    own_sizes = (groups, row_devices, capacity, lane_len)
    sent = run(
        lambda *refs: source_kernel(own_sizes, *refs),
        sent_shape,
        [smem(), smem(), vmem(), vmem()],
        [
            scratch(SUBS * SUBS * SUBS, LANES),
            scratch(count_blocks * (1 + groups) * FEATS, LANES),
        ],
        cams,
        send_counts,
        send_list,
        params,
    )
    arrived = lax.all_to_all(sent, ("view", "tile"), split_axis=0, concat_axis=0, tiled=True)

    arrived, truth_blur = lax.optimization_barrier((arrived, truth_blur))
    tile_sizes = (capacity, lane_len, col_groups, list_len, image_width, image_height)
    place = jnp.stack([tile_row, lax.axis_index("view")])
    entries = 2 * tile_cols * list_len
    names = lists.reshape(-1, GROUP, list_len).transpose(0, 2, 1).reshape(-1, LANES)
    rendered, left, shapes = run(
        lambda *refs: render_kernel(tile_sizes, *refs),
        (
            jax.ShapeDtypeStruct(ground_truth.shape, jnp.float32),
            jax.ShapeDtypeStruct((entries, COEF_ROWS), jnp.bfloat16),
            jax.ShapeDtypeStruct((5, entries // LANES, LANES), jnp.float32),
        ),
        [smem(), smem(), smem(), vmem(), vmem(), vmem(), vmem()],
        [
            scratch(count_blocks * PAIR, LANES),
            scratch(2 * per_device // LANES * FEATS, LANES),
            scratch(count_blocks, LANES),
            scratch(blocks * PAIR, LANES),
            scratch(blocks * COEF_ROWS, LANES),
            scratch(blocks * LANES, 5 * LANES),
        ],
        place,
        cams,
        flat_lengths,
        lens_rows,
        names,
        expand_matrix(),
        arrived,
    )

    images = rendered.reshape(true_own.shape)
    count = images.shape[0]
    grad_image = run(
        lambda *refs: loss_kernel(TILE * row_devices, *refs),
        jax.ShapeDtypeStruct(images.shape, jnp.float32),
        [smem()] + [vmem()] * 8,
        [
            scratch(3, 3 * TILE, width),
            scratch(3 * count * 2 * TILE, width),
            scratch(3 * count * 2 * TILE, width),
            scratch(3 * count * TILE, width),
        ],
        place,
        band,
        truth_blur,
        true_above,
        true_own,
        true_below,
        from_behind(images, "tile", 1),
        images,
        from_behind(images, "tile", -1),
    ).reshape(ground_truth.shape)

    spread_rows = count_blocks * (2 * FEATS + 2)
    grad_slots = run(
        lambda *refs: back_kernel(tile_sizes, *refs),
        sent_shape,
        [smem()] * 3 + [vmem()] * 7,
        [
            scratch(blocks * LANES, 5 * LANES),
            scratch(blocks * LANES, 2 * LANES),
            scratch(blocks * LANES, 2 * LANES),
            scratch(blocks * LANES, 2 * LANES),
            scratch(LANES, 2 * LANES),
            scratch(blocks * TILE, LANES),
            scratch(blocks * PAIR, LANES),
            pltpu.VMEM((spread_rows, JOIN * LANES), jnp.bfloat16),
            pltpu.VMEM((LANES, JOIN * LANES), jnp.bfloat16),
            scratch(2, spread_rows, LANES),
            scratch(count_blocks * PAIR, LANES),
        ],
        place,
        cams,
        flat_lengths,
        names,
        expand_matrix(),
        moment_matrix(),
        left,
        shapes,
        arrived,
        grad_image,
    )
    grad_slots, late_counts = lax.optimization_barrier((grad_slots, send_counts))
    returned = lax.all_to_all(
        grad_slots, ("view", "tile"), split_axis=0, concat_axis=0, tiled=True
    )
    own_slots, own_parts = run(
        lambda *refs: prepare_kernel((groups, row_devices, capacity), *refs),
        (
            jax.ShapeDtypeStruct((count_blocks, LANES), jnp.int32),
            jax.ShapeDtypeStruct((2 * (TILE - 1 + 9), count_blocks, LANES), jnp.float32),
        ),
        [smem(), smem(), vmem(), vmem()],
        [scratch(SUBS * SUBS * SUBS, LANES), scratch(3, count_blocks, LANES)],
        cams,
        late_counts,
        send_list,
        params,
    )
    return run(
        lambda *refs: owner_kernel(lane_len, *refs),
        jax.ShapeDtypeStruct(params.shape, jnp.float32),
        [vmem()] * 4,
        [
            scratch(SUBS * SUBS * SUBS, LANES),
            scratch(SUBS * PAIR, LANES),
            scratch(count_blocks * PAIR, LANES),
        ],
        own_slots,
        own_parts,
        params,
        returned,
    )


def solution(mesh):
    in_specs = (
        P(None, ("view", "tile")),
        P(("view", "tile"), None),
        P(("view", "tile"), None),
        P(),
        P("view", None, "tile", None),
        P("view", "tile", None, None),
        P("view", "tile", None),
    )
    out_specs = P(None, ("view", "tile"))
    return jax.shard_map(shards, mesh=mesh, in_specs=in_specs, out_specs=out_specs, check_vma=False)
```

```python
import jax
import jax.numpy as jnp
import numpy as np
from jax import lax
from jax.experimental import pallas as pl
from jax.experimental.pallas import tpu as pltpu
from jax.sharding import PartitionSpec as P

TILE = 16


FOCAL = 1000.0
LOW_PASS = 0.3
SSIM_SHARE = 0.2
SMOOTH_EPS = 1e-06
SSIM_ONE = 0.0001
SSIM_TWO = 0.0009
HARMONIC_ZERO = 0.28209479177387814
HARMONIC_ONE = 0.4886025119029199
HARMONIC_TWO = (
    1.0925484305920792,
    -1.0925484305920792,
    0.31539156525252005,
    -1.0925484305920792,
    0.5462742152960396,
)
HARMONIC_THREE = (
    -0.5900435899266435,
    2.890611442640554,
    -0.4570457994644658,
    0.3731763325901154,
    -0.4570457994644658,
    1.445305721320277,
    -0.5900435899266435,
)


def from_behind(block, axis, distance):
    devices = range(lax.axis_size(axis))
    route = [(i - distance, i) for i in devices if i - distance in devices]
    return lax.ppermute(block, axis, route)


def window_taps():
    offsets_np = np.arange(11) - 5.0
    weights = np.exp(-offsets_np * offsets_np / 4.5)
    weights = weights / weights.sum()
    return [float(weight) for weight in weights]


def matrix_product(left_side, right_side):
    return [
        [
            left_side[row_idx][0] * right_side[0][col_idx]
            + left_side[row_idx][1] * right_side[1][col_idx]
            + left_side[row_idx][2] * right_side[2][col_idx]
            for col_idx in range(3)
        ]
        for row_idx in range(3)
    ]


def rotation(angles):
    cos_a, sin_a = (jnp.cos(angles[0]), jnp.sin(angles[0]))
    cos_b, sin_b = (jnp.cos(angles[1]), jnp.sin(angles[1]))
    cos_c, sin_c = (jnp.cos(angles[2]), jnp.sin(angles[2]))
    about_x = [[1.0, 0.0, 0.0], [0.0, cos_a, -sin_a], [0.0, sin_a, cos_a]]
    about_y = [[cos_b, 0.0, sin_b], [0.0, 1.0, 0.0], [-sin_b, 0.0, cos_b]]
    about_z = [[cos_c, -sin_c, 0.0], [sin_c, cos_c, 0.0], [0.0, 0.0, 1.0]]
    return matrix_product(about_z, matrix_product(about_y, about_x))


def harmonics(dir_x, dir_y, dir_z):
    sq_x, sq_y, sq_z = (dir_x * dir_x, dir_y * dir_y, dir_z * dir_z)
    prod_xy, prod_yz, prod_xz = (dir_x * dir_y, dir_y * dir_z, dir_x * dir_z)
    return [
        HARMONIC_ZERO + 0.0 * dir_x,
        -HARMONIC_ONE * dir_y,
        HARMONIC_ONE * dir_z,
        -HARMONIC_ONE * dir_x,
        HARMONIC_TWO[0] * prod_xy,
        HARMONIC_TWO[1] * prod_yz,
        HARMONIC_TWO[2] * (2.0 * sq_z - sq_x - sq_y),
        HARMONIC_TWO[3] * prod_xz,
        HARMONIC_TWO[4] * (sq_x - sq_y),
        HARMONIC_THREE[0] * dir_y * (3.0 * sq_x - sq_y),
        HARMONIC_THREE[1] * prod_xy * dir_z,
        HARMONIC_THREE[2] * dir_y * (4.0 * sq_z - sq_x - sq_y),
        HARMONIC_THREE[3] * dir_z * (2.0 * sq_z - 3.0 * sq_x - 3.0 * sq_y),
        HARMONIC_THREE[4] * dir_x * (4.0 * sq_z - sq_x - sq_y),
        HARMONIC_THREE[5] * dir_z * (sq_x - sq_y),
        HARMONIC_THREE[6] * dir_x * (sq_x - 3.0 * sq_y),
    ]


LANES = 128
SUBS = 8
GROUP = 16
STEP_ROWS = LANES // GROUP
FEATS = 8
PAIR = 2 * FEATS
OPACITY, COLOUR = 9, 10
COEF_ROWS = 32
JOIN = 4
UNROLL = 8
TAPS = 11
NOWHERE = 1 << 20
DEAD = -1e30
LOG_TOP = float(np.log(0.99))


def stepped(total, width, body, state):
    def step(block, held):
        for k in range(width):
            held = body(block * width + k, held)
        return held

    return lax.fori_loop(0, (total + width - 1) // width, step, state)


def lane_spread(index):
    return index // LANES, index % LANES


def take_blocks(read, count, block, place):
    result = jnp.zeros(place.shape, jnp.float32)
    for num in range(count):
        taken = jnp.take_along_axis(read(num), place, axis=1, mode="promise_in_bounds")
        result = jnp.where(block == num, taken, result)
    return result


def take_line(read, count, block, place):
    sub = lax.broadcasted_iota(jnp.int32, (SUBS, LANES), 0)
    result = take_blocks(read, -(-count // SUBS), block // SUBS, place)
    return jnp.sum(jnp.where(sub == block % SUBS, result, 0.0), axis=0, keepdims=True)


def camera_table(camera):
    columns = [camera[:, entry : entry + 1] for entry in range(6)]
    turn = rotation(columns[0:3])
    shift = columns[3:6]
    anchor = [
        -(turn[0][c] * shift[0] + turn[1][c] * shift[1] + turn[2][c] * shift[2]) for c in range(3)
    ]
    flat = [turn[r][c] for r in range(3) for c in range(3)] + shift + anchor
    lane = lax.broadcasted_iota(jnp.int32, (camera.shape[0], LANES), 1)
    table = jnp.zeros((camera.shape[0], LANES), jnp.float32)
    for num, value in enumerate(flat):
        table = jnp.where(lane == num, value, table)
    return table


def covariance(params):
    scales = [jnp.exp(params[3 + axis_num]) for axis_num in range(3)]
    inv_norm = 1.0 / jnp.sqrt(
        params[6] * params[6]
        + params[7] * params[7]
        + params[8] * params[8]
        + params[9] * params[9]
    )
    quat_w, quat_x, quat_y, quat_z = [params[6 + k] * inv_norm for k in range(4)]
    quat_rot = [
        [
            1.0 - 2.0 * (quat_y * quat_y + quat_z * quat_z),
            2.0 * (quat_x * quat_y - quat_w * quat_z),
            2.0 * (quat_x * quat_z + quat_w * quat_y),
        ],
        [
            2.0 * (quat_x * quat_y + quat_w * quat_z),
            1.0 - 2.0 * (quat_x * quat_x + quat_z * quat_z),
            2.0 * (quat_y * quat_z - quat_w * quat_x),
        ],
        [
            2.0 * (quat_x * quat_z - quat_w * quat_y),
            2.0 * (quat_y * quat_z + quat_w * quat_x),
            1.0 - 2.0 * (quat_x * quat_x + quat_y * quat_y),
        ],
    ]
    root = [[quat_rot[r][c] * scales[c] for c in range(3)] for r in range(3)]
    return [
        root[r][0] * root[k][0] + root[r][1] * root[k][1] + root[r][2] * root[k][2]
        for r, k in ((0, 0), (0, 1), (0, 2), (1, 1), (1, 2), (2, 2))
    ]


def view_basis(mean, cam):
    ray = [mean[c] - cam[12 + c] for c in range(3)]
    inv_len = 1.0 / jnp.sqrt(ray[0] * ray[0] + ray[1] * ray[1] + ray[2] * ray[2])
    return harmonics(ray[0] * inv_len, ray[1] * inv_len, ray[2] * inv_len)[1:]


def view_colours(params, cam):
    basis = [HARMONIC_ZERO] + view_basis(params[0:3], cam)
    colours = []
    for channel in range(3):
        summed = 0.5 + HARMONIC_ZERO * params[11 + 16 * channel]
        for harmonic in range(1, 16):
            summed = summed + basis[harmonic] * params[11 + 16 * channel + harmonic]
        colours.append(summed)
    return colours


def footprint(mean, cov, cam, image_width, image_height):
    turn = [[cam[3 * r + c] for c in range(3)] for r in range(3)]
    point = [
        turn[r][0] * mean[0] + turn[r][1] * mean[1] + turn[r][2] * mean[2] + cam[9 + r]
        for r in range(3)
    ]
    inv_depth = 1.0 / point[2]
    ratio_x, ratio_y = point[0] * inv_depth, point[1] * inv_depth
    zoom = FOCAL * inv_depth
    row_x = [zoom * (turn[0][c] - ratio_x * turn[2][c]) for c in range(3)]
    row_y = [zoom * (turn[1][c] - ratio_y * turn[2][c]) for c in range(3)]
    full = [[cov[0], cov[1], cov[2]], [cov[1], cov[3], cov[4]], [cov[2], cov[4], cov[5]]]
    spread_x = [
        row_x[0] * full[0][c] + row_x[1] * full[1][c] + row_x[2] * full[2][c] for c in range(3)
    ]
    spread_y = [
        row_y[0] * full[0][c] + row_y[1] * full[1][c] + row_y[2] * full[2][c] for c in range(3)
    ]
    cov_xx = spread_x[0] * row_x[0] + spread_x[1] * row_x[1] + spread_x[2] * row_x[2] + LOW_PASS
    cov_xy = spread_x[0] * row_y[0] + spread_x[1] * row_y[1] + spread_x[2] * row_y[2]
    cov_yy = spread_y[0] * row_y[0] + spread_y[1] * row_y[1] + spread_y[2] * row_y[2] + LOW_PASS
    inv_det = 1.0 / (cov_xx * cov_yy - cov_xy * cov_xy)
    return [
        FOCAL * ratio_x + image_width / 2.0,
        FOCAL * ratio_y + image_height / 2.0,
        cov_yy * inv_det,
        -cov_xy * inv_det,
        cov_xx * inv_det,
    ]


def log_opacity(logit):
    return LOG_TOP - jnp.log(1.0 + jnp.exp(-logit))


def load_params(params_ref, tile_scr, block, count):
    for band in range(0, count, SUBS):
        high = min(band + SUBS, count)
        for j in range(SUBS):
            lane_at = pl.multiple_of(block * SUBS * LANES + j * LANES, LANES)
            tile_scr[band * SUBS + j * SUBS : band * SUBS + j * SUBS + high - band, :] = params_ref[
                band:high, pl.ds(lane_at, LANES)
            ]
    return [
        tile_scr[pl.ds((r // SUBS) * SUBS * SUBS + r % SUBS, SUBS, stride=SUBS), :]
        for r in range(count)
    ]


def source_kernel(
    sizes,
    camera_ref,
    counts_ref,
    list_hbm,
    params_hbm,
    out_ref,
    cam_out,
    tile_scr,
    table,
    params_ref,
    list_ref,
    cam_ref,
    params_sem,
    small_sem,
):
    groups, rows, cap, lane_len = sizes
    per = params_ref.shape[1]
    wide = SUBS * LANES

    def params_copy(block):
        lanes = pl.ds(pl.multiple_of(block * wide, wide), wide)
        return pltpu.make_async_copy(
            params_hbm.at[:, lanes], params_ref.at[:, lanes], params_sem.at[block]
        )

    for block in range(per // wide):
        params_copy(block).start()
    list_copy = pltpu.make_async_copy(list_hbm, list_ref, small_sem.at[0])
    list_copy.start()
    cam_out[...] = camera_table(camera_ref[...])
    cam_copy = pltpu.make_async_copy(cam_out, cam_ref, small_sem.at[1])
    cam_copy.start()
    cam_copy.wait()
    parts = cap // lane_len
    used = (1 + groups) * FEATS
    count_blocks = per // LANES

    def project_block(block, carry):
        params_copy(block).wait()
        params = load_params(params_ref, tile_scr, block, params_ref.shape[0])
        at = block * SUBS * used
        shared = params[0:3] + covariance(params) + [log_opacity(params[10])]
        for num, value in enumerate(shared[0:FEATS]):
            table[pl.ds(at + num, SUBS, stride=used), :] = value
        for group in range(groups):
            lines = shared[FEATS:]
            for view in range(2):
                lines = lines + view_colours(
                    params, [cam_ref[2 * group + view, k] for k in range(15)]
                )
            for num, value in enumerate(lines):
                table[pl.ds(at + (1 + group) * FEATS + num, SUBS, stride=used), :] = value
        return carry

    lax.fori_loop(0, per // wide, project_block, 0)
    list_copy.wait()
    lane = lax.broadcasted_iota(jnp.int32, (SUBS, LANES), 1)

    def send_block(dest, start_at):
        count = counts_ref[0, dest]
        line = pl.multiple_of((1 + dest // rows) * FEATS, FEATS)
        for part in range(parts):

            @pl.when(count > part * lane_len)
            def _(part=part):
                first = start_at + part * lane_len
                block, turn = first // LANES, first % LANES
                pieces = []
                for step in range(2):
                    at = jnp.minimum(block + step, count_blocks - 1) * LANES
                    names = list_ref[0:1, pl.ds(pl.multiple_of(at, LANES), LANES)]
                    pieces.append(
                        pltpu.roll(jnp.broadcast_to(names, (SUBS, LANES)), LANES - turn, 1)
                    )
                index = jnp.where(lane < LANES - turn, pieces[0], pieces[1])
                home, place = lane_spread(index)
                for side in range(2):
                    at = line if side else 0
                    taken = take_blocks(
                        lambda num, at=at: table[pl.ds(num * used + at, FEATS), :],
                        count_blocks,
                        home,
                        place,
                    )
                    line_at = part * PAIR + side * FEATS
                    out_ref[dest, line_at : line_at + FEATS, :] = taken[:, 0:lane_len]

        return start_at + count

    lax.fori_loop(0, groups * rows, send_block, jnp.int32(0))


def split_three(value):
    first = value.astype(jnp.bfloat16).astype(jnp.float32)
    rest = value - first
    second = rest.astype(jnp.bfloat16).astype(jnp.float32)
    return [first, second, rest - second]


def in_two(value):
    high = value.astype(jnp.bfloat16).astype(jnp.float32)
    return [high, value - high]


def swap_grain(cells):
    sub = lax.broadcasted_iota(jnp.int32, (SUBS, LANES), 0)
    lane = lax.broadcasted_iota(jnp.int32, (SUBS, LANES), 1) // TILE
    for bit in (1, 2, 4):
        sub_bit, lane_bit = (sub & bit) != 0, (lane & bit) != 0
        from_high = pltpu.roll(pltpu.roll(cells, SUBS - bit, 0), bit * TILE, 1)
        from_low = pltpu.roll(pltpu.roll(cells, bit, 0), LANES - bit * TILE, 1)
        cells = jnp.where(sub_bit == lane_bit, cells, jnp.where(lane_bit, from_high, from_low))
    return cells


def longest(lens_ref, group):
    most = lens_ref[group * GROUP]
    for t in range(1, GROUP):
        most = jnp.maximum(most, lens_ref[group * GROUP + t])
    return most


def gather_slots(arrived_ref, slot_scr, lane_len):
    parts = arrived_ref.shape[1] // PAIR
    joined = LANES // lane_len

    def unpack(block, carry):
        line_at = pl.multiple_of(block * PAIR, PAIR)
        for k in range(joined):
            source = block * joined // parts + k
            part_at = pl.multiple_of(block * joined % parts * PAIR, PAIR)
            slot_scr[pl.ds(line_at, PAIR), k * lane_len : (k + 1) * lane_len] = arrived_ref[
                source, pl.ds(part_at, PAIR), :
            ]
        return carry

    lax.fori_loop(0, slot_scr.shape[0] // PAIR, unpack, 0)


def slot_lines(slot_scr, first):
    return [slot_scr[pl.ds(first * PAIR + num, SUBS, stride=PAIR), :] for num in range(PAIR)]


def render_kernel(
    sizes,
    place_ref,
    cam_ref,
    lens_ref,
    lens_rows_ref,
    names_ref,
    basis_ref,
    arrived_ref,
    image_ref,
    left_ref,
    shape_ref,
    slot_scr,
    table,
    logs,
    feat_scr,
    pieces,
    mm,
):
    cap, lane_len, col_groups, list_len, image_width, image_height = sizes
    devices = arrived_ref.shape[0]
    blocks = list_len // STEP_ROWS
    count_blocks = devices * cap // LANES
    gather_slots(arrived_ref, slot_scr, lane_len)

    def project_block(step, carry):
        first = step * SUBS
        lines = slot_lines(slot_scr, first)
        logs[pl.ds(pl.multiple_of(first, SUBS), SUBS), :] = lines[OPACITY]
        for view in range(2):
            cam = [cam_ref[2 * place_ref[1] + view, k] for k in range(15)]
            feats = footprint(lines[0:3], lines[3:9], cam, image_width, image_height)
            feats = feats + lines[COLOUR + 3 * view : COLOUR + 3 * view + 3]
            for num, value in enumerate(feats):
                row_at = (view * count_blocks + first) * FEATS + num
                table[pl.ds(row_at, SUBS, stride=FEATS), :] = value
        return carry

    lax.fori_loop(0, count_blocks // SUBS, project_block, 0)
    centre_y = (place_ref[0] * TILE).astype(jnp.float32) + (TILE - 1) / 2.0
    sub = lax.broadcasted_iota(jnp.int32, (blocks, LANES), 0)
    lane = lax.broadcasted_iota(jnp.int32, (blocks, LANES), 1)
    zero = jnp.zeros((GROUP, LANES), jnp.float32)

    def one_group(group, carry):
        view, col_group = group // col_groups, group % col_groups
        most = longest(lens_ref, group)

        def fetch(block, inner):
            names = names_ref[pl.ds(group * blocks + block, 1), :]
            home, place = lane_spread(jnp.broadcast_to(names, (SUBS, LANES)))
            feat_at = pl.multiple_of(block * PAIR, PAIR)
            feat_scr[pl.ds(feat_at, FEATS), :] = take_blocks(
                lambda num: table[
                    pl.ds(pl.multiple_of((view * count_blocks + num) * FEATS, FEATS), FEATS), :
                ],
                count_blocks,
                home,
                place,
            )
            feat_scr[pl.ds(feat_at + FEATS, 1), :] = take_line(
                lambda num: logs[num * SUBS : (num + 1) * SUBS, :], count_blocks, home, place
            )
            return inner

        stepped((most + STEP_ROWS - 1) // STEP_ROWS, 2, fetch, 0)
        feats = [feat_scr[pl.ds(num, blocks, stride=PAIR), :] for num in range(FEATS)]
        log_o = feat_scr[pl.ds(FEATS, blocks, stride=PAIR), :]
        live = sub * STEP_ROWS + lane // GROUP < lens_rows_ref[pl.ds(group, 1), :]
        centre_x = ((col_group * GROUP + lane % GROUP) * TILE).astype(jnp.float32) + (
            TILE - 1
        ) / 2.0
        off_x, off_y = feats[0] - centre_x, feats[1] - centre_y
        lin_x = feats[2] * off_x + feats[3] * off_y
        lin_y = feats[4] * off_y + feats[3] * off_x
        coefs = [
            log_o - 0.5 * (off_x * lin_x + off_y * lin_y),
            lin_x,
            lin_y,
            -0.5 * feats[2],
            -feats[3],
            -0.5 * feats[4],
        ]
        coefs = [
            jnp.where(live, value, DEAD if num == 0 else 0.0) for num, value in enumerate(coefs)
        ]
        lines = [None] * COEF_ROWS
        for num, value in enumerate(coefs):
            for piece, part in enumerate(split_three(value)):
                lines[piece * 6 + num] = part
        for num in range(3):
            for piece, part in enumerate(split_three(jnp.where(live, feats[5 + num], 0.0))):
                lines[18 + piece * 3 + num] = part
        for num, value in enumerate(lines):
            pieces[pl.ds(num, blocks, stride=COEF_ROWS), :] = (
                jnp.zeros((blocks, LANES), jnp.float32) if value is None else value
            )
        for num, value in enumerate(feats[2:5] + [off_x, off_y]):
            shape_ref[num, pl.ds(pl.multiple_of(group * blocks, blocks), blocks), :] = jnp.where(
                live, value, 0.0
            )
        left_at = pl.multiple_of(group * blocks * LANES, LANES)
        for block in range(blocks):
            left_ref[pl.ds(left_at + block * LANES, LANES), :] = pieces[
                block * COEF_ROWS : (block + 1) * COEF_ROWS, :
            ].T.astype(jnp.bfloat16)
        expand(left_ref, basis_ref, mm, left_at)

        def entry(n, state):
            keep, colour = state
            row_at = pl.multiple_of(n * GROUP, GROUP)
            shade = [
                mm[pl.ds(row_at, GROUP), (2 + c) * LANES : (3 + c) * LANES] for c in range(3)
            ]
            new_keep, new_colour = [], []
            for half in range(2):
                alpha = jnp.exp(mm[pl.ds(row_at, GROUP), half * LANES : (half + 1) * LANES])
                weight = keep[half] * alpha
                new_keep.append(keep[half] * (1.0 - alpha))
                new_colour.append([colour[half][c] + weight * shade[c] for c in range(3)])
            return new_keep, new_colour

        state = ([zero + 1.0] * 2, [[zero] * 3] * 2)
        _, colour = stepped(most, UNROLL, entry, state)
        for side in range(GROUP // SUBS):
            lane_at = pl.multiple_of(col_group * GROUP * TILE + side * LANES, LANES)
            for half in range(2):
                for c in range(3):
                    image_ref[view, c, half * SUBS : (half + 1) * SUBS, pl.ds(lane_at, LANES)] = (
                        swap_grain(colour[half][c][side * SUBS : (side + 1) * SUBS])
                    )
        return carry

    lax.fori_loop(0, 2 * col_groups, one_group, 0)


def expand(left_ref, basis_ref, mm, left_at):
    mm[...] = jnp.dot(
        left_ref[pl.ds(left_at, mm.shape[0]), :],
        basis_ref[...],
        preferred_element_type=jnp.float32,
    )


def back_kernel(
    sizes,
    place_ref,
    cam_ref,
    lens_ref,
    names_ref,
    basis_ref,
    moment_ref,
    left_ref,
    shape_ref,
    arrived_ref,
    grad_ref,
    out_ref,
    mm,
    alphas,
    weights,
    slopes,
    grad_scr,
    mom_scr,
    line_scr,
    masked,
    places,
    total_scr,
    slot_scr,
):
    cap, lane_len, col_groups, list_len, image_width, image_height = sizes
    devices = out_ref.shape[0]
    parts = cap // lane_len
    blocks = list_len // STEP_ROWS
    count_blocks = devices * cap // LANES
    joined = LANES // lane_len
    value_rows = count_blocks * 2 * FEATS
    total_scr[...] = jnp.zeros_like(total_scr)
    line_scr[...] = jnp.zeros_like(line_scr)
    grad_scr[...] = jnp.zeros_like(grad_scr)
    zero = jnp.zeros((GROUP, LANES), jnp.float32)
    sub = lax.broadcasted_iota(jnp.int32, (GROUP, LANES), 0)
    lane = lax.broadcasted_iota(jnp.int32, (GROUP, LANES), 1)
    own_tile = lane % GROUP == sub

    def one_group(group, carry):
        view, col_group = group // col_groups, group % col_groups
        most = longest(lens_ref, group)
        lane_at = pl.multiple_of(col_group * GROUP * TILE, LANES)
        grads = [
            [
                jnp.concatenate(
                    [
                        swap_grain(
                            grad_ref[
                                view,
                                c,
                                half * SUBS : (half + 1) * SUBS,
                                pl.ds(lane_at + side * LANES, LANES),
                            ]
                        )
                        for side in range(GROUP // SUBS)
                    ],
                    axis=0,
                )
                for c in range(3)
            ]
            for half in range(2)
        ]
        for half in range(2):
            for c in range(3):
                for piece, part in enumerate(in_two(grads[half][c])):
                    line = (piece * 3 + c) * GROUP
                    grad_scr[line : line + GROUP, half * LANES : (half + 1) * LANES] = part
        expand(left_ref, basis_ref, mm, pl.multiple_of(group * blocks * LANES, LANES))

        def ahead(n, keep):
            row_at = pl.multiple_of(n * GROUP, GROUP)
            new_keep = []
            for half in range(2):
                lanes = slice(half * LANES, (half + 1) * LANES)
                alpha = jnp.exp(mm[pl.ds(row_at, GROUP), lanes])
                weight = keep[half] * alpha
                alphas[pl.ds(row_at, GROUP), lanes] = alpha
                weights[pl.ds(row_at, GROUP), lanes] = weight
                new_keep.append(keep[half] * (1.0 - alpha))
            return new_keep

        stepped(most, UNROLL, ahead, [zero + 1.0] * 2)

        last = (most + UNROLL - 1) // UNROLL * UNROLL - 1

        def behind(step, seen):
            row_at = pl.multiple_of((last - step) * GROUP, GROUP)
            shade = [
                mm[pl.ds(row_at, GROUP), (2 + c) * LANES : (3 + c) * LANES] for c in range(3)
            ]
            new_seen = []
            for half in range(2):
                lanes = slice(half * LANES, (half + 1) * LANES)
                own = (
                    grads[half][0] * shade[0]
                    + grads[half][1] * shade[1]
                    + grads[half][2] * shade[2]
                )
                alpha = alphas[pl.ds(row_at, GROUP), lanes]
                slopes[pl.ds(row_at, GROUP), lanes] = weights[pl.ds(row_at, GROUP), lanes] * (
                    own - seen[half]
                )
                new_seen.append(seen[half] * (1.0 - alpha) + alpha * own)
            return new_seen

        stepped(most, UNROLL, behind, [zero] * 2)
        total = jnp.zeros((blocks * LANES, LANES), jnp.float32)
        for value, right in (
            (slopes[...], moment_ref[...]),
            (weights[...], grad_scr[...].T.astype(jnp.bfloat16)),
        ):
            high = value.astype(jnp.bfloat16)
            low = (value - high.astype(jnp.float32)).astype(jnp.bfloat16)
            total = total + jnp.dot(high, right, preferred_element_type=jnp.float32)
            total = total + jnp.dot(low, right, preferred_element_type=jnp.float32)
        for block in range(blocks):
            turned = total[block * LANES : (block + 1) * LANES].T
            mom_scr[block * TILE : block * TILE + 8, :] = turned[6 * GROUP : 6 * GROUP + 8]
            for c in range(3):
                summed = (
                    turned[c * GROUP : (c + 1) * GROUP]
                    + turned[(3 + c) * GROUP : (4 + c) * GROUP]
                )
                mom_scr[block * TILE + 8 + c : block * TILE + 9 + c, :] = jnp.sum(
                    jnp.where(own_tile, summed, 0.0), axis=0, keepdims=True
                )
        mom = [mom_scr[pl.ds(num, blocks, stride=TILE), :] for num in range(11)]
        con_xx, con_xy, con_yy, off_x, off_y = [
            shape_ref[num, pl.ds(pl.multiple_of(group * blocks, blocks), blocks), :]
            for num in range(5)
        ]
        sum_x = off_x * mom[0] - mom[1]
        sum_y = off_y * mom[0] - mom[2]
        results = [
            -(con_xx * sum_x + con_xy * sum_y),
            -(con_yy * sum_y + con_xy * sum_x),
            -0.5 * (off_x * (sum_x - mom[1]) + mom[3]),
            -(off_x * sum_y - off_y * mom[1] + mom[4]),
            -0.5 * (off_y * (sum_y - mom[2]) + mom[5]),
        ] + mom[8:11]
        for num, value in enumerate(results + [mom[0]]):
            line_scr[pl.ds(num, blocks, stride=PAIR), :] = value

        def spread(step, inner):
            for k in range(JOIN):
                block = step * JOIN + k
                lanes = slice(k * LANES, (k + 1) * LANES)
                names = names_ref[pl.ds(group * blocks + block, 1), :]
                home, place = names // LANES, names % LANES
                line_at = pl.multiple_of(block * PAIR, PAIR)
                values = in_two(line_scr[pl.ds(line_at, FEATS), :])
                logs = in_two(line_scr[pl.ds(line_at + FEATS, 1), :])
                home_wide = jnp.broadcast_to(home, (2 * FEATS, LANES)).astype(jnp.bfloat16)
                pair = jnp.concatenate(values, axis=0).astype(jnp.bfloat16)
                for num in range(count_blocks):
                    masked[num * 2 * FEATS : (num + 1) * 2 * FEATS, lanes] = jnp.where(
                        home_wide == jnp.bfloat16(num), pair, jnp.bfloat16(0)
                    )
                rank = lax.broadcasted_iota(jnp.int32, (count_blocks, LANES), 0)
                for piece, value in enumerate(logs):
                    first = value_rows + piece * count_blocks
                    masked[first : first + count_blocks, lanes] = jnp.where(
                        rank == home, value, 0.0
                    ).astype(jnp.bfloat16)
                seat = lax.broadcasted_iota(jnp.int32, (LANES, LANES), 0)
                places[:, lanes] = jnp.where(seat == place, 1.0, 0.0).astype(jnp.bfloat16)
            total_scr[view] += lax.dot_general(
                masked[...],
                places[...],
                (((1,), (1,)), ((), ())),
                preferred_element_type=jnp.float32,
            )
            return inner

        width = JOIN * STEP_ROWS
        lax.fori_loop(0, (most + width - 1) // width, spread, 0)
        return carry

    lax.fori_loop(0, 2 * col_groups, one_group, 0)

    gather_slots(arrived_ref, slot_scr, lane_len)

    def pull_block(step, carry):
        first = step * SUBS
        lines = slot_lines(slot_scr, first)
        cams = [[cam_ref[2 * place_ref[1] + view, k] for k in range(15)] for view in range(2)]

        def both(*values):
            return [
                footprint(values[0:3], values[3:9], cam, image_width, image_height)
                for cam in cams
            ]

        cots = []
        log_sum = jnp.zeros((SUBS, LANES), jnp.float32)
        for view in range(2):
            row_at = first * 2 * FEATS
            cots.append(
                [
                    total_scr[view, pl.ds(row_at + num, SUBS, stride=2 * FEATS), :]
                    + total_scr[view, pl.ds(row_at + FEATS + num, SUBS, stride=2 * FEATS), :]
                    for num in range(FEATS)
                ]
            )
            for piece in range(2):
                row = pl.multiple_of(value_rows + piece * count_blocks + first, SUBS)
                log_sum = log_sum + total_scr[view, pl.ds(row, SUBS), :]
        _, pull = jax.vjp(both, *lines[0:9])
        results = list(pull([cot[0:5] for cot in cots])) + [log_sum] + cots[0][5:] + cots[1][5:]
        for num, value in enumerate(results):
            slot_scr[pl.ds(first * PAIR + num, SUBS, stride=PAIR), :] = value
        return carry

    lax.fori_loop(0, count_blocks // SUBS, pull_block, 0)

    def pack(block, carry):
        line_at = pl.multiple_of(block * PAIR, PAIR)
        for k in range(joined):
            source = block * joined // parts + k
            part_at = pl.multiple_of(block * joined % parts * PAIR, PAIR)
            out_ref[source, pl.ds(part_at, PAIR), :] = slot_scr[
                pl.ds(line_at, PAIR), k * lane_len : (k + 1) * lane_len
            ]
        return carry

    lax.fori_loop(0, count_blocks, pack, 0)


def prepare_kernel(
    sizes, cam_ref, counts_ref, list_ref, params_ref, slot_ref, parts_ref, tile_scr, rows_scr
):
    groups, rows = sizes
    per = params_ref.shape[1]
    blocks = per // LANES
    devices = groups * rows
    rank = lax.broadcasted_iota(jnp.int32, (blocks, LANES), 0)
    lane = lax.broadcasted_iota(jnp.int32, (blocks, LANES), 1)
    spot = rank * LANES + lane

    def pass_run(dest, state):
        start, home = state
        start = start + counts_ref[0, dest]
        return start, home + jnp.where(spot >= start, 1, 0)

    start, home = lax.fori_loop(0, devices, pass_run, (jnp.int32(0), jnp.zeros_like(spot)))
    for num, value in enumerate((rank, lane, home // rows + 1)):
        rows_scr[num] = jnp.where(spot < start, value, 0).astype(jnp.float32)

    def place_names(step, total):
        masked, places = [], []
        for k in range(JOIN):
            block = step * JOIN + k
            names = list_ref[0:1, pl.ds(pl.multiple_of(block * LANES, LANES), LANES)]
            home, place = names // LANES, names % LANES
            masked.append(
                jnp.concatenate(
                    [
                        jnp.where(rank == home, rows_scr[num, pl.ds(block, 1), :], 0.0)
                        for num in range(3)
                    ],
                    axis=0,
                ).astype(jnp.bfloat16)
            )
            seat = lax.broadcasted_iota(jnp.int32, (LANES, LANES), 0)
            places.append(jnp.where(seat == place, 1.0, 0.0).astype(jnp.bfloat16))
        return total + lax.dot_general(
            jnp.concatenate(masked, axis=1),
            jnp.concatenate(places, axis=1),
            (((1,), (1,)), ((), ())),
            preferred_element_type=jnp.float32,
        )

    total = lax.fori_loop(
        0, blocks // JOIN, place_names, jnp.zeros((3 * blocks, LANES), jnp.float32)
    )
    own = (total[0:blocks] * LANES + total[blocks : 2 * blocks]).astype(jnp.int32)
    group_of = total[2 * blocks :]
    slot_ref[...] = jnp.where(group_of > 0.5, own, NOWHERE)
    rows_scr[0] = group_of

    def one_block(block, carry):
        params = load_params(params_ref, tile_scr, block, params_ref.shape[0])
        at = pl.multiple_of(block * SUBS, SUBS)
        home = rows_scr[0, pl.ds(at, SUBS), :]
        one, none = jnp.ones((SUBS, LANES), jnp.float32), jnp.zeros((SUBS, LANES), jnp.float32)
        for view in range(2):
            cam = []
            for k in range(15):
                value = jnp.full((SUBS, LANES), cam_ref[view, k], jnp.float32)
                for group in range(1, groups):
                    value = jnp.where(home > group + 0.5, cam_ref[2 * group + view, k], value)
                cam.append(value)
            first = view * (TILE - 1 + 9)
            for axis in range(3):
                toward = [one if k == axis else none for k in range(3)]
                basis, slopes = jax.jvp(
                    lambda *mean, cam=cam: view_basis(mean, cam), tuple(params[0:3]), tuple(toward)
                )
                if axis == 0:
                    for k in range(15):
                        parts_ref[first + k, pl.ds(at, SUBS), :] = basis[k]
                for channel in range(3):
                    summed = none
                    for k in range(15):
                        summed = summed + slopes[k] * params[12 + 16 * channel + k]
                    parts_ref[first + 15 + 3 * channel + axis, pl.ds(at, SUBS), :] = summed
        return carry

    lax.fori_loop(0, blocks // SUBS, one_block, 0)


def owner_kernel(
    lane_len,
    counts_ref,
    slot_ref,
    parts_ref,
    params_ref,
    back_ref,
    out_ref,
    tile_scr,
    line_scr,
    slot_scr,
):
    count_params, per = params_ref.shape
    count_blocks = per // LANES
    lane = lax.broadcasted_iota(jnp.int32, (PAIR, LANES), 1)

    def close_up(dest, start):
        count = counts_ref[0, dest]
        for part in range(back_ref.shape[1] // PAIR):

            @pl.when(count > part * lane_len)
            def _(part=part):
                lines = back_ref[dest, part * PAIR : (part + 1) * PAIR, :]
                if lane_len < LANES:
                    lines = jnp.concatenate(
                        [lines, jnp.zeros((PAIR, LANES - lane_len), jnp.float32)], axis=1
                    )
                valid = jnp.minimum(count - part * lane_len, lane_len)
                first = start + part * lane_len
                block, turn = first // LANES, first % LANES
                lines = pltpu.roll(lines, turn, 1)
                for step in range(2):
                    place = lane - turn + step * LANES
                    rows = pl.ds(pl.multiple_of((block + step) * PAIR, PAIR), PAIR)
                    slot_scr[rows, :] = jnp.where(
                        (place >= 0) & (place < valid), lines, slot_scr[rows, :]
                    )

        return start + count

    total = lax.fori_loop(0, counts_ref.shape[1], close_up, jnp.int32(0))
    live_blocks = (total + LANES - 1) // LANES

    def pull_block(block, carry):
        at = pl.multiple_of(block * SUBS, SUBS)
        own = slot_ref[pl.ds(at, SUBS), :]

        homes, places = [], []
        for j in range(SUBS):
            home, place = lane_spread(jnp.broadcast_to(own[j : j + 1], (SUBS, LANES)))
            homes.append(home)
            places.append(place)

        def fetch(num, held):
            sides = [
                slot_scr[pl.ds(pl.multiple_of(num * PAIR + side * FEATS, FEATS), FEATS), :]
                for side in range(2)
            ]
            taken = []
            for j in range(SUBS):
                here = homes[j] == num
                taken.append(
                    [
                        jnp.where(
                            here,
                            jnp.take_along_axis(
                                sides[side], places[j], axis=1, mode="promise_in_bounds"
                            ),
                            held[j][side],
                        )
                        for side in range(2)
                    ]
                )
            return taken

        none = jnp.zeros((FEATS, LANES), jnp.float32)
        held = stepped(live_blocks, 4, fetch, [[none, none]] * SUBS)
        for j in range(SUBS):
            for side in range(2):
                at_line = j * PAIR + side * FEATS
                line_scr[at_line : at_line + FEATS, :] = held[j][side]
        cots = [line_scr[pl.ds(num, SUBS, stride=PAIR), :] for num in range(PAIR)]
        sent = own < count_blocks * LANES
        params = load_params(params_ref, tile_scr, block, PAIR)

        def both(*values):
            every = params[0:3] + list(values)
            return covariance(every) + [log_opacity(every[10])]

        _, pull = jax.vjp(both, *params[3:11])
        grads = cots[0:3] + list(pull(cots[3:COLOUR])) + [None] * 48
        for channel in range(3):
            tints = [cots[COLOUR + 3 * view + channel] for view in range(2)]
            grads[11 + 16 * channel] = HARMONIC_ZERO * (tints[0] + tints[1])
            for k in range(15):
                grads[12 + 16 * channel + k] = (
                    tints[0] * parts_ref[k, pl.ds(at, SUBS), :]
                    + tints[1] * parts_ref[24 + k, pl.ds(at, SUBS), :]
                )
            for axis in range(3):
                for view in range(2):
                    line = 24 * view + 15 + 3 * channel + axis
                    grads[axis] = grads[axis] + tints[view] * parts_ref[line, pl.ds(at, SUBS), :]
        for num, value in enumerate(grads):
            tile_scr[pl.ds((num // SUBS) * SUBS * SUBS + num % SUBS, SUBS, stride=SUBS), :] = (
                jnp.where(sent, value, 0.0)
            )
        for band in range(0, count_params, SUBS):
            high = min(band + SUBS, count_params)
            for j in range(SUBS):
                lane_at = pl.multiple_of(block * SUBS * LANES + j * LANES, LANES)
                out_ref[band:high, pl.ds(lane_at, LANES)] = tile_scr[
                    band * SUBS + j * SUBS : band * SUBS + j * SUBS + high - band, :
                ]
        return carry

    lax.fori_loop(0, count_blocks // SUBS, pull_block, 0)


def tap_rows(read, first, count):
    taps = window_taps()
    total = taps[5] * read(first + 5, count)
    for k in range(5):
        total = total + taps[k] * (read(first + k, count) + read(first + TAPS - 1 - k, count))
    return total


def blur_lanes(value, band):
    return jnp.dot(
        value, band, precision=lax.Precision.HIGHEST, preferred_element_type=jnp.float32
    )


def truth_kernel(band_ref, above_ref, own_ref, below_ref, out_ref, tall, mixed):
    images = own_ref.shape[0]

    def one_image(m, carry):
        whole = jnp.concatenate([above_ref[m], own_ref[m], below_ref[m]], axis=0)
        for field, value in enumerate((whole, whole * whole)):
            tall[...] = value
            row_at = pl.multiple_of((field * images + m) * 2 * TILE, 2 * TILE)
            mixed[pl.ds(row_at, 2 * TILE), :] = tap_rows(
                lambda at, count: tall[at : at + count, :], 6, 2 * TILE
            )
        return carry

    lax.fori_loop(0, images, one_image, 0)
    out_ref[...] = blur_lanes(mixed[...], band_ref[...])


def loss_kernel(
    image_rows,
    row_ref,
    band_ref,
    truth_ref,
    true_above,
    true_own,
    true_below,
    above_ref,
    own_ref,
    below_ref,
    out_ref,
    tall,
    mixed,
    blurred,
    slim,
):
    images = own_ref.shape[0]
    tall_rows = 2 * TILE
    width = own_ref.shape[2]

    def one_image(m, carry):
        whole = jnp.concatenate([above_ref[m], own_ref[m], below_ref[m]], axis=0)
        true = jnp.concatenate([true_above[m], true_own[m], true_below[m]], axis=0)
        for field, value in enumerate((whole, whole * whole, whole * true)):
            tall[field] = value
            row_at = pl.multiple_of((field * images + m) * tall_rows, tall_rows)
            mixed[pl.ds(row_at, tall_rows), :] = tap_rows(
                lambda at, count, field=field: tall[field, at : at + count, :], 6, tall_rows
            )
        return carry

    lax.fori_loop(0, images, one_image, 0)
    blurred[...] = blur_lanes(mixed[...], band_ref[...])
    sub = lax.broadcasted_iota(jnp.int32, (tall_rows, width), 0)
    image_row = row_ref[0] * TILE + sub - 5
    inside = (image_row >= 0) & (image_row < image_rows) & (sub < TILE + 10)

    def one_map(m, carry):
        def field_of(ref, field):
            row_at = pl.multiple_of((field * images + m) * tall_rows, tall_rows)
            return ref[pl.ds(row_at, tall_rows), :]

        mean_one, both_one, cross = [field_of(blurred, field) for field in range(3)]
        mean_two, both_two = field_of(truth_ref, 0), field_of(truth_ref, 1)
        square_one, square_two = mean_one * mean_one, mean_two * mean_two
        mean_cross = mean_one * mean_two
        top_one = 2.0 * mean_cross + SSIM_ONE
        top_two = 2.0 * (cross - mean_cross) + SSIM_TWO
        low_one = square_one + square_two + SSIM_ONE
        low_two = (both_one - square_one) + (both_two - square_two) + SSIM_TWO
        inv_one, inv_two = 1.0 / low_one, 1.0 / low_two
        inv_both = inv_one * inv_two
        value = top_one * top_two * inv_both
        grads = [
            2.0 * mean_two * (top_two - top_one) * inv_both
            - 2.0 * mean_one * value * (inv_one - inv_two),
            -value * inv_two,
            2.0 * top_one * inv_both,
        ]
        for field, grad in enumerate(grads):
            tall[field, 0:tall_rows] = jnp.where(inside, grad, 0.0)
            row_at = pl.multiple_of((field * images + m) * TILE, TILE)
            slim[pl.ds(row_at, TILE), :] = tap_rows(
                lambda at, count, field=field: tall[field, at : at + count, :], 0, TILE
            )
        return carry

    lax.fori_loop(0, images, one_map, 0)
    spread = blur_lanes(slim[...], band_ref[...]).reshape(3, images, TILE, width)
    own, true = own_ref[...], true_own[...]
    gap = own - true
    out_ref[...] = (1.0 - SSIM_SHARE) * gap / jnp.sqrt(gap * gap + SMOOTH_EPS) - SSIM_SHARE * (
        spread[0] + 2.0 * own * spread[1] + true * spread[2]
    )


def band_matrix(width):
    taps = window_taps()
    band = np.zeros((width, width), np.float32)
    for k in range(TAPS):
        band += np.diag(np.full(width - abs(k - 5), taps[k], np.float32), k - 5)
    return jnp.asarray(band)


def pixel_basis():
    pixel = np.arange(TILE * TILE)
    x = (pixel % TILE) - (TILE - 1) / 2.0
    y = (pixel // TILE) - (TILE - 1) / 2.0
    return np.stack([np.ones_like(x), x, y, x * x, x * y, y * y])


def expand_matrix():
    terms = pixel_basis()
    matrix = np.zeros((COEF_ROWS, 5 * LANES), np.float32)
    for piece in range(3):
        matrix[piece * 6 : piece * 6 + 6, 0 : 2 * LANES] = terms
        for c in range(3):
            matrix[18 + piece * 3 + c, (2 + c) * LANES : (3 + c) * LANES] = 1.0
    return jnp.asarray(matrix, jnp.bfloat16)


def moment_matrix():
    matrix = np.zeros((2 * LANES, LANES), np.float32)
    matrix[:, 6 * GROUP : 6 * GROUP + 6] = pixel_basis().T
    return jnp.asarray(matrix, jnp.bfloat16)


def smem():
    return pl.BlockSpec(memory_space=pltpu.SMEM)


def vmem():
    return pl.BlockSpec(memory_space=pltpu.VMEM)


def scratch(*shape):
    return pltpu.VMEM(shape, jnp.float32)


def run(kernel, megabytes, out_shapes, in_specs, scratches, *operands):
    return pl.pallas_call(
        kernel,
        out_shape=out_shapes,
        in_specs=in_specs,
        out_specs=jax.tree.map(lambda _: vmem(), out_shapes),
        scratch_shapes=scratches,
        compiler_params=pltpu.CompilerParams(vmem_limit_bytes=megabytes << 20),
    )(*operands)


def shards(params, send_list, send_counts, camera, ground_truth, tile_lists, list_lengths):
    devices = lax.axis_size(("view", "tile"))
    row_devices = lax.axis_size("tile")
    groups = lax.axis_size("view")
    count_params, per_device = params.shape
    capacity = per_device // devices
    tile_cols, list_len = tile_lists.shape[2:]
    col_groups = tile_cols // GROUP
    blocks = list_len // STEP_ROWS
    tile_row = lax.axis_index("tile")
    image_width = float(ground_truth.shape[3])
    image_height = float(ground_truth.shape[2] * row_devices)
    lane_len = min(capacity, LANES)
    sent_shape = jax.ShapeDtypeStruct(
        (devices, capacity // lane_len * PAIR, lane_len), jnp.float32
    )
    count_blocks = per_device // LANES

    flat_lengths = list_lengths.reshape(-1)
    entry_rank = jnp.arange(list_len, dtype=jnp.int32)
    tile_num = jnp.arange(2 * tile_cols, dtype=jnp.int32)
    lists = jnp.where(
        entry_rank[None, :] < flat_lengths[:, None],
        tile_lists.reshape(2 * tile_cols, list_len),
        per_device + tile_num[:, None] % GROUP,
    )
    lens_rows = jnp.tile(flat_lengths.reshape(-1, GROUP), (1, LANES // GROUP))

    width = ground_truth.shape[3]
    true_own = ground_truth.reshape(-1, TILE, width)
    true_above = from_behind(true_own, "tile", 1)
    true_below = from_behind(true_own, "tile", -1)
    band = band_matrix(width)
    truth_rows = 2 * true_own.shape[0] * 2 * TILE
    truth_blur = run(
        truth_kernel,
        16,
        jax.ShapeDtypeStruct((truth_rows, width), jnp.float32),
        [vmem()] * 4,
        [scratch(3 * TILE, width), scratch(truth_rows, width)],
        band,
        true_above,
        true_own,
        true_below,
    )

    own_sizes = (groups, row_devices, capacity, lane_len)
    sent, cams = run(
        lambda *refs: source_kernel(own_sizes, *refs),
        24,
        (sent_shape, jax.ShapeDtypeStruct((camera.shape[0], LANES), jnp.float32)),
        [vmem(), smem(), pl.BlockSpec(memory_space=pl.ANY), pl.BlockSpec(memory_space=pl.ANY)],
        [
            scratch(SUBS * SUBS * SUBS, LANES),
            scratch(count_blocks * (1 + groups) * FEATS, LANES),
            scratch(*params.shape),
            pltpu.VMEM(send_list.shape, jnp.int32),
            pltpu.SMEM((camera.shape[0], LANES), jnp.float32),
            pltpu.SemaphoreType.DMA((count_blocks // SUBS,)),
            pltpu.SemaphoreType.DMA((2,)),
        ],
        camera,
        send_counts,
        send_list,
        params,
    )
    arrived = lax.all_to_all(sent, ("view", "tile"), split_axis=0, concat_axis=0, tiled=True)

    arrived, truth_blur = lax.optimization_barrier((arrived, truth_blur))
    tile_sizes = (capacity, lane_len, col_groups, list_len, image_width, image_height)
    place = jnp.stack([tile_row, lax.axis_index("view")])
    entries = 2 * tile_cols * list_len
    names = lists.reshape(-1, GROUP, list_len).transpose(0, 2, 1).reshape(-1, LANES)
    rendered, left, shapes = run(
        lambda *refs: render_kernel(tile_sizes, *refs),
        32,
        (
            jax.ShapeDtypeStruct(ground_truth.shape, jnp.float32),
            jax.ShapeDtypeStruct((entries, COEF_ROWS), jnp.bfloat16),
            jax.ShapeDtypeStruct((5, entries // LANES, LANES), jnp.float32),
        ),
        [smem(), smem(), smem(), vmem(), vmem(), vmem(), vmem()],
        [
            scratch(count_blocks * PAIR, LANES),
            scratch(2 * per_device // LANES * FEATS, LANES),
            scratch(count_blocks, LANES),
            scratch(blocks * PAIR, LANES),
            scratch(blocks * COEF_ROWS, LANES),
            scratch(blocks * LANES, 5 * LANES),
        ],
        place,
        cams,
        flat_lengths,
        lens_rows,
        names,
        expand_matrix(),
        arrived,
    )

    images = rendered.reshape(true_own.shape)
    count = images.shape[0]
    grad_image = run(
        lambda *refs: loss_kernel(TILE * row_devices, *refs),
        24,
        jax.ShapeDtypeStruct(images.shape, jnp.float32),
        [smem()] + [vmem()] * 8,
        [
            scratch(3, 3 * TILE, width),
            scratch(3 * count * 2 * TILE, width),
            scratch(3 * count * 2 * TILE, width),
            scratch(3 * count * TILE, width),
        ],
        place,
        band,
        truth_blur,
        true_above,
        true_own,
        true_below,
        from_behind(images, "tile", 1),
        images,
        from_behind(images, "tile", -1),
    ).reshape(ground_truth.shape)

    spread_rows = count_blocks * (2 * FEATS + 2)
    grad_slots = run(
        lambda *refs: back_kernel(tile_sizes, *refs),
        40,
        sent_shape,
        [smem()] * 3 + [vmem()] * 7,
        [
            scratch(blocks * LANES, 5 * LANES),
            scratch(blocks * LANES, 2 * LANES),
            scratch(blocks * LANES, 2 * LANES),
            scratch(blocks * LANES, 2 * LANES),
            scratch(LANES, 2 * LANES),
            scratch(blocks * TILE, LANES),
            scratch(blocks * PAIR, LANES),
            pltpu.VMEM((spread_rows, JOIN * LANES), jnp.bfloat16),
            pltpu.VMEM((LANES, JOIN * LANES), jnp.bfloat16),
            scratch(2, spread_rows, LANES),
            scratch(count_blocks * PAIR, LANES),
        ],
        place,
        cams,
        flat_lengths,
        names,
        expand_matrix(),
        moment_matrix(),
        left,
        shapes,
        arrived,
        grad_image,
    )
    grad_slots, late_counts = lax.optimization_barrier((grad_slots, send_counts))
    returned = lax.all_to_all(
        grad_slots, ("view", "tile"), split_axis=0, concat_axis=0, tiled=True
    )
    own_slots, own_parts = run(
        lambda *refs: prepare_kernel((groups, row_devices), *refs),
        24,
        (
            jax.ShapeDtypeStruct((count_blocks, LANES), jnp.int32),
            jax.ShapeDtypeStruct((2 * (TILE - 1 + 9), count_blocks, LANES), jnp.float32),
        ),
        [smem(), smem(), vmem(), vmem()],
        [scratch(SUBS * SUBS * SUBS, LANES), scratch(3, count_blocks, LANES)],
        cams,
        late_counts,
        send_list,
        params,
    )
    return run(
        lambda *refs: owner_kernel(lane_len, *refs),
        24,
        jax.ShapeDtypeStruct(params.shape, jnp.float32),
        [smem()] + [vmem()] * 4,
        [
            scratch(SUBS * SUBS * SUBS, LANES),
            scratch(SUBS * PAIR, LANES),
            scratch((count_blocks + 4) * PAIR, LANES),
        ],
        send_counts,
        own_slots,
        own_parts,
        params,
        returned,
    )


def solution(mesh):
    in_specs = (
        P(None, ("view", "tile")),
        P(("view", "tile"), None),
        P(("view", "tile"), None),
        P(),
        P("view", None, "tile", None),
        P("view", "tile", None, None),
        P("view", "tile", None),
    )
    out_specs = P(None, ("view", "tile"))
    return jax.shard_map(shards, mesh=mesh, in_specs=in_specs, out_specs=out_specs, check_vma=False)
```

```python
import jax
import jax.numpy as jnp
import numpy as np
from jax import lax
from jax.experimental import pallas as pl
from jax.experimental.pallas import tpu as pltpu
from jax.sharding import PartitionSpec as P

TILE = 16


FOCAL = 1000.0
LOW_PASS = 0.3
SSIM_SHARE = 0.2
SMOOTH_EPS = 1e-06
SSIM_ONE = 0.0001
SSIM_TWO = 0.0009
HARMONIC_ZERO = 0.28209479177387814
HARMONIC_ONE = 0.4886025119029199
HARMONIC_TWO = (
    1.0925484305920792,
    -1.0925484305920792,
    0.31539156525252005,
    -1.0925484305920792,
    0.5462742152960396,
)
HARMONIC_THREE = (
    -0.5900435899266435,
    2.890611442640554,
    -0.4570457994644658,
    0.3731763325901154,
    -0.4570457994644658,
    1.445305721320277,
    -0.5900435899266435,
)


def from_behind(block, axis, distance):
    devices = range(lax.axis_size(axis))
    route = [(i - distance, i) for i in devices if i - distance in devices]
    return lax.ppermute(block, axis, route)


def window_taps():
    offsets_np = np.arange(11) - 5.0
    weights = np.exp(-offsets_np * offsets_np / 4.5)
    weights = weights / weights.sum()
    return [float(weight) for weight in weights]


def matrix_product(left_side, right_side):
    return [
        [
            left_side[row_idx][0] * right_side[0][col_idx]
            + left_side[row_idx][1] * right_side[1][col_idx]
            + left_side[row_idx][2] * right_side[2][col_idx]
            for col_idx in range(3)
        ]
        for row_idx in range(3)
    ]


def rotation(angles):
    cos_a, sin_a = (jnp.cos(angles[0]), jnp.sin(angles[0]))
    cos_b, sin_b = (jnp.cos(angles[1]), jnp.sin(angles[1]))
    cos_c, sin_c = (jnp.cos(angles[2]), jnp.sin(angles[2]))
    about_x = [[1.0, 0.0, 0.0], [0.0, cos_a, -sin_a], [0.0, sin_a, cos_a]]
    about_y = [[cos_b, 0.0, sin_b], [0.0, 1.0, 0.0], [-sin_b, 0.0, cos_b]]
    about_z = [[cos_c, -sin_c, 0.0], [sin_c, cos_c, 0.0], [0.0, 0.0, 1.0]]
    return matrix_product(about_z, matrix_product(about_y, about_x))


def harmonics(dir_x, dir_y, dir_z):
    sq_x, sq_y, sq_z = (dir_x * dir_x, dir_y * dir_y, dir_z * dir_z)
    prod_xy, prod_yz, prod_xz = (dir_x * dir_y, dir_y * dir_z, dir_x * dir_z)
    return [
        HARMONIC_ZERO + 0.0 * dir_x,
        -HARMONIC_ONE * dir_y,
        HARMONIC_ONE * dir_z,
        -HARMONIC_ONE * dir_x,
        HARMONIC_TWO[0] * prod_xy,
        HARMONIC_TWO[1] * prod_yz,
        HARMONIC_TWO[2] * (2.0 * sq_z - sq_x - sq_y),
        HARMONIC_TWO[3] * prod_xz,
        HARMONIC_TWO[4] * (sq_x - sq_y),
        HARMONIC_THREE[0] * dir_y * (3.0 * sq_x - sq_y),
        HARMONIC_THREE[1] * prod_xy * dir_z,
        HARMONIC_THREE[2] * dir_y * (4.0 * sq_z - sq_x - sq_y),
        HARMONIC_THREE[3] * dir_z * (2.0 * sq_z - 3.0 * sq_x - 3.0 * sq_y),
        HARMONIC_THREE[4] * dir_x * (4.0 * sq_z - sq_x - sq_y),
        HARMONIC_THREE[5] * dir_z * (sq_x - sq_y),
        HARMONIC_THREE[6] * dir_x * (sq_x - 3.0 * sq_y),
    ]


LANES = 128
SUBS = 8
GROUP = 16
STEP_ROWS = LANES // GROUP
FEATS = 8
PAIR = 2 * FEATS
OPACITY, COLOUR = 9, 10
COEF_ROWS = 32
JOIN = 4
UNROLL = 8
TAPS = 11
DEAD = -1e30
LOG_TOP = float(np.log(0.99))


def stepped(total, width, body, state):
    def step(block, held):
        for k in range(width):
            held = body(block * width + k, held)
        return held

    return lax.fori_loop(0, (total + width - 1) // width, step, state)


def lane_spread(index):
    return index // LANES, index % LANES


def take_blocks(read, count, block, place):
    result = jnp.zeros(place.shape, jnp.float32)
    for num in range(count):
        taken = jnp.take_along_axis(read(num), place, axis=1, mode="promise_in_bounds")
        result = jnp.where(block == num, taken, result)
    return result


def take_line(read, count, block, place):
    sub = lax.broadcasted_iota(jnp.int32, (SUBS, LANES), 0)
    result = take_blocks(read, -(-count // SUBS), block // SUBS, place)
    return jnp.sum(jnp.where(sub == block % SUBS, result, 0.0), axis=0, keepdims=True)


def camera_table(camera):
    columns = [camera[:, entry : entry + 1] for entry in range(6)]
    turn = rotation(columns[0:3])
    shift = columns[3:6]
    anchor = [
        -(turn[0][c] * shift[0] + turn[1][c] * shift[1] + turn[2][c] * shift[2]) for c in range(3)
    ]
    flat = [turn[r][c] for r in range(3) for c in range(3)] + shift + anchor
    lane = lax.broadcasted_iota(jnp.int32, (camera.shape[0], LANES), 1)
    table = jnp.zeros((camera.shape[0], LANES), jnp.float32)
    for num, value in enumerate(flat):
        table = jnp.where(lane == num, value, table)
    return table


def covariance(params):
    scales = [jnp.exp(params[3 + axis_num]) for axis_num in range(3)]
    inv_norm = 1.0 / jnp.sqrt(
        params[6] * params[6]
        + params[7] * params[7]
        + params[8] * params[8]
        + params[9] * params[9]
    )
    quat_w, quat_x, quat_y, quat_z = [params[6 + k] * inv_norm for k in range(4)]
    quat_rot = [
        [
            1.0 - 2.0 * (quat_y * quat_y + quat_z * quat_z),
            2.0 * (quat_x * quat_y - quat_w * quat_z),
            2.0 * (quat_x * quat_z + quat_w * quat_y),
        ],
        [
            2.0 * (quat_x * quat_y + quat_w * quat_z),
            1.0 - 2.0 * (quat_x * quat_x + quat_z * quat_z),
            2.0 * (quat_y * quat_z - quat_w * quat_x),
        ],
        [
            2.0 * (quat_x * quat_z - quat_w * quat_y),
            2.0 * (quat_y * quat_z + quat_w * quat_x),
            1.0 - 2.0 * (quat_x * quat_x + quat_y * quat_y),
        ],
    ]
    root = [[quat_rot[r][c] * scales[c] for c in range(3)] for r in range(3)]
    return [
        root[r][0] * root[k][0] + root[r][1] * root[k][1] + root[r][2] * root[k][2]
        for r, k in ((0, 0), (0, 1), (0, 2), (1, 1), (1, 2), (2, 2))
    ]


def view_basis(mean, cam):
    ray = [mean[c] - cam[12 + c] for c in range(3)]
    inv_len = 1.0 / jnp.sqrt(ray[0] * ray[0] + ray[1] * ray[1] + ray[2] * ray[2])
    return harmonics(ray[0] * inv_len, ray[1] * inv_len, ray[2] * inv_len)[1:]


def view_colours(params, cam):
    basis = [HARMONIC_ZERO] + view_basis(params[0:3], cam)
    colours = []
    for channel in range(3):
        summed = 0.5 + HARMONIC_ZERO * params[11 + 16 * channel]
        for harmonic in range(1, 16):
            summed = summed + basis[harmonic] * params[11 + 16 * channel + harmonic]
        colours.append(summed)
    return colours


def footprint(mean, cov, cam, image_width, image_height):
    turn = [[cam[3 * r + c] for c in range(3)] for r in range(3)]
    point = [
        turn[r][0] * mean[0] + turn[r][1] * mean[1] + turn[r][2] * mean[2] + cam[9 + r]
        for r in range(3)
    ]
    inv_depth = 1.0 / point[2]
    ratio_x, ratio_y = point[0] * inv_depth, point[1] * inv_depth
    zoom = FOCAL * inv_depth
    row_x = [zoom * (turn[0][c] - ratio_x * turn[2][c]) for c in range(3)]
    row_y = [zoom * (turn[1][c] - ratio_y * turn[2][c]) for c in range(3)]
    full = [[cov[0], cov[1], cov[2]], [cov[1], cov[3], cov[4]], [cov[2], cov[4], cov[5]]]
    spread_x = [
        row_x[0] * full[0][c] + row_x[1] * full[1][c] + row_x[2] * full[2][c] for c in range(3)
    ]
    spread_y = [
        row_y[0] * full[0][c] + row_y[1] * full[1][c] + row_y[2] * full[2][c] for c in range(3)
    ]
    cov_xx = spread_x[0] * row_x[0] + spread_x[1] * row_x[1] + spread_x[2] * row_x[2] + LOW_PASS
    cov_xy = spread_x[0] * row_y[0] + spread_x[1] * row_y[1] + spread_x[2] * row_y[2]
    cov_yy = spread_y[0] * row_y[0] + spread_y[1] * row_y[1] + spread_y[2] * row_y[2] + LOW_PASS
    inv_det = 1.0 / (cov_xx * cov_yy - cov_xy * cov_xy)
    return [
        FOCAL * ratio_x + image_width / 2.0,
        FOCAL * ratio_y + image_height / 2.0,
        cov_yy * inv_det,
        -cov_xy * inv_det,
        cov_xx * inv_det,
    ]


def log_opacity(logit):
    return LOG_TOP - jnp.log(1.0 + jnp.exp(-logit))


def load_params(params_ref, tile_scr, block, count):
    for band in range(0, count, SUBS):
        high = min(band + SUBS, count)
        for j in range(SUBS):
            lane_at = pl.multiple_of(block * SUBS * LANES + j * LANES, LANES)
            tile_scr[band * SUBS + j * SUBS : band * SUBS + j * SUBS + high - band, :] = params_ref[
                band:high, pl.ds(lane_at, LANES)
            ]
    return [
        tile_scr[pl.ds((r // SUBS) * SUBS * SUBS + r % SUBS, SUBS, stride=SUBS), :]
        for r in range(count)
    ]


def source_kernel(
    sizes,
    camera_hbm,
    counts_hbm,
    list_hbm,
    params_hbm,
    out_ref,
    cam_out,
    tile_scr,
    table,
    params_ref,
    list_ref,
    camera_ref,
    counts_ref,
    cam_ref,
    params_sem,
    small_sem,
):
    groups, rows, cap, lane_len = sizes
    per = params_ref.shape[1]
    wide = SUBS * LANES

    def params_copy(block):
        lanes = pl.ds(pl.multiple_of(block * wide, wide), wide)
        return pltpu.make_async_copy(
            params_hbm.at[:, lanes], params_ref.at[:, lanes], params_sem.at[block]
        )

    camera_copy = pltpu.make_async_copy(camera_hbm, camera_ref, small_sem.at[2])
    camera_copy.start()
    for block in range(per // wide):
        params_copy(block).start()
    list_copy = pltpu.make_async_copy(list_hbm, list_ref, small_sem.at[0])
    list_copy.start()
    counts_copy = pltpu.make_async_copy(counts_hbm, counts_ref, small_sem.at[3])
    counts_copy.start()
    camera_copy.wait()
    cam_out[...] = camera_table(camera_ref[...])
    cam_copy = pltpu.make_async_copy(cam_out, cam_ref, small_sem.at[1])
    cam_copy.start()
    cam_copy.wait()
    parts = cap // lane_len
    used = (1 + groups) * FEATS
    count_blocks = per // LANES

    def project_block(block, carry):
        params_copy(block).wait()
        params = load_params(params_ref, tile_scr, block, params_ref.shape[0])
        at = block * SUBS * used
        shared = params[0:3] + covariance(params) + [log_opacity(params[10])]
        for num, value in enumerate(shared[0:FEATS]):
            table[pl.ds(at + num, SUBS, stride=used), :] = value
        for group in range(groups):
            lines = shared[FEATS:]
            for view in range(2):
                lines = lines + view_colours(
                    params, [cam_ref[2 * group + view, k] for k in range(15)]
                )
            for num, value in enumerate(lines):
                table[pl.ds(at + (1 + group) * FEATS + num, SUBS, stride=used), :] = value
        return carry

    lax.fori_loop(0, per // wide, project_block, 0)
    list_copy.wait()
    counts_copy.wait()
    lane = lax.broadcasted_iota(jnp.int32, (SUBS, LANES), 1)

    def send_block(dest, start_at):
        count = counts_ref[0, dest]
        line = pl.multiple_of((1 + dest // rows) * FEATS, FEATS)
        for part in range(parts):

            @pl.when(count > part * lane_len)
            def _(part=part):
                first = start_at + part * lane_len
                block, turn = first // LANES, first % LANES
                pieces = []
                for step in range(2):
                    at = jnp.minimum(block + step, count_blocks - 1) * LANES
                    names = list_ref[0:1, pl.ds(pl.multiple_of(at, LANES), LANES)]
                    pieces.append(
                        pltpu.roll(jnp.broadcast_to(names, (SUBS, LANES)), LANES - turn, 1)
                    )
                index = jnp.where(lane < LANES - turn, pieces[0], pieces[1])
                home, place = lane_spread(index)
                for side in range(2):
                    at = line if side else 0
                    taken = take_blocks(
                        lambda num, at=at: table[pl.ds(num * used + at, FEATS), :],
                        count_blocks,
                        home,
                        place,
                    )
                    line_at = part * PAIR + side * FEATS
                    out_ref[dest, line_at : line_at + FEATS, :] = taken[:, 0:lane_len]

        return start_at + count

    lax.fori_loop(0, groups * rows, send_block, jnp.int32(0))


def split_three(value):
    first = value.astype(jnp.bfloat16).astype(jnp.float32)
    rest = value - first
    second = rest.astype(jnp.bfloat16).astype(jnp.float32)
    return [first, second, rest - second]


def in_two(value):
    high = value.astype(jnp.bfloat16).astype(jnp.float32)
    return [high, value - high]


def swap_grain(cells):
    sub = lax.broadcasted_iota(jnp.int32, (SUBS, LANES), 0)
    lane = lax.broadcasted_iota(jnp.int32, (SUBS, LANES), 1) // TILE
    for bit in (1, 2, 4):
        sub_bit, lane_bit = (sub & bit) != 0, (lane & bit) != 0
        from_high = pltpu.roll(pltpu.roll(cells, SUBS - bit, 0), bit * TILE, 1)
        from_low = pltpu.roll(pltpu.roll(cells, bit, 0), LANES - bit * TILE, 1)
        cells = jnp.where(sub_bit == lane_bit, cells, jnp.where(lane_bit, from_high, from_low))
    return cells


def longest(lens_ref, group):
    most = lens_ref[group * GROUP]
    for t in range(1, GROUP):
        most = jnp.maximum(most, lens_ref[group * GROUP + t])
    return most


def gather_slots(arrived_ref, slot_scr, lane_len):
    parts = arrived_ref.shape[1] // PAIR
    joined = LANES // lane_len

    def unpack(block, carry):
        line_at = pl.multiple_of(block * PAIR, PAIR)
        for k in range(joined):
            source = block * joined // parts + k
            part_at = pl.multiple_of(block * joined % parts * PAIR, PAIR)
            slot_scr[pl.ds(line_at, PAIR), k * lane_len : (k + 1) * lane_len] = arrived_ref[
                source, pl.ds(part_at, PAIR), :
            ]
        return carry

    lax.fori_loop(0, slot_scr.shape[0] // PAIR, unpack, 0)


def slot_lines(slot_scr, first):
    return [slot_scr[pl.ds(first * PAIR + num, SUBS, stride=PAIR), :] for num in range(PAIR)]


def render_kernel(
    sizes,
    place_ref,
    cam_ref,
    lens_ref,
    lens_rows_ref,
    names_ref,
    basis_ref,
    arrived_ref,
    image_ref,
    left_ref,
    shape_ref,
    slot_scr,
    table,
    logs,
    feat_scr,
    pieces,
    mm,
):
    cap, lane_len, col_groups, list_len, image_width, image_height = sizes
    devices = arrived_ref.shape[0]
    blocks = list_len // STEP_ROWS
    count_blocks = devices * cap // LANES
    gather_slots(arrived_ref, slot_scr, lane_len)

    def project_block(step, carry):
        first = step * SUBS
        lines = slot_lines(slot_scr, first)
        logs[pl.ds(pl.multiple_of(first, SUBS), SUBS), :] = lines[OPACITY]
        for view in range(2):
            cam = [cam_ref[2 * place_ref[1] + view, k] for k in range(15)]
            feats = footprint(lines[0:3], lines[3:9], cam, image_width, image_height)
            feats = feats + lines[COLOUR + 3 * view : COLOUR + 3 * view + 3]
            for num, value in enumerate(feats):
                row_at = (view * count_blocks + first) * FEATS + num
                table[pl.ds(row_at, SUBS, stride=FEATS), :] = value
        return carry

    lax.fori_loop(0, count_blocks // SUBS, project_block, 0)
    centre_y = (place_ref[0] * TILE).astype(jnp.float32) + (TILE - 1) / 2.0
    sub = lax.broadcasted_iota(jnp.int32, (blocks, LANES), 0)
    lane = lax.broadcasted_iota(jnp.int32, (blocks, LANES), 1)
    zero = jnp.zeros((GROUP, LANES), jnp.float32)

    def one_group(group, carry):
        view, col_group = group // col_groups, group % col_groups
        most = longest(lens_ref, group)

        def fetch(block, inner):
            names = names_ref[pl.ds(group * blocks + block, 1), :]
            home, place = lane_spread(jnp.broadcast_to(names, (SUBS, LANES)))
            feat_at = pl.multiple_of(block * PAIR, PAIR)
            feat_scr[pl.ds(feat_at, FEATS), :] = take_blocks(
                lambda num: table[
                    pl.ds(pl.multiple_of((view * count_blocks + num) * FEATS, FEATS), FEATS), :
                ],
                count_blocks,
                home,
                place,
            )
            feat_scr[pl.ds(feat_at + FEATS, 1), :] = take_line(
                lambda num: logs[num * SUBS : (num + 1) * SUBS, :], count_blocks, home, place
            )
            return inner

        stepped((most + STEP_ROWS - 1) // STEP_ROWS, 2, fetch, 0)
        feats = [feat_scr[pl.ds(num, blocks, stride=PAIR), :] for num in range(FEATS)]
        log_o = feat_scr[pl.ds(FEATS, blocks, stride=PAIR), :]
        live = sub * STEP_ROWS + lane // GROUP < lens_rows_ref[pl.ds(group, 1), :]
        centre_x = ((col_group * GROUP + lane % GROUP) * TILE).astype(jnp.float32) + (
            TILE - 1
        ) / 2.0
        off_x, off_y = feats[0] - centre_x, feats[1] - centre_y
        lin_x = feats[2] * off_x + feats[3] * off_y
        lin_y = feats[4] * off_y + feats[3] * off_x
        coefs = [
            log_o - 0.5 * (off_x * lin_x + off_y * lin_y),
            lin_x,
            lin_y,
            -0.5 * feats[2],
            -feats[3],
            -0.5 * feats[4],
        ]
        coefs = [
            jnp.where(live, value, DEAD if num == 0 else 0.0) for num, value in enumerate(coefs)
        ]
        lines = [None] * COEF_ROWS
        for num, value in enumerate(coefs):
            for piece, part in enumerate(split_three(value)):
                lines[piece * 6 + num] = part
        for num in range(3):
            for piece, part in enumerate(split_three(jnp.where(live, feats[5 + num], 0.0))):
                lines[18 + piece * 3 + num] = part
        for num, value in enumerate(lines):
            pieces[pl.ds(num, blocks, stride=COEF_ROWS), :] = (
                jnp.zeros((blocks, LANES), jnp.float32) if value is None else value
            )
        for num, value in enumerate(feats[2:5] + [off_x, off_y]):
            shape_ref[num, pl.ds(pl.multiple_of(group * blocks, blocks), blocks), :] = jnp.where(
                live, value, 0.0
            )
        left_at = pl.multiple_of(group * blocks * LANES, LANES)
        for block in range(blocks):
            left_ref[pl.ds(left_at + block * LANES, LANES), :] = pieces[
                block * COEF_ROWS : (block + 1) * COEF_ROWS, :
            ].T.astype(jnp.bfloat16)
        expand(left_ref, basis_ref, mm, left_at)

        def entry(n, state):
            keep, colour = state
            row_at = pl.multiple_of(n * GROUP, GROUP)
            shade = [
                mm[pl.ds(row_at, GROUP), (2 + c) * LANES : (3 + c) * LANES] for c in range(3)
            ]
            new_keep, new_colour = [], []
            for half in range(2):
                alpha = jnp.exp(mm[pl.ds(row_at, GROUP), half * LANES : (half + 1) * LANES])
                weight = keep[half] * alpha
                new_keep.append(keep[half] * (1.0 - alpha))
                new_colour.append([colour[half][c] + weight * shade[c] for c in range(3)])
            return new_keep, new_colour

        state = ([zero + 1.0] * 2, [[zero] * 3] * 2)
        _, colour = stepped(most, UNROLL, entry, state)
        for side in range(GROUP // SUBS):
            lane_at = pl.multiple_of(col_group * GROUP * TILE + side * LANES, LANES)
            for half in range(2):
                for c in range(3):
                    image_ref[view, c, half * SUBS : (half + 1) * SUBS, pl.ds(lane_at, LANES)] = (
                        swap_grain(colour[half][c][side * SUBS : (side + 1) * SUBS])
                    )
        return carry

    lax.fori_loop(0, 2 * col_groups, one_group, 0)


def expand(left_ref, basis_ref, mm, left_at):
    mm[...] = jnp.dot(
        left_ref[pl.ds(left_at, mm.shape[0]), :],
        basis_ref[...],
        preferred_element_type=jnp.float32,
    )


def back_kernel(
    sizes,
    place_ref,
    cam_ref,
    lens_ref,
    names_ref,
    basis_ref,
    moment_ref,
    left_ref,
    shape_ref,
    arrived_ref,
    grad_ref,
    out_ref,
    mm,
    alphas,
    weights,
    slopes,
    grad_scr,
    mom_scr,
    line_scr,
    masked,
    places,
    total_scr,
    slot_scr,
):
    cap, lane_len, col_groups, list_len, image_width, image_height = sizes
    devices = out_ref.shape[0]
    parts = cap // lane_len
    blocks = list_len // STEP_ROWS
    count_blocks = devices * cap // LANES
    joined = LANES // lane_len
    value_rows = count_blocks * 2 * FEATS
    total_scr[...] = jnp.zeros_like(total_scr)
    line_scr[...] = jnp.zeros_like(line_scr)
    grad_scr[...] = jnp.zeros_like(grad_scr)
    zero = jnp.zeros((GROUP, LANES), jnp.float32)
    sub = lax.broadcasted_iota(jnp.int32, (GROUP, LANES), 0)
    lane = lax.broadcasted_iota(jnp.int32, (GROUP, LANES), 1)
    own_tile = lane % GROUP == sub

    def one_group(group, carry):
        view, col_group = group // col_groups, group % col_groups
        most = longest(lens_ref, group)
        lane_at = pl.multiple_of(col_group * GROUP * TILE, LANES)
        grads = [
            [
                jnp.concatenate(
                    [
                        swap_grain(
                            grad_ref[
                                view,
                                c,
                                half * SUBS : (half + 1) * SUBS,
                                pl.ds(lane_at + side * LANES, LANES),
                            ]
                        )
                        for side in range(GROUP // SUBS)
                    ],
                    axis=0,
                )
                for c in range(3)
            ]
            for half in range(2)
        ]
        for half in range(2):
            for c in range(3):
                for piece, part in enumerate(in_two(grads[half][c])):
                    line = (piece * 3 + c) * GROUP
                    grad_scr[line : line + GROUP, half * LANES : (half + 1) * LANES] = part
        expand(left_ref, basis_ref, mm, pl.multiple_of(group * blocks * LANES, LANES))

        def ahead(n, keep):
            row_at = pl.multiple_of(n * GROUP, GROUP)
            new_keep = []
            for half in range(2):
                lanes = slice(half * LANES, (half + 1) * LANES)
                alpha = jnp.exp(mm[pl.ds(row_at, GROUP), lanes])
                weight = keep[half] * alpha
                alphas[pl.ds(row_at, GROUP), lanes] = alpha
                weights[pl.ds(row_at, GROUP), lanes] = weight
                new_keep.append(keep[half] * (1.0 - alpha))
            return new_keep

        stepped(most, UNROLL, ahead, [zero + 1.0] * 2)

        last = (most + UNROLL - 1) // UNROLL * UNROLL - 1

        def behind(step, seen):
            row_at = pl.multiple_of((last - step) * GROUP, GROUP)
            shade = [
                mm[pl.ds(row_at, GROUP), (2 + c) * LANES : (3 + c) * LANES] for c in range(3)
            ]
            new_seen = []
            for half in range(2):
                lanes = slice(half * LANES, (half + 1) * LANES)
                own = (
                    grads[half][0] * shade[0]
                    + grads[half][1] * shade[1]
                    + grads[half][2] * shade[2]
                )
                alpha = alphas[pl.ds(row_at, GROUP), lanes]
                slopes[pl.ds(row_at, GROUP), lanes] = weights[pl.ds(row_at, GROUP), lanes] * (
                    own - seen[half]
                )
                new_seen.append(seen[half] * (1.0 - alpha) + alpha * own)
            return new_seen

        stepped(most, UNROLL, behind, [zero] * 2)
        total = jnp.zeros((blocks * LANES, LANES), jnp.float32)
        for value, right in (
            (slopes[...], moment_ref[...]),
            (weights[...], grad_scr[...].T.astype(jnp.bfloat16)),
        ):
            high = value.astype(jnp.bfloat16)
            low = (value - high.astype(jnp.float32)).astype(jnp.bfloat16)
            total = total + jnp.dot(high, right, preferred_element_type=jnp.float32)
            total = total + jnp.dot(low, right, preferred_element_type=jnp.float32)
        for block in range(blocks):
            turned = total[block * LANES : (block + 1) * LANES].T
            mom_scr[block * TILE : block * TILE + 8, :] = turned[6 * GROUP : 6 * GROUP + 8]
            for c in range(3):
                summed = (
                    turned[c * GROUP : (c + 1) * GROUP]
                    + turned[(3 + c) * GROUP : (4 + c) * GROUP]
                )
                mom_scr[block * TILE + 8 + c : block * TILE + 9 + c, :] = jnp.sum(
                    jnp.where(own_tile, summed, 0.0), axis=0, keepdims=True
                )
        mom = [mom_scr[pl.ds(num, blocks, stride=TILE), :] for num in range(11)]
        con_xx, con_xy, con_yy, off_x, off_y = [
            shape_ref[num, pl.ds(pl.multiple_of(group * blocks, blocks), blocks), :]
            for num in range(5)
        ]
        sum_x = off_x * mom[0] - mom[1]
        sum_y = off_y * mom[0] - mom[2]
        results = [
            -(con_xx * sum_x + con_xy * sum_y),
            -(con_yy * sum_y + con_xy * sum_x),
            -0.5 * (off_x * (sum_x - mom[1]) + mom[3]),
            -(off_x * sum_y - off_y * mom[1] + mom[4]),
            -0.5 * (off_y * (sum_y - mom[2]) + mom[5]),
        ] + mom[8:11]
        for num, value in enumerate(results + [mom[0]]):
            line_scr[pl.ds(num, blocks, stride=PAIR), :] = value

        def spread(step, inner):
            for k in range(JOIN):
                block = step * JOIN + k
                lanes = slice(k * LANES, (k + 1) * LANES)
                names = names_ref[pl.ds(group * blocks + block, 1), :]
                home, place = names // LANES, names % LANES
                line_at = pl.multiple_of(block * PAIR, PAIR)
                values = in_two(line_scr[pl.ds(line_at, FEATS), :])
                logs = in_two(line_scr[pl.ds(line_at + FEATS, 1), :])
                home_wide = jnp.broadcast_to(home, (2 * FEATS, LANES)).astype(jnp.bfloat16)
                pair = jnp.concatenate(values, axis=0).astype(jnp.bfloat16)
                for num in range(count_blocks):
                    masked[num * 2 * FEATS : (num + 1) * 2 * FEATS, lanes] = jnp.where(
                        home_wide == jnp.bfloat16(num), pair, jnp.bfloat16(0)
                    )
                rank = lax.broadcasted_iota(jnp.int32, (count_blocks, LANES), 0)
                for piece, value in enumerate(logs):
                    first = value_rows + piece * count_blocks
                    masked[first : first + count_blocks, lanes] = jnp.where(
                        rank == home, value, 0.0
                    ).astype(jnp.bfloat16)
                seat = lax.broadcasted_iota(jnp.int32, (LANES, LANES), 0)
                places[:, lanes] = jnp.where(seat == place, 1.0, 0.0).astype(jnp.bfloat16)
            total_scr[view] += lax.dot_general(
                masked[...],
                places[...],
                (((1,), (1,)), ((), ())),
                preferred_element_type=jnp.float32,
            )
            return inner

        width = JOIN * STEP_ROWS
        lax.fori_loop(0, (most + width - 1) // width, spread, 0)
        return carry

    lax.fori_loop(0, 2 * col_groups, one_group, 0)

    gather_slots(arrived_ref, slot_scr, lane_len)

    def pull_block(step, carry):
        first = step * SUBS
        lines = slot_lines(slot_scr, first)
        cams = [[cam_ref[2 * place_ref[1] + view, k] for k in range(15)] for view in range(2)]

        def both(*values):
            return [
                footprint(values[0:3], values[3:9], cam, image_width, image_height)
                for cam in cams
            ]

        cots = []
        log_sum = jnp.zeros((SUBS, LANES), jnp.float32)
        for view in range(2):
            row_at = first * 2 * FEATS
            cots.append(
                [
                    total_scr[view, pl.ds(row_at + num, SUBS, stride=2 * FEATS), :]
                    + total_scr[view, pl.ds(row_at + FEATS + num, SUBS, stride=2 * FEATS), :]
                    for num in range(FEATS)
                ]
            )
            for piece in range(2):
                row = pl.multiple_of(value_rows + piece * count_blocks + first, SUBS)
                log_sum = log_sum + total_scr[view, pl.ds(row, SUBS), :]
        _, pull = jax.vjp(both, *lines[0:9])
        results = list(pull([cot[0:5] for cot in cots])) + [log_sum] + cots[0][5:] + cots[1][5:]
        for num, value in enumerate(results):
            slot_scr[pl.ds(first * PAIR + num, SUBS, stride=PAIR), :] = value
        return carry

    lax.fori_loop(0, count_blocks // SUBS, pull_block, 0)

    def pack(block, carry):
        line_at = pl.multiple_of(block * PAIR, PAIR)
        for k in range(joined):
            source = block * joined // parts + k
            part_at = pl.multiple_of(block * joined % parts * PAIR, PAIR)
            out_ref[source, pl.ds(part_at, PAIR), :] = slot_scr[
                pl.ds(line_at, PAIR), k * lane_len : (k + 1) * lane_len
            ]
        return carry

    lax.fori_loop(0, count_blocks, pack, 0)


def prepare_kernel(
    sizes, cam_ref, counts_ref, list_ref, params_ref, sent_ref, parts_ref, tile_scr, rows_scr
):
    groups, rows = sizes
    per = params_ref.shape[1]
    blocks = per // LANES
    devices = groups * rows
    rank = lax.broadcasted_iota(jnp.int32, (blocks, LANES), 0)
    lane = lax.broadcasted_iota(jnp.int32, (blocks, LANES), 1)
    spot = rank * LANES + lane

    def pass_run(dest, state):
        start, home = state
        start = start + counts_ref[0, dest]
        return start, home + jnp.where(spot >= start, 1, 0)

    start, home = lax.fori_loop(0, devices, pass_run, (jnp.int32(0), jnp.zeros_like(spot)))
    rows_scr[...] = jnp.where(spot < start, home // rows + 1, 0).astype(jnp.float32)

    def place_names(step, total):
        masked, places = [], []
        for k in range(JOIN):
            block = step * JOIN + k
            names = list_ref[0:1, pl.ds(pl.multiple_of(block * LANES, LANES), LANES)]
            home, place = names // LANES, names % LANES
            masked.append(
                jnp.where(rank == home, rows_scr[pl.ds(block, 1), :], 0.0).astype(jnp.bfloat16)
            )
            seat = lax.broadcasted_iota(jnp.int32, (LANES, LANES), 0)
            places.append(jnp.where(seat == place, 1.0, 0.0).astype(jnp.bfloat16))
        return total + lax.dot_general(
            jnp.concatenate(masked, axis=1),
            jnp.concatenate(places, axis=1),
            (((1,), (1,)), ((), ())),
            preferred_element_type=jnp.float32,
        )

    sent_ref[...] = lax.fori_loop(
        0, blocks // JOIN, place_names, jnp.zeros((blocks, LANES), jnp.float32)
    )

    def one_block(block, carry):
        params = load_params(params_ref, tile_scr, block, params_ref.shape[0])
        at = pl.multiple_of(block * SUBS, SUBS)
        home = sent_ref[pl.ds(at, SUBS), :]
        one, none = jnp.ones((SUBS, LANES), jnp.float32), jnp.zeros((SUBS, LANES), jnp.float32)
        for view in range(2):
            cam = []
            for k in range(15):
                value = jnp.full((SUBS, LANES), cam_ref[view, k], jnp.float32)
                for group in range(1, groups):
                    value = jnp.where(home > group + 0.5, cam_ref[2 * group + view, k], value)
                cam.append(value)
            first = view * (TILE - 1 + 9)
            for axis in range(3):
                toward = [one if k == axis else none for k in range(3)]
                basis, slopes = jax.jvp(
                    lambda *mean, cam=cam: view_basis(mean, cam), tuple(params[0:3]), tuple(toward)
                )
                if axis == 0:
                    for k in range(15):
                        parts_ref[first + k, pl.ds(at, SUBS), :] = basis[k]
                for channel in range(3):
                    summed = none
                    for k in range(15):
                        summed = summed + slopes[k] * params[12 + 16 * channel + k]
                    parts_ref[first + 15 + 3 * channel + axis, pl.ds(at, SUBS), :] = summed
        return carry

    lax.fori_loop(0, blocks // SUBS, one_block, 0)


def owner_kernel(
    lane_len,
    counts_ref,
    list_ref,
    sent_ref,
    parts_hbm,
    params_ref,
    back_ref,
    out_ref,
    tile_scr,
    parts_ref,
    slot_scr,
    masked,
    places,
    total_scr,
    parts_sem,
):
    count_params, per = params_ref.shape
    count_blocks = per // LANES
    parts_copy = pltpu.make_async_copy(parts_hbm, parts_ref, parts_sem)
    parts_copy.start()
    slot_scr[...] = jnp.zeros_like(slot_scr)
    total_scr[...] = jnp.zeros_like(total_scr)
    lane = lax.broadcasted_iota(jnp.int32, (PAIR, LANES), 1)

    def close_up(dest, start):
        count = counts_ref[0, dest]
        for part in range(back_ref.shape[1] // PAIR):

            @pl.when(count > part * lane_len)
            def _(part=part):
                lines = back_ref[dest, part * PAIR : (part + 1) * PAIR, :]
                if lane_len < LANES:
                    lines = jnp.concatenate(
                        [lines, jnp.zeros((PAIR, LANES - lane_len), jnp.float32)], axis=1
                    )
                valid = jnp.minimum(count - part * lane_len, lane_len)
                first = start + part * lane_len
                block, turn = first // LANES, first % LANES
                lines = pltpu.roll(lines, turn, 1)
                for step in range(2):
                    place = lane - turn + step * LANES
                    rows = pl.ds(pl.multiple_of((block + step) * PAIR, PAIR), PAIR)
                    slot_scr[rows, :] = jnp.where(
                        (place >= 0) & (place < valid), lines, slot_scr[rows, :]
                    )

        return start + count

    total = lax.fori_loop(0, counts_ref.shape[1], close_up, jnp.int32(0))
    wide = 2 * PAIR

    def spread(step, carry):
        for k in range(JOIN):
            block = step * JOIN + k
            lanes = slice(k * LANES, (k + 1) * LANES)
            names = list_ref[0:1, pl.ds(pl.multiple_of(block * LANES, LANES), LANES)]
            home, place = names // LANES, names % LANES
            home_wide = jnp.broadcast_to(home, (wide, LANES)).astype(jnp.bfloat16)
            pieces = in_two(slot_scr[pl.ds(pl.multiple_of(block * PAIR, PAIR), PAIR), :])
            both = jnp.concatenate(pieces, axis=0).astype(jnp.bfloat16)
            for num in range(count_blocks):
                masked[num * wide : (num + 1) * wide, lanes] = jnp.where(
                    home_wide == jnp.bfloat16(num), both, jnp.bfloat16(0)
                )
            seat = lax.broadcasted_iota(jnp.int32, (LANES, LANES), 0)
            places[:, lanes] = jnp.where(seat == place, 1.0, 0.0).astype(jnp.bfloat16)
        total_scr[...] += lax.dot_general(
            masked[...], places[...], (((1,), (1,)), ((), ())), preferred_element_type=jnp.float32
        )
        return carry

    span = JOIN * LANES
    lax.fori_loop(0, (total + span - 1) // span, spread, 0)
    parts_copy.wait()

    def pull_block(block, carry):
        at = pl.multiple_of(block * SUBS, SUBS)
        first = block * SUBS * wide
        cots = [
            total_scr[pl.ds(first + num, SUBS, stride=wide), :]
            + total_scr[pl.ds(first + PAIR + num, SUBS, stride=wide), :]
            for num in range(PAIR)
        ]
        sent = sent_ref[pl.ds(at, SUBS), :] > 0.5
        params = load_params(params_ref, tile_scr, block, PAIR)

        def both(*values):
            every = params[0:3] + list(values)
            return covariance(every) + [log_opacity(every[10])]

        _, pull = jax.vjp(both, *params[3:11])
        grads = cots[0:3] + list(pull(cots[3:COLOUR])) + [None] * 48
        for channel in range(3):
            tints = [cots[COLOUR + 3 * view + channel] for view in range(2)]
            grads[11 + 16 * channel] = HARMONIC_ZERO * (tints[0] + tints[1])
            for k in range(15):
                grads[12 + 16 * channel + k] = (
                    tints[0] * parts_ref[k, pl.ds(at, SUBS), :]
                    + tints[1] * parts_ref[24 + k, pl.ds(at, SUBS), :]
                )
            for axis in range(3):
                for view in range(2):
                    line = 24 * view + 15 + 3 * channel + axis
                    grads[axis] = grads[axis] + tints[view] * parts_ref[line, pl.ds(at, SUBS), :]
        for num, value in enumerate(grads):
            tile_scr[pl.ds((num // SUBS) * SUBS * SUBS + num % SUBS, SUBS, stride=SUBS), :] = (
                jnp.where(sent, value, 0.0)
            )
        for band in range(0, count_params, SUBS):
            high = min(band + SUBS, count_params)
            for j in range(SUBS):
                lane_at = pl.multiple_of(block * SUBS * LANES + j * LANES, LANES)
                out_ref[band:high, pl.ds(lane_at, LANES)] = tile_scr[
                    band * SUBS + j * SUBS : band * SUBS + j * SUBS + high - band, :
                ]
        return carry

    lax.fori_loop(0, count_blocks // SUBS, pull_block, 0)


def tap_rows(read, first, count):
    taps = window_taps()
    total = taps[5] * read(first + 5, count)
    for k in range(5):
        total = total + taps[k] * (read(first + k, count) + read(first + TAPS - 1 - k, count))
    return total


def blur_lanes(value, band):
    return jnp.dot(
        value, band, precision=lax.Precision.HIGHEST, preferred_element_type=jnp.float32
    )


def truth_kernel(band_ref, above_ref, own_ref, below_ref, out_ref, tall, mixed):
    images = own_ref.shape[0]

    def one_image(m, carry):
        whole = jnp.concatenate([above_ref[m], own_ref[m], below_ref[m]], axis=0)
        for field, value in enumerate((whole, whole * whole)):
            tall[...] = value
            row_at = pl.multiple_of((field * images + m) * 2 * TILE, 2 * TILE)
            mixed[pl.ds(row_at, 2 * TILE), :] = tap_rows(
                lambda at, count: tall[at : at + count, :], 6, 2 * TILE
            )
        return carry

    lax.fori_loop(0, images, one_image, 0)
    out_ref[...] = blur_lanes(mixed[...], band_ref[...])


def loss_kernel(
    image_rows,
    row_ref,
    band_ref,
    truth_ref,
    true_above,
    true_own,
    true_below,
    above_ref,
    own_ref,
    below_ref,
    out_ref,
    tall,
    mixed,
    blurred,
    slim,
):
    images = own_ref.shape[0]
    tall_rows = 2 * TILE
    width = own_ref.shape[2]

    def one_image(m, carry):
        whole = jnp.concatenate([above_ref[m], own_ref[m], below_ref[m]], axis=0)
        true = jnp.concatenate([true_above[m], true_own[m], true_below[m]], axis=0)
        for field, value in enumerate((whole, whole * whole, whole * true)):
            tall[field] = value
            row_at = pl.multiple_of((field * images + m) * tall_rows, tall_rows)
            mixed[pl.ds(row_at, tall_rows), :] = tap_rows(
                lambda at, count, field=field: tall[field, at : at + count, :], 6, tall_rows
            )
        return carry

    lax.fori_loop(0, images, one_image, 0)
    blurred[...] = blur_lanes(mixed[...], band_ref[...])
    sub = lax.broadcasted_iota(jnp.int32, (tall_rows, width), 0)
    image_row = row_ref[0] * TILE + sub - 5
    inside = (image_row >= 0) & (image_row < image_rows) & (sub < TILE + 10)

    def one_map(m, carry):
        def field_of(ref, field):
            row_at = pl.multiple_of((field * images + m) * tall_rows, tall_rows)
            return ref[pl.ds(row_at, tall_rows), :]

        mean_one, both_one, cross = [field_of(blurred, field) for field in range(3)]
        mean_two, both_two = field_of(truth_ref, 0), field_of(truth_ref, 1)
        square_one, square_two = mean_one * mean_one, mean_two * mean_two
        mean_cross = mean_one * mean_two
        top_one = 2.0 * mean_cross + SSIM_ONE
        top_two = 2.0 * (cross - mean_cross) + SSIM_TWO
        low_one = square_one + square_two + SSIM_ONE
        low_two = (both_one - square_one) + (both_two - square_two) + SSIM_TWO
        inv_one, inv_two = 1.0 / low_one, 1.0 / low_two
        inv_both = inv_one * inv_two
        value = top_one * top_two * inv_both
        grads = [
            2.0 * mean_two * (top_two - top_one) * inv_both
            - 2.0 * mean_one * value * (inv_one - inv_two),
            -value * inv_two,
            2.0 * top_one * inv_both,
        ]
        for field, grad in enumerate(grads):
            tall[field, 0:tall_rows] = jnp.where(inside, grad, 0.0)
            row_at = pl.multiple_of((field * images + m) * TILE, TILE)
            slim[pl.ds(row_at, TILE), :] = tap_rows(
                lambda at, count, field=field: tall[field, at : at + count, :], 0, TILE
            )
        return carry

    lax.fori_loop(0, images, one_map, 0)
    spread = blur_lanes(slim[...], band_ref[...]).reshape(3, images, TILE, width)
    own, true = own_ref[...], true_own[...]
    gap = own - true
    out_ref[...] = (1.0 - SSIM_SHARE) * gap / jnp.sqrt(gap * gap + SMOOTH_EPS) - SSIM_SHARE * (
        spread[0] + 2.0 * own * spread[1] + true * spread[2]
    )


def band_matrix(width):
    taps = window_taps()
    band = np.zeros((width, width), np.float32)
    for k in range(TAPS):
        band += np.diag(np.full(width - abs(k - 5), taps[k], np.float32), k - 5)
    return jnp.asarray(band)


def pixel_basis():
    pixel = np.arange(TILE * TILE)
    x = (pixel % TILE) - (TILE - 1) / 2.0
    y = (pixel // TILE) - (TILE - 1) / 2.0
    return np.stack([np.ones_like(x), x, y, x * x, x * y, y * y])


def expand_matrix():
    terms = pixel_basis()
    matrix = np.zeros((COEF_ROWS, 5 * LANES), np.float32)
    for piece in range(3):
        matrix[piece * 6 : piece * 6 + 6, 0 : 2 * LANES] = terms
        for c in range(3):
            matrix[18 + piece * 3 + c, (2 + c) * LANES : (3 + c) * LANES] = 1.0
    return jnp.asarray(matrix, jnp.bfloat16)


def moment_matrix():
    matrix = np.zeros((2 * LANES, LANES), np.float32)
    matrix[:, 6 * GROUP : 6 * GROUP + 6] = pixel_basis().T
    return jnp.asarray(matrix, jnp.bfloat16)


def smem():
    return pl.BlockSpec(memory_space=pltpu.SMEM)


def vmem():
    return pl.BlockSpec(memory_space=pltpu.VMEM)


def hbm():
    return pl.BlockSpec(memory_space=pltpu.HBM)


def scratch(*shape):
    return pltpu.VMEM(shape, jnp.float32)


def run(kernel, megabytes, out_shapes, in_specs, scratches, *operands):
    return pl.pallas_call(
        kernel,
        out_shape=out_shapes,
        in_specs=in_specs,
        out_specs=jax.tree.map(lambda _: vmem(), out_shapes),
        scratch_shapes=scratches,
        compiler_params=pltpu.CompilerParams(vmem_limit_bytes=megabytes << 20),
    )(*operands)


def shards(params, send_list, send_counts, camera, ground_truth, tile_lists, list_lengths):
    devices = lax.axis_size(("view", "tile"))
    row_devices = lax.axis_size("tile")
    groups = lax.axis_size("view")
    count_params, per_device = params.shape
    capacity = per_device // devices
    tile_cols, list_len = tile_lists.shape[2:]
    col_groups = tile_cols // GROUP
    blocks = list_len // STEP_ROWS
    tile_row = lax.axis_index("tile")
    image_width = float(ground_truth.shape[3])
    image_height = float(ground_truth.shape[2] * row_devices)
    lane_len = min(capacity, LANES)
    sent_shape = jax.ShapeDtypeStruct(
        (devices, capacity // lane_len * PAIR, lane_len), jnp.float32
    )
    count_blocks = per_device // LANES

    flat_lengths = list_lengths.reshape(-1)
    entry_rank = jnp.arange(list_len, dtype=jnp.int32)
    tile_num = jnp.arange(2 * tile_cols, dtype=jnp.int32)
    lists = jnp.where(
        entry_rank[None, :] < flat_lengths[:, None],
        tile_lists.reshape(2 * tile_cols, list_len),
        per_device + tile_num[:, None] % GROUP,
    )
    lens_rows = jnp.tile(flat_lengths.reshape(-1, GROUP), (1, LANES // GROUP))

    width = ground_truth.shape[3]
    true_own = ground_truth.reshape(-1, TILE, width)
    true_above = from_behind(true_own, "tile", 1)
    true_below = from_behind(true_own, "tile", -1)
    band = band_matrix(width)
    truth_rows = 2 * true_own.shape[0] * 2 * TILE
    truth_blur = run(
        truth_kernel,
        16,
        jax.ShapeDtypeStruct((truth_rows, width), jnp.float32),
        [vmem()] * 4,
        [scratch(3 * TILE, width), scratch(truth_rows, width)],
        band,
        true_above,
        true_own,
        true_below,
    )

    own_sizes = (groups, row_devices, capacity, lane_len)
    sent, cams = run(
        lambda *refs: source_kernel(own_sizes, *refs),
        24,
        (sent_shape, jax.ShapeDtypeStruct((camera.shape[0], LANES), jnp.float32)),
        [hbm()] * 4,
        [
            scratch(SUBS * SUBS * SUBS, LANES),
            scratch(count_blocks * (1 + groups) * FEATS, LANES),
            scratch(*params.shape),
            pltpu.VMEM(send_list.shape, jnp.int32),
            scratch(*camera.shape),
            pltpu.SMEM(send_counts.shape, jnp.int32),
            pltpu.SMEM((camera.shape[0], LANES), jnp.float32),
            pltpu.SemaphoreType.DMA((count_blocks // SUBS,)),
            pltpu.SemaphoreType.DMA((4,)),
        ],
        camera,
        send_counts,
        send_list,
        params,
    )
    arrived = lax.all_to_all(sent, ("view", "tile"), split_axis=0, concat_axis=0, tiled=True)

    arrived, truth_blur = lax.optimization_barrier((arrived, truth_blur))
    tile_sizes = (capacity, lane_len, col_groups, list_len, image_width, image_height)
    place = jnp.stack([tile_row, lax.axis_index("view")])
    entries = 2 * tile_cols * list_len
    names = lists.reshape(-1, GROUP, list_len).transpose(0, 2, 1).reshape(-1, LANES)
    rendered, left, shapes = run(
        lambda *refs: render_kernel(tile_sizes, *refs),
        32,
        (
            jax.ShapeDtypeStruct(ground_truth.shape, jnp.float32),
            jax.ShapeDtypeStruct((entries, COEF_ROWS), jnp.bfloat16),
            jax.ShapeDtypeStruct((5, entries // LANES, LANES), jnp.float32),
        ),
        [smem(), smem(), smem(), vmem(), vmem(), vmem(), vmem()],
        [
            scratch(count_blocks * PAIR, LANES),
            scratch(2 * per_device // LANES * FEATS, LANES),
            scratch(count_blocks, LANES),
            scratch(blocks * PAIR, LANES),
            scratch(blocks * COEF_ROWS, LANES),
            scratch(blocks * LANES, 5 * LANES),
        ],
        place,
        cams,
        flat_lengths,
        lens_rows,
        names,
        expand_matrix(),
        arrived,
    )

    images = rendered.reshape(true_own.shape)
    count = images.shape[0]
    grad_image = run(
        lambda *refs: loss_kernel(TILE * row_devices, *refs),
        24,
        jax.ShapeDtypeStruct(images.shape, jnp.float32),
        [smem()] + [vmem()] * 8,
        [
            scratch(3, 3 * TILE, width),
            scratch(3 * count * 2 * TILE, width),
            scratch(3 * count * 2 * TILE, width),
            scratch(3 * count * TILE, width),
        ],
        place,
        band,
        truth_blur,
        true_above,
        true_own,
        true_below,
        from_behind(images, "tile", 1),
        images,
        from_behind(images, "tile", -1),
    ).reshape(ground_truth.shape)

    spread_rows = count_blocks * (2 * FEATS + 2)
    grad_slots = run(
        lambda *refs: back_kernel(tile_sizes, *refs),
        40,
        sent_shape,
        [smem()] * 3 + [vmem()] * 7,
        [
            scratch(blocks * LANES, 5 * LANES),
            scratch(blocks * LANES, 2 * LANES),
            scratch(blocks * LANES, 2 * LANES),
            scratch(blocks * LANES, 2 * LANES),
            scratch(LANES, 2 * LANES),
            scratch(blocks * TILE, LANES),
            scratch(blocks * PAIR, LANES),
            pltpu.VMEM((spread_rows, JOIN * LANES), jnp.bfloat16),
            pltpu.VMEM((LANES, JOIN * LANES), jnp.bfloat16),
            scratch(2, spread_rows, LANES),
            scratch(count_blocks * PAIR, LANES),
        ],
        place,
        cams,
        flat_lengths,
        names,
        expand_matrix(),
        moment_matrix(),
        left,
        shapes,
        arrived,
        grad_image,
    )
    grad_slots, late_counts = lax.optimization_barrier((grad_slots, send_counts))
    returned = lax.all_to_all(
        grad_slots, ("view", "tile"), split_axis=0, concat_axis=0, tiled=True
    )
    sent_to, own_parts = run(
        lambda *refs: prepare_kernel((groups, row_devices), *refs),
        24,
        (
            jax.ShapeDtypeStruct((count_blocks, LANES), jnp.float32),
            jax.ShapeDtypeStruct((2 * (TILE - 1 + 9), count_blocks, LANES), jnp.float32),
        ),
        [smem(), smem(), vmem(), vmem()],
        [scratch(SUBS * SUBS * SUBS, LANES), scratch(count_blocks, LANES)],
        cams,
        late_counts,
        send_list,
        params,
    )
    return run(
        lambda *refs: owner_kernel(lane_len, *refs),
        24,
        jax.ShapeDtypeStruct(params.shape, jnp.float32),
        [smem(), vmem(), vmem(), hbm(), vmem(), vmem()],
        [
            scratch(SUBS * SUBS * SUBS, LANES),
            scratch(*own_parts.shape),
            scratch((count_blocks + 1) * PAIR, LANES),
            pltpu.VMEM((count_blocks * 2 * PAIR, JOIN * LANES), jnp.bfloat16),
            pltpu.VMEM((LANES, JOIN * LANES), jnp.bfloat16),
            scratch(count_blocks * 2 * PAIR, LANES),
            pltpu.SemaphoreType.DMA,
        ],
        send_counts,
        send_list,
        sent_to,
        own_parts,
        params,
        returned,
    )


def solution(mesh):
    in_specs = (
        P(None, ("view", "tile")),
        P(("view", "tile"), None),
        P(("view", "tile"), None),
        P(),
        P("view", None, "tile", None),
        P("view", "tile", None, None),
        P("view", "tile", None),
    )
    out_specs = P(None, ("view", "tile"))
    return jax.shard_map(shards, mesh=mesh, in_specs=in_specs, out_specs=out_specs, check_vma=False)
```

```python
import jax
import jax.numpy as jnp
import numpy as np
from jax import lax
from jax.experimental import pallas as pl
from jax.experimental.pallas import tpu as pltpu
from jax.sharding import PartitionSpec as P

TILE = 16


FOCAL = 1000.0
LOW_PASS = 0.3
SSIM_SHARE = 0.2
SMOOTH_EPS = 1e-06
SSIM_ONE = 0.0001
SSIM_TWO = 0.0009
HARMONIC_ZERO = 0.28209479177387814
HARMONIC_ONE = 0.4886025119029199
HARMONIC_TWO = (
    1.0925484305920792,
    -1.0925484305920792,
    0.31539156525252005,
    -1.0925484305920792,
    0.5462742152960396,
)
HARMONIC_THREE = (
    -0.5900435899266435,
    2.890611442640554,
    -0.4570457994644658,
    0.3731763325901154,
    -0.4570457994644658,
    1.445305721320277,
    -0.5900435899266435,
)


def from_behind(block, axis, distance):
    devices = range(lax.axis_size(axis))
    route = [(i - distance, i) for i in devices if i - distance in devices]
    return lax.ppermute(block, axis, route)


def window_taps():
    offsets_np = np.arange(11) - 5.0
    weights = np.exp(-offsets_np * offsets_np / 4.5)
    weights = weights / weights.sum()
    return [float(weight) for weight in weights]


def matrix_product(left_side, right_side):
    return [
        [
            left_side[row_idx][0] * right_side[0][col_idx]
            + left_side[row_idx][1] * right_side[1][col_idx]
            + left_side[row_idx][2] * right_side[2][col_idx]
            for col_idx in range(3)
        ]
        for row_idx in range(3)
    ]


def rotation(angles):
    cos_a, sin_a = (jnp.cos(angles[0]), jnp.sin(angles[0]))
    cos_b, sin_b = (jnp.cos(angles[1]), jnp.sin(angles[1]))
    cos_c, sin_c = (jnp.cos(angles[2]), jnp.sin(angles[2]))
    about_x = [[1.0, 0.0, 0.0], [0.0, cos_a, -sin_a], [0.0, sin_a, cos_a]]
    about_y = [[cos_b, 0.0, sin_b], [0.0, 1.0, 0.0], [-sin_b, 0.0, cos_b]]
    about_z = [[cos_c, -sin_c, 0.0], [sin_c, cos_c, 0.0], [0.0, 0.0, 1.0]]
    return matrix_product(about_z, matrix_product(about_y, about_x))


def harmonics(dir_x, dir_y, dir_z):
    sq_x, sq_y, sq_z = (dir_x * dir_x, dir_y * dir_y, dir_z * dir_z)
    prod_xy, prod_yz, prod_xz = (dir_x * dir_y, dir_y * dir_z, dir_x * dir_z)
    return [
        HARMONIC_ZERO + 0.0 * dir_x,
        -HARMONIC_ONE * dir_y,
        HARMONIC_ONE * dir_z,
        -HARMONIC_ONE * dir_x,
        HARMONIC_TWO[0] * prod_xy,
        HARMONIC_TWO[1] * prod_yz,
        HARMONIC_TWO[2] * (2.0 * sq_z - sq_x - sq_y),
        HARMONIC_TWO[3] * prod_xz,
        HARMONIC_TWO[4] * (sq_x - sq_y),
        HARMONIC_THREE[0] * dir_y * (3.0 * sq_x - sq_y),
        HARMONIC_THREE[1] * prod_xy * dir_z,
        HARMONIC_THREE[2] * dir_y * (4.0 * sq_z - sq_x - sq_y),
        HARMONIC_THREE[3] * dir_z * (2.0 * sq_z - 3.0 * sq_x - 3.0 * sq_y),
        HARMONIC_THREE[4] * dir_x * (4.0 * sq_z - sq_x - sq_y),
        HARMONIC_THREE[5] * dir_z * (sq_x - sq_y),
        HARMONIC_THREE[6] * dir_x * (sq_x - 3.0 * sq_y),
    ]


LANES = 128
SUBS = 8
GROUP = 16
STEP_ROWS = LANES // GROUP
FEATS = 8
PAIR = 2 * FEATS
OPACITY, COLOUR = 9, 10
COEF_ROWS = 32
JOIN = 4
UNROLL = 8
MOVES = 16
TAPS = 11
DEAD = -1e30
LOG_TOP = float(np.log(0.99))


def stepped(total, width, body, state):
    def step(block, held):
        for k in range(width):
            held = body(block * width + k, held)
        return held

    return lax.fori_loop(0, (total + width - 1) // width, step, state)


def lane_spread(index):
    return index // LANES, index % LANES


def take_blocks(read, count, block, place):
    result = jnp.zeros(place.shape, jnp.float32)
    for num in range(count):
        taken = jnp.take_along_axis(read(num), place, axis=1, mode="promise_in_bounds")
        result = jnp.where(block == num, taken, result)
    return result


def take_line(read, count, block, place):
    sub = lax.broadcasted_iota(jnp.int32, (SUBS, LANES), 0)
    result = take_blocks(read, -(-count // SUBS), block // SUBS, place)
    return jnp.sum(jnp.where(sub == block % SUBS, result, 0.0), axis=0, keepdims=True)


def camera_table(camera):
    columns = [camera[:, entry] for entry in range(6)]
    turn = rotation(columns[0:3])
    shift = columns[3:6]
    anchor = [
        -(turn[0][c] * shift[0] + turn[1][c] * shift[1] + turn[2][c] * shift[2]) for c in range(3)
    ]
    flat = [turn[r][c] for r in range(3) for c in range(3)] + shift + anchor
    return jnp.stack(flat + [jnp.zeros_like(shift[0])], axis=1)


def covariance(params):
    scales = [jnp.exp(params[3 + axis_num]) for axis_num in range(3)]
    inv_norm = 1.0 / jnp.sqrt(
        params[6] * params[6]
        + params[7] * params[7]
        + params[8] * params[8]
        + params[9] * params[9]
    )
    quat_w, quat_x, quat_y, quat_z = [params[6 + k] * inv_norm for k in range(4)]
    quat_rot = [
        [
            1.0 - 2.0 * (quat_y * quat_y + quat_z * quat_z),
            2.0 * (quat_x * quat_y - quat_w * quat_z),
            2.0 * (quat_x * quat_z + quat_w * quat_y),
        ],
        [
            2.0 * (quat_x * quat_y + quat_w * quat_z),
            1.0 - 2.0 * (quat_x * quat_x + quat_z * quat_z),
            2.0 * (quat_y * quat_z - quat_w * quat_x),
        ],
        [
            2.0 * (quat_x * quat_z - quat_w * quat_y),
            2.0 * (quat_y * quat_z + quat_w * quat_x),
            1.0 - 2.0 * (quat_x * quat_x + quat_y * quat_y),
        ],
    ]
    root = [[quat_rot[r][c] * scales[c] for c in range(3)] for r in range(3)]
    return [
        root[r][0] * root[k][0] + root[r][1] * root[k][1] + root[r][2] * root[k][2]
        for r, k in ((0, 0), (0, 1), (0, 2), (1, 1), (1, 2), (2, 2))
    ]


def view_colours(params, cam):
    ray = [params[c] - cam[12 + c] for c in range(3)]
    inv_len = 1.0 / jnp.sqrt(ray[0] * ray[0] + ray[1] * ray[1] + ray[2] * ray[2])
    basis = harmonics(ray[0] * inv_len, ray[1] * inv_len, ray[2] * inv_len)
    colours = []
    for channel in range(3):
        summed = 0.5 + HARMONIC_ZERO * params[11 + 16 * channel]
        for harmonic in range(1, 16):
            summed = summed + basis[harmonic] * params[11 + 16 * channel + harmonic]
        colours.append(summed)
    return colours


def footprint(mean, cov, cam, image_width, image_height):
    turn = [[cam[3 * r + c] for c in range(3)] for r in range(3)]
    point = [
        turn[r][0] * mean[0] + turn[r][1] * mean[1] + turn[r][2] * mean[2] + cam[9 + r]
        for r in range(3)
    ]
    inv_depth = 1.0 / point[2]
    ratio_x, ratio_y = point[0] * inv_depth, point[1] * inv_depth
    zoom = FOCAL * inv_depth
    row_x = [zoom * (turn[0][c] - ratio_x * turn[2][c]) for c in range(3)]
    row_y = [zoom * (turn[1][c] - ratio_y * turn[2][c]) for c in range(3)]
    full = [[cov[0], cov[1], cov[2]], [cov[1], cov[3], cov[4]], [cov[2], cov[4], cov[5]]]
    spread_x = [
        row_x[0] * full[0][c] + row_x[1] * full[1][c] + row_x[2] * full[2][c] for c in range(3)
    ]
    spread_y = [
        row_y[0] * full[0][c] + row_y[1] * full[1][c] + row_y[2] * full[2][c] for c in range(3)
    ]
    cov_xx = spread_x[0] * row_x[0] + spread_x[1] * row_x[1] + spread_x[2] * row_x[2] + LOW_PASS
    cov_xy = spread_x[0] * row_y[0] + spread_x[1] * row_y[1] + spread_x[2] * row_y[2]
    cov_yy = spread_y[0] * row_y[0] + spread_y[1] * row_y[1] + spread_y[2] * row_y[2] + LOW_PASS
    inv_det = 1.0 / (cov_xx * cov_yy - cov_xy * cov_xy)
    return [
        FOCAL * ratio_x + image_width / 2.0,
        FOCAL * ratio_y + image_height / 2.0,
        cov_yy * inv_det,
        -cov_xy * inv_det,
        cov_xx * inv_det,
    ]


def log_opacity(logit):
    return LOG_TOP - jnp.log(1.0 + jnp.exp(-logit))


def load_params(params_ref, tile_scr, block):
    count = params_ref.shape[0]
    for band in range(0, count, SUBS):
        high = min(band + SUBS, count)
        for j in range(SUBS):
            lane_at = pl.multiple_of(block * SUBS * LANES + j * LANES, LANES)
            tile_scr[band * SUBS + j * SUBS : band * SUBS + j * SUBS + high - band, :] = params_ref[
                band:high, pl.ds(lane_at, LANES)
            ]
    return [
        tile_scr[pl.ds((r // SUBS) * SUBS * SUBS + r % SUBS, SUBS, stride=SUBS), :]
        for r in range(count)
    ]


def source_kernel(
    sizes, cam_ref, counts_ref, list_ref, params_ref, out_ref, tile_scr, table
):
    groups, rows, cap, lane_len = sizes
    per = params_ref.shape[1]
    parts = cap // lane_len
    used = (1 + groups) * FEATS
    count_blocks = per // LANES

    def project_block(block, carry):
        params = load_params(params_ref, tile_scr, block)
        at = block * SUBS * used
        shared = params[0:3] + covariance(params) + [log_opacity(params[10])]
        for num, value in enumerate(shared[0:FEATS]):
            table[pl.ds(at + num, SUBS, stride=used), :] = value
        for group in range(groups):
            lines = shared[FEATS:]
            for view in range(2):
                lines = lines + view_colours(
                    params, [cam_ref[2 * group + view, k] for k in range(15)]
                )
            for num, value in enumerate(lines):
                table[pl.ds(at + (1 + group) * FEATS + num, SUBS, stride=used), :] = value
        return carry

    lax.fori_loop(0, per // (SUBS * LANES), project_block, 0)
    lane = lax.broadcasted_iota(jnp.int32, (SUBS, LANES), 1)

    def send_block(dest, start_at):
        count = counts_ref[0, dest]
        line = pl.multiple_of((1 + dest // rows) * FEATS, FEATS)
        for part in range(parts):

            @pl.when(count > part * lane_len)
            def _(part=part):
                first = start_at + part * lane_len
                block, turn = first // LANES, first % LANES
                pieces = []
                for step in range(2):
                    at = jnp.minimum(block + step, count_blocks - 1) * LANES
                    names = list_ref[0:1, pl.ds(pl.multiple_of(at, LANES), LANES)]
                    pieces.append(
                        pltpu.roll(jnp.broadcast_to(names, (SUBS, LANES)), LANES - turn, 1)
                    )
                index = jnp.where(lane < LANES - turn, pieces[0], pieces[1])
                home, place = lane_spread(index)
                for side in range(2):
                    at = line if side else 0
                    taken = take_blocks(
                        lambda num, at=at: table[pl.ds(num * used + at, FEATS), :],
                        count_blocks,
                        home,
                        place,
                    )
                    line_at = part * PAIR + side * FEATS
                    out_ref[dest, line_at : line_at + FEATS, :] = taken[:, 0:lane_len]

        return start_at + count

    lax.fori_loop(0, groups * rows, send_block, jnp.int32(0))


def split_three(value):
    first = value.astype(jnp.bfloat16).astype(jnp.float32)
    rest = value - first
    second = rest.astype(jnp.bfloat16).astype(jnp.float32)
    return [first, second, rest - second]


def in_two(value):
    high = value.astype(jnp.bfloat16).astype(jnp.float32)
    return [high, value - high]


def swap_grain(cells):
    sub = lax.broadcasted_iota(jnp.int32, (SUBS, LANES), 0)
    lane = lax.broadcasted_iota(jnp.int32, (SUBS, LANES), 1) // TILE
    for bit in (1, 2, 4):
        sub_bit, lane_bit = (sub & bit) != 0, (lane & bit) != 0
        from_high = pltpu.roll(pltpu.roll(cells, SUBS - bit, 0), bit * TILE, 1)
        from_low = pltpu.roll(pltpu.roll(cells, bit, 0), LANES - bit * TILE, 1)
        cells = jnp.where(sub_bit == lane_bit, cells, jnp.where(lane_bit, from_high, from_low))
    return cells


def longest(lens_ref, group):
    most = lens_ref[group * GROUP]
    for t in range(1, GROUP):
        most = jnp.maximum(most, lens_ref[group * GROUP + t])
    return most


def gather_slots(arrived_ref, slot_scr, lane_len):
    parts = arrived_ref.shape[1] // PAIR
    joined = LANES // lane_len

    def unpack(block, carry):
        line_at = pl.multiple_of(block * PAIR, PAIR)
        for k in range(joined):
            source = block * joined // parts + k
            part_at = pl.multiple_of(block * joined % parts * PAIR, PAIR)
            slot_scr[pl.ds(line_at, PAIR), k * lane_len : (k + 1) * lane_len] = arrived_ref[
                source, pl.ds(part_at, PAIR), :
            ]
        return carry

    lax.fori_loop(0, slot_scr.shape[0] // PAIR, unpack, 0)


def slot_lines(slot_scr, first):
    return [slot_scr[pl.ds(first * PAIR + num, SUBS, stride=PAIR), :] for num in range(PAIR)]


def render_kernel(
    sizes,
    place_ref,
    cam_ref,
    lens_ref,
    lens_rows_ref,
    names_ref,
    basis_ref,
    arrived_ref,
    image_ref,
    left_ref,
    shape_ref,
    alphas_ref,
    weights_ref,
    slot_scr,
    table,
    logs,
    feat_scr,
    pieces,
    mm,
):
    cap, lane_len, col_groups, list_len, image_width, image_height = sizes
    devices = arrived_ref.shape[0]
    blocks = list_len // STEP_ROWS
    count_blocks = devices * cap // LANES
    gather_slots(arrived_ref, slot_scr, lane_len)

    def project_block(step, carry):
        first = step * SUBS
        lines = slot_lines(slot_scr, first)
        logs[pl.ds(pl.multiple_of(first, SUBS), SUBS), :] = lines[OPACITY]
        for view in range(2):
            cam = [cam_ref[2 * place_ref[1] + view, k] for k in range(15)]
            feats = footprint(lines[0:3], lines[3:9], cam, image_width, image_height)
            feats = feats + lines[COLOUR + 3 * view : COLOUR + 3 * view + 3]
            for num, value in enumerate(feats):
                row_at = (view * count_blocks + first) * FEATS + num
                table[pl.ds(row_at, SUBS, stride=FEATS), :] = value
        return carry

    lax.fori_loop(0, count_blocks // SUBS, project_block, 0)
    centre_y = (place_ref[0] * TILE).astype(jnp.float32) + (TILE - 1) / 2.0
    sub = lax.broadcasted_iota(jnp.int32, (blocks, LANES), 0)
    lane = lax.broadcasted_iota(jnp.int32, (blocks, LANES), 1)
    zero = jnp.zeros((GROUP, LANES), jnp.float32)

    def one_group(group, carry):
        view, col_group = group // col_groups, group % col_groups
        most = longest(lens_ref, group)

        def fetch(block, inner):
            names = names_ref[pl.ds(group * blocks + block, 1), :]
            home, place = lane_spread(jnp.broadcast_to(names, (SUBS, LANES)))
            feat_at = pl.multiple_of(block * PAIR, PAIR)
            feat_scr[pl.ds(feat_at, FEATS), :] = take_blocks(
                lambda num: table[
                    pl.ds(pl.multiple_of((view * count_blocks + num) * FEATS, FEATS), FEATS), :
                ],
                count_blocks,
                home,
                place,
            )
            feat_scr[pl.ds(feat_at + FEATS, 1), :] = take_line(
                lambda num: logs[num * SUBS : (num + 1) * SUBS, :], count_blocks, home, place
            )
            return inner

        stepped((most + STEP_ROWS - 1) // STEP_ROWS, 2, fetch, 0)
        feats = [feat_scr[pl.ds(num, blocks, stride=PAIR), :] for num in range(FEATS)]
        log_o = feat_scr[pl.ds(FEATS, blocks, stride=PAIR), :]
        live = sub * STEP_ROWS + lane // GROUP < lens_rows_ref[pl.ds(group, 1), :]
        centre_x = ((col_group * GROUP + lane % GROUP) * TILE).astype(jnp.float32) + (
            TILE - 1
        ) / 2.0
        off_x, off_y = feats[0] - centre_x, feats[1] - centre_y
        lin_x = feats[2] * off_x + feats[3] * off_y
        lin_y = feats[4] * off_y + feats[3] * off_x
        coefs = [
            log_o - 0.5 * (off_x * lin_x + off_y * lin_y),
            lin_x,
            lin_y,
            -0.5 * feats[2],
            -feats[3],
            -0.5 * feats[4],
        ]
        coefs = [
            jnp.where(live, value, DEAD if num == 0 else 0.0) for num, value in enumerate(coefs)
        ]
        lines = [None] * COEF_ROWS
        for num, value in enumerate(coefs):
            for piece, part in enumerate(split_three(value)):
                lines[piece * 6 + num] = part
        for num in range(3):
            for piece, part in enumerate(split_three(jnp.where(live, feats[5 + num], 0.0))):
                lines[18 + piece * 3 + num] = part
        for num, value in enumerate(lines):
            pieces[pl.ds(num, blocks, stride=COEF_ROWS), :] = (
                jnp.zeros((blocks, LANES), jnp.float32) if value is None else value
            )
        for num, value in enumerate(feats[2:5] + [off_x, off_y]):
            shape_ref[num, pl.ds(pl.multiple_of(group * blocks, blocks), blocks), :] = jnp.where(
                live, value, 0.0
            )
        left_at = pl.multiple_of(group * blocks * LANES, LANES)
        for block in range(blocks):
            left_ref[pl.ds(left_at + block * LANES, LANES), :] = pieces[
                block * COEF_ROWS : (block + 1) * COEF_ROWS, :
            ].T.astype(jnp.bfloat16)
        expand(left_ref, basis_ref, mm, left_at)

        def entry(n, state):
            keep, colour = state
            row_at = pl.multiple_of(n * GROUP, GROUP)
            shade = [
                mm[pl.ds(row_at, GROUP), (2 + c) * LANES : (3 + c) * LANES] for c in range(3)
            ]
            new_keep, new_colour = [], []
            for half in range(2):
                lanes = slice(half * LANES, (half + 1) * LANES)
                alpha = jnp.exp(mm[pl.ds(row_at, GROUP), lanes])
                weight = keep[half] * alpha
                alphas_ref[pl.ds(left_at + row_at, GROUP), lanes] = alpha
                weights_ref[pl.ds(left_at + row_at, GROUP), lanes] = weight
                new_keep.append(keep[half] * (1.0 - alpha))
                new_colour.append([colour[half][c] + weight * shade[c] for c in range(3)])
            return new_keep, new_colour

        state = ([zero + 1.0] * 2, [[zero] * 3] * 2)
        _, colour = stepped(most, UNROLL, entry, state)
        for side in range(GROUP // SUBS):
            lane_at = pl.multiple_of(col_group * GROUP * TILE + side * LANES, LANES)
            for half in range(2):
                for c in range(3):
                    image_ref[view, c, half * SUBS : (half + 1) * SUBS, pl.ds(lane_at, LANES)] = (
                        swap_grain(colour[half][c][side * SUBS : (side + 1) * SUBS])
                    )
        return carry

    lax.fori_loop(0, 2 * col_groups, one_group, 0)


def expand(left_ref, basis_ref, mm, left_at):
    mm[...] = jnp.dot(
        left_ref[pl.ds(left_at, mm.shape[0]), :],
        basis_ref[...],
        preferred_element_type=jnp.float32,
    )


def back_kernel(
    sizes,
    place_ref,
    cam_ref,
    lens_ref,
    names_ref,
    basis_ref,
    moment_ref,
    left_ref,
    shape_ref,
    alphas,
    weights,
    arrived_ref,
    grad_ref,
    out_ref,
    mm,
    slopes,
    grad_scr,
    mom_scr,
    line_scr,
    masked,
    places,
    total_scr,
    slot_scr,
):
    cap, lane_len, col_groups, list_len, image_width, image_height = sizes
    devices = out_ref.shape[0]
    parts = cap // lane_len
    blocks = list_len // STEP_ROWS
    count_blocks = devices * cap // LANES
    joined = LANES // lane_len
    value_rows = count_blocks * 2 * FEATS
    total_scr[...] = jnp.zeros_like(total_scr)
    line_scr[...] = jnp.zeros_like(line_scr)
    grad_scr[...] = jnp.zeros_like(grad_scr)
    zero = jnp.zeros((GROUP, LANES), jnp.float32)
    sub = lax.broadcasted_iota(jnp.int32, (GROUP, LANES), 0)
    lane = lax.broadcasted_iota(jnp.int32, (GROUP, LANES), 1)
    own_tile = lane % GROUP == sub

    def one_group(group, carry):
        view, col_group = group // col_groups, group % col_groups
        most = longest(lens_ref, group)
        lane_at = pl.multiple_of(col_group * GROUP * TILE, LANES)
        grads = [
            [
                jnp.concatenate(
                    [
                        swap_grain(
                            grad_ref[
                                view,
                                c,
                                half * SUBS : (half + 1) * SUBS,
                                pl.ds(lane_at + side * LANES, LANES),
                            ]
                        )
                        for side in range(GROUP // SUBS)
                    ],
                    axis=0,
                )
                for c in range(3)
            ]
            for half in range(2)
        ]
        for half in range(2):
            for c in range(3):
                for piece, part in enumerate(in_two(grads[half][c])):
                    line = (piece * 3 + c) * GROUP
                    grad_scr[line : line + GROUP, half * LANES : (half + 1) * LANES] = part
        first = pl.multiple_of(group * blocks * LANES, LANES)
        expand(left_ref, basis_ref, mm, first)
        last = (most + UNROLL - 1) // UNROLL * UNROLL - 1

        def behind(step, seen):
            row_at = pl.multiple_of((last - step) * GROUP, GROUP)
            shade = [mm[pl.ds(row_at, GROUP), c * LANES : (c + 1) * LANES] for c in range(3)]
            new_seen = []
            for half in range(2):
                lanes = slice(half * LANES, (half + 1) * LANES)
                own = (
                    grads[half][0] * shade[0]
                    + grads[half][1] * shade[1]
                    + grads[half][2] * shade[2]
                )
                alpha = alphas[pl.ds(first + row_at, GROUP), lanes]
                weight = weights[pl.ds(first + row_at, GROUP), lanes]
                slopes[pl.ds(row_at, GROUP), lanes] = weight * (own - seen[half])
                new_seen.append(seen[half] * (1.0 - alpha) + alpha * own)
            return new_seen

        stepped(most, UNROLL, behind, [zero] * 2)
        total = jnp.zeros((blocks * LANES, LANES), jnp.float32)
        for value, right in (
            (slopes[...], moment_ref[...]),
            (
                weights[pl.ds(first, blocks * LANES), :],
                grad_scr[...].T.astype(jnp.bfloat16),
            ),
        ):
            high = value.astype(jnp.bfloat16)
            low = (value - high.astype(jnp.float32)).astype(jnp.bfloat16)
            total = total + jnp.dot(high, right, preferred_element_type=jnp.float32)
            total = total + jnp.dot(low, right, preferred_element_type=jnp.float32)
        for block in range(blocks):
            turned = total[block * LANES : (block + 1) * LANES].T
            mom_scr[block * TILE : block * TILE + 8, :] = turned[6 * GROUP : 6 * GROUP + 8]
            for c in range(3):
                summed = (
                    turned[c * GROUP : (c + 1) * GROUP]
                    + turned[(3 + c) * GROUP : (4 + c) * GROUP]
                )
                mom_scr[block * TILE + 8 + c : block * TILE + 9 + c, :] = jnp.sum(
                    jnp.where(own_tile, summed, 0.0), axis=0, keepdims=True
                )
        mom = [mom_scr[pl.ds(num, blocks, stride=TILE), :] for num in range(11)]
        con_xx, con_xy, con_yy, off_x, off_y = [
            shape_ref[num, pl.ds(pl.multiple_of(group * blocks, blocks), blocks), :]
            for num in range(5)
        ]
        sum_x = off_x * mom[0] - mom[1]
        sum_y = off_y * mom[0] - mom[2]
        results = [
            -(con_xx * sum_x + con_xy * sum_y),
            -(con_yy * sum_y + con_xy * sum_x),
            -0.5 * (off_x * (sum_x - mom[1]) + mom[3]),
            -(off_x * sum_y - off_y * mom[1] + mom[4]),
            -0.5 * (off_y * (sum_y - mom[2]) + mom[5]),
        ] + mom[8:11]
        for num, value in enumerate(results + [mom[0]]):
            line_scr[pl.ds(num, blocks, stride=PAIR), :] = value

        def spread(step, inner):
            for k in range(JOIN):
                block = step * JOIN + k
                lanes = slice(k * LANES, (k + 1) * LANES)
                names = names_ref[pl.ds(group * blocks + block, 1), :]
                home, place = names // LANES, names % LANES
                line_at = pl.multiple_of(block * PAIR, PAIR)
                values = in_two(line_scr[pl.ds(line_at, FEATS), :])
                logs = in_two(line_scr[pl.ds(line_at + FEATS, 1), :])
                home_wide = jnp.broadcast_to(home, (2 * FEATS, LANES)).astype(jnp.bfloat16)
                pair = jnp.concatenate(values, axis=0).astype(jnp.bfloat16)
                for num in range(count_blocks):
                    masked[num * 2 * FEATS : (num + 1) * 2 * FEATS, lanes] = jnp.where(
                        home_wide == jnp.bfloat16(num), pair, jnp.bfloat16(0)
                    )
                rank = lax.broadcasted_iota(jnp.int32, (count_blocks, LANES), 0)
                for piece, value in enumerate(logs):
                    first = value_rows + piece * count_blocks
                    masked[first : first + count_blocks, lanes] = jnp.where(
                        rank == home, value, 0.0
                    ).astype(jnp.bfloat16)
                seat = lax.broadcasted_iota(jnp.int32, (LANES, LANES), 0)
                places[:, lanes] = jnp.where(seat == place, 1.0, 0.0).astype(jnp.bfloat16)
            total_scr[view] += lax.dot_general(
                masked[...],
                places[...],
                (((1,), (1,)), ((), ())),
                preferred_element_type=jnp.float32,
            )
            return inner

        width = JOIN * STEP_ROWS
        lax.fori_loop(0, (most + width - 1) // width, spread, 0)
        return carry

    lax.fori_loop(0, 2 * col_groups, one_group, 0)

    gather_slots(arrived_ref, slot_scr, lane_len)

    def pull_block(step, carry):
        first = step * SUBS
        lines = slot_lines(slot_scr, first)
        cams = [[cam_ref[2 * place_ref[1] + view, k] for k in range(15)] for view in range(2)]

        def both(*values):
            return [
                footprint(values[0:3], values[3:9], cam, image_width, image_height)
                for cam in cams
            ]

        cots = []
        log_sum = jnp.zeros((SUBS, LANES), jnp.float32)
        for view in range(2):
            row_at = first * 2 * FEATS
            cots.append(
                [
                    total_scr[view, pl.ds(row_at + num, SUBS, stride=2 * FEATS), :]
                    + total_scr[view, pl.ds(row_at + FEATS + num, SUBS, stride=2 * FEATS), :]
                    for num in range(FEATS)
                ]
            )
            for piece in range(2):
                row = pl.multiple_of(value_rows + piece * count_blocks + first, SUBS)
                log_sum = log_sum + total_scr[view, pl.ds(row, SUBS), :]
        _, pull = jax.vjp(both, *lines[0:9])
        results = list(pull([cot[0:5] for cot in cots])) + [log_sum] + cots[0][5:] + cots[1][5:]
        for num, value in enumerate(results):
            slot_scr[pl.ds(first * PAIR + num, SUBS, stride=PAIR), :] = value
        return carry

    lax.fori_loop(0, count_blocks // SUBS, pull_block, 0)

    def pack(block, carry):
        line_at = pl.multiple_of(block * PAIR, PAIR)
        for k in range(joined):
            source = block * joined // parts + k
            part_at = pl.multiple_of(block * joined % parts * PAIR, PAIR)
            out_ref[source, pl.ds(part_at, PAIR), :] = slot_scr[
                pl.ds(line_at, PAIR), k * lane_len : (k + 1) * lane_len
            ]
        return carry

    lax.fori_loop(0, count_blocks, pack, 0)


def owner_kernel(
    sizes,
    cam_ref,
    list_ref,
    counts_ref,
    params_ref,
    back_ref,
    out_hbm,
    out_ref,
    tile_scr,
    feat_scr,
    turn_scr,
    table,
    slots,
    out_sem,
):
    groups, rows, cap, lane_len = sizes
    count_params, per = params_ref.shape
    parts = cap // lane_len
    table[...] = jnp.zeros_like(table)
    turn_scr[...] = jnp.zeros_like(turn_scr)
    start = jnp.int32(0)
    for group in range(groups):
        turn_scr[PAIR : PAIR + 1, :] = jnp.full((1, LANES), 1.0 + group, jnp.float32)

        def take_block(t, start_at, group=group):
            dest = group * rows + t
            count = counts_ref[0, dest]

            for part in range(parts):
                turn_scr[0:PAIR, 0:lane_len] = back_ref[dest, part * PAIR : (part + 1) * PAIR, :]
                slots[part * lane_len : (part + 1) * lane_len, 0:24] = turn_scr[
                    :, 0:lane_len
                ].T

            def move(k, carry):
                spot = list_ref[0, start_at + k]
                table[pl.ds(spot, 1), :] = slots[pl.ds(k, 1), :]
                return carry

            rounded = (count + MOVES - 1) // MOVES * MOVES
            whole = jnp.where(start_at + rounded <= per, rounded, count // MOVES * MOVES)
            stepped(whole, MOVES, move, 0)
            lax.fori_loop(whole, count, move, 0)
            return start_at + count

        start = lax.fori_loop(0, rows, take_block, start)

    def clear(k, carry):
        table[pl.ds(list_ref[0, k], 1), :] = jnp.zeros((1, LANES), jnp.float32)
        return carry

    lax.fori_loop(start, jnp.minimum(start + MOVES, per), clear, 0)

    wide = SUBS * LANES

    def out_copy(block):
        lanes = pl.ds(pl.multiple_of(block * wide, wide), wide)
        return pltpu.make_async_copy(
            out_ref.at[:, lanes], out_hbm.at[:, lanes], out_sem.at[block]
        )

    def pull_block(block, carry):
        params = load_params(params_ref, tile_scr, block)
        for j in range(SUBS):
            row_at = pl.multiple_of(block * SUBS * LANES + j * LANES, LANES)
            feat_scr[j * 24 : (j + 1) * 24, :] = table[pl.ds(row_at, LANES), 0:24].T
        cots = [feat_scr[pl.ds(num, SUBS, stride=24), :] for num in range(PAIR + 1)]
        home = cots[PAIR]
        sent = home > 0.5
        cams = []
        for view in range(2):
            cam = []
            for k in range(15):
                value = jnp.full((SUBS, LANES), cam_ref[view, k], jnp.float32)
                for group in range(1, groups):
                    value = jnp.where(home > 0.5 + group, cam_ref[2 * group + view, k], value)
                cam.append(value)
            cams.append(cam)

        def both(*values):
            return (
                covariance(values)
                + [log_opacity(values[10])]
                + view_colours(values, cams[0])
                + view_colours(values, cams[1])
            )

        _, pull = jax.vjp(both, *params)
        grads = list(pull(cots[3:PAIR]))
        for num in range(3):
            grads[num] = grads[num] + cots[num]
        for num, value in enumerate(grads):
            tile_scr[pl.ds((num // SUBS) * SUBS * SUBS + num % SUBS, SUBS, stride=SUBS), :] = (
                jnp.where(sent, value, 0.0)
            )
        for band in range(0, count_params, SUBS):
            high = min(band + SUBS, count_params)
            for j in range(SUBS):
                lane_at = pl.multiple_of(block * SUBS * LANES + j * LANES, LANES)
                out_ref[band:high, pl.ds(lane_at, LANES)] = tile_scr[
                    band * SUBS + j * SUBS : band * SUBS + j * SUBS + high - band, :
                ]
        out_copy(block).start()
        return carry

    lax.fori_loop(0, per // wide, pull_block, 0)
    for block in range(per // wide):
        out_copy(block).wait()


def tap_rows(read, first, count):
    taps = window_taps()
    total = taps[5] * read(first + 5, count)
    for k in range(5):
        total = total + taps[k] * (read(first + k, count) + read(first + TAPS - 1 - k, count))
    return total


def blur_lanes(value, band):
    return jnp.dot(
        value, band, precision=lax.Precision.HIGHEST, preferred_element_type=jnp.float32
    )


def truth_kernel(band_ref, above_ref, own_ref, below_ref, out_ref, tall, mixed):
    images = own_ref.shape[0]

    def one_image(m, carry):
        whole = jnp.concatenate([above_ref[m], own_ref[m], below_ref[m]], axis=0)
        for field, value in enumerate((whole, whole * whole)):
            tall[...] = value
            row_at = pl.multiple_of((field * images + m) * 2 * TILE, 2 * TILE)
            mixed[pl.ds(row_at, 2 * TILE), :] = tap_rows(
                lambda at, count: tall[at : at + count, :], 6, 2 * TILE
            )
        return carry

    lax.fori_loop(0, images, one_image, 0)
    out_ref[...] = blur_lanes(mixed[...], band_ref[...])


def loss_kernel(
    image_rows,
    row_ref,
    band_ref,
    truth_ref,
    true_above,
    true_own,
    true_below,
    above_ref,
    own_ref,
    below_ref,
    out_ref,
    tall,
    mixed,
    blurred,
    slim,
):
    images = own_ref.shape[0]
    tall_rows = 2 * TILE
    width = own_ref.shape[2]

    def one_image(m, carry):
        whole = jnp.concatenate([above_ref[m], own_ref[m], below_ref[m]], axis=0)
        true = jnp.concatenate([true_above[m], true_own[m], true_below[m]], axis=0)
        for field, value in enumerate((whole, whole * whole, whole * true)):
            tall[field] = value
            row_at = pl.multiple_of((field * images + m) * tall_rows, tall_rows)
            mixed[pl.ds(row_at, tall_rows), :] = tap_rows(
                lambda at, count, field=field: tall[field, at : at + count, :], 6, tall_rows
            )
        return carry

    lax.fori_loop(0, images, one_image, 0)
    blurred[...] = blur_lanes(mixed[...], band_ref[...])
    sub = lax.broadcasted_iota(jnp.int32, (tall_rows, width), 0)
    image_row = row_ref[0] * TILE + sub - 5
    inside = (image_row >= 0) & (image_row < image_rows) & (sub < TILE + 10)

    def one_map(m, carry):
        def field_of(ref, field):
            row_at = pl.multiple_of((field * images + m) * tall_rows, tall_rows)
            return ref[pl.ds(row_at, tall_rows), :]

        mean_one, both_one, cross = [field_of(blurred, field) for field in range(3)]
        mean_two, both_two = field_of(truth_ref, 0), field_of(truth_ref, 1)
        square_one, square_two = mean_one * mean_one, mean_two * mean_two
        mean_cross = mean_one * mean_two
        top_one = 2.0 * mean_cross + SSIM_ONE
        top_two = 2.0 * (cross - mean_cross) + SSIM_TWO
        low_one = square_one + square_two + SSIM_ONE
        low_two = (both_one - square_one) + (both_two - square_two) + SSIM_TWO
        inv_one, inv_two = 1.0 / low_one, 1.0 / low_two
        inv_both = inv_one * inv_two
        value = top_one * top_two * inv_both
        grads = [
            2.0 * mean_two * (top_two - top_one) * inv_both
            - 2.0 * mean_one * value * (inv_one - inv_two),
            -value * inv_two,
            2.0 * top_one * inv_both,
        ]
        for field, grad in enumerate(grads):
            tall[field, 0:tall_rows] = jnp.where(inside, grad, 0.0)
            row_at = pl.multiple_of((field * images + m) * TILE, TILE)
            slim[pl.ds(row_at, TILE), :] = tap_rows(
                lambda at, count, field=field: tall[field, at : at + count, :], 0, TILE
            )
        return carry

    lax.fori_loop(0, images, one_map, 0)
    spread = blur_lanes(slim[...], band_ref[...]).reshape(3, images, TILE, width)
    own, true = own_ref[...], true_own[...]
    gap = own - true
    out_ref[...] = (1.0 - SSIM_SHARE) * gap / jnp.sqrt(gap * gap + SMOOTH_EPS) - SSIM_SHARE * (
        spread[0] + 2.0 * own * spread[1] + true * spread[2]
    )


def band_matrix(width):
    taps = window_taps()
    band = np.zeros((width, width), np.float32)
    for k in range(TAPS):
        band += np.diag(np.full(width - abs(k - 5), taps[k], np.float32), k - 5)
    return jnp.asarray(band)


def pixel_basis():
    pixel = np.arange(TILE * TILE)
    x = (pixel % TILE) - (TILE - 1) / 2.0
    y = (pixel // TILE) - (TILE - 1) / 2.0
    return np.stack([np.ones_like(x), x, y, x * x, x * y, y * y])


def expand_matrix(first=0):
    terms = pixel_basis()
    matrix = np.zeros((COEF_ROWS, 5 * LANES), np.float32)
    for piece in range(3):
        matrix[piece * 6 : piece * 6 + 6, 0 : 2 * LANES] = terms
        for c in range(3):
            matrix[18 + piece * 3 + c, (2 + c) * LANES : (3 + c) * LANES] = 1.0
    return jnp.asarray(matrix[:, first:], jnp.bfloat16)


def moment_matrix():
    matrix = np.zeros((2 * LANES, LANES), np.float32)
    matrix[:, 6 * GROUP : 6 * GROUP + 6] = pixel_basis().T
    return jnp.asarray(matrix, jnp.bfloat16)


def smem():
    return pl.BlockSpec(memory_space=pltpu.SMEM)


def vmem():
    return pl.BlockSpec(memory_space=pltpu.VMEM)


def scratch(*shape):
    return pltpu.VMEM(shape, jnp.float32)


def run(kernel, megabytes, out_shapes, in_specs, scratches, *operands, out_specs=None):
    return pl.pallas_call(
        kernel,
        out_shape=out_shapes,
        in_specs=in_specs,
        out_specs=out_specs or jax.tree.map(lambda _: vmem(), out_shapes),
        scratch_shapes=scratches,
        compiler_params=pltpu.CompilerParams(vmem_limit_bytes=megabytes << 20),
    )(*operands)


def shards(params, send_list, send_counts, camera, ground_truth, tile_lists, list_lengths):
    devices = lax.axis_size(("view", "tile"))
    row_devices = lax.axis_size("tile")
    groups = lax.axis_size("view")
    count_params, per_device = params.shape
    capacity = per_device // devices
    tile_cols, list_len = tile_lists.shape[2:]
    col_groups = tile_cols // GROUP
    blocks = list_len // STEP_ROWS
    tile_row = lax.axis_index("tile")
    image_width = float(ground_truth.shape[3])
    image_height = float(ground_truth.shape[2] * row_devices)
    lane_len = min(capacity, LANES)
    sent_shape = jax.ShapeDtypeStruct(
        (devices, capacity // lane_len * PAIR, lane_len), jnp.float32
    )
    count_blocks = per_device // LANES
    cams = camera_table(camera)

    flat_lengths = list_lengths.reshape(-1)
    entry_rank = jnp.arange(list_len, dtype=jnp.int32)
    tile_num = jnp.arange(2 * tile_cols, dtype=jnp.int32)
    lists = jnp.where(
        entry_rank[None, :] < flat_lengths[:, None],
        tile_lists.reshape(2 * tile_cols, list_len),
        per_device + tile_num[:, None] % GROUP,
    )
    lens_rows = jnp.tile(flat_lengths.reshape(-1, GROUP), (1, LANES // GROUP))

    width = ground_truth.shape[3]
    true_own = ground_truth.reshape(-1, TILE, width)
    true_above = from_behind(true_own, "tile", 1)
    true_below = from_behind(true_own, "tile", -1)
    band = band_matrix(width)
    truth_rows = 2 * true_own.shape[0] * 2 * TILE
    truth_blur = run(
        truth_kernel,
        16,
        jax.ShapeDtypeStruct((truth_rows, width), jnp.float32),
        [vmem()] * 4,
        [scratch(3 * TILE, width), scratch(truth_rows, width)],
        band,
        true_above,
        true_own,
        true_below,
    )

    own_sizes = (groups, row_devices, capacity, lane_len)
    sent = run(
        lambda *refs: source_kernel(own_sizes, *refs),
        24,
        sent_shape,
        [smem(), smem(), vmem(), vmem()],
        [
            scratch(SUBS * SUBS * SUBS, LANES),
            scratch(count_blocks * (1 + groups) * FEATS, LANES),
        ],
        cams,
        send_counts,
        send_list,
        params,
    )
    arrived = lax.all_to_all(sent, ("view", "tile"), split_axis=0, concat_axis=0, tiled=True)

    arrived, truth_blur = lax.optimization_barrier((arrived, truth_blur))
    tile_sizes = (capacity, lane_len, col_groups, list_len, image_width, image_height)
    place = jnp.stack([tile_row, lax.axis_index("view")])
    entries = 2 * tile_cols * list_len
    names = lists.reshape(-1, GROUP, list_len).transpose(0, 2, 1).reshape(-1, LANES)
    rendered, left, shapes, alphas, weights = run(
        lambda *refs: render_kernel(tile_sizes, *refs),
        32,
        (
            jax.ShapeDtypeStruct(ground_truth.shape, jnp.float32),
            jax.ShapeDtypeStruct((entries, COEF_ROWS), jnp.bfloat16),
            jax.ShapeDtypeStruct((5, entries // LANES, LANES), jnp.float32),
            jax.ShapeDtypeStruct((entries, 2 * LANES), jnp.float32),
            jax.ShapeDtypeStruct((entries, 2 * LANES), jnp.float32),
        ),
        [smem(), smem(), smem(), vmem(), vmem(), vmem(), vmem()],
        [
            scratch(count_blocks * PAIR, LANES),
            scratch(2 * per_device // LANES * FEATS, LANES),
            scratch(count_blocks, LANES),
            scratch(blocks * PAIR, LANES),
            scratch(blocks * COEF_ROWS, LANES),
            scratch(blocks * LANES, 5 * LANES),
        ],
        place,
        cams,
        flat_lengths,
        lens_rows,
        names,
        expand_matrix(),
        arrived,
    )

    images = rendered.reshape(true_own.shape)
    count = images.shape[0]
    grad_image = run(
        lambda *refs: loss_kernel(TILE * row_devices, *refs),
        16,
        jax.ShapeDtypeStruct(images.shape, jnp.float32),
        [smem()] + [vmem()] * 8,
        [
            scratch(3, 3 * TILE, width),
            scratch(3 * count * 2 * TILE, width),
            scratch(3 * count * 2 * TILE, width),
            scratch(3 * count * TILE, width),
        ],
        place,
        band,
        truth_blur,
        true_above,
        true_own,
        true_below,
        from_behind(images, "tile", 1),
        images,
        from_behind(images, "tile", -1),
    ).reshape(ground_truth.shape)

    spread_rows = count_blocks * (2 * FEATS + 2)
    grad_slots = run(
        lambda *refs: back_kernel(tile_sizes, *refs),
        34,
        sent_shape,
        [smem()] * 3 + [vmem()] * 9,
        [
            scratch(blocks * LANES, 3 * LANES),
            scratch(blocks * LANES, 2 * LANES),
            scratch(LANES, 2 * LANES),
            scratch(blocks * TILE, LANES),
            scratch(blocks * PAIR, LANES),
            pltpu.VMEM((spread_rows, JOIN * LANES), jnp.bfloat16),
            pltpu.VMEM((LANES, JOIN * LANES), jnp.bfloat16),
            scratch(2, spread_rows, LANES),
            scratch(count_blocks * PAIR, LANES),
        ],
        place,
        cams,
        flat_lengths,
        names,
        expand_matrix(2 * LANES),
        moment_matrix(),
        left,
        shapes,
        alphas,
        weights,
        arrived,
        grad_image,
    )
    returned = lax.all_to_all(
        grad_slots, ("view", "tile"), split_axis=0, concat_axis=0, tiled=True
    )
    return run(
        lambda *refs: owner_kernel(own_sizes, *refs),
        24,
        jax.ShapeDtypeStruct(params.shape, jnp.float32),
        [smem(), smem(), smem(), vmem(), vmem()],
        [
            scratch(*params.shape),
            scratch(SUBS * SUBS * SUBS, LANES),
            scratch(SUBS * 24, LANES),
            scratch(24, LANES),
            scratch(per_device, LANES),
            scratch(capacity, LANES),
            pltpu.SemaphoreType.DMA((count_blocks // SUBS,)),
        ],
        cams,
        send_list,
        send_counts,
        params,
        returned,
        out_specs=pl.BlockSpec(memory_space=pl.ANY),
    )


def solution(mesh):
    in_specs = (
        P(None, ("view", "tile")),
        P(("view", "tile"), None),
        P(("view", "tile"), None),
        P(),
        P("view", None, "tile", None),
        P("view", "tile", None, None),
        P("view", "tile", None),
    )
    out_specs = P(None, ("view", "tile"))
    return jax.shard_map(shards, mesh=mesh, in_specs=in_specs, out_specs=out_specs, check_vma=False)
```

```python
import jax
import jax.numpy as jnp
import numpy as np
from jax import lax
from jax.experimental import pallas as pl
from jax.experimental.pallas import tpu as pltpu
from jax.sharding import PartitionSpec as P

TILE = 16


FOCAL = 1000.0
LOW_PASS = 0.3
SSIM_SHARE = 0.2
SMOOTH_EPS = 1e-06
SSIM_ONE = 0.0001
SSIM_TWO = 0.0009
HARMONIC_ZERO = 0.28209479177387814
HARMONIC_ONE = 0.4886025119029199
HARMONIC_TWO = (
    1.0925484305920792,
    -1.0925484305920792,
    0.31539156525252005,
    -1.0925484305920792,
    0.5462742152960396,
)
HARMONIC_THREE = (
    -0.5900435899266435,
    2.890611442640554,
    -0.4570457994644658,
    0.3731763325901154,
    -0.4570457994644658,
    1.445305721320277,
    -0.5900435899266435,
)


def from_behind(block, axis, distance):
    devices = range(lax.axis_size(axis))
    route = [(i - distance, i) for i in devices if i - distance in devices]
    return lax.ppermute(block, axis, route)


def window_taps():
    offsets_np = np.arange(11) - 5.0
    weights = np.exp(-offsets_np * offsets_np / 4.5)
    weights = weights / weights.sum()
    return [float(weight) for weight in weights]


def matrix_product(left_side, right_side):
    return [
        [
            left_side[row_idx][0] * right_side[0][col_idx]
            + left_side[row_idx][1] * right_side[1][col_idx]
            + left_side[row_idx][2] * right_side[2][col_idx]
            for col_idx in range(3)
        ]
        for row_idx in range(3)
    ]


def rotation(angles):
    cos_a, sin_a = (jnp.cos(angles[0]), jnp.sin(angles[0]))
    cos_b, sin_b = (jnp.cos(angles[1]), jnp.sin(angles[1]))
    cos_c, sin_c = (jnp.cos(angles[2]), jnp.sin(angles[2]))
    about_x = [[1.0, 0.0, 0.0], [0.0, cos_a, -sin_a], [0.0, sin_a, cos_a]]
    about_y = [[cos_b, 0.0, sin_b], [0.0, 1.0, 0.0], [-sin_b, 0.0, cos_b]]
    about_z = [[cos_c, -sin_c, 0.0], [sin_c, cos_c, 0.0], [0.0, 0.0, 1.0]]
    return matrix_product(about_z, matrix_product(about_y, about_x))


def harmonics(dir_x, dir_y, dir_z):
    sq_x, sq_y, sq_z = (dir_x * dir_x, dir_y * dir_y, dir_z * dir_z)
    prod_xy, prod_yz, prod_xz = (dir_x * dir_y, dir_y * dir_z, dir_x * dir_z)
    return [
        HARMONIC_ZERO + 0.0 * dir_x,
        -HARMONIC_ONE * dir_y,
        HARMONIC_ONE * dir_z,
        -HARMONIC_ONE * dir_x,
        HARMONIC_TWO[0] * prod_xy,
        HARMONIC_TWO[1] * prod_yz,
        HARMONIC_TWO[2] * (2.0 * sq_z - sq_x - sq_y),
        HARMONIC_TWO[3] * prod_xz,
        HARMONIC_TWO[4] * (sq_x - sq_y),
        HARMONIC_THREE[0] * dir_y * (3.0 * sq_x - sq_y),
        HARMONIC_THREE[1] * prod_xy * dir_z,
        HARMONIC_THREE[2] * dir_y * (4.0 * sq_z - sq_x - sq_y),
        HARMONIC_THREE[3] * dir_z * (2.0 * sq_z - 3.0 * sq_x - 3.0 * sq_y),
        HARMONIC_THREE[4] * dir_x * (4.0 * sq_z - sq_x - sq_y),
        HARMONIC_THREE[5] * dir_z * (sq_x - sq_y),
        HARMONIC_THREE[6] * dir_x * (sq_x - 3.0 * sq_y),
    ]


LANES = 128
SUBS = 8
GROUP = 16
STEP_ROWS = LANES // GROUP
FEATS = 8
PAIR = 2 * FEATS
OPACITY, COLOUR = 9, 10
COEF_ROWS = 32
JOIN = 4
UNROLL = 8
MOVES = 16
TAPS = 11
DEAD = -1e30
LOG_TOP = float(np.log(0.99))


def stepped(total, width, body, state):
    def step(block, held):
        for k in range(width):
            held = body(block * width + k, held)
        return held

    return lax.fori_loop(0, (total + width - 1) // width, step, state)


def lane_spread(index):
    return index // LANES, index % LANES


def take_blocks(read, count, block, place):
    result = jnp.zeros(place.shape, jnp.float32)
    for num in range(count):
        taken = jnp.take_along_axis(read(num), place, axis=1, mode="promise_in_bounds")
        result = jnp.where(block == num, taken, result)
    return result


def take_line(read, count, block, place):
    sub = lax.broadcasted_iota(jnp.int32, (SUBS, LANES), 0)
    result = take_blocks(read, -(-count // SUBS), block // SUBS, place)
    return jnp.sum(jnp.where(sub == block % SUBS, result, 0.0), axis=0, keepdims=True)


def camera_table(camera):
    columns = [camera[:, entry] for entry in range(6)]
    turn = rotation(columns[0:3])
    shift = columns[3:6]
    anchor = [
        -(turn[0][c] * shift[0] + turn[1][c] * shift[1] + turn[2][c] * shift[2]) for c in range(3)
    ]
    flat = [turn[r][c] for r in range(3) for c in range(3)] + shift + anchor
    return jnp.stack(flat + [jnp.zeros_like(shift[0])], axis=1)


def covariance(params):
    scales = [jnp.exp(params[3 + axis_num]) for axis_num in range(3)]
    inv_norm = 1.0 / jnp.sqrt(
        params[6] * params[6]
        + params[7] * params[7]
        + params[8] * params[8]
        + params[9] * params[9]
    )
    quat_w, quat_x, quat_y, quat_z = [params[6 + k] * inv_norm for k in range(4)]
    quat_rot = [
        [
            1.0 - 2.0 * (quat_y * quat_y + quat_z * quat_z),
            2.0 * (quat_x * quat_y - quat_w * quat_z),
            2.0 * (quat_x * quat_z + quat_w * quat_y),
        ],
        [
            2.0 * (quat_x * quat_y + quat_w * quat_z),
            1.0 - 2.0 * (quat_x * quat_x + quat_z * quat_z),
            2.0 * (quat_y * quat_z - quat_w * quat_x),
        ],
        [
            2.0 * (quat_x * quat_z - quat_w * quat_y),
            2.0 * (quat_y * quat_z + quat_w * quat_x),
            1.0 - 2.0 * (quat_x * quat_x + quat_y * quat_y),
        ],
    ]
    root = [[quat_rot[r][c] * scales[c] for c in range(3)] for r in range(3)]
    return [
        root[r][0] * root[k][0] + root[r][1] * root[k][1] + root[r][2] * root[k][2]
        for r, k in ((0, 0), (0, 1), (0, 2), (1, 1), (1, 2), (2, 2))
    ]


def view_colours(params, cam):
    ray = [params[c] - cam[12 + c] for c in range(3)]
    inv_len = 1.0 / jnp.sqrt(ray[0] * ray[0] + ray[1] * ray[1] + ray[2] * ray[2])
    basis = harmonics(ray[0] * inv_len, ray[1] * inv_len, ray[2] * inv_len)
    colours = []
    for channel in range(3):
        summed = 0.5 + HARMONIC_ZERO * params[11 + 16 * channel]
        for harmonic in range(1, 16):
            summed = summed + basis[harmonic] * params[11 + 16 * channel + harmonic]
        colours.append(summed)
    return colours


def footprint(mean, cov, cam, image_width, image_height):
    turn = [[cam[3 * r + c] for c in range(3)] for r in range(3)]
    point = [
        turn[r][0] * mean[0] + turn[r][1] * mean[1] + turn[r][2] * mean[2] + cam[9 + r]
        for r in range(3)
    ]
    inv_depth = 1.0 / point[2]
    ratio_x, ratio_y = point[0] * inv_depth, point[1] * inv_depth
    zoom = FOCAL * inv_depth
    row_x = [zoom * (turn[0][c] - ratio_x * turn[2][c]) for c in range(3)]
    row_y = [zoom * (turn[1][c] - ratio_y * turn[2][c]) for c in range(3)]
    full = [[cov[0], cov[1], cov[2]], [cov[1], cov[3], cov[4]], [cov[2], cov[4], cov[5]]]
    spread_x = [
        row_x[0] * full[0][c] + row_x[1] * full[1][c] + row_x[2] * full[2][c] for c in range(3)
    ]
    spread_y = [
        row_y[0] * full[0][c] + row_y[1] * full[1][c] + row_y[2] * full[2][c] for c in range(3)
    ]
    cov_xx = spread_x[0] * row_x[0] + spread_x[1] * row_x[1] + spread_x[2] * row_x[2] + LOW_PASS
    cov_xy = spread_x[0] * row_y[0] + spread_x[1] * row_y[1] + spread_x[2] * row_y[2]
    cov_yy = spread_y[0] * row_y[0] + spread_y[1] * row_y[1] + spread_y[2] * row_y[2] + LOW_PASS
    inv_det = 1.0 / (cov_xx * cov_yy - cov_xy * cov_xy)
    return [
        FOCAL * ratio_x + image_width / 2.0,
        FOCAL * ratio_y + image_height / 2.0,
        cov_yy * inv_det,
        -cov_xy * inv_det,
        cov_xx * inv_det,
    ]


def log_opacity(logit):
    return LOG_TOP - jnp.log(1.0 + jnp.exp(-logit))


def load_params(params_ref, tile_scr, block):
    count = params_ref.shape[0]
    for band in range(0, count, SUBS):
        high = min(band + SUBS, count)
        for j in range(SUBS):
            lane_at = pl.multiple_of(block * SUBS * LANES + j * LANES, LANES)
            tile_scr[band * SUBS + j * SUBS : band * SUBS + j * SUBS + high - band, :] = params_ref[
                band:high, pl.ds(lane_at, LANES)
            ]
    return [
        tile_scr[pl.ds((r // SUBS) * SUBS * SUBS + r % SUBS, SUBS, stride=SUBS), :]
        for r in range(count)
    ]


def source_kernel(
    sizes, cam_ref, counts_ref, list_ref, params_ref, out_ref, tile_scr, table, queue
):
    groups, rows, cap, lane_len = sizes
    per = params_ref.shape[1]
    parts = cap // lane_len
    used = (1 + groups) * FEATS
    count_blocks = per // LANES

    def project_block(block, carry):
        params = load_params(params_ref, tile_scr, block)
        at = block * SUBS * used
        shared = params[0:3] + covariance(params) + [log_opacity(params[10])]
        for num, value in enumerate(shared[0:FEATS]):
            table[pl.ds(at + num, SUBS, stride=used), :] = value
        for group in range(groups):
            lines = shared[FEATS:]
            for view in range(2):
                lines = lines + view_colours(
                    params, [cam_ref[2 * group + view, k] for k in range(15)]
                )
            for num, value in enumerate(lines):
                table[pl.ds(at + (1 + group) * FEATS + num, SUBS, stride=used), :] = value
        return carry

    lax.fori_loop(0, per // (SUBS * LANES), project_block, 0)
    bounds = [jnp.int32(0)]
    for group in range(groups):
        bounds.append(
            lax.fori_loop(
                group * rows, (group + 1) * rows, lambda d, sum_: sum_ + counts_ref[0, d], bounds[-1]
            )
        )
    lane = lax.broadcasted_iota(jnp.int32, (FEATS, LANES), 1)

    def pick(block, carry):
        first = pl.multiple_of(block * LANES, LANES)
        names = jnp.broadcast_to(list_ref[0:1, pl.ds(first, LANES)], (SUBS, LANES))
        home, place = lane_spread(names)
        line_at = pl.multiple_of(block * PAIR, PAIR)
        queue[pl.ds(line_at, FEATS), :] = take_blocks(
            lambda num: table[num * used : num * used + FEATS, :], count_blocks, home, place
        )
        spot = first + lane
        for group in range(groups):
            low, high = bounds[group], bounds[group + 1]

            @pl.when((low < first + LANES) & (high > first))
            def _(group=group, low=low, high=high):
                at = (1 + group) * FEATS
                taken = take_blocks(
                    lambda num: table[num * used + at : num * used + at + FEATS, :],
                    count_blocks,
                    home,
                    place,
                )
                lines = pl.ds(line_at + FEATS, FEATS)
                queue[lines, :] = jnp.where((spot >= low) & (spot < high), taken, queue[lines, :])

        return carry

    lax.fori_loop(0, (bounds[-1] + LANES - 1) // LANES, pick, 0)
    lane_pair = lax.broadcasted_iota(jnp.int32, (PAIR, LANES), 1)

    def send_block(dest, start_at):
        count = counts_ref[0, dest]
        for part in range(parts):

            @pl.when(count > part * lane_len)
            def _(part=part):
                first = start_at + part * lane_len
                block, turn = first // LANES, first % LANES
                pieces = [
                    pltpu.roll(
                        queue[pl.ds(pl.multiple_of((block + step) * PAIR, PAIR), PAIR), :],
                        LANES - turn,
                        1,
                    )
                    for step in range(2)
                ]
                lines = jnp.where(lane_pair < LANES - turn, pieces[0], pieces[1])
                out_ref[dest, part * PAIR : (part + 1) * PAIR, :] = lines[:, 0:lane_len]

        return start_at + count

    lax.fori_loop(0, groups * rows, send_block, jnp.int32(0))


def split_three(value):
    first = value.astype(jnp.bfloat16).astype(jnp.float32)
    rest = value - first
    second = rest.astype(jnp.bfloat16).astype(jnp.float32)
    return [first, second, rest - second]


def in_two(value):
    high = value.astype(jnp.bfloat16).astype(jnp.float32)
    return [high, value - high]


def swap_grain(cells):
    sub = lax.broadcasted_iota(jnp.int32, (SUBS, LANES), 0)
    lane = lax.broadcasted_iota(jnp.int32, (SUBS, LANES), 1) // TILE
    for bit in (1, 2, 4):
        sub_bit, lane_bit = (sub & bit) != 0, (lane & bit) != 0
        from_high = pltpu.roll(pltpu.roll(cells, SUBS - bit, 0), bit * TILE, 1)
        from_low = pltpu.roll(pltpu.roll(cells, bit, 0), LANES - bit * TILE, 1)
        cells = jnp.where(sub_bit == lane_bit, cells, jnp.where(lane_bit, from_high, from_low))
    return cells


def longest(lens_ref, group):
    most = lens_ref[group * GROUP]
    for t in range(1, GROUP):
        most = jnp.maximum(most, lens_ref[group * GROUP + t])
    return most


def gather_slots(arrived_ref, slot_scr, lane_len):
    parts = arrived_ref.shape[1] // PAIR
    joined = LANES // lane_len

    def unpack(block, carry):
        line_at = pl.multiple_of(block * PAIR, PAIR)
        for k in range(joined):
            source = block * joined // parts + k
            part_at = pl.multiple_of(block * joined % parts * PAIR, PAIR)
            slot_scr[pl.ds(line_at, PAIR), k * lane_len : (k + 1) * lane_len] = arrived_ref[
                source, pl.ds(part_at, PAIR), :
            ]
        return carry

    lax.fori_loop(0, slot_scr.shape[0] // PAIR, unpack, 0)


def slot_lines(slot_scr, first):
    return [slot_scr[pl.ds(first * PAIR + num, SUBS, stride=PAIR), :] for num in range(PAIR)]


def render_kernel(
    sizes,
    place_ref,
    cam_ref,
    lens_ref,
    lens_rows_ref,
    names_ref,
    basis_ref,
    arrived_ref,
    image_ref,
    left_ref,
    shape_ref,
    alphas_ref,
    weights_ref,
    slot_scr,
    table,
    logs,
    feat_scr,
    pieces,
    mm,
):
    cap, lane_len, col_groups, list_len, image_width, image_height = sizes
    devices = arrived_ref.shape[0]
    blocks = list_len // STEP_ROWS
    count_blocks = devices * cap // LANES
    gather_slots(arrived_ref, slot_scr, lane_len)

    def project_block(step, carry):
        first = step * SUBS
        lines = slot_lines(slot_scr, first)
        logs[pl.ds(pl.multiple_of(first, SUBS), SUBS), :] = lines[OPACITY]
        for view in range(2):
            cam = [cam_ref[2 * place_ref[1] + view, k] for k in range(15)]
            feats = footprint(lines[0:3], lines[3:9], cam, image_width, image_height)
            feats = feats + lines[COLOUR + 3 * view : COLOUR + 3 * view + 3]
            for num, value in enumerate(feats):
                row_at = (view * count_blocks + first) * FEATS + num
                table[pl.ds(row_at, SUBS, stride=FEATS), :] = value
        return carry

    lax.fori_loop(0, count_blocks // SUBS, project_block, 0)
    centre_y = (place_ref[0] * TILE).astype(jnp.float32) + (TILE - 1) / 2.0
    sub = lax.broadcasted_iota(jnp.int32, (blocks, LANES), 0)
    lane = lax.broadcasted_iota(jnp.int32, (blocks, LANES), 1)
    zero = jnp.zeros((GROUP, LANES), jnp.float32)

    def one_group(group, carry):
        view, col_group = group // col_groups, group % col_groups
        most = longest(lens_ref, group)

        def fetch(block, inner):
            names = names_ref[pl.ds(group * blocks + block, 1), :]
            home, place = lane_spread(jnp.broadcast_to(names, (SUBS, LANES)))
            feat_at = pl.multiple_of(block * PAIR, PAIR)
            feat_scr[pl.ds(feat_at, FEATS), :] = take_blocks(
                lambda num: table[
                    pl.ds(pl.multiple_of((view * count_blocks + num) * FEATS, FEATS), FEATS), :
                ],
                count_blocks,
                home,
                place,
            )
            feat_scr[pl.ds(feat_at + FEATS, 1), :] = take_line(
                lambda num: logs[num * SUBS : (num + 1) * SUBS, :], count_blocks, home, place
            )
            return inner

        stepped((most + STEP_ROWS - 1) // STEP_ROWS, 2, fetch, 0)
        feats = [feat_scr[pl.ds(num, blocks, stride=PAIR), :] for num in range(FEATS)]
        log_o = feat_scr[pl.ds(FEATS, blocks, stride=PAIR), :]
        live = sub * STEP_ROWS + lane // GROUP < lens_rows_ref[pl.ds(group, 1), :]
        centre_x = ((col_group * GROUP + lane % GROUP) * TILE).astype(jnp.float32) + (
            TILE - 1
        ) / 2.0
        off_x, off_y = feats[0] - centre_x, feats[1] - centre_y
        lin_x = feats[2] * off_x + feats[3] * off_y
        lin_y = feats[4] * off_y + feats[3] * off_x
        coefs = [
            log_o - 0.5 * (off_x * lin_x + off_y * lin_y),
            lin_x,
            lin_y,
            -0.5 * feats[2],
            -feats[3],
            -0.5 * feats[4],
        ]
        coefs = [
            jnp.where(live, value, DEAD if num == 0 else 0.0) for num, value in enumerate(coefs)
        ]
        lines = [None] * COEF_ROWS
        for num, value in enumerate(coefs):
            for piece, part in enumerate(split_three(value)):
                lines[piece * 6 + num] = part
        for num in range(3):
            for piece, part in enumerate(split_three(jnp.where(live, feats[5 + num], 0.0))):
                lines[18 + piece * 3 + num] = part
        for num, value in enumerate(lines):
            pieces[pl.ds(num, blocks, stride=COEF_ROWS), :] = (
                jnp.zeros((blocks, LANES), jnp.float32) if value is None else value
            )
        for num, value in enumerate(feats[2:5] + [off_x, off_y]):
            shape_ref[num, pl.ds(pl.multiple_of(group * blocks, blocks), blocks), :] = jnp.where(
                live, value, 0.0
            )
        left_at = pl.multiple_of(group * blocks * LANES, LANES)
        for block in range(blocks):
            left_ref[pl.ds(left_at + block * LANES, LANES), :] = pieces[
                block * COEF_ROWS : (block + 1) * COEF_ROWS, :
            ].T.astype(jnp.bfloat16)
        expand(left_ref, basis_ref, mm, left_at)

        def entry(n, state):
            keep, colour = state
            row_at = pl.multiple_of(n * GROUP, GROUP)
            shade = [
                mm[pl.ds(row_at, GROUP), (2 + c) * LANES : (3 + c) * LANES] for c in range(3)
            ]
            new_keep, new_colour = [], []
            for half in range(2):
                lanes = slice(half * LANES, (half + 1) * LANES)
                alpha = jnp.exp(mm[pl.ds(row_at, GROUP), lanes])
                weight = keep[half] * alpha
                alphas_ref[pl.ds(left_at + row_at, GROUP), lanes] = alpha
                weights_ref[pl.ds(left_at + row_at, GROUP), lanes] = weight
                new_keep.append(keep[half] * (1.0 - alpha))
                new_colour.append([colour[half][c] + weight * shade[c] for c in range(3)])
            return new_keep, new_colour

        state = ([zero + 1.0] * 2, [[zero] * 3] * 2)
        _, colour = stepped(most, UNROLL, entry, state)
        for side in range(GROUP // SUBS):
            lane_at = pl.multiple_of(col_group * GROUP * TILE + side * LANES, LANES)
            for half in range(2):
                for c in range(3):
                    image_ref[view, c, half * SUBS : (half + 1) * SUBS, pl.ds(lane_at, LANES)] = (
                        swap_grain(colour[half][c][side * SUBS : (side + 1) * SUBS])
                    )
        return carry

    lax.fori_loop(0, 2 * col_groups, one_group, 0)


def expand(left_ref, basis_ref, mm, left_at):
    mm[...] = jnp.dot(
        left_ref[pl.ds(left_at, mm.shape[0]), :],
        basis_ref[...],
        preferred_element_type=jnp.float32,
    )


def back_kernel(
    sizes,
    place_ref,
    cam_ref,
    lens_ref,
    names_ref,
    basis_ref,
    moment_ref,
    left_ref,
    shape_ref,
    alphas,
    weights,
    arrived_ref,
    grad_ref,
    out_ref,
    mm,
    slopes,
    grad_scr,
    mom_scr,
    line_scr,
    masked,
    places,
    total_scr,
    slot_scr,
):
    cap, lane_len, col_groups, list_len, image_width, image_height = sizes
    devices = out_ref.shape[0]
    parts = cap // lane_len
    blocks = list_len // STEP_ROWS
    count_blocks = devices * cap // LANES
    joined = LANES // lane_len
    value_rows = count_blocks * 2 * FEATS
    total_scr[...] = jnp.zeros_like(total_scr)
    line_scr[...] = jnp.zeros_like(line_scr)
    grad_scr[...] = jnp.zeros_like(grad_scr)
    zero = jnp.zeros((GROUP, LANES), jnp.float32)
    sub = lax.broadcasted_iota(jnp.int32, (GROUP, LANES), 0)
    lane = lax.broadcasted_iota(jnp.int32, (GROUP, LANES), 1)
    own_tile = lane % GROUP == sub

    def one_group(group, carry):
        view, col_group = group // col_groups, group % col_groups
        most = longest(lens_ref, group)
        lane_at = pl.multiple_of(col_group * GROUP * TILE, LANES)
        grads = [
            [
                jnp.concatenate(
                    [
                        swap_grain(
                            grad_ref[
                                view,
                                c,
                                half * SUBS : (half + 1) * SUBS,
                                pl.ds(lane_at + side * LANES, LANES),
                            ]
                        )
                        for side in range(GROUP // SUBS)
                    ],
                    axis=0,
                )
                for c in range(3)
            ]
            for half in range(2)
        ]
        for half in range(2):
            for c in range(3):
                for piece, part in enumerate(in_two(grads[half][c])):
                    line = (piece * 3 + c) * GROUP
                    grad_scr[line : line + GROUP, half * LANES : (half + 1) * LANES] = part
        first = pl.multiple_of(group * blocks * LANES, LANES)
        expand(left_ref, basis_ref, mm, first)
        last = (most + UNROLL - 1) // UNROLL * UNROLL - 1

        def behind(step, seen):
            row_at = pl.multiple_of((last - step) * GROUP, GROUP)
            shade = [mm[pl.ds(row_at, GROUP), c * LANES : (c + 1) * LANES] for c in range(3)]
            new_seen = []
            for half in range(2):
                lanes = slice(half * LANES, (half + 1) * LANES)
                own = (
                    grads[half][0] * shade[0]
                    + grads[half][1] * shade[1]
                    + grads[half][2] * shade[2]
                )
                alpha = alphas[pl.ds(first + row_at, GROUP), lanes]
                weight = weights[pl.ds(first + row_at, GROUP), lanes]
                slopes[pl.ds(row_at, GROUP), lanes] = weight * (own - seen[half])
                new_seen.append(seen[half] * (1.0 - alpha) + alpha * own)
            return new_seen

        stepped(most, UNROLL, behind, [zero] * 2)
        total = jnp.zeros((blocks * LANES, LANES), jnp.float32)
        for value, right in (
            (slopes[...], moment_ref[...]),
            (
                weights[pl.ds(first, blocks * LANES), :],
                grad_scr[...].T.astype(jnp.bfloat16),
            ),
        ):
            high = value.astype(jnp.bfloat16)
            low = (value - high.astype(jnp.float32)).astype(jnp.bfloat16)
            total = total + jnp.dot(high, right, preferred_element_type=jnp.float32)
            total = total + jnp.dot(low, right, preferred_element_type=jnp.float32)
        for block in range(blocks):
            turned = total[block * LANES : (block + 1) * LANES].T
            mom_scr[block * TILE : block * TILE + 8, :] = turned[6 * GROUP : 6 * GROUP + 8]
            for c in range(3):
                summed = (
                    turned[c * GROUP : (c + 1) * GROUP]
                    + turned[(3 + c) * GROUP : (4 + c) * GROUP]
                )
                mom_scr[block * TILE + 8 + c : block * TILE + 9 + c, :] = jnp.sum(
                    jnp.where(own_tile, summed, 0.0), axis=0, keepdims=True
                )
        mom = [mom_scr[pl.ds(num, blocks, stride=TILE), :] for num in range(11)]
        con_xx, con_xy, con_yy, off_x, off_y = [
            shape_ref[num, pl.ds(pl.multiple_of(group * blocks, blocks), blocks), :]
            for num in range(5)
        ]
        sum_x = off_x * mom[0] - mom[1]
        sum_y = off_y * mom[0] - mom[2]
        results = [
            -(con_xx * sum_x + con_xy * sum_y),
            -(con_yy * sum_y + con_xy * sum_x),
            -0.5 * (off_x * (sum_x - mom[1]) + mom[3]),
            -(off_x * sum_y - off_y * mom[1] + mom[4]),
            -0.5 * (off_y * (sum_y - mom[2]) + mom[5]),
        ] + mom[8:11]
        for num, value in enumerate(results + [mom[0]]):
            line_scr[pl.ds(num, blocks, stride=PAIR), :] = value

        def spread(step, inner):
            for k in range(JOIN):
                block = step * JOIN + k
                lanes = slice(k * LANES, (k + 1) * LANES)
                names = names_ref[pl.ds(group * blocks + block, 1), :]
                home, place = names // LANES, names % LANES
                line_at = pl.multiple_of(block * PAIR, PAIR)
                values = in_two(line_scr[pl.ds(line_at, FEATS), :])
                logs = in_two(line_scr[pl.ds(line_at + FEATS, 1), :])
                home_wide = jnp.broadcast_to(home, (2 * FEATS, LANES)).astype(jnp.bfloat16)
                pair = jnp.concatenate(values, axis=0).astype(jnp.bfloat16)
                for num in range(count_blocks):
                    masked[num * 2 * FEATS : (num + 1) * 2 * FEATS, lanes] = jnp.where(
                        home_wide == jnp.bfloat16(num), pair, jnp.bfloat16(0)
                    )
                rank = lax.broadcasted_iota(jnp.int32, (count_blocks, LANES), 0)
                for piece, value in enumerate(logs):
                    first = value_rows + piece * count_blocks
                    masked[first : first + count_blocks, lanes] = jnp.where(
                        rank == home, value, 0.0
                    ).astype(jnp.bfloat16)
                seat = lax.broadcasted_iota(jnp.int32, (LANES, LANES), 0)
                places[:, lanes] = jnp.where(seat == place, 1.0, 0.0).astype(jnp.bfloat16)
            total_scr[view] += lax.dot_general(
                masked[...],
                places[...],
                (((1,), (1,)), ((), ())),
                preferred_element_type=jnp.float32,
            )
            return inner

        width = JOIN * STEP_ROWS
        lax.fori_loop(0, (most + width - 1) // width, spread, 0)
        return carry

    lax.fori_loop(0, 2 * col_groups, one_group, 0)

    gather_slots(arrived_ref, slot_scr, lane_len)

    def pull_block(step, carry):
        first = step * SUBS
        lines = slot_lines(slot_scr, first)
        cams = [[cam_ref[2 * place_ref[1] + view, k] for k in range(15)] for view in range(2)]

        def both(*values):
            return [
                footprint(values[0:3], values[3:9], cam, image_width, image_height)
                for cam in cams
            ]

        cots = []
        log_sum = jnp.zeros((SUBS, LANES), jnp.float32)
        for view in range(2):
            row_at = first * 2 * FEATS
            cots.append(
                [
                    total_scr[view, pl.ds(row_at + num, SUBS, stride=2 * FEATS), :]
                    + total_scr[view, pl.ds(row_at + FEATS + num, SUBS, stride=2 * FEATS), :]
                    for num in range(FEATS)
                ]
            )
            for piece in range(2):
                row = pl.multiple_of(value_rows + piece * count_blocks + first, SUBS)
                log_sum = log_sum + total_scr[view, pl.ds(row, SUBS), :]
        _, pull = jax.vjp(both, *lines[0:9])
        results = list(pull([cot[0:5] for cot in cots])) + [log_sum] + cots[0][5:] + cots[1][5:]
        for num, value in enumerate(results):
            slot_scr[pl.ds(first * PAIR + num, SUBS, stride=PAIR), :] = value
        return carry

    lax.fori_loop(0, count_blocks // SUBS, pull_block, 0)

    def pack(block, carry):
        line_at = pl.multiple_of(block * PAIR, PAIR)
        for k in range(joined):
            source = block * joined // parts + k
            part_at = pl.multiple_of(block * joined % parts * PAIR, PAIR)
            out_ref[source, pl.ds(part_at, PAIR), :] = slot_scr[
                pl.ds(line_at, PAIR), k * lane_len : (k + 1) * lane_len
            ]
        return carry

    lax.fori_loop(0, count_blocks, pack, 0)


def owner_kernel(
    sizes,
    cam_ref,
    list_ref,
    counts_ref,
    params_ref,
    back_ref,
    out_hbm,
    out_ref,
    tile_scr,
    feat_scr,
    turn_scr,
    table,
    slots,
    out_sem,
):
    groups, rows, cap, lane_len = sizes
    count_params, per = params_ref.shape
    parts = cap // lane_len
    table[...] = jnp.zeros_like(table)
    turn_scr[...] = jnp.zeros_like(turn_scr)
    start = jnp.int32(0)
    for group in range(groups):
        turn_scr[PAIR : PAIR + 1, :] = jnp.full((1, LANES), 1.0 + group, jnp.float32)

        def take_block(t, start_at, group=group):
            dest = group * rows + t
            count = counts_ref[0, dest]

            for part in range(parts):
                turn_scr[0:PAIR, 0:lane_len] = back_ref[dest, part * PAIR : (part + 1) * PAIR, :]
                slots[part * lane_len : (part + 1) * lane_len, 0:24] = turn_scr[
                    :, 0:lane_len
                ].T

            def move(k, carry):
                spot = list_ref[0, start_at + k]
                table[pl.ds(spot, 1), :] = slots[pl.ds(k, 1), :]
                return carry

            rounded = (count + MOVES - 1) // MOVES * MOVES
            whole = jnp.where(start_at + rounded <= per, rounded, count // MOVES * MOVES)
            stepped(whole, MOVES, move, 0)
            lax.fori_loop(whole, count, move, 0)
            return start_at + count

        start = lax.fori_loop(0, rows, take_block, start)

    def clear(k, carry):
        table[pl.ds(list_ref[0, k], 1), :] = jnp.zeros((1, LANES), jnp.float32)
        return carry

    lax.fori_loop(start, jnp.minimum(start + MOVES, per), clear, 0)

    wide = SUBS * LANES

    def out_copy(block):
        lanes = pl.ds(pl.multiple_of(block * wide, wide), wide)
        return pltpu.make_async_copy(
            out_ref.at[:, lanes], out_hbm.at[:, lanes], out_sem.at[block]
        )

    def pull_block(block, carry):
        params = load_params(params_ref, tile_scr, block)
        for j in range(SUBS):
            row_at = pl.multiple_of(block * SUBS * LANES + j * LANES, LANES)
            feat_scr[j * 24 : (j + 1) * 24, :] = table[pl.ds(row_at, LANES), 0:24].T
        cots = [feat_scr[pl.ds(num, SUBS, stride=24), :] for num in range(PAIR + 1)]
        home = cots[PAIR]
        sent = home > 0.5
        cams = []
        for view in range(2):
            cam = []
            for k in range(15):
                value = jnp.full((SUBS, LANES), cam_ref[view, k], jnp.float32)
                for group in range(1, groups):
                    value = jnp.where(home > 0.5 + group, cam_ref[2 * group + view, k], value)
                cam.append(value)
            cams.append(cam)

        def both(*values):
            return (
                covariance(values)
                + [log_opacity(values[10])]
                + view_colours(values, cams[0])
                + view_colours(values, cams[1])
            )

        _, pull = jax.vjp(both, *params)
        grads = list(pull(cots[3:PAIR]))
        for num in range(3):
            grads[num] = grads[num] + cots[num]
        for num, value in enumerate(grads):
            tile_scr[pl.ds((num // SUBS) * SUBS * SUBS + num % SUBS, SUBS, stride=SUBS), :] = (
                jnp.where(sent, value, 0.0)
            )
        for band in range(0, count_params, SUBS):
            high = min(band + SUBS, count_params)
            for j in range(SUBS):
                lane_at = pl.multiple_of(block * SUBS * LANES + j * LANES, LANES)
                out_ref[band:high, pl.ds(lane_at, LANES)] = tile_scr[
                    band * SUBS + j * SUBS : band * SUBS + j * SUBS + high - band, :
                ]
        out_copy(block).start()
        return carry

    lax.fori_loop(0, per // wide, pull_block, 0)
    for block in range(per // wide):
        out_copy(block).wait()


def tap_rows(read, first, count):
    taps = window_taps()
    total = taps[5] * read(first + 5, count)
    for k in range(5):
        total = total + taps[k] * (read(first + k, count) + read(first + TAPS - 1 - k, count))
    return total


def blur_lanes(value, band):
    return jnp.dot(
        value, band, precision=lax.Precision.HIGHEST, preferred_element_type=jnp.float32
    )


def truth_kernel(band_ref, above_ref, own_ref, below_ref, out_ref, tall, mixed):
    images = own_ref.shape[0]

    def one_image(m, carry):
        whole = jnp.concatenate([above_ref[m], own_ref[m], below_ref[m]], axis=0)
        for field, value in enumerate((whole, whole * whole)):
            tall[...] = value
            row_at = pl.multiple_of((field * images + m) * 2 * TILE, 2 * TILE)
            mixed[pl.ds(row_at, 2 * TILE), :] = tap_rows(
                lambda at, count: tall[at : at + count, :], 6, 2 * TILE
            )
        return carry

    lax.fori_loop(0, images, one_image, 0)
    out_ref[...] = blur_lanes(mixed[...], band_ref[...])


def loss_kernel(
    image_rows,
    row_ref,
    band_ref,
    truth_ref,
    true_above,
    true_own,
    true_below,
    above_ref,
    own_ref,
    below_ref,
    out_ref,
    tall,
    mixed,
    blurred,
    slim,
):
    images = own_ref.shape[0]
    tall_rows = 2 * TILE
    width = own_ref.shape[2]

    def one_image(m, carry):
        whole = jnp.concatenate([above_ref[m], own_ref[m], below_ref[m]], axis=0)
        true = jnp.concatenate([true_above[m], true_own[m], true_below[m]], axis=0)
        for field, value in enumerate((whole, whole * whole, whole * true)):
            tall[field] = value
            row_at = pl.multiple_of((field * images + m) * tall_rows, tall_rows)
            mixed[pl.ds(row_at, tall_rows), :] = tap_rows(
                lambda at, count, field=field: tall[field, at : at + count, :], 6, tall_rows
            )
        return carry

    lax.fori_loop(0, images, one_image, 0)
    blurred[...] = blur_lanes(mixed[...], band_ref[...])
    sub = lax.broadcasted_iota(jnp.int32, (tall_rows, width), 0)
    image_row = row_ref[0] * TILE + sub - 5
    inside = (image_row >= 0) & (image_row < image_rows) & (sub < TILE + 10)

    def one_map(m, carry):
        def field_of(ref, field):
            row_at = pl.multiple_of((field * images + m) * tall_rows, tall_rows)
            return ref[pl.ds(row_at, tall_rows), :]

        mean_one, both_one, cross = [field_of(blurred, field) for field in range(3)]
        mean_two, both_two = field_of(truth_ref, 0), field_of(truth_ref, 1)
        square_one, square_two = mean_one * mean_one, mean_two * mean_two
        mean_cross = mean_one * mean_two
        top_one = 2.0 * mean_cross + SSIM_ONE
        top_two = 2.0 * (cross - mean_cross) + SSIM_TWO
        low_one = square_one + square_two + SSIM_ONE
        low_two = (both_one - square_one) + (both_two - square_two) + SSIM_TWO
        inv_one, inv_two = 1.0 / low_one, 1.0 / low_two
        inv_both = inv_one * inv_two
        value = top_one * top_two * inv_both
        grads = [
            2.0 * mean_two * (top_two - top_one) * inv_both
            - 2.0 * mean_one * value * (inv_one - inv_two),
            -value * inv_two,
            2.0 * top_one * inv_both,
        ]
        for field, grad in enumerate(grads):
            tall[field, 0:tall_rows] = jnp.where(inside, grad, 0.0)
            row_at = pl.multiple_of((field * images + m) * TILE, TILE)
            slim[pl.ds(row_at, TILE), :] = tap_rows(
                lambda at, count, field=field: tall[field, at : at + count, :], 0, TILE
            )
        return carry

    lax.fori_loop(0, images, one_map, 0)
    spread = blur_lanes(slim[...], band_ref[...]).reshape(3, images, TILE, width)
    own, true = own_ref[...], true_own[...]
    gap = own - true
    out_ref[...] = (1.0 - SSIM_SHARE) * gap / jnp.sqrt(gap * gap + SMOOTH_EPS) - SSIM_SHARE * (
        spread[0] + 2.0 * own * spread[1] + true * spread[2]
    )


def band_matrix(width):
    taps = window_taps()
    band = np.zeros((width, width), np.float32)
    for k in range(TAPS):
        band += np.diag(np.full(width - abs(k - 5), taps[k], np.float32), k - 5)
    return jnp.asarray(band)


def pixel_basis():
    pixel = np.arange(TILE * TILE)
    x = (pixel % TILE) - (TILE - 1) / 2.0
    y = (pixel // TILE) - (TILE - 1) / 2.0
    return np.stack([np.ones_like(x), x, y, x * x, x * y, y * y])


def expand_matrix(first=0):
    terms = pixel_basis()
    matrix = np.zeros((COEF_ROWS, 5 * LANES), np.float32)
    for piece in range(3):
        matrix[piece * 6 : piece * 6 + 6, 0 : 2 * LANES] = terms
        for c in range(3):
            matrix[18 + piece * 3 + c, (2 + c) * LANES : (3 + c) * LANES] = 1.0
    return jnp.asarray(matrix[:, first:], jnp.bfloat16)


def moment_matrix():
    matrix = np.zeros((2 * LANES, LANES), np.float32)
    matrix[:, 6 * GROUP : 6 * GROUP + 6] = pixel_basis().T
    return jnp.asarray(matrix, jnp.bfloat16)


def smem():
    return pl.BlockSpec(memory_space=pltpu.SMEM)


def vmem():
    return pl.BlockSpec(memory_space=pltpu.VMEM)


def scratch(*shape):
    return pltpu.VMEM(shape, jnp.float32)


def run(kernel, megabytes, out_shapes, in_specs, scratches, *operands, out_specs=None):
    return pl.pallas_call(
        kernel,
        out_shape=out_shapes,
        in_specs=in_specs,
        out_specs=out_specs or jax.tree.map(lambda _: vmem(), out_shapes),
        scratch_shapes=scratches,
        compiler_params=pltpu.CompilerParams(vmem_limit_bytes=megabytes << 20),
    )(*operands)


def shards(params, send_list, send_counts, camera, ground_truth, tile_lists, list_lengths):
    devices = lax.axis_size(("view", "tile"))
    row_devices = lax.axis_size("tile")
    groups = lax.axis_size("view")
    count_params, per_device = params.shape
    capacity = per_device // devices
    tile_cols, list_len = tile_lists.shape[2:]
    col_groups = tile_cols // GROUP
    blocks = list_len // STEP_ROWS
    tile_row = lax.axis_index("tile")
    image_width = float(ground_truth.shape[3])
    image_height = float(ground_truth.shape[2] * row_devices)
    lane_len = min(capacity, LANES)
    sent_shape = jax.ShapeDtypeStruct(
        (devices, capacity // lane_len * PAIR, lane_len), jnp.float32
    )
    count_blocks = per_device // LANES
    cams = camera_table(camera)

    flat_lengths = list_lengths.reshape(-1)
    entry_rank = jnp.arange(list_len, dtype=jnp.int32)
    tile_num = jnp.arange(2 * tile_cols, dtype=jnp.int32)
    lists = jnp.where(
        entry_rank[None, :] < flat_lengths[:, None],
        tile_lists.reshape(2 * tile_cols, list_len),
        per_device + tile_num[:, None] % GROUP,
    )
    lens_rows = jnp.tile(flat_lengths.reshape(-1, GROUP), (1, LANES // GROUP))

    width = ground_truth.shape[3]
    true_own = ground_truth.reshape(-1, TILE, width)
    true_above = from_behind(true_own, "tile", 1)
    true_below = from_behind(true_own, "tile", -1)
    band = band_matrix(width)
    truth_rows = 2 * true_own.shape[0] * 2 * TILE
    truth_blur = run(
        truth_kernel,
        16,
        jax.ShapeDtypeStruct((truth_rows, width), jnp.float32),
        [vmem()] * 4,
        [scratch(3 * TILE, width), scratch(truth_rows, width)],
        band,
        true_above,
        true_own,
        true_below,
    )

    own_sizes = (groups, row_devices, capacity, lane_len)
    sent = run(
        lambda *refs: source_kernel(own_sizes, *refs),
        24,
        sent_shape,
        [smem(), smem(), vmem(), vmem()],
        [
            scratch(SUBS * SUBS * SUBS, LANES),
            scratch(count_blocks * (1 + groups) * FEATS, LANES),
            scratch((count_blocks + 1) * PAIR, LANES),
        ],
        cams,
        send_counts,
        send_list,
        params,
    )
    arrived = lax.all_to_all(sent, ("view", "tile"), split_axis=0, concat_axis=0, tiled=True)

    arrived, truth_blur = lax.optimization_barrier((arrived, truth_blur))
    tile_sizes = (capacity, lane_len, col_groups, list_len, image_width, image_height)
    place = jnp.stack([tile_row, lax.axis_index("view")])
    entries = 2 * tile_cols * list_len
    names = lists.reshape(-1, GROUP, list_len).transpose(0, 2, 1).reshape(-1, LANES)
    rendered, left, shapes, alphas, weights = run(
        lambda *refs: render_kernel(tile_sizes, *refs),
        28,
        (
            jax.ShapeDtypeStruct(ground_truth.shape, jnp.float32),
            jax.ShapeDtypeStruct((entries, COEF_ROWS), jnp.bfloat16),
            jax.ShapeDtypeStruct((5, entries // LANES, LANES), jnp.float32),
            jax.ShapeDtypeStruct((entries, 2 * LANES), jnp.float32),
            jax.ShapeDtypeStruct((entries, 2 * LANES), jnp.float32),
        ),
        [smem(), smem(), smem(), vmem(), vmem(), vmem(), vmem()],
        [
            scratch(count_blocks * PAIR, LANES),
            scratch(2 * per_device // LANES * FEATS, LANES),
            scratch(count_blocks, LANES),
            scratch(blocks * PAIR, LANES),
            scratch(blocks * COEF_ROWS, LANES),
            scratch(blocks * LANES, 5 * LANES),
        ],
        place,
        cams,
        flat_lengths,
        lens_rows,
        names,
        expand_matrix(),
        arrived,
    )

    images = rendered.reshape(true_own.shape)
    count = images.shape[0]
    grad_image = run(
        lambda *refs: loss_kernel(TILE * row_devices, *refs),
        16,
        jax.ShapeDtypeStruct(images.shape, jnp.float32),
        [smem()] + [vmem()] * 8,
        [
            scratch(3, 3 * TILE, width),
            scratch(3 * count * 2 * TILE, width),
            scratch(3 * count * 2 * TILE, width),
            scratch(3 * count * TILE, width),
        ],
        place,
        band,
        truth_blur,
        true_above,
        true_own,
        true_below,
        from_behind(images, "tile", 1),
        images,
        from_behind(images, "tile", -1),
    ).reshape(ground_truth.shape)

    spread_rows = count_blocks * (2 * FEATS + 2)
    grad_slots = run(
        lambda *refs: back_kernel(tile_sizes, *refs),
        31,
        sent_shape,
        [smem()] * 3 + [vmem()] * 9,
        [
            scratch(blocks * LANES, 3 * LANES),
            scratch(blocks * LANES, 2 * LANES),
            scratch(LANES, 2 * LANES),
            scratch(blocks * TILE, LANES),
            scratch(blocks * PAIR, LANES),
            pltpu.VMEM((spread_rows, JOIN * LANES), jnp.bfloat16),
            pltpu.VMEM((LANES, JOIN * LANES), jnp.bfloat16),
            scratch(2, spread_rows, LANES),
            scratch(count_blocks * PAIR, LANES),
        ],
        place,
        cams,
        flat_lengths,
        names,
        expand_matrix(2 * LANES),
        moment_matrix(),
        left,
        shapes,
        alphas,
        weights,
        arrived,
        grad_image,
    )
    returned = lax.all_to_all(
        grad_slots, ("view", "tile"), split_axis=0, concat_axis=0, tiled=True
    )
    return run(
        lambda *refs: owner_kernel(own_sizes, *refs),
        24,
        jax.ShapeDtypeStruct(params.shape, jnp.float32),
        [smem(), smem(), smem(), vmem(), vmem()],
        [
            scratch(*params.shape),
            scratch(SUBS * SUBS * SUBS, LANES),
            scratch(SUBS * 24, LANES),
            scratch(24, LANES),
            scratch(per_device, LANES),
            scratch(capacity, LANES),
            pltpu.SemaphoreType.DMA((count_blocks // SUBS,)),
        ],
        cams,
        send_list,
        send_counts,
        params,
        returned,
        out_specs=pl.BlockSpec(memory_space=pl.ANY),
    )


def solution(mesh):
    in_specs = (
        P(None, ("view", "tile")),
        P(("view", "tile"), None),
        P(("view", "tile"), None),
        P(),
        P("view", None, "tile", None),
        P("view", "tile", None, None),
        P("view", "tile", None),
    )
    out_specs = P(None, ("view", "tile"))
    return jax.shard_map(shards, mesh=mesh, in_specs=in_specs, out_specs=out_specs, check_vma=False)
```

```python
import jax
import jax.numpy as jnp
import numpy as np
from jax import lax
from jax.experimental import pallas as pl
from jax.experimental.pallas import tpu as pltpu
from jax.sharding import PartitionSpec as P

TILE = 16


FOCAL = 1000.0
LOW_PASS = 0.3
SSIM_SHARE = 0.2
SMOOTH_EPS = 1e-06
SSIM_ONE = 0.0001
SSIM_TWO = 0.0009
HARMONIC_ZERO = 0.28209479177387814
HARMONIC_ONE = 0.4886025119029199
HARMONIC_TWO = (
    1.0925484305920792,
    -1.0925484305920792,
    0.31539156525252005,
    -1.0925484305920792,
    0.5462742152960396,
)
HARMONIC_THREE = (
    -0.5900435899266435,
    2.890611442640554,
    -0.4570457994644658,
    0.3731763325901154,
    -0.4570457994644658,
    1.445305721320277,
    -0.5900435899266435,
)


def from_behind(block, axis, distance):
    devices = range(lax.axis_size(axis))
    route = [(i - distance, i) for i in devices if i - distance in devices]
    return lax.ppermute(block, axis, route)


def window_taps():
    offsets_np = np.arange(11) - 5.0
    weights = np.exp(-offsets_np * offsets_np / 4.5)
    weights = weights / weights.sum()
    return [float(weight) for weight in weights]


def matrix_product(left_side, right_side):
    return [
        [
            left_side[row_idx][0] * right_side[0][col_idx]
            + left_side[row_idx][1] * right_side[1][col_idx]
            + left_side[row_idx][2] * right_side[2][col_idx]
            for col_idx in range(3)
        ]
        for row_idx in range(3)
    ]


def rotation(angles):
    cos_a, sin_a = (jnp.cos(angles[0]), jnp.sin(angles[0]))
    cos_b, sin_b = (jnp.cos(angles[1]), jnp.sin(angles[1]))
    cos_c, sin_c = (jnp.cos(angles[2]), jnp.sin(angles[2]))
    about_x = [[1.0, 0.0, 0.0], [0.0, cos_a, -sin_a], [0.0, sin_a, cos_a]]
    about_y = [[cos_b, 0.0, sin_b], [0.0, 1.0, 0.0], [-sin_b, 0.0, cos_b]]
    about_z = [[cos_c, -sin_c, 0.0], [sin_c, cos_c, 0.0], [0.0, 0.0, 1.0]]
    return matrix_product(about_z, matrix_product(about_y, about_x))


def harmonics(dir_x, dir_y, dir_z):
    sq_x, sq_y, sq_z = (dir_x * dir_x, dir_y * dir_y, dir_z * dir_z)
    prod_xy, prod_yz, prod_xz = (dir_x * dir_y, dir_y * dir_z, dir_x * dir_z)
    return [
        HARMONIC_ZERO + 0.0 * dir_x,
        -HARMONIC_ONE * dir_y,
        HARMONIC_ONE * dir_z,
        -HARMONIC_ONE * dir_x,
        HARMONIC_TWO[0] * prod_xy,
        HARMONIC_TWO[1] * prod_yz,
        HARMONIC_TWO[2] * (2.0 * sq_z - sq_x - sq_y),
        HARMONIC_TWO[3] * prod_xz,
        HARMONIC_TWO[4] * (sq_x - sq_y),
        HARMONIC_THREE[0] * dir_y * (3.0 * sq_x - sq_y),
        HARMONIC_THREE[1] * prod_xy * dir_z,
        HARMONIC_THREE[2] * dir_y * (4.0 * sq_z - sq_x - sq_y),
        HARMONIC_THREE[3] * dir_z * (2.0 * sq_z - 3.0 * sq_x - 3.0 * sq_y),
        HARMONIC_THREE[4] * dir_x * (4.0 * sq_z - sq_x - sq_y),
        HARMONIC_THREE[5] * dir_z * (sq_x - sq_y),
        HARMONIC_THREE[6] * dir_x * (sq_x - 3.0 * sq_y),
    ]


LANES = 128
SUBS = 8
GROUP = 16
STEP_ROWS = LANES // GROUP
FEATS = 8
PAIR = 2 * FEATS
OPACITY, COLOUR = 9, 10
COEF_ROWS = 32
JOIN = 8
UNROLL = 8
MOVES = 16
TAPS = 11
COARSE = ((1, 0), (0, 1), (0, 0))
FINE = ((2, 0), (0, 2), (1, 1)) + COARSE
DEAD = -1e30
LOG_TOP = float(np.log(0.99))


def stepped(total, width, body, state):
    def step(block, held):
        for k in range(width):
            held = body(block * width + k, held)
        return held

    return lax.fori_loop(0, (total + width - 1) // width, step, state)


def lane_spread(index):
    return index // LANES, index % LANES


def take_blocks(read, count, block, place):
    result = jnp.zeros(place.shape, jnp.float32)
    for num in range(count):
        taken = jnp.take_along_axis(read(num), place, axis=1, mode="promise_in_bounds")
        result = jnp.where(block == num, taken, result)
    return result


def take_line(read, count, block, place):
    sub = lax.broadcasted_iota(jnp.int32, (SUBS, LANES), 0)
    result = take_blocks(read, -(-count // SUBS), block // SUBS, place)
    return jnp.sum(jnp.where(sub == block % SUBS, result, 0.0), axis=0, keepdims=True)


def camera_table(camera):
    columns = [camera[:, entry] for entry in range(6)]
    turn = rotation(columns[0:3])
    shift = columns[3:6]
    anchor = [
        -(turn[0][c] * shift[0] + turn[1][c] * shift[1] + turn[2][c] * shift[2]) for c in range(3)
    ]
    flat = [turn[r][c] for r in range(3) for c in range(3)] + shift + anchor
    return jnp.stack(flat + [jnp.zeros_like(shift[0])], axis=1)


def covariance(params):
    scales = [jnp.exp(params[3 + axis_num]) for axis_num in range(3)]
    inv_norm = 1.0 / jnp.sqrt(
        params[6] * params[6]
        + params[7] * params[7]
        + params[8] * params[8]
        + params[9] * params[9]
    )
    quat_w, quat_x, quat_y, quat_z = [params[6 + k] * inv_norm for k in range(4)]
    quat_rot = [
        [
            1.0 - 2.0 * (quat_y * quat_y + quat_z * quat_z),
            2.0 * (quat_x * quat_y - quat_w * quat_z),
            2.0 * (quat_x * quat_z + quat_w * quat_y),
        ],
        [
            2.0 * (quat_x * quat_y + quat_w * quat_z),
            1.0 - 2.0 * (quat_x * quat_x + quat_z * quat_z),
            2.0 * (quat_y * quat_z - quat_w * quat_x),
        ],
        [
            2.0 * (quat_x * quat_z - quat_w * quat_y),
            2.0 * (quat_y * quat_z + quat_w * quat_x),
            1.0 - 2.0 * (quat_x * quat_x + quat_y * quat_y),
        ],
    ]
    root = [[quat_rot[r][c] * scales[c] for c in range(3)] for r in range(3)]
    return [
        root[r][0] * root[k][0] + root[r][1] * root[k][1] + root[r][2] * root[k][2]
        for r, k in ((0, 0), (0, 1), (0, 2), (1, 1), (1, 2), (2, 2))
    ]


def view_colours(params, cam):
    ray = [params[c] - cam[12 + c] for c in range(3)]
    inv_len = 1.0 / jnp.sqrt(ray[0] * ray[0] + ray[1] * ray[1] + ray[2] * ray[2])
    basis = harmonics(ray[0] * inv_len, ray[1] * inv_len, ray[2] * inv_len)
    colours = []
    for channel in range(3):
        summed = 0.5 + HARMONIC_ZERO * params[11 + 16 * channel]
        for harmonic in range(1, 16):
            summed = summed + basis[harmonic] * params[11 + 16 * channel + harmonic]
        colours.append(summed)
    return colours


def footprint(mean, cov, cam, image_width, image_height):
    turn = [[cam[3 * r + c] for c in range(3)] for r in range(3)]
    point = [
        turn[r][0] * mean[0] + turn[r][1] * mean[1] + turn[r][2] * mean[2] + cam[9 + r]
        for r in range(3)
    ]
    inv_depth = 1.0 / point[2]
    ratio_x, ratio_y = point[0] * inv_depth, point[1] * inv_depth
    zoom = FOCAL * inv_depth
    row_x = [zoom * (turn[0][c] - ratio_x * turn[2][c]) for c in range(3)]
    row_y = [zoom * (turn[1][c] - ratio_y * turn[2][c]) for c in range(3)]
    full = [[cov[0], cov[1], cov[2]], [cov[1], cov[3], cov[4]], [cov[2], cov[4], cov[5]]]
    spread_x = [
        row_x[0] * full[0][c] + row_x[1] * full[1][c] + row_x[2] * full[2][c] for c in range(3)
    ]
    spread_y = [
        row_y[0] * full[0][c] + row_y[1] * full[1][c] + row_y[2] * full[2][c] for c in range(3)
    ]
    cov_xx = spread_x[0] * row_x[0] + spread_x[1] * row_x[1] + spread_x[2] * row_x[2] + LOW_PASS
    cov_xy = spread_x[0] * row_y[0] + spread_x[1] * row_y[1] + spread_x[2] * row_y[2]
    cov_yy = spread_y[0] * row_y[0] + spread_y[1] * row_y[1] + spread_y[2] * row_y[2] + LOW_PASS
    inv_det = 1.0 / (cov_xx * cov_yy - cov_xy * cov_xy)
    return [
        FOCAL * ratio_x + image_width / 2.0,
        FOCAL * ratio_y + image_height / 2.0,
        cov_yy * inv_det,
        -cov_xy * inv_det,
        cov_xx * inv_det,
    ]


def log_opacity(logit):
    return LOG_TOP - jnp.log(1.0 + jnp.exp(-logit))


def load_params(params_ref, tile_scr, block):
    count = params_ref.shape[0]
    for band in range(0, count, SUBS):
        high = min(band + SUBS, count)
        for j in range(SUBS):
            lane_at = pl.multiple_of(block * SUBS * LANES + j * LANES, LANES)
            tile_scr[band * SUBS + j * SUBS : band * SUBS + j * SUBS + high - band, :] = params_ref[
                band:high, pl.ds(lane_at, LANES)
            ]
    return [
        tile_scr[pl.ds((r // SUBS) * SUBS * SUBS + r % SUBS, SUBS, stride=SUBS), :]
        for r in range(count)
    ]


def source_kernel(
    sizes, cam_ref, counts_ref, list_ref, params_ref, out_ref, tile_scr, table, queue
):
    groups, rows, cap, lane_len = sizes
    per = params_ref.shape[1]
    parts = cap // lane_len
    used = (1 + groups) * FEATS
    count_blocks = per // LANES

    def project_block(block, carry):
        params = load_params(params_ref, tile_scr, block)
        at = block * SUBS * used
        shared = params[0:3] + covariance(params) + [log_opacity(params[10])]
        for num, value in enumerate(shared[0:FEATS]):
            table[pl.ds(at + num, SUBS, stride=used), :] = value
        for group in range(groups):
            lines = shared[FEATS:]
            for view in range(2):
                lines = lines + view_colours(
                    params, [cam_ref[2 * group + view, k] for k in range(15)]
                )
            for num, value in enumerate(lines):
                table[pl.ds(at + (1 + group) * FEATS + num, SUBS, stride=used), :] = value
        return carry

    lax.fori_loop(0, per // (SUBS * LANES), project_block, 0)
    bounds = [jnp.int32(0)]
    for group in range(groups):
        bounds.append(
            lax.fori_loop(
                group * rows, (group + 1) * rows, lambda d, sum_: sum_ + counts_ref[0, d], bounds[-1]
            )
        )
    lane = lax.broadcasted_iota(jnp.int32, (FEATS, LANES), 1)

    def pick(block, carry):
        first = pl.multiple_of(block * LANES, LANES)
        names = jnp.broadcast_to(list_ref[0:1, pl.ds(first, LANES)], (SUBS, LANES))
        home, place = lane_spread(names)
        line_at = pl.multiple_of(block * PAIR, PAIR)
        queue[pl.ds(line_at, FEATS), :] = take_blocks(
            lambda num: table[num * used : num * used + FEATS, :], count_blocks, home, place
        )
        spot = first + lane
        for group in range(groups):
            low, high = bounds[group], bounds[group + 1]

            @pl.when((low < first + LANES) & (high > first))
            def _(group=group, low=low, high=high):
                at = (1 + group) * FEATS
                taken = take_blocks(
                    lambda num: table[num * used + at : num * used + at + FEATS, :],
                    count_blocks,
                    home,
                    place,
                )
                lines = pl.ds(line_at + FEATS, FEATS)
                queue[lines, :] = jnp.where((spot >= low) & (spot < high), taken, queue[lines, :])

        return carry

    lax.fori_loop(0, (bounds[-1] + LANES - 1) // LANES, pick, 0)
    lane_pair = lax.broadcasted_iota(jnp.int32, (PAIR, LANES), 1)

    def send_block(dest, start_at):
        count = counts_ref[0, dest]
        for part in range(parts):

            @pl.when(count > part * lane_len)
            def _(part=part):
                first = start_at + part * lane_len
                block, turn = first // LANES, first % LANES
                pieces = [
                    pltpu.roll(
                        queue[pl.ds(pl.multiple_of((block + step) * PAIR, PAIR), PAIR), :],
                        LANES - turn,
                        1,
                    )
                    for step in range(2)
                ]
                lines = jnp.where(lane_pair < LANES - turn, pieces[0], pieces[1])
                out_ref[dest, part * PAIR : (part + 1) * PAIR, :] = lines[:, 0:lane_len]

        return start_at + count

    lax.fori_loop(0, groups * rows, send_block, jnp.int32(0))


def split_three(value):
    first = value.astype(jnp.bfloat16).astype(jnp.float32)
    rest = value - first
    second = rest.astype(jnp.bfloat16).astype(jnp.float32)
    return [first, second, rest - second]


def in_two(value):
    high = value.astype(jnp.bfloat16).astype(jnp.float32)
    return [high, value - high]


def swap_grain(cells):
    sub = lax.broadcasted_iota(jnp.int32, (SUBS, LANES), 0)
    lane = lax.broadcasted_iota(jnp.int32, (SUBS, LANES), 1) // TILE
    for bit in (1, 2, 4):
        sub_bit, lane_bit = (sub & bit) != 0, (lane & bit) != 0
        from_high = pltpu.roll(pltpu.roll(cells, SUBS - bit, 0), bit * TILE, 1)
        from_low = pltpu.roll(pltpu.roll(cells, bit, 0), LANES - bit * TILE, 1)
        cells = jnp.where(sub_bit == lane_bit, cells, jnp.where(lane_bit, from_high, from_low))
    return cells


def longest(lens_ref, group):
    most = lens_ref[group * GROUP]
    for t in range(1, GROUP):
        most = jnp.maximum(most, lens_ref[group * GROUP + t])
    return most


def gather_slots(arrived_ref, slot_scr, lane_len):
    parts = arrived_ref.shape[1] // PAIR
    joined = LANES // lane_len

    def unpack(block, carry):
        line_at = pl.multiple_of(block * PAIR, PAIR)
        for k in range(joined):
            source = block * joined // parts + k
            part_at = pl.multiple_of(block * joined % parts * PAIR, PAIR)
            slot_scr[pl.ds(line_at, PAIR), k * lane_len : (k + 1) * lane_len] = arrived_ref[
                source, pl.ds(part_at, PAIR), :
            ]
        return carry

    lax.fori_loop(0, slot_scr.shape[0] // PAIR, unpack, 0)


def slot_lines(slot_scr, first):
    return [slot_scr[pl.ds(first * PAIR + num, SUBS, stride=PAIR), :] for num in range(PAIR)]


def render_kernel(
    sizes,
    place_ref,
    cam_ref,
    lens_ref,
    lens_rows_ref,
    names_ref,
    basis_ref,
    arrived_ref,
    image_ref,
    left_ref,
    shape_ref,
    alphas_ref,
    weights_ref,
    slot_scr,
    table,
    logs,
    feat_scr,
    pieces,
    mm,
):
    cap, lane_len, col_groups, list_len, image_width, image_height = sizes
    devices = arrived_ref.shape[0]
    blocks = list_len // STEP_ROWS
    count_blocks = devices * cap // LANES
    gather_slots(arrived_ref, slot_scr, lane_len)

    def project_block(step, carry):
        first = step * SUBS
        lines = slot_lines(slot_scr, first)
        logs[pl.ds(pl.multiple_of(first, SUBS), SUBS), :] = lines[OPACITY]
        for view in range(2):
            cam = [cam_ref[2 * place_ref[1] + view, k] for k in range(15)]
            feats = footprint(lines[0:3], lines[3:9], cam, image_width, image_height)
            feats = feats + lines[COLOUR + 3 * view : COLOUR + 3 * view + 3]
            for num, value in enumerate(feats):
                row_at = (view * count_blocks + first) * FEATS + num
                table[pl.ds(row_at, SUBS, stride=FEATS), :] = value
        return carry

    lax.fori_loop(0, count_blocks // SUBS, project_block, 0)
    centre_y = (place_ref[0] * TILE).astype(jnp.float32) + (TILE - 1) / 2.0
    sub = lax.broadcasted_iota(jnp.int32, (blocks, LANES), 0)
    lane = lax.broadcasted_iota(jnp.int32, (blocks, LANES), 1)
    zero = jnp.zeros((GROUP, LANES), jnp.float32)

    def one_group(group, carry):
        view, col_group = group // col_groups, group % col_groups
        most = longest(lens_ref, group)

        def fetch(block, inner):
            names = names_ref[pl.ds(group * blocks + block, 1), :]
            home, place = lane_spread(jnp.broadcast_to(names, (SUBS, LANES)))
            feat_at = pl.multiple_of(block * PAIR, PAIR)
            feat_scr[pl.ds(feat_at, FEATS), :] = take_blocks(
                lambda num: table[
                    pl.ds(pl.multiple_of((view * count_blocks + num) * FEATS, FEATS), FEATS), :
                ],
                count_blocks,
                home,
                place,
            )
            feat_scr[pl.ds(feat_at + FEATS, 1), :] = take_line(
                lambda num: logs[num * SUBS : (num + 1) * SUBS, :], count_blocks, home, place
            )
            return inner

        stepped((most + STEP_ROWS - 1) // STEP_ROWS, 2, fetch, 0)
        feats = [feat_scr[pl.ds(num, blocks, stride=PAIR), :] for num in range(FEATS)]
        log_o = feat_scr[pl.ds(FEATS, blocks, stride=PAIR), :]
        live = sub * STEP_ROWS + lane // GROUP < lens_rows_ref[pl.ds(group, 1), :]
        centre_x = ((col_group * GROUP + lane % GROUP) * TILE).astype(jnp.float32) + (
            TILE - 1
        ) / 2.0
        off_x, off_y = feats[0] - centre_x, feats[1] - centre_y
        lin_x = feats[2] * off_x + feats[3] * off_y
        lin_y = feats[4] * off_y + feats[3] * off_x
        coefs = [
            log_o - 0.5 * (off_x * lin_x + off_y * lin_y),
            lin_x,
            lin_y,
            -0.5 * feats[2],
            -feats[3],
            -0.5 * feats[4],
        ]
        coefs = [
            jnp.where(live, value, DEAD if num == 0 else 0.0) for num, value in enumerate(coefs)
        ]
        lines = [None] * COEF_ROWS
        for num, value in enumerate(coefs):
            for piece, part in enumerate(split_three(value)):
                lines[piece * 6 + num] = part
        for num in range(3):
            for piece, part in enumerate(split_three(jnp.where(live, feats[5 + num], 0.0))):
                lines[18 + piece * 3 + num] = part
        for num, value in enumerate(lines):
            pieces[pl.ds(num, blocks, stride=COEF_ROWS), :] = (
                jnp.zeros((blocks, LANES), jnp.float32) if value is None else value
            )
        for num, value in enumerate(feats[2:5] + [off_x, off_y]):
            shape_ref[num, pl.ds(pl.multiple_of(group * blocks, blocks), blocks), :] = jnp.where(
                live, value, 0.0
            )
        left_at = pl.multiple_of(group * blocks * LANES, LANES)
        for block in range(blocks):
            left_ref[pl.ds(left_at + block * LANES, LANES), :] = pieces[
                block * COEF_ROWS : (block + 1) * COEF_ROWS, :
            ].T.astype(jnp.bfloat16)
        expand(left_ref, basis_ref, mm, left_at)

        def entry(n, state):
            keep, colour = state
            row_at = pl.multiple_of(n * GROUP, GROUP)
            shade = [
                mm[pl.ds(row_at, GROUP), (2 + c) * LANES : (3 + c) * LANES] for c in range(3)
            ]
            new_keep, new_colour = [], []
            for half in range(2):
                lanes = slice(half * LANES, (half + 1) * LANES)
                alpha = jnp.exp(mm[pl.ds(row_at, GROUP), lanes])
                weight = keep[half] * alpha
                alphas_ref[pl.ds(left_at + row_at, GROUP), lanes] = alpha
                weights_ref[pl.ds(left_at + row_at, GROUP), lanes] = weight
                new_keep.append(keep[half] * (1.0 - alpha))
                new_colour.append([colour[half][c] + weight * shade[c] for c in range(3)])
            return new_keep, new_colour

        state = ([zero + 1.0] * 2, [[zero] * 3] * 2)
        _, colour = stepped(most, UNROLL, entry, state)
        for side in range(GROUP // SUBS):
            lane_at = pl.multiple_of(col_group * GROUP * TILE + side * LANES, LANES)
            for half in range(2):
                for c in range(3):
                    image_ref[view, c, half * SUBS : (half + 1) * SUBS, pl.ds(lane_at, LANES)] = (
                        swap_grain(colour[half][c][side * SUBS : (side + 1) * SUBS])
                    )
        return carry

    lax.fori_loop(0, 2 * col_groups, one_group, 0)


def expand(left_ref, basis_ref, mm, left_at):
    mm[...] = jnp.dot(
        left_ref[pl.ds(left_at, mm.shape[0]), :],
        basis_ref[...],
        preferred_element_type=jnp.float32,
    )


def back_kernel(
    sizes,
    place_ref,
    cam_ref,
    lens_ref,
    names_ref,
    basis_ref,
    moment_ref,
    left_ref,
    shape_ref,
    alphas,
    weights,
    arrived_ref,
    grad_ref,
    out_ref,
    mm,
    slopes,
    grad_scr,
    mom_scr,
    line_scr,
    masked,
    places,
    total_scr,
    slot_scr,
):
    cap, lane_len, col_groups, list_len, image_width, image_height = sizes
    devices = out_ref.shape[0]
    parts = cap // lane_len
    blocks = list_len // STEP_ROWS
    count_blocks = devices * cap // LANES
    joined = LANES // lane_len
    value_rows = count_blocks * 2 * FEATS
    total_scr[...] = jnp.zeros_like(total_scr)
    line_scr[...] = jnp.zeros_like(line_scr)
    grad_scr[...] = jnp.zeros_like(grad_scr)
    zero = jnp.zeros((GROUP, LANES), jnp.float32)
    sub = lax.broadcasted_iota(jnp.int32, (GROUP, LANES), 0)
    lane = lax.broadcasted_iota(jnp.int32, (GROUP, LANES), 1)
    own_tile = lane % GROUP == sub

    def one_group(group, carry):
        view, col_group = group // col_groups, group % col_groups
        most = longest(lens_ref, group)
        lane_at = pl.multiple_of(col_group * GROUP * TILE, LANES)
        grads = [
            [
                jnp.concatenate(
                    [
                        swap_grain(
                            grad_ref[
                                view,
                                c,
                                half * SUBS : (half + 1) * SUBS,
                                pl.ds(lane_at + side * LANES, LANES),
                            ]
                        )
                        for side in range(GROUP // SUBS)
                    ],
                    axis=0,
                )
                for c in range(3)
            ]
            for half in range(2)
        ]
        for half in range(2):
            for c in range(3):
                for piece, part in enumerate(in_two(grads[half][c])):
                    line = (piece * 3 + c) * GROUP
                    grad_scr[line : line + GROUP, half * LANES : (half + 1) * LANES] = part
        first = pl.multiple_of(group * blocks * LANES, LANES)
        expand(left_ref, basis_ref, mm, first)
        last = (most + UNROLL - 1) // UNROLL * UNROLL - 1

        def behind(step, seen):
            row_at = pl.multiple_of((last - step) * GROUP, GROUP)
            shade = [mm[pl.ds(row_at, GROUP), c * LANES : (c + 1) * LANES] for c in range(3)]
            new_seen = []
            for half in range(2):
                lanes = slice(half * LANES, (half + 1) * LANES)
                own = (
                    grads[half][0] * shade[0]
                    + grads[half][1] * shade[1]
                    + grads[half][2] * shade[2]
                )
                alpha = alphas[pl.ds(first + row_at, GROUP), lanes]
                weight = weights[pl.ds(first + row_at, GROUP), lanes]
                slopes[pl.ds(row_at, GROUP), lanes] = weight * (own - seen[half])
                new_seen.append(seen[half] * (1.0 - alpha) + alpha * own)
            return new_seen

        stepped(most, UNROLL, behind, [zero] * 2)
        left, right = [], []
        for value, columns in (
            (slopes[...], moment_ref[...]),
            (
                weights[pl.ds(first, blocks * LANES), :],
                grad_scr[...].T.astype(jnp.bfloat16),
            ),
        ):
            high = value.astype(jnp.bfloat16)
            left += [high, (value - high.astype(jnp.float32)).astype(jnp.bfloat16)]
            right += [columns, columns]
        total = jnp.dot(
            jnp.concatenate(left, axis=1),
            jnp.concatenate(right, axis=0),
            preferred_element_type=jnp.float32,
        )
        for block in range(blocks):
            turned = total[block * LANES : (block + 1) * LANES].T
            mom_scr[block * TILE : block * TILE + 8, :] = turned[6 * GROUP : 6 * GROUP + 8]
            for c in range(3):
                summed = (
                    turned[c * GROUP : (c + 1) * GROUP]
                    + turned[(3 + c) * GROUP : (4 + c) * GROUP]
                )
                mom_scr[block * TILE + 8 + c : block * TILE + 9 + c, :] = jnp.sum(
                    jnp.where(own_tile, summed, 0.0), axis=0, keepdims=True
                )
        mom = [mom_scr[pl.ds(num, blocks, stride=TILE), :] for num in range(11)]
        con_xx, con_xy, con_yy, off_x, off_y = [
            shape_ref[num, pl.ds(pl.multiple_of(group * blocks, blocks), blocks), :]
            for num in range(5)
        ]
        sum_x = off_x * mom[0] - mom[1]
        sum_y = off_y * mom[0] - mom[2]
        results = [
            -(con_xx * sum_x + con_xy * sum_y),
            -(con_yy * sum_y + con_xy * sum_x),
            -0.5 * (off_x * (sum_x - mom[1]) + mom[3]),
            -(off_x * sum_y - off_y * mom[1] + mom[4]),
            -0.5 * (off_y * (sum_y - mom[2]) + mom[5]),
        ] + mom[8:11]
        for num, value in enumerate(results + [mom[0]]):
            line_scr[pl.ds(num, blocks, stride=PAIR), :] = value

        def spread(step, inner):
            for k in range(JOIN):
                block = step * JOIN + k
                lanes = slice(k * LANES, (k + 1) * LANES)
                names = names_ref[pl.ds(group * blocks + block, 1), :]
                home, place = names // LANES, names % LANES
                line_at = pl.multiple_of(block * PAIR, PAIR)
                values = in_two(line_scr[pl.ds(line_at, FEATS), :])
                logs = in_two(line_scr[pl.ds(line_at + FEATS, 1), :])
                home_wide = jnp.broadcast_to(home, (2 * FEATS, LANES)).astype(jnp.bfloat16)
                pair = jnp.concatenate(values, axis=0).astype(jnp.bfloat16)
                for num in range(count_blocks):
                    masked[num * 2 * FEATS : (num + 1) * 2 * FEATS, lanes] = jnp.where(
                        home_wide == jnp.bfloat16(num), pair, jnp.bfloat16(0)
                    )
                rank = lax.broadcasted_iota(jnp.int32, (count_blocks, LANES), 0)
                for piece, value in enumerate(logs):
                    first = value_rows + piece * count_blocks
                    masked[first : first + count_blocks, lanes] = jnp.where(
                        rank == home, value, 0.0
                    ).astype(jnp.bfloat16)
                seat = lax.broadcasted_iota(jnp.int32, (LANES, LANES), 0)
                places[:, lanes] = jnp.where(seat == place, 1.0, 0.0).astype(jnp.bfloat16)
            total_scr[view] += lax.dot_general(
                masked[...],
                places[...],
                (((1,), (1,)), ((), ())),
                preferred_element_type=jnp.float32,
            )
            return inner

        width = JOIN * STEP_ROWS
        lax.fori_loop(0, (most + width - 1) // width, spread, 0)
        return carry

    lax.fori_loop(0, 2 * col_groups, one_group, 0)

    gather_slots(arrived_ref, slot_scr, lane_len)

    def pull_block(step, carry):
        first = step * SUBS
        lines = slot_lines(slot_scr, first)
        cams = [[cam_ref[2 * place_ref[1] + view, k] for k in range(15)] for view in range(2)]

        def both(*values):
            return [
                footprint(values[0:3], values[3:9], cam, image_width, image_height)
                for cam in cams
            ]

        cots = []
        log_sum = jnp.zeros((SUBS, LANES), jnp.float32)
        for view in range(2):
            row_at = first * 2 * FEATS
            cots.append(
                [
                    total_scr[view, pl.ds(row_at + num, SUBS, stride=2 * FEATS), :]
                    + total_scr[view, pl.ds(row_at + FEATS + num, SUBS, stride=2 * FEATS), :]
                    for num in range(FEATS)
                ]
            )
            for piece in range(2):
                row = pl.multiple_of(value_rows + piece * count_blocks + first, SUBS)
                log_sum = log_sum + total_scr[view, pl.ds(row, SUBS), :]
        _, pull = jax.vjp(both, *lines[0:9])
        results = list(pull([cot[0:5] for cot in cots])) + [log_sum] + cots[0][5:] + cots[1][5:]
        for num, value in enumerate(results):
            slot_scr[pl.ds(first * PAIR + num, SUBS, stride=PAIR), :] = value
        return carry

    lax.fori_loop(0, count_blocks // SUBS, pull_block, 0)

    def pack(block, carry):
        line_at = pl.multiple_of(block * PAIR, PAIR)
        for k in range(joined):
            source = block * joined // parts + k
            part_at = pl.multiple_of(block * joined % parts * PAIR, PAIR)
            out_ref[source, pl.ds(part_at, PAIR), :] = slot_scr[
                pl.ds(line_at, PAIR), k * lane_len : (k + 1) * lane_len
            ]
        return carry

    lax.fori_loop(0, count_blocks, pack, 0)


def owner_kernel(
    sizes,
    cam_ref,
    list_ref,
    counts_ref,
    params_ref,
    back_ref,
    out_hbm,
    out_ref,
    tile_scr,
    feat_scr,
    turn_scr,
    table,
    slots,
    out_sem,
):
    groups, rows, cap, lane_len = sizes
    count_params, per = params_ref.shape
    parts = cap // lane_len
    table[...] = jnp.zeros_like(table)
    turn_scr[...] = jnp.zeros_like(turn_scr)
    start = jnp.int32(0)
    for group in range(groups):
        turn_scr[PAIR : PAIR + 1, :] = jnp.full((1, LANES), 1.0 + group, jnp.float32)

        def take_block(t, start_at, group=group):
            dest = group * rows + t
            count = counts_ref[0, dest]

            for part in range(parts):
                turn_scr[0:PAIR, 0:lane_len] = back_ref[dest, part * PAIR : (part + 1) * PAIR, :]
                slots[part * lane_len : (part + 1) * lane_len, 0:24] = turn_scr[
                    :, 0:lane_len
                ].T

            def move(k, carry):
                spot = list_ref[0, start_at + k]
                table[pl.ds(spot, 1), :] = slots[pl.ds(k, 1), :]
                return carry

            rounded = (count + MOVES - 1) // MOVES * MOVES
            whole = jnp.where(start_at + rounded <= per, rounded, count // MOVES * MOVES)
            stepped(whole, MOVES, move, 0)
            lax.fori_loop(whole, count, move, 0)
            return start_at + count

        start = lax.fori_loop(0, rows, take_block, start)

    def clear(k, carry):
        table[pl.ds(list_ref[0, k], 1), :] = jnp.zeros((1, LANES), jnp.float32)
        return carry

    lax.fori_loop(start, jnp.minimum(start + MOVES, per), clear, 0)

    wide = SUBS * LANES

    def out_copy(block):
        lanes = pl.ds(pl.multiple_of(block * wide, wide), wide)
        return pltpu.make_async_copy(
            out_ref.at[:, lanes], out_hbm.at[:, lanes], out_sem.at[block]
        )

    def pull_block(block, carry):
        params = load_params(params_ref, tile_scr, block)
        for j in range(SUBS):
            row_at = pl.multiple_of(block * SUBS * LANES + j * LANES, LANES)
            feat_scr[j * 24 : (j + 1) * 24, :] = table[pl.ds(row_at, LANES), 0:24].T
        cots = [feat_scr[pl.ds(num, SUBS, stride=24), :] for num in range(PAIR + 1)]
        home = cots[PAIR]
        sent = home > 0.5
        cams = []
        for view in range(2):
            cam = []
            for k in range(15):
                value = jnp.full((SUBS, LANES), cam_ref[view, k], jnp.float32)
                for group in range(1, groups):
                    value = jnp.where(home > 0.5 + group, cam_ref[2 * group + view, k], value)
                cam.append(value)
            cams.append(cam)

        def both(*values):
            return (
                covariance(values)
                + [log_opacity(values[10])]
                + view_colours(values, cams[0])
                + view_colours(values, cams[1])
            )

        _, pull = jax.vjp(both, *params)
        grads = list(pull(cots[3:PAIR]))
        for num in range(3):
            grads[num] = grads[num] + cots[num]
        for num, value in enumerate(grads):
            tile_scr[pl.ds((num // SUBS) * SUBS * SUBS + num % SUBS, SUBS, stride=SUBS), :] = (
                jnp.where(sent, value, 0.0)
            )
        for band in range(0, count_params, SUBS):
            high = min(band + SUBS, count_params)
            for j in range(SUBS):
                lane_at = pl.multiple_of(block * SUBS * LANES + j * LANES, LANES)
                out_ref[band:high, pl.ds(lane_at, LANES)] = tile_scr[
                    band * SUBS + j * SUBS : band * SUBS + j * SUBS + high - band, :
                ]
        out_copy(block).start()
        return carry

    lax.fori_loop(0, per // wide, pull_block, 0)
    for block in range(per // wide):
        out_copy(block).wait()


def tap_rows(read, first, count):
    taps = window_taps()
    total = taps[5] * read(first + 5, count)
    for k in range(5):
        total = total + taps[k] * (read(first + k, count) + read(first + TAPS - 1 - k, count))
    return total


def blur_lanes(value, band_ref, pairs):
    pieces = [piece.astype(jnp.bfloat16) for piece in split_three(value)]
    total = 0.0
    for mine, other in pairs:
        total = total + jnp.dot(
            pieces[mine], band_ref[other], preferred_element_type=jnp.float32
        )
    return total


def truth_kernel(band_ref, above_ref, own_ref, below_ref, out_ref, tall, mixed):
    images = own_ref.shape[0]

    def one_image(m, carry):
        whole = jnp.concatenate([above_ref[m], own_ref[m], below_ref[m]], axis=0)
        for field, value in enumerate((whole, whole * whole)):
            tall[...] = value
            row_at = pl.multiple_of((field * images + m) * 2 * TILE, 2 * TILE)
            mixed[pl.ds(row_at, 2 * TILE), :] = tap_rows(
                lambda at, count: tall[at : at + count, :], 6, 2 * TILE
            )
        return carry

    lax.fori_loop(0, images, one_image, 0)
    out_ref[...] = blur_lanes(mixed[...], band_ref, FINE)


def loss_kernel(
    image_rows,
    row_ref,
    band_ref,
    truth_ref,
    true_above,
    true_own,
    true_below,
    above_ref,
    own_ref,
    below_ref,
    out_ref,
    tall,
    mixed,
    blurred,
    slim,
):
    images = own_ref.shape[0]
    tall_rows = 2 * TILE
    width = own_ref.shape[2]

    def one_image(m, carry):
        whole = jnp.concatenate([above_ref[m], own_ref[m], below_ref[m]], axis=0)
        true = jnp.concatenate([true_above[m], true_own[m], true_below[m]], axis=0)
        for field, value in enumerate((whole, whole * whole, whole * true)):
            tall[field] = value
            row_at = pl.multiple_of((field * images + m) * tall_rows, tall_rows)
            mixed[pl.ds(row_at, tall_rows), :] = tap_rows(
                lambda at, count, field=field: tall[field, at : at + count, :], 6, tall_rows
            )
        return carry

    lax.fori_loop(0, images, one_image, 0)
    blurred[...] = blur_lanes(mixed[...], band_ref, FINE)
    sub = lax.broadcasted_iota(jnp.int32, (tall_rows, width), 0)
    image_row = row_ref[0] * TILE + sub - 5
    inside = (image_row >= 0) & (image_row < image_rows) & (sub < TILE + 10)

    def one_map(m, carry):
        def field_of(ref, field):
            row_at = pl.multiple_of((field * images + m) * tall_rows, tall_rows)
            return ref[pl.ds(row_at, tall_rows), :]

        mean_one, both_one, cross = [field_of(blurred, field) for field in range(3)]
        mean_two, both_two = field_of(truth_ref, 0), field_of(truth_ref, 1)
        square_one, square_two = mean_one * mean_one, mean_two * mean_two
        mean_cross = mean_one * mean_two
        top_one = 2.0 * mean_cross + SSIM_ONE
        top_two = 2.0 * (cross - mean_cross) + SSIM_TWO
        low_one = square_one + square_two + SSIM_ONE
        low_two = (both_one - square_one) + (both_two - square_two) + SSIM_TWO
        inv_one, inv_two = 1.0 / low_one, 1.0 / low_two
        inv_both = inv_one * inv_two
        value = top_one * top_two * inv_both
        grads = [
            2.0 * mean_two * (top_two - top_one) * inv_both
            - 2.0 * mean_one * value * (inv_one - inv_two),
            -value * inv_two,
            2.0 * top_one * inv_both,
        ]
        for field, grad in enumerate(grads):
            tall[field, 0:tall_rows] = jnp.where(inside, grad, 0.0)
            row_at = pl.multiple_of((field * images + m) * TILE, TILE)
            slim[pl.ds(row_at, TILE), :] = tap_rows(
                lambda at, count, field=field: tall[field, at : at + count, :], 0, TILE
            )
        return carry

    lax.fori_loop(0, images, one_map, 0)
    spread = blur_lanes(slim[...], band_ref, COARSE).reshape(3, images, TILE, width)
    own, true = own_ref[...], true_own[...]
    gap = own - true
    out_ref[...] = (1.0 - SSIM_SHARE) * gap / jnp.sqrt(gap * gap + SMOOTH_EPS) - SSIM_SHARE * (
        spread[0] + 2.0 * own * spread[1] + true * spread[2]
    )


def band_matrix(width):
    taps = window_taps()
    band = np.zeros((width, width), np.float32)
    for k in range(TAPS):
        band += np.diag(np.full(width - abs(k - 5), taps[k], np.float32), k - 5)
    pieces = []
    for _ in range(3):
        pieces.append(band.astype(jnp.bfloat16))
        band = band - pieces[-1].astype(np.float32)
    return jnp.asarray(np.stack(pieces))


def pixel_basis():
    pixel = np.arange(TILE * TILE)
    x = (pixel % TILE) - (TILE - 1) / 2.0
    y = (pixel // TILE) - (TILE - 1) / 2.0
    return np.stack([np.ones_like(x), x, y, x * x, x * y, y * y])


def expand_matrix(first=0):
    terms = pixel_basis()
    matrix = np.zeros((COEF_ROWS, 5 * LANES), np.float32)
    for piece in range(3):
        matrix[piece * 6 : piece * 6 + 6, 0 : 2 * LANES] = terms
        for c in range(3):
            matrix[18 + piece * 3 + c, (2 + c) * LANES : (3 + c) * LANES] = 1.0
    return jnp.asarray(matrix[:, first:], jnp.bfloat16)


def moment_matrix():
    matrix = np.zeros((2 * LANES, LANES), np.float32)
    matrix[:, 6 * GROUP : 6 * GROUP + 6] = pixel_basis().T
    return jnp.asarray(matrix, jnp.bfloat16)


def smem():
    return pl.BlockSpec(memory_space=pltpu.SMEM)


def vmem():
    return pl.BlockSpec(memory_space=pltpu.VMEM)


def scratch(*shape):
    return pltpu.VMEM(shape, jnp.float32)


def run(kernel, megabytes, out_shapes, in_specs, scratches, *operands, out_specs=None):
    return pl.pallas_call(
        kernel,
        out_shape=out_shapes,
        in_specs=in_specs,
        out_specs=out_specs or jax.tree.map(lambda _: vmem(), out_shapes),
        scratch_shapes=scratches,
        compiler_params=pltpu.CompilerParams(vmem_limit_bytes=megabytes << 20),
    )(*operands)


def shards(params, send_list, send_counts, camera, ground_truth, tile_lists, list_lengths):
    devices = lax.axis_size(("view", "tile"))
    row_devices = lax.axis_size("tile")
    groups = lax.axis_size("view")
    count_params, per_device = params.shape
    capacity = per_device // devices
    tile_cols, list_len = tile_lists.shape[2:]
    col_groups = tile_cols // GROUP
    blocks = list_len // STEP_ROWS
    tile_row = lax.axis_index("tile")
    image_width = float(ground_truth.shape[3])
    image_height = float(ground_truth.shape[2] * row_devices)
    lane_len = min(capacity, LANES)
    sent_shape = jax.ShapeDtypeStruct(
        (devices, capacity // lane_len * PAIR, lane_len), jnp.float32
    )
    count_blocks = per_device // LANES
    cams = camera_table(camera)

    flat_lengths = list_lengths.reshape(-1)
    entry_rank = jnp.arange(list_len, dtype=jnp.int32)
    tile_num = jnp.arange(2 * tile_cols, dtype=jnp.int32)
    lists = jnp.where(
        entry_rank[None, :] < flat_lengths[:, None],
        tile_lists.reshape(2 * tile_cols, list_len),
        per_device + tile_num[:, None] % GROUP,
    )
    lens_rows = jnp.tile(flat_lengths.reshape(-1, GROUP), (1, LANES // GROUP))

    width = ground_truth.shape[3]
    true_own = ground_truth.reshape(-1, TILE, width)
    true_above = from_behind(true_own, "tile", 1)
    true_below = from_behind(true_own, "tile", -1)
    band = band_matrix(width)
    truth_rows = 2 * true_own.shape[0] * 2 * TILE
    truth_blur = run(
        truth_kernel,
        16,
        jax.ShapeDtypeStruct((truth_rows, width), jnp.float32),
        [vmem()] * 4,
        [scratch(3 * TILE, width), scratch(truth_rows, width)],
        band,
        true_above,
        true_own,
        true_below,
    )

    own_sizes = (groups, row_devices, capacity, lane_len)
    sent = run(
        lambda *refs: source_kernel(own_sizes, *refs),
        24,
        sent_shape,
        [smem(), smem(), vmem(), vmem()],
        [
            scratch(SUBS * SUBS * SUBS, LANES),
            scratch(count_blocks * (1 + groups) * FEATS, LANES),
            scratch((count_blocks + 1) * PAIR, LANES),
        ],
        cams,
        send_counts,
        send_list,
        params,
    )
    arrived = lax.all_to_all(sent, ("view", "tile"), split_axis=0, concat_axis=0, tiled=True)

    arrived, truth_blur = lax.optimization_barrier((arrived, truth_blur))
    tile_sizes = (capacity, lane_len, col_groups, list_len, image_width, image_height)
    place = jnp.stack([tile_row, lax.axis_index("view")])
    entries = 2 * tile_cols * list_len
    names = lists.reshape(-1, GROUP, list_len).transpose(0, 2, 1).reshape(-1, LANES)
    rendered, left, shapes, alphas, weights = run(
        lambda *refs: render_kernel(tile_sizes, *refs),
        28,
        (
            jax.ShapeDtypeStruct(ground_truth.shape, jnp.float32),
            jax.ShapeDtypeStruct((entries, COEF_ROWS), jnp.bfloat16),
            jax.ShapeDtypeStruct((5, entries // LANES, LANES), jnp.float32),
            jax.ShapeDtypeStruct((entries, 2 * LANES), jnp.float32),
            jax.ShapeDtypeStruct((entries, 2 * LANES), jnp.float32),
        ),
        [smem(), smem(), smem(), vmem(), vmem(), vmem(), vmem()],
        [
            scratch(count_blocks * PAIR, LANES),
            scratch(2 * per_device // LANES * FEATS, LANES),
            scratch(count_blocks, LANES),
            scratch(blocks * PAIR, LANES),
            scratch(blocks * COEF_ROWS, LANES),
            scratch(blocks * LANES, 5 * LANES),
        ],
        place,
        cams,
        flat_lengths,
        lens_rows,
        names,
        expand_matrix(),
        arrived,
    )

    images = rendered.reshape(true_own.shape)
    count = images.shape[0]
    grad_image = run(
        lambda *refs: loss_kernel(TILE * row_devices, *refs),
        16,
        jax.ShapeDtypeStruct(images.shape, jnp.float32),
        [smem()] + [vmem()] * 8,
        [
            scratch(3, 3 * TILE, width),
            scratch(3 * count * 2 * TILE, width),
            scratch(3 * count * 2 * TILE, width),
            scratch(3 * count * TILE, width),
        ],
        place,
        band,
        truth_blur,
        true_above,
        true_own,
        true_below,
        from_behind(images, "tile", 1),
        images,
        from_behind(images, "tile", -1),
    ).reshape(ground_truth.shape)

    spread_rows = count_blocks * (2 * FEATS + 2)
    grad_slots = run(
        lambda *refs: back_kernel(tile_sizes, *refs),
        31,
        sent_shape,
        [smem()] * 3 + [vmem()] * 9,
        [
            scratch(blocks * LANES, 3 * LANES),
            scratch(blocks * LANES, 2 * LANES),
            scratch(LANES, 2 * LANES),
            scratch(blocks * TILE, LANES),
            scratch(blocks * PAIR, LANES),
            pltpu.VMEM((spread_rows, JOIN * LANES), jnp.bfloat16),
            pltpu.VMEM((LANES, JOIN * LANES), jnp.bfloat16),
            scratch(2, spread_rows, LANES),
            scratch(count_blocks * PAIR, LANES),
        ],
        place,
        cams,
        flat_lengths,
        names,
        expand_matrix(2 * LANES),
        moment_matrix(),
        left,
        shapes,
        alphas,
        weights,
        arrived,
        grad_image,
    )
    returned = lax.all_to_all(
        grad_slots, ("view", "tile"), split_axis=0, concat_axis=0, tiled=True
    )
    return run(
        lambda *refs: owner_kernel(own_sizes, *refs),
        24,
        jax.ShapeDtypeStruct(params.shape, jnp.float32),
        [smem(), smem(), smem(), vmem(), vmem()],
        [
            scratch(*params.shape),
            scratch(SUBS * SUBS * SUBS, LANES),
            scratch(SUBS * 24, LANES),
            scratch(24, LANES),
            scratch(per_device, LANES),
            scratch(capacity, LANES),
            pltpu.SemaphoreType.DMA((count_blocks // SUBS,)),
        ],
        cams,
        send_list,
        send_counts,
        params,
        returned,
        out_specs=pl.BlockSpec(memory_space=pl.ANY),
    )


def solution(mesh):
    in_specs = (
        P(None, ("view", "tile")),
        P(("view", "tile"), None),
        P(("view", "tile"), None),
        P(),
        P("view", None, "tile", None),
        P("view", "tile", None, None),
        P("view", "tile", None),
    )
    out_specs = P(None, ("view", "tile"))
    return jax.shard_map(shards, mesh=mesh, in_specs=in_specs, out_specs=out_specs, check_vma=False)
```

```python
import jax
import jax.numpy as jnp
import numpy as np
from jax import lax
from jax.experimental import pallas as pl
from jax.experimental.pallas import tpu as pltpu
from jax.sharding import PartitionSpec as P

TILE = 16


FOCAL = 1000.0
LOW_PASS = 0.3
SSIM_SHARE = 0.2
SMOOTH_EPS = 1e-06
SSIM_ONE = 0.0001
SSIM_TWO = 0.0009
HARMONIC_ZERO = 0.28209479177387814
HARMONIC_ONE = 0.4886025119029199
HARMONIC_TWO = (
    1.0925484305920792,
    -1.0925484305920792,
    0.31539156525252005,
    -1.0925484305920792,
    0.5462742152960396,
)
HARMONIC_THREE = (
    -0.5900435899266435,
    2.890611442640554,
    -0.4570457994644658,
    0.3731763325901154,
    -0.4570457994644658,
    1.445305721320277,
    -0.5900435899266435,
)


def from_behind(block, axis, distance):
    devices = range(lax.axis_size(axis))
    route = [(i - distance, i) for i in devices if i - distance in devices]
    return lax.ppermute(block, axis, route)


def window_taps():
    offsets_np = np.arange(11) - 5.0
    weights = np.exp(-offsets_np * offsets_np / 4.5)
    weights = weights / weights.sum()
    return [float(weight) for weight in weights]


def matrix_product(left_side, right_side):
    return [
        [
            left_side[row_idx][0] * right_side[0][col_idx]
            + left_side[row_idx][1] * right_side[1][col_idx]
            + left_side[row_idx][2] * right_side[2][col_idx]
            for col_idx in range(3)
        ]
        for row_idx in range(3)
    ]


def rotation(angles):
    cos_a, sin_a = (jnp.cos(angles[0]), jnp.sin(angles[0]))
    cos_b, sin_b = (jnp.cos(angles[1]), jnp.sin(angles[1]))
    cos_c, sin_c = (jnp.cos(angles[2]), jnp.sin(angles[2]))
    about_x = [[1.0, 0.0, 0.0], [0.0, cos_a, -sin_a], [0.0, sin_a, cos_a]]
    about_y = [[cos_b, 0.0, sin_b], [0.0, 1.0, 0.0], [-sin_b, 0.0, cos_b]]
    about_z = [[cos_c, -sin_c, 0.0], [sin_c, cos_c, 0.0], [0.0, 0.0, 1.0]]
    return matrix_product(about_z, matrix_product(about_y, about_x))


def harmonics(dir_x, dir_y, dir_z):
    sq_x, sq_y, sq_z = (dir_x * dir_x, dir_y * dir_y, dir_z * dir_z)
    prod_xy, prod_yz, prod_xz = (dir_x * dir_y, dir_y * dir_z, dir_x * dir_z)
    return [
        HARMONIC_ZERO + 0.0 * dir_x,
        -HARMONIC_ONE * dir_y,
        HARMONIC_ONE * dir_z,
        -HARMONIC_ONE * dir_x,
        HARMONIC_TWO[0] * prod_xy,
        HARMONIC_TWO[1] * prod_yz,
        HARMONIC_TWO[2] * (2.0 * sq_z - sq_x - sq_y),
        HARMONIC_TWO[3] * prod_xz,
        HARMONIC_TWO[4] * (sq_x - sq_y),
        HARMONIC_THREE[0] * dir_y * (3.0 * sq_x - sq_y),
        HARMONIC_THREE[1] * prod_xy * dir_z,
        HARMONIC_THREE[2] * dir_y * (4.0 * sq_z - sq_x - sq_y),
        HARMONIC_THREE[3] * dir_z * (2.0 * sq_z - 3.0 * sq_x - 3.0 * sq_y),
        HARMONIC_THREE[4] * dir_x * (4.0 * sq_z - sq_x - sq_y),
        HARMONIC_THREE[5] * dir_z * (sq_x - sq_y),
        HARMONIC_THREE[6] * dir_x * (sq_x - 3.0 * sq_y),
    ]


LANES = 128
SUBS = 8
GROUP = 16
STEP_ROWS = LANES // GROUP
FEATS = 8
PAIR = 2 * FEATS
OPACITY, COLOUR = 9, 10
COEF_ROWS = 32
JOIN = 8
UNROLL = 8
MOVES = 16
TAPS = 11
COARSE = ((1, 0), (0, 1), (0, 0))
FINE = ((2, 0), (0, 2), (1, 1)) + COARSE
DEAD = -1e30
LOG_TOP = float(np.log(0.99))


def stepped(total, width, body, state):
    def step(block, held):
        for k in range(width):
            held = body(block * width + k, held)
        return held

    return lax.fori_loop(0, (total + width - 1) // width, step, state)


def lane_spread(index):
    return index // LANES, index % LANES


def take_blocks(read, count, block, place):
    result = jnp.zeros(place.shape, jnp.float32)
    for num in range(count):
        taken = jnp.take_along_axis(read(num), place, axis=1, mode="promise_in_bounds")
        result = jnp.where(block == num, taken, result)
    return result


def take_line(read, count, block, place):
    sub = lax.broadcasted_iota(jnp.int32, (SUBS, LANES), 0)
    result = take_blocks(read, -(-count // SUBS), block // SUBS, place)
    return jnp.sum(jnp.where(sub == block % SUBS, result, 0.0), axis=0, keepdims=True)


def camera_table(camera):
    columns = [camera[:, entry] for entry in range(6)]
    turn = rotation(columns[0:3])
    shift = columns[3:6]
    anchor = [
        -(turn[0][c] * shift[0] + turn[1][c] * shift[1] + turn[2][c] * shift[2]) for c in range(3)
    ]
    flat = [turn[r][c] for r in range(3) for c in range(3)] + shift + anchor
    return jnp.stack(flat + [jnp.zeros_like(shift[0])], axis=1)


def covariance(params):
    scales = [jnp.exp(params[3 + axis_num]) for axis_num in range(3)]
    inv_norm = 1.0 / jnp.sqrt(
        params[6] * params[6]
        + params[7] * params[7]
        + params[8] * params[8]
        + params[9] * params[9]
    )
    quat_w, quat_x, quat_y, quat_z = [params[6 + k] * inv_norm for k in range(4)]
    quat_rot = [
        [
            1.0 - 2.0 * (quat_y * quat_y + quat_z * quat_z),
            2.0 * (quat_x * quat_y - quat_w * quat_z),
            2.0 * (quat_x * quat_z + quat_w * quat_y),
        ],
        [
            2.0 * (quat_x * quat_y + quat_w * quat_z),
            1.0 - 2.0 * (quat_x * quat_x + quat_z * quat_z),
            2.0 * (quat_y * quat_z - quat_w * quat_x),
        ],
        [
            2.0 * (quat_x * quat_z - quat_w * quat_y),
            2.0 * (quat_y * quat_z + quat_w * quat_x),
            1.0 - 2.0 * (quat_x * quat_x + quat_y * quat_y),
        ],
    ]
    root = [[quat_rot[r][c] * scales[c] for c in range(3)] for r in range(3)]
    return [
        root[r][0] * root[k][0] + root[r][1] * root[k][1] + root[r][2] * root[k][2]
        for r, k in ((0, 0), (0, 1), (0, 2), (1, 1), (1, 2), (2, 2))
    ]


def view_colours(params, cam):
    ray = [params[c] - cam[12 + c] for c in range(3)]
    inv_len = 1.0 / jnp.sqrt(ray[0] * ray[0] + ray[1] * ray[1] + ray[2] * ray[2])
    basis = harmonics(ray[0] * inv_len, ray[1] * inv_len, ray[2] * inv_len)
    colours = []
    for channel in range(3):
        summed = 0.5 + HARMONIC_ZERO * params[11 + 16 * channel]
        for harmonic in range(1, 16):
            summed = summed + basis[harmonic] * params[11 + 16 * channel + harmonic]
        colours.append(summed)
    return colours


def footprint(mean, cov, cam, image_width, image_height):
    turn = [[cam[3 * r + c] for c in range(3)] for r in range(3)]
    point = [
        turn[r][0] * mean[0] + turn[r][1] * mean[1] + turn[r][2] * mean[2] + cam[9 + r]
        for r in range(3)
    ]
    inv_depth = 1.0 / point[2]
    ratio_x, ratio_y = point[0] * inv_depth, point[1] * inv_depth
    zoom = FOCAL * inv_depth
    row_x = [zoom * (turn[0][c] - ratio_x * turn[2][c]) for c in range(3)]
    row_y = [zoom * (turn[1][c] - ratio_y * turn[2][c]) for c in range(3)]
    full = [[cov[0], cov[1], cov[2]], [cov[1], cov[3], cov[4]], [cov[2], cov[4], cov[5]]]
    spread_x = [
        row_x[0] * full[0][c] + row_x[1] * full[1][c] + row_x[2] * full[2][c] for c in range(3)
    ]
    spread_y = [
        row_y[0] * full[0][c] + row_y[1] * full[1][c] + row_y[2] * full[2][c] for c in range(3)
    ]
    cov_xx = spread_x[0] * row_x[0] + spread_x[1] * row_x[1] + spread_x[2] * row_x[2] + LOW_PASS
    cov_xy = spread_x[0] * row_y[0] + spread_x[1] * row_y[1] + spread_x[2] * row_y[2]
    cov_yy = spread_y[0] * row_y[0] + spread_y[1] * row_y[1] + spread_y[2] * row_y[2] + LOW_PASS
    inv_det = 1.0 / (cov_xx * cov_yy - cov_xy * cov_xy)
    return [
        FOCAL * ratio_x + image_width / 2.0,
        FOCAL * ratio_y + image_height / 2.0,
        cov_yy * inv_det,
        -cov_xy * inv_det,
        cov_xx * inv_det,
    ]


def log_opacity(logit):
    return LOG_TOP - jnp.log(1.0 + jnp.exp(-logit))


def load_params(params_ref, tile_scr, block):
    count = params_ref.shape[0]
    for band in range(0, count, SUBS):
        high = min(band + SUBS, count)
        for j in range(SUBS):
            lane_at = pl.multiple_of(block * SUBS * LANES + j * LANES, LANES)
            tile_scr[band * SUBS + j * SUBS : band * SUBS + j * SUBS + high - band, :] = params_ref[
                band:high, pl.ds(lane_at, LANES)
            ]
    return [
        tile_scr[pl.ds((r // SUBS) * SUBS * SUBS + r % SUBS, SUBS, stride=SUBS), :]
        for r in range(count)
    ]


def source_kernel(
    sizes, cam_ref, counts_ref, list_ref, params_ref, out_ref, tile_scr, table, queue
):
    groups, rows, cap, lane_len = sizes
    per = params_ref.shape[1]
    parts = cap // lane_len
    used = (1 + groups) * FEATS
    count_blocks = per // LANES

    def project_block(block, carry):
        params = load_params(params_ref, tile_scr, block)
        at = block * SUBS * used
        shared = params[0:3] + covariance(params) + [log_opacity(params[10])]
        for num, value in enumerate(shared[0:FEATS]):
            table[pl.ds(at + num, SUBS, stride=used), :] = value
        for group in range(groups):
            lines = shared[FEATS:]
            for view in range(2):
                lines = lines + view_colours(
                    params, [cam_ref[2 * group + view, k] for k in range(15)]
                )
            for num, value in enumerate(lines):
                table[pl.ds(at + (1 + group) * FEATS + num, SUBS, stride=used), :] = value
        return carry

    lax.fori_loop(0, per // (SUBS * LANES), project_block, 0)
    bounds = [jnp.int32(0)]
    for group in range(groups):
        bounds.append(
            lax.fori_loop(
                group * rows, (group + 1) * rows, lambda d, sum_: sum_ + counts_ref[0, d], bounds[-1]
            )
        )
    lane = lax.broadcasted_iota(jnp.int32, (FEATS, LANES), 1)

    def pick(block, carry):
        first = pl.multiple_of(block * LANES, LANES)
        names = jnp.broadcast_to(list_ref[0:1, pl.ds(first, LANES)], (SUBS, LANES))
        home, place = lane_spread(names)
        line_at = pl.multiple_of(block * PAIR, PAIR)
        queue[pl.ds(line_at, FEATS), :] = take_blocks(
            lambda num: table[num * used : num * used + FEATS, :], count_blocks, home, place
        )
        spot = first + lane
        for group in range(groups):
            low, high = bounds[group], bounds[group + 1]

            @pl.when((low < first + LANES) & (high > first))
            def _(group=group, low=low, high=high):
                at = (1 + group) * FEATS
                taken = take_blocks(
                    lambda num: table[num * used + at : num * used + at + FEATS, :],
                    count_blocks,
                    home,
                    place,
                )
                lines = pl.ds(line_at + FEATS, FEATS)
                queue[lines, :] = jnp.where((spot >= low) & (spot < high), taken, queue[lines, :])

        return carry

    lax.fori_loop(0, (bounds[-1] + LANES - 1) // LANES, pick, 0)
    lane_pair = lax.broadcasted_iota(jnp.int32, (PAIR, LANES), 1)

    def send_block(dest, start_at):
        count = counts_ref[0, dest]
        for part in range(parts):

            @pl.when(count > part * lane_len)
            def _(part=part):
                first = start_at + part * lane_len
                block, turn = first // LANES, first % LANES
                pieces = [
                    pltpu.roll(
                        queue[pl.ds(pl.multiple_of((block + step) * PAIR, PAIR), PAIR), :],
                        LANES - turn,
                        1,
                    )
                    for step in range(2)
                ]
                lines = jnp.where(lane_pair < LANES - turn, pieces[0], pieces[1])
                out_ref[dest, part * PAIR : (part + 1) * PAIR, :] = lines[:, 0:lane_len]

        return start_at + count

    lax.fori_loop(0, groups * rows, send_block, jnp.int32(0))


def split_three(value):
    first = value.astype(jnp.bfloat16).astype(jnp.float32)
    rest = value - first
    second = rest.astype(jnp.bfloat16).astype(jnp.float32)
    return [first, second, rest - second]


def in_two(value):
    high = value.astype(jnp.bfloat16).astype(jnp.float32)
    return [high, value - high]


def swap_grain(cells):
    sub = lax.broadcasted_iota(jnp.int32, (SUBS, LANES), 0)
    lane = lax.broadcasted_iota(jnp.int32, (SUBS, LANES), 1) // TILE
    for bit in (1, 2, 4):
        sub_bit, lane_bit = (sub & bit) != 0, (lane & bit) != 0
        from_high = pltpu.roll(pltpu.roll(cells, SUBS - bit, 0), bit * TILE, 1)
        from_low = pltpu.roll(pltpu.roll(cells, bit, 0), LANES - bit * TILE, 1)
        cells = jnp.where(sub_bit == lane_bit, cells, jnp.where(lane_bit, from_high, from_low))
    return cells


def longest(lens_ref, group):
    most = lens_ref[group * GROUP]
    for t in range(1, GROUP):
        most = jnp.maximum(most, lens_ref[group * GROUP + t])
    return most


def gather_slots(arrived_ref, slot_scr, lane_len):
    parts = arrived_ref.shape[1] // PAIR
    joined = LANES // lane_len

    def unpack(block, carry):
        line_at = pl.multiple_of(block * PAIR, PAIR)
        for k in range(joined):
            source = block * joined // parts + k
            part_at = pl.multiple_of(block * joined % parts * PAIR, PAIR)
            slot_scr[pl.ds(line_at, PAIR), k * lane_len : (k + 1) * lane_len] = arrived_ref[
                source, pl.ds(part_at, PAIR), :
            ]
        return carry

    lax.fori_loop(0, slot_scr.shape[0] // PAIR, unpack, 0)


def slot_lines(slot_scr, first):
    return [slot_scr[pl.ds(first * PAIR + num, SUBS, stride=PAIR), :] for num in range(PAIR)]


def render_kernel(
    sizes,
    place_ref,
    cam_ref,
    lens_ref,
    lens_rows_ref,
    names_ref,
    basis_ref,
    arrived_ref,
    image_ref,
    left_ref,
    shape_ref,
    alphas_ref,
    weights_ref,
    slot_scr,
    table,
    logs,
    feat_scr,
    pieces,
    mm,
):
    cap, lane_len, col_groups, list_len, image_width, image_height = sizes
    devices = arrived_ref.shape[0]
    blocks = list_len // STEP_ROWS
    count_blocks = devices * cap // LANES
    gather_slots(arrived_ref, slot_scr, lane_len)

    def project_block(step, carry):
        first = step * SUBS
        lines = slot_lines(slot_scr, first)
        logs[pl.ds(pl.multiple_of(first, SUBS), SUBS), :] = lines[OPACITY]
        for view in range(2):
            cam = [cam_ref[2 * place_ref[1] + view, k] for k in range(15)]
            feats = footprint(lines[0:3], lines[3:9], cam, image_width, image_height)
            feats = feats + lines[COLOUR + 3 * view : COLOUR + 3 * view + 3]
            for num, value in enumerate(feats):
                row_at = (view * count_blocks + first) * FEATS + num
                table[pl.ds(row_at, SUBS, stride=FEATS), :] = value
        return carry

    lax.fori_loop(0, count_blocks // SUBS, project_block, 0)
    centre_y = (place_ref[0] * TILE).astype(jnp.float32) + (TILE - 1) / 2.0
    sub = lax.broadcasted_iota(jnp.int32, (blocks, LANES), 0)
    lane = lax.broadcasted_iota(jnp.int32, (blocks, LANES), 1)
    zero = jnp.zeros((GROUP, LANES), jnp.float32)

    def one_group(group, carry):
        view, col_group = group // col_groups, group % col_groups
        most = longest(lens_ref, group)

        def fetch(block, inner):
            names = names_ref[pl.ds(group * blocks + block, 1), :]
            home, place = lane_spread(jnp.broadcast_to(names, (SUBS, LANES)))
            feat_at = pl.multiple_of(block * PAIR, PAIR)
            feat_scr[pl.ds(feat_at, FEATS), :] = take_blocks(
                lambda num: table[
                    pl.ds(pl.multiple_of((view * count_blocks + num) * FEATS, FEATS), FEATS), :
                ],
                count_blocks,
                home,
                place,
            )
            feat_scr[pl.ds(feat_at + FEATS, 1), :] = take_line(
                lambda num: logs[num * SUBS : (num + 1) * SUBS, :], count_blocks, home, place
            )
            return inner

        stepped((most + STEP_ROWS - 1) // STEP_ROWS, 2, fetch, 0)
        feats = [feat_scr[pl.ds(num, blocks, stride=PAIR), :] for num in range(FEATS)]
        log_o = feat_scr[pl.ds(FEATS, blocks, stride=PAIR), :]
        live = sub * STEP_ROWS + lane // GROUP < lens_rows_ref[pl.ds(group, 1), :]
        centre_x = ((col_group * GROUP + lane % GROUP) * TILE).astype(jnp.float32) + (
            TILE - 1
        ) / 2.0
        off_x, off_y = feats[0] - centre_x, feats[1] - centre_y
        lin_x = feats[2] * off_x + feats[3] * off_y
        lin_y = feats[4] * off_y + feats[3] * off_x
        coefs = [
            log_o - 0.5 * (off_x * lin_x + off_y * lin_y),
            lin_x,
            lin_y,
            -0.5 * feats[2],
            -feats[3],
            -0.5 * feats[4],
        ]
        coefs = [
            jnp.where(live, value, DEAD if num == 0 else 0.0) for num, value in enumerate(coefs)
        ]
        lines = [None] * COEF_ROWS
        for num, value in enumerate(coefs):
            for piece, part in enumerate(split_three(value)):
                lines[piece * 6 + num] = part
        for num in range(3):
            for piece, part in enumerate(split_three(jnp.where(live, feats[5 + num], 0.0))):
                lines[18 + piece * 3 + num] = part
        for num, value in enumerate(lines):
            pieces[pl.ds(num, blocks, stride=COEF_ROWS), :] = (
                jnp.zeros((blocks, LANES), jnp.float32) if value is None else value
            )
        for num, value in enumerate(feats[2:5] + [off_x, off_y]):
            shape_ref[num, pl.ds(pl.multiple_of(group * blocks, blocks), blocks), :] = jnp.where(
                live, value, 0.0
            )
        left_at = pl.multiple_of(group * blocks * LANES, LANES)
        for block in range(blocks):
            left_ref[pl.ds(left_at + block * LANES, LANES), :] = pieces[
                block * COEF_ROWS : (block + 1) * COEF_ROWS, :
            ].T.astype(jnp.bfloat16)
        expand(left_ref, basis_ref, mm, left_at)

        def entry(n, state):
            keep, colour = state
            row_at = pl.multiple_of(n * GROUP, GROUP)
            shade = [
                mm[pl.ds(row_at, GROUP), (2 + c) * LANES : (3 + c) * LANES] for c in range(3)
            ]
            new_keep, new_colour = [], []
            for half in range(2):
                lanes = slice(half * LANES, (half + 1) * LANES)
                alpha = jnp.exp(mm[pl.ds(row_at, GROUP), lanes])
                weight = keep[half] * alpha
                alphas_ref[pl.ds(left_at + row_at, GROUP), lanes] = alpha
                weights_ref[pl.ds(left_at + row_at, GROUP), lanes] = weight
                new_keep.append(keep[half] * (1.0 - alpha))
                new_colour.append([colour[half][c] + weight * shade[c] for c in range(3)])
            return new_keep, new_colour

        state = ([zero + 1.0] * 2, [[zero] * 3] * 2)
        _, colour = stepped(most, UNROLL, entry, state)
        for side in range(GROUP // SUBS):
            lane_at = pl.multiple_of(col_group * GROUP * TILE + side * LANES, LANES)
            for half in range(2):
                for c in range(3):
                    image_ref[view, c, half * SUBS : (half + 1) * SUBS, pl.ds(lane_at, LANES)] = (
                        swap_grain(colour[half][c][side * SUBS : (side + 1) * SUBS])
                    )
        return carry

    lax.fori_loop(0, 2 * col_groups, one_group, 0)


def expand(left_ref, basis_ref, mm, left_at):
    mm[...] = jnp.dot(
        left_ref[pl.ds(left_at, mm.shape[0]), :],
        basis_ref[...],
        preferred_element_type=jnp.float32,
    )


def back_kernel(
    sizes,
    place_ref,
    cam_ref,
    lens_ref,
    names_ref,
    basis_ref,
    moment_ref,
    left_ref,
    shape_ref,
    alphas,
    weights,
    arrived_ref,
    grad_ref,
    out_ref,
    mm,
    slopes,
    grad_scr,
    mom_scr,
    line_scr,
    masked,
    places,
    total_scr,
    slot_scr,
):
    cap, lane_len, col_groups, list_len, image_width, image_height = sizes
    devices = out_ref.shape[0]
    parts = cap // lane_len
    blocks = list_len // STEP_ROWS
    count_blocks = devices * cap // LANES
    joined = LANES // lane_len
    value_rows = count_blocks * 2 * FEATS
    total_scr[...] = jnp.zeros_like(total_scr)
    line_scr[...] = jnp.zeros_like(line_scr)
    grad_scr[...] = jnp.zeros_like(grad_scr)
    zero = jnp.zeros((GROUP, LANES), jnp.float32)
    sub = lax.broadcasted_iota(jnp.int32, (GROUP, LANES), 0)
    lane = lax.broadcasted_iota(jnp.int32, (GROUP, LANES), 1)
    own_tile = lane % GROUP == sub

    def one_group(group, carry):
        view, col_group = group // col_groups, group % col_groups
        most = longest(lens_ref, group)
        lane_at = pl.multiple_of(col_group * GROUP * TILE, LANES)
        grads = [
            [
                jnp.concatenate(
                    [
                        swap_grain(
                            grad_ref[
                                view,
                                c,
                                half * SUBS : (half + 1) * SUBS,
                                pl.ds(lane_at + side * LANES, LANES),
                            ]
                        )
                        for side in range(GROUP // SUBS)
                    ],
                    axis=0,
                )
                for c in range(3)
            ]
            for half in range(2)
        ]
        for half in range(2):
            for c in range(3):
                for piece, part in enumerate(in_two(grads[half][c])):
                    line = (piece * 3 + c) * GROUP
                    grad_scr[line : line + GROUP, half * LANES : (half + 1) * LANES] = part
        first = pl.multiple_of(group * blocks * LANES, LANES)
        expand(left_ref, basis_ref, mm, first)
        last = (most + UNROLL - 1) // UNROLL * UNROLL - 1

        def behind(step, seen):
            row_at = pl.multiple_of((last - step) * GROUP, GROUP)
            shade = [mm[pl.ds(row_at, GROUP), c * LANES : (c + 1) * LANES] for c in range(3)]
            new_seen = []
            for half in range(2):
                lanes = slice(half * LANES, (half + 1) * LANES)
                own = (
                    grads[half][0] * shade[0]
                    + grads[half][1] * shade[1]
                    + grads[half][2] * shade[2]
                )
                alpha = alphas[pl.ds(first + row_at, GROUP), lanes]
                weight = weights[pl.ds(first + row_at, GROUP), lanes]
                slopes[pl.ds(row_at, GROUP), lanes] = weight * (own - seen[half])
                new_seen.append(seen[half] * (1.0 - alpha) + alpha * own)
            return new_seen

        stepped(most, UNROLL, behind, [zero] * 2)
        left, right = [], []
        for value, columns in (
            (slopes[...], moment_ref[...]),
            (
                weights[pl.ds(first, blocks * LANES), :],
                grad_scr[...].T.astype(jnp.bfloat16),
            ),
        ):
            high = value.astype(jnp.bfloat16)
            left += [high, (value - high.astype(jnp.float32)).astype(jnp.bfloat16)]
            right += [columns, columns]
        total = jnp.dot(
            jnp.concatenate(left, axis=1),
            jnp.concatenate(right, axis=0),
            preferred_element_type=jnp.float32,
        )
        for block in range(blocks):
            turned = total[block * LANES : (block + 1) * LANES].T
            mom_scr[block * TILE : block * TILE + 8, :] = turned[6 * GROUP : 6 * GROUP + 8]
            for c in range(3):
                summed = (
                    turned[c * GROUP : (c + 1) * GROUP]
                    + turned[(3 + c) * GROUP : (4 + c) * GROUP]
                )
                mom_scr[block * TILE + 8 + c : block * TILE + 9 + c, :] = jnp.sum(
                    jnp.where(own_tile, summed, 0.0), axis=0, keepdims=True
                )
        mom = [mom_scr[pl.ds(num, blocks, stride=TILE), :] for num in range(11)]
        con_xx, con_xy, con_yy, off_x, off_y = [
            shape_ref[num, pl.ds(pl.multiple_of(group * blocks, blocks), blocks), :]
            for num in range(5)
        ]
        sum_x = off_x * mom[0] - mom[1]
        sum_y = off_y * mom[0] - mom[2]
        results = [
            -(con_xx * sum_x + con_xy * sum_y),
            -(con_yy * sum_y + con_xy * sum_x),
            -0.5 * (off_x * (sum_x - mom[1]) + mom[3]),
            -(off_x * sum_y - off_y * mom[1] + mom[4]),
            -0.5 * (off_y * (sum_y - mom[2]) + mom[5]),
        ] + mom[8:11]
        for num, value in enumerate(results + [mom[0]]):
            line_scr[pl.ds(num, blocks, stride=PAIR), :] = value

        def spread(step, inner):
            for k in range(JOIN):
                block = step * JOIN + k
                lanes = slice(k * LANES, (k + 1) * LANES)
                names = names_ref[pl.ds(group * blocks + block, 1), :]
                home, place = names // LANES, names % LANES
                line_at = pl.multiple_of(block * PAIR, PAIR)
                values = in_two(line_scr[pl.ds(line_at, FEATS), :])
                logs = in_two(line_scr[pl.ds(line_at + FEATS, 1), :])
                home_wide = jnp.broadcast_to(home, (2 * FEATS, LANES)).astype(jnp.bfloat16)
                pair = jnp.concatenate(values, axis=0).astype(jnp.bfloat16)
                for num in range(count_blocks):
                    masked[num * 2 * FEATS : (num + 1) * 2 * FEATS, lanes] = jnp.where(
                        home_wide == jnp.bfloat16(num), pair, jnp.bfloat16(0)
                    )
                rank = lax.broadcasted_iota(jnp.int32, (count_blocks, LANES), 0)
                for piece, value in enumerate(logs):
                    first = value_rows + piece * count_blocks
                    masked[first : first + count_blocks, lanes] = jnp.where(
                        rank == home, value, 0.0
                    ).astype(jnp.bfloat16)
                seat = lax.broadcasted_iota(jnp.int32, (LANES, LANES), 0)
                places[:, lanes] = jnp.where(seat == place, 1.0, 0.0).astype(jnp.bfloat16)
            total_scr[view] += lax.dot_general(
                masked[...],
                places[...],
                (((1,), (1,)), ((), ())),
                preferred_element_type=jnp.float32,
            )
            return inner

        width = JOIN * STEP_ROWS
        lax.fori_loop(0, (most + width - 1) // width, spread, 0)
        return carry

    lax.fori_loop(0, 2 * col_groups, one_group, 0)

    gather_slots(arrived_ref, slot_scr, lane_len)

    def pull_block(step, carry):
        first = step * SUBS
        lines = slot_lines(slot_scr, first)
        cams = [[cam_ref[2 * place_ref[1] + view, k] for k in range(15)] for view in range(2)]

        def both(*values):
            return [
                footprint(values[0:3], values[3:9], cam, image_width, image_height)
                for cam in cams
            ]

        cots = []
        log_sum = jnp.zeros((SUBS, LANES), jnp.float32)
        for view in range(2):
            row_at = first * 2 * FEATS
            cots.append(
                [
                    total_scr[view, pl.ds(row_at + num, SUBS, stride=2 * FEATS), :]
                    + total_scr[view, pl.ds(row_at + FEATS + num, SUBS, stride=2 * FEATS), :]
                    for num in range(FEATS)
                ]
            )
            for piece in range(2):
                row = pl.multiple_of(value_rows + piece * count_blocks + first, SUBS)
                log_sum = log_sum + total_scr[view, pl.ds(row, SUBS), :]
        _, pull = jax.vjp(both, *lines[0:9])
        results = list(pull([cot[0:5] for cot in cots])) + [log_sum] + cots[0][5:] + cots[1][5:]
        for num, value in enumerate(results):
            slot_scr[pl.ds(first * PAIR + num, SUBS, stride=PAIR), :] = value
        return carry

    lax.fori_loop(0, count_blocks // SUBS, pull_block, 0)

    def pack(block, carry):
        line_at = pl.multiple_of(block * PAIR, PAIR)
        for k in range(joined):
            source = block * joined // parts + k
            part_at = pl.multiple_of(block * joined % parts * PAIR, PAIR)
            out_ref[source, pl.ds(part_at, PAIR), :] = slot_scr[
                pl.ds(line_at, PAIR), k * lane_len : (k + 1) * lane_len
            ]
        return carry

    lax.fori_loop(0, count_blocks, pack, 0)


def owner_kernel(
    sizes,
    cam_ref,
    list_ref,
    counts_ref,
    params_ref,
    back_ref,
    out_hbm,
    out_ref,
    tile_scr,
    feat_scr,
    turn_scr,
    table,
    slots,
    out_sem,
):
    groups, rows, cap, lane_len = sizes
    count_params, per = params_ref.shape
    parts = cap // lane_len
    table[...] = jnp.zeros_like(table)
    turn_scr[...] = jnp.zeros_like(turn_scr)
    start = jnp.int32(0)
    for group in range(groups):
        turn_scr[PAIR : PAIR + 1, :] = jnp.full((1, LANES), 1.0 + group, jnp.float32)

        def take_block(t, start_at, group=group):
            dest = group * rows + t
            count = counts_ref[0, dest]

            for part in range(parts):
                turn_scr[0:PAIR, 0:lane_len] = back_ref[dest, part * PAIR : (part + 1) * PAIR, :]
                slots[part * lane_len : (part + 1) * lane_len, 0:24] = turn_scr[
                    :, 0:lane_len
                ].T

            def move(k, carry):
                spot = list_ref[0, start_at + k]
                table[pl.ds(spot, 1), :] = slots[pl.ds(k, 1), :]
                return carry

            rounded = (count + MOVES - 1) // MOVES * MOVES
            whole = jnp.where(start_at + rounded <= per, rounded, count // MOVES * MOVES)
            stepped(whole, MOVES, move, 0)
            lax.fori_loop(whole, count, move, 0)
            return start_at + count

        start = lax.fori_loop(0, rows, take_block, start)

    def clear(k, carry):
        table[pl.ds(list_ref[0, k], 1), :] = jnp.zeros((1, LANES), jnp.float32)
        return carry

    lax.fori_loop(start, jnp.minimum(start + MOVES, per), clear, 0)

    wide = SUBS * LANES

    def out_copy(block):
        lanes = pl.ds(pl.multiple_of(block * wide, wide), wide)
        return pltpu.make_async_copy(
            out_ref.at[:, lanes], out_hbm.at[:, lanes], out_sem.at[block]
        )

    def pull_block(block, carry):
        params = load_params(params_ref, tile_scr, block)
        for j in range(SUBS):
            row_at = pl.multiple_of(block * SUBS * LANES + j * LANES, LANES)
            feat_scr[j * 24 : (j + 1) * 24, :] = table[pl.ds(row_at, LANES), 0:24].T
        cots = [feat_scr[pl.ds(num, SUBS, stride=24), :] for num in range(PAIR + 1)]
        home = cots[PAIR]
        sent = home > 0.5
        cams = []
        for view in range(2):
            cam = []
            for k in range(15):
                value = jnp.full((SUBS, LANES), cam_ref[view, k], jnp.float32)
                for group in range(1, groups):
                    value = jnp.where(home > 0.5 + group, cam_ref[2 * group + view, k], value)
                cam.append(value)
            cams.append(cam)

        def both(*values):
            return (
                covariance(values)
                + [log_opacity(values[10])]
                + view_colours(values, cams[0])
                + view_colours(values, cams[1])
            )

        _, pull = jax.vjp(both, *params)
        grads = list(pull(cots[3:PAIR]))
        for num in range(3):
            grads[num] = grads[num] + cots[num]
        for num, value in enumerate(grads):
            tile_scr[pl.ds((num // SUBS) * SUBS * SUBS + num % SUBS, SUBS, stride=SUBS), :] = (
                jnp.where(sent, value, 0.0)
            )
        for band in range(0, count_params, SUBS):
            high = min(band + SUBS, count_params)
            for j in range(SUBS):
                lane_at = pl.multiple_of(block * SUBS * LANES + j * LANES, LANES)
                out_ref[band:high, pl.ds(lane_at, LANES)] = tile_scr[
                    band * SUBS + j * SUBS : band * SUBS + j * SUBS + high - band, :
                ]
        out_copy(block).start()
        return carry

    lax.fori_loop(0, per // wide, pull_block, 0)
    for block in range(per // wide):
        out_copy(block).wait()


def tap_rows(read, first, count):
    taps = window_taps()
    total = taps[5] * read(first + 5, count)
    for k in range(5):
        total = total + taps[k] * (read(first + k, count) + read(first + TAPS - 1 - k, count))
    return total


def blur_lanes(value, band_ref, pairs):
    pieces = [piece.astype(jnp.bfloat16) for piece in split_three(value)]
    total = 0.0
    for mine, other in pairs:
        total = total + jnp.dot(
            pieces[mine], band_ref[other], preferred_element_type=jnp.float32
        )
    return total


def truth_kernel(band_ref, above_ref, own_ref, below_ref, out_ref, tall, mixed):
    images = own_ref.shape[0]

    def one_image(m, carry):
        whole = jnp.concatenate([above_ref[m], own_ref[m], below_ref[m]], axis=0)
        for field, value in enumerate((whole, whole * whole)):
            tall[...] = value
            row_at = pl.multiple_of((field * images + m) * 2 * TILE, 2 * TILE)
            mixed[pl.ds(row_at, 2 * TILE), :] = tap_rows(
                lambda at, count: tall[at : at + count, :], 6, 2 * TILE
            )
        return carry

    lax.fori_loop(0, images, one_image, 0)
    out_ref[...] = blur_lanes(mixed[...], band_ref, FINE)


def loss_kernel(
    image_rows,
    row_ref,
    band_ref,
    truth_ref,
    true_above,
    true_own,
    true_below,
    above_ref,
    own_ref,
    below_ref,
    out_ref,
    tall,
    mixed,
    blurred,
    slim,
):
    images = own_ref.shape[0]
    tall_rows = 2 * TILE
    width = own_ref.shape[2]

    def one_image(m, carry):
        whole = jnp.concatenate([above_ref[m], own_ref[m], below_ref[m]], axis=0)
        true = jnp.concatenate([true_above[m], true_own[m], true_below[m]], axis=0)
        for field, value in enumerate((whole, whole * whole, whole * true)):
            tall[field] = value
            row_at = pl.multiple_of((field * images + m) * tall_rows, tall_rows)
            mixed[pl.ds(row_at, tall_rows), :] = tap_rows(
                lambda at, count, field=field: tall[field, at : at + count, :], 6, tall_rows
            )
        return carry

    lax.fori_loop(0, images, one_image, 0)
    blurred[...] = blur_lanes(mixed[...], band_ref, FINE)
    sub = lax.broadcasted_iota(jnp.int32, (tall_rows, width), 0)
    image_row = row_ref[0] * TILE + sub - 5
    inside = (image_row >= 0) & (image_row < image_rows) & (sub < TILE + 10)

    def one_map(m, carry):
        def field_of(ref, field):
            row_at = pl.multiple_of((field * images + m) * tall_rows, tall_rows)
            return ref[pl.ds(row_at, tall_rows), :]

        mean_one, both_one, cross = [field_of(blurred, field) for field in range(3)]
        mean_two, both_two = field_of(truth_ref, 0), field_of(truth_ref, 1)
        square_one, square_two = mean_one * mean_one, mean_two * mean_two
        mean_cross = mean_one * mean_two
        top_one = 2.0 * mean_cross + SSIM_ONE
        top_two = 2.0 * (cross - mean_cross) + SSIM_TWO
        low_one = square_one + square_two + SSIM_ONE
        low_two = (both_one - square_one) + (both_two - square_two) + SSIM_TWO
        inv_one, inv_two = 1.0 / low_one, 1.0 / low_two
        inv_both = inv_one * inv_two
        value = top_one * top_two * inv_both
        grads = [
            2.0 * mean_two * (top_two - top_one) * inv_both
            - 2.0 * mean_one * value * (inv_one - inv_two),
            -value * inv_two,
            2.0 * top_one * inv_both,
        ]
        for field, grad in enumerate(grads):
            tall[field, 0:tall_rows] = jnp.where(inside, grad, 0.0)
            row_at = pl.multiple_of((field * images + m) * TILE, TILE)
            slim[pl.ds(row_at, TILE), :] = tap_rows(
                lambda at, count, field=field: tall[field, at : at + count, :], 0, TILE
            )
        return carry

    lax.fori_loop(0, images, one_map, 0)
    spread = blur_lanes(slim[...], band_ref, COARSE).reshape(3, images, TILE, width)
    own, true = own_ref[...], true_own[...]
    gap = own - true
    out_ref[...] = (1.0 - SSIM_SHARE) * gap / jnp.sqrt(gap * gap + SMOOTH_EPS) - SSIM_SHARE * (
        spread[0] + 2.0 * own * spread[1] + true * spread[2]
    )


def band_matrix(width):
    taps = window_taps()
    band = np.zeros((width, width), np.float32)
    for k in range(TAPS):
        band += np.diag(np.full(width - abs(k - 5), taps[k], np.float32), k - 5)
    pieces = []
    for _ in range(3):
        pieces.append(band.astype(jnp.bfloat16))
        band = band - pieces[-1].astype(np.float32)
    return jnp.asarray(np.stack(pieces))


def pixel_basis():
    pixel = np.arange(TILE * TILE)
    x = (pixel % TILE) - (TILE - 1) / 2.0
    y = (pixel // TILE) - (TILE - 1) / 2.0
    return np.stack([np.ones_like(x), x, y, x * x, x * y, y * y])


def expand_matrix(first=0):
    terms = pixel_basis()
    matrix = np.zeros((COEF_ROWS, 5 * LANES), np.float32)
    for piece in range(3):
        matrix[piece * 6 : piece * 6 + 6, 0 : 2 * LANES] = terms
        for c in range(3):
            matrix[18 + piece * 3 + c, (2 + c) * LANES : (3 + c) * LANES] = 1.0
    return jnp.asarray(matrix[:, first:], jnp.bfloat16)


def moment_matrix():
    matrix = np.zeros((2 * LANES, LANES), np.float32)
    matrix[:, 6 * GROUP : 6 * GROUP + 6] = pixel_basis().T
    return jnp.asarray(matrix, jnp.bfloat16)


def smem():
    return pl.BlockSpec(memory_space=pltpu.SMEM)


def vmem():
    return pl.BlockSpec(memory_space=pltpu.VMEM)


def scratch(*shape):
    return pltpu.VMEM(shape, jnp.float32)


def run(kernel, megabytes, out_shapes, in_specs, scratches, *operands, out_specs=None):
    return pl.pallas_call(
        kernel,
        out_shape=out_shapes,
        in_specs=in_specs,
        out_specs=out_specs or jax.tree.map(lambda _: vmem(), out_shapes),
        scratch_shapes=scratches,
        compiler_params=pltpu.CompilerParams(vmem_limit_bytes=megabytes << 20),
    )(*operands)


def shards(params, send_list, send_counts, camera, ground_truth, tile_lists, list_lengths):
    devices = lax.axis_size(("view", "tile"))
    row_devices = lax.axis_size("tile")
    groups = lax.axis_size("view")
    count_params, per_device = params.shape
    capacity = per_device // devices
    tile_cols, list_len = tile_lists.shape[2:]
    col_groups = tile_cols // GROUP
    blocks = list_len // STEP_ROWS
    tile_row = lax.axis_index("tile")
    image_width = float(ground_truth.shape[3])
    image_height = float(ground_truth.shape[2] * row_devices)
    lane_len = min(capacity, LANES)
    sent_shape = jax.ShapeDtypeStruct(
        (devices, capacity // lane_len * PAIR, lane_len), jnp.float32
    )
    count_blocks = per_device // LANES
    cams = camera_table(camera)

    flat_lengths = list_lengths.reshape(-1)
    entry_rank = jnp.arange(list_len, dtype=jnp.int32)
    tile_num = jnp.arange(2 * tile_cols, dtype=jnp.int32)
    lists = jnp.where(
        entry_rank[None, :] < flat_lengths[:, None],
        tile_lists.reshape(2 * tile_cols, list_len),
        per_device + tile_num[:, None] % GROUP,
    )
    lens_rows = jnp.tile(flat_lengths.reshape(-1, GROUP), (1, LANES // GROUP))

    width = ground_truth.shape[3]
    true_own = ground_truth.reshape(-1, TILE, width)
    true_above = from_behind(true_own, "tile", 1)
    true_below = from_behind(true_own, "tile", -1)
    band = band_matrix(width)
    truth_rows = 2 * true_own.shape[0] * 2 * TILE
    truth_blur = run(
        truth_kernel,
        16,
        jax.ShapeDtypeStruct((truth_rows, width), jnp.float32),
        [vmem()] * 4,
        [scratch(3 * TILE, width), scratch(truth_rows, width)],
        band,
        true_above,
        true_own,
        true_below,
    )

    own_sizes = (groups, row_devices, capacity, lane_len)
    sent = run(
        lambda *refs: source_kernel(own_sizes, *refs),
        24,
        sent_shape,
        [smem(), smem(), vmem(), vmem()],
        [
            scratch(SUBS * SUBS * SUBS, LANES),
            scratch(count_blocks * (1 + groups) * FEATS, LANES),
            scratch((count_blocks + 1) * PAIR, LANES),
        ],
        cams,
        send_counts,
        send_list,
        params,
    )
    arrived = lax.all_to_all(sent, ("view", "tile"), split_axis=0, concat_axis=0, tiled=True)

    arrived, truth_blur = lax.optimization_barrier((arrived, truth_blur))
    tile_sizes = (capacity, lane_len, col_groups, list_len, image_width, image_height)
    place = jnp.stack([tile_row, lax.axis_index("view")])
    entries = 2 * tile_cols * list_len
    names = lists.reshape(-1, GROUP, list_len).transpose(0, 2, 1).reshape(-1, LANES)
    rendered, left, shapes, alphas, weights = run(
        lambda *refs: render_kernel(tile_sizes, *refs),
        27,
        (
            jax.ShapeDtypeStruct(ground_truth.shape, jnp.float32),
            jax.ShapeDtypeStruct((entries, COEF_ROWS), jnp.bfloat16),
            jax.ShapeDtypeStruct((5, entries // LANES, LANES), jnp.float32),
            jax.ShapeDtypeStruct((entries, 2 * LANES), jnp.float32),
            jax.ShapeDtypeStruct((entries, 2 * LANES), jnp.float32),
        ),
        [smem(), smem(), smem(), vmem(), vmem(), vmem(), vmem()],
        [
            scratch(count_blocks * PAIR, LANES),
            scratch(2 * per_device // LANES * FEATS, LANES),
            scratch(count_blocks, LANES),
            scratch(blocks * PAIR, LANES),
            scratch(blocks * COEF_ROWS, LANES),
            scratch(blocks * LANES, 5 * LANES),
        ],
        place,
        cams,
        flat_lengths,
        lens_rows,
        names,
        expand_matrix(),
        arrived,
    )

    images = rendered.reshape(true_own.shape)
    count = images.shape[0]
    grad_image = run(
        lambda *refs: loss_kernel(TILE * row_devices, *refs),
        16,
        jax.ShapeDtypeStruct(images.shape, jnp.float32),
        [smem()] + [vmem()] * 8,
        [
            scratch(3, 3 * TILE, width),
            scratch(3 * count * 2 * TILE, width),
            scratch(3 * count * 2 * TILE, width),
            scratch(3 * count * TILE, width),
        ],
        place,
        band,
        truth_blur,
        true_above,
        true_own,
        true_below,
        from_behind(images, "tile", 1),
        images,
        from_behind(images, "tile", -1),
    ).reshape(ground_truth.shape)

    spread_rows = count_blocks * (2 * FEATS + 2)
    grad_slots = run(
        lambda *refs: back_kernel(tile_sizes, *refs),
        31,
        sent_shape,
        [smem()] * 3 + [vmem()] * 9,
        [
            scratch(blocks * LANES, 3 * LANES),
            scratch(blocks * LANES, 2 * LANES),
            scratch(LANES, 2 * LANES),
            scratch(blocks * TILE, LANES),
            scratch(blocks * PAIR, LANES),
            pltpu.VMEM((spread_rows, JOIN * LANES), jnp.bfloat16),
            pltpu.VMEM((LANES, JOIN * LANES), jnp.bfloat16),
            scratch(2, spread_rows, LANES),
            scratch(count_blocks * PAIR, LANES),
        ],
        place,
        cams,
        flat_lengths,
        names,
        expand_matrix(2 * LANES),
        moment_matrix(),
        left,
        shapes,
        alphas,
        weights,
        arrived,
        grad_image,
    )
    returned = lax.all_to_all(
        grad_slots, ("view", "tile"), split_axis=0, concat_axis=0, tiled=True
    )
    return run(
        lambda *refs: owner_kernel(own_sizes, *refs),
        24,
        jax.ShapeDtypeStruct(params.shape, jnp.float32),
        [smem(), smem(), smem(), vmem(), vmem()],
        [
            scratch(*params.shape),
            scratch(SUBS * SUBS * SUBS, LANES),
            scratch(SUBS * 24, LANES),
            scratch(24, LANES),
            scratch(per_device, LANES),
            scratch(capacity, LANES),
            pltpu.SemaphoreType.DMA((count_blocks // SUBS,)),
        ],
        cams,
        send_list,
        send_counts,
        params,
        returned,
        out_specs=pl.BlockSpec(memory_space=pl.ANY),
    )


def solution(mesh):
    in_specs = (
        P(None, ("view", "tile")),
        P(("view", "tile"), None),
        P(("view", "tile"), None),
        P(),
        P("view", None, "tile", None),
        P("view", "tile", None, None),
        P("view", "tile", None),
    )
    out_specs = P(None, ("view", "tile"))
    return jax.shard_map(shards, mesh=mesh, in_specs=in_specs, out_specs=out_specs, check_vma=False)
```
